32 devices in a mesh: ctx: 16 (over z, y, x), fsdp: 2 (over core).
Axes of the slice: x: 2, y: 2, z: 4, core: 2. Of those that a mesh axis runs over, the one named last changes fastest.
Arguments:
- tokens: bfloat16 [2, 4096, 1024], P('fsdp', 'ctx'), may hold values from -6 to 6
- cotangent: bfloat16 [2, 4096, 1024], P('fsdp', 'ctx'), may hold values from -6 to 6
- sequence_adapter_index: int32 [2], P('fsdp'), may hold values from 0 to 1, as said below
- query_key_value_weight: bfloat16 [1024, 3072], P('fsdp'), may hold values from -0.1875 to 0.1875
- output_weight: bfloat16 [1024, 1024], P('fsdp'), may hold values from -6 to 6
- first_feed_weight: bfloat16 [1024, 4096], P('fsdp'), may hold values from -0.1875 to 0.1875
- second_feed_weight: bfloat16 [4096, 1024], P('fsdp'), may hold values from -0.09375 to 0.09375
- biases: float32 [5, 1024], replicated, may hold values from -1.25 to 1.25
- value_bias_vector: float32 [1024], replicated, may hold values from -0.0625 to 0.0625
- first_feed_bias: float32 [4096], replicated, may hold values from -1.25 to 1.25
- norm_gain_pair: float32 [2, 1024], replicated, may hold values from 0.5 to 1.5
- adapter_down_factors: bfloat16 [8, 4, 16, 1024], replicated, may hold values from -0.1875 to 0.1875
- output_down_factor: bfloat16 [8, 16, 1024], replicated, may hold values from -6 to 6
- adapter_up_factors: bfloat16 [8, 5, 16, 1024], replicated, may hold values from -0.75 to 0.75
- hidden_up_factor: bfloat16 [8, 16, 4096], replicated, may hold values from -0.75 to 0.75
- hidden_down_factor: bfloat16 [8, 16, 4096], replicated, may hold values from -0.09375 to 0.09375
Outputs:
- outcome: bfloat16 [2, 4096, 1024], P('fsdp', 'ctx')
- grad_tokens: float32 [2, 4096, 1024], P('fsdp', 'ctx')
- grad_lora_down: float32 [8, 4, 16, 1024], replicated
- grad_lora_out_down: float32 [8, 16, 1024], replicated
- grad_lora_up: float32 [8, 5, 16, 1024], replicated
- grad_hid_up: float32 [8, 16, 4096], replicated
- grad_hid_down: float32 [8, 16, 4096], replicated
The draws below stay inside these ranges and needn't reach their ends.
Inputs may be any that keep to these rules, and one draw needn't show every extreme that they name: `sequence_adapter_index`: each of the values 0 .. min(8, 2) - 1 is used by the same number of sequences: 0 where 2 is 8 or more, else one.
All inputs are finite; a program needn't handle non-finite values.
Results may differ from the reference program's by a relative error of at most 0.023.
Values may be sent and summed in bfloat16 or wider, within the bound.
A program may use at most 256 MiB of HBM per device.

```python
import jax
import jax.numpy as jnp
from jax import lax

MODEL_DIM = 1024
H = 16
HD = 64
FF = 4096
ADAPTER_RANK = 16
ADAPTER_TOTAL = 8
LOCAL_POSITIONS = 256
SEQS = 2
LEN = 4096
N_CTX = 16


def draw_sequence_adapter_index(key, part):
    key = jax.random.fold_in(key, 7)
    base_order = jnp.arange(SEQS, dtype=jnp.int32) % ADAPTER_TOTAL
    return jax.random.permutation(key, base_order).astype(jnp.int32)


def steps_of(rng, extent, cuts, smallest, largest):
    def one(axis_at, shards_of):
        draws = jax.random.uniform(jax.random.fold_in(jax.random.fold_in(rng, 6), axis_at), (shards_of,), jnp.float32, smallest / len(cuts), largest / len(cuts))
        return jnp.repeat(jnp.exp(draws), extent[axis_at] // shards_of).reshape((-1,) + (1,) * (len(extent) - axis_at - 1))

    level = one(*cuts[0])
    for cut in cuts[1:]:
        level = level * one(*cut)
    return level


def normal_values(rng, shape, scale, reach, split=(), held_as=jnp.bfloat16):
    factor_of = steps_of(rng, shape, split, -0.22, 0.18) if split else 1.0
    array = jax.random.normal(rng, shape, jnp.float32) * scale * factor_of
    return jnp.minimum(jnp.maximum(array, -reach), reach).astype(held_as)


def setup_inputs(seed: int = 0) -> dict:
    streams_of = jax.random.split(jax.random.key(seed), 17)
    tokens = normal_values(streams_of[0], (SEQS, LEN, MODEL_DIM), 1.0, 6.0, ((0, 2), (1, 16)))
    cotangent = normal_values(streams_of[1], (SEQS, LEN, MODEL_DIM), 1.0, 6.0, ((0, 2), (1, 16)))
    sequence_adapter_index = draw_sequence_adapter_index(jax.random.fold_in(streams_of[16], 71), 0)
    query_key_value_weight = normal_values(streams_of[3], (MODEL_DIM, 3 * MODEL_DIM), MODEL_DIM ** -0.5, 0.1875, ((0, 2),))
    output_weight = normal_values(streams_of[4], (MODEL_DIM, MODEL_DIM), (0.5 * (LOCAL_POSITIONS * N_CTX) ** 0.5 * MODEL_DIM ** -0.5), 6.0, ((0, 2),))
    first_feed_weight = normal_values(streams_of[5], (MODEL_DIM, FF), MODEL_DIM ** -0.5, 0.1875, ((0, 2),))
    second_feed_weight = normal_values(streams_of[6], (FF, MODEL_DIM), FF ** -0.5, 0.09375, ((0, 2),))
    biases = normal_values(streams_of[7], (5, MODEL_DIM), 0.2, 1.25, (), jnp.float32)
    value_bias_vector = normal_values(streams_of[8], (MODEL_DIM,), 0.01, 0.0625, (), jnp.float32)
    first_feed_bias = normal_values(streams_of[9], (FF,), 0.2, 1.25, (), jnp.float32)
    norm_gain_pair = jnp.clip(1.0 + 0.1 * jax.random.normal(streams_of[10], (2, MODEL_DIM), jnp.float32), 0.5, 1.5)
    adapter_down_factors = normal_values(streams_of[11], (ADAPTER_TOTAL, 4, ADAPTER_RANK, MODEL_DIM), MODEL_DIM ** -0.5, 0.1875)
    output_down_factor = normal_values(streams_of[12], (ADAPTER_TOTAL, ADAPTER_RANK, MODEL_DIM), (0.5 * (LOCAL_POSITIONS * N_CTX) ** 0.5 * MODEL_DIM ** -0.5), 6.0)
    adapter_up_factors = normal_values(streams_of[13], (ADAPTER_TOTAL, 5, ADAPTER_RANK, MODEL_DIM), (4 * ADAPTER_RANK) ** -0.5, 0.75)
    hidden_up_factor = normal_values(streams_of[14], (ADAPTER_TOTAL, ADAPTER_RANK, FF), (4 * ADAPTER_RANK) ** -0.5, 0.75)
    hidden_down_factor = normal_values(streams_of[15], (ADAPTER_TOTAL, ADAPTER_RANK, FF), FF ** -0.5, 0.09375)
    return dict(tokens=tokens, cotangent=cotangent, sequence_adapter_index=sequence_adapter_index, query_key_value_weight=query_key_value_weight, output_weight=output_weight, first_feed_weight=first_feed_weight, second_feed_weight=second_feed_weight, biases=biases, value_bias_vector=value_bias_vector, first_feed_bias=first_feed_bias, norm_gain_pair=norm_gain_pair, adapter_down_factors=adapter_down_factors, output_down_factor=output_down_factor, adapter_up_factors=adapter_up_factors, hidden_up_factor=hidden_up_factor, hidden_down_factor=hidden_down_factor)


@jax.custom_vjp
def low(v):
    return lax.optimization_barrier(v.astype(jnp.bfloat16)).astype(jnp.float32)

@jax.custom_vjp
def low_back(v):
    return v

def low_keep(v):
    return (low(v), None)

def low_pass(kept, grad):
    return (grad,)

def back_keep(v):
    return (v, None)

def back_low(kept, grad):
    return (low(grad),)
low.defvjp(low_keep, low_pass)
low_back.defvjp(back_keep, back_low)
EPSILON = 1e-05

def exact_dot(left, right):
    return jnp.dot(left, right, precision=lax.Precision.HIGHEST, preferred_element_type=jnp.float32)

def round_both(value):
    return low(low_back(value))

def layer_norm(value, gain, shift):
    center = value - lax.optimization_barrier(jnp.mean(value, -1, keepdims=True))
    spread = lax.optimization_barrier(jnp.mean(center * center, -1, keepdims=True))
    return center * lax.rsqrt(spread + EPSILON) * gain + shift

def sequence_layer(seq_tokens, selected_rows, frozen, factor_table):
    query_key_value_weight, output_weight, first_feed_weight, second_feed_weight, biases, value_bias_vector, first_feed_bias, norm_gain_pair = frozen
    adapter_down_factors, output_down_factor, adapter_up_factors, hidden_up_factor, hidden_down_factor = factor_table
    selected_down = adapter_down_factors[selected_rows]
    selected_output = output_down_factor[selected_rows]
    selected_up = adapter_up_factors[selected_rows]
    hup_sel = hidden_up_factor[selected_rows]
    hdown_sel = hidden_down_factor[selected_rows]
    query_rank = low_back(exact_dot(seq_tokens, selected_down[0].T))
    key_rank = low_back(exact_dot(seq_tokens, selected_down[1].T))
    value_rank = low_back(exact_dot(seq_tokens, selected_down[2].T))
    projected = exact_dot(seq_tokens, query_key_value_weight)
    queries = round_both((projected[:, :MODEL_DIM] + biases[0] + exact_dot(query_rank, selected_up[0])) * 0.125)
    keys = round_both(projected[:, MODEL_DIM:2 * MODEL_DIM] + exact_dot(key_rank, selected_up[1]))
    values = round_both(projected[:, 2 * MODEL_DIM:] + value_bias_vector + exact_dot(value_rank, selected_up[2]))
    keys_heads = keys.reshape(LEN, H, HD)
    values_heads = values.reshape(LEN, H, HD)
    rows_block = min(512, LEN)

    def attend(query_block):
        scores = low_back(jnp.einsum('qhd,khd->hqk', query_block, keys_heads, precision=lax.Precision.HIGHEST))
        weights = low(jax.nn.softmax(scores, axis=-1))
        return jnp.einsum('hqk,khd->qhd', weights, values_heads, precision=lax.Precision.HIGHEST).reshape(rows_block, MODEL_DIM)
    context = lax.map(jax.checkpoint(attend), queries.reshape(LEN // rows_block, rows_block, H, HD)).reshape(LEN, MODEL_DIM)
    context_low = round_both(context)
    out_rank = low_back(exact_dot(context_low, selected_output.T))
    branch = low_back(exact_dot(context_low, output_weight) + biases[1] + exact_dot(out_rank, selected_up[3]))
    normed = layer_norm(seq_tokens + branch, norm_gain_pair[0], biases[3])
    normed_low = round_both(normed)
    first_rank = low_back(exact_dot(normed_low, selected_down[3].T))
    hidden_pre = low_back(exact_dot(normed_low, first_feed_weight) + first_feed_bias + exact_dot(first_rank, hup_sel))
    act_low = round_both(jax.nn.gelu(hidden_pre, approximate=False))
    second_rank = low_back(exact_dot(act_low, hdown_sel.T))
    mixed_out = low_back(exact_dot(act_low, second_feed_weight) + biases[2] + exact_dot(second_rank, selected_up[4]))
    return layer_norm(normed + mixed_out, norm_gain_pair[1], biases[4])

def reference(tokens, cotangent, sequence_adapter_index, query_key_value_weight, output_weight, first_feed_weight, second_feed_weight, biases, value_bias_vector, first_feed_bias, norm_gain_pair, adapter_down_factors, output_down_factor, adapter_up_factors, hidden_up_factor, hidden_down_factor):
    frozen = tuple((input_array.astype(jnp.float32) for input_array in (query_key_value_weight, output_weight, first_feed_weight, second_feed_weight, biases, value_bias_vector, first_feed_bias, norm_gain_pair)))
    input_factors = tuple((input_array.astype(jnp.float32) for input_array in (adapter_down_factors, output_down_factor, adapter_up_factors, hidden_up_factor, hidden_down_factor)))

    def forward(layer_in, factor_table):

        def one_sequence(seq_tokens, selected_rows):
            return sequence_layer(seq_tokens, selected_rows, frozen, factor_table)
        saved = jax.checkpoint(one_sequence)

        def apply_one(packed):
            return saved(packed[0], packed[1])
        return lax.map(apply_one, (layer_in, sequence_adapter_index))
    outcome, pullback = jax.vjp(forward, tokens.astype(jnp.float32), input_factors)
    grad_tokens, grad_factors = pullback(cotangent.astype(jnp.float32))
    return (outcome.astype(jnp.bfloat16), grad_tokens, grad_factors[0], grad_factors[1], grad_factors[2], grad_factors[3], grad_factors[4])
```

```python
import functools

import jax
import jax.numpy as jnp
from jax import lax
from jax.experimental import pallas as pl
from jax.experimental.pallas import tpu as pltpu
from jax.sharding import PartitionSpec as P

H = 16


EPSILON = 1e-05
HIGHEST = lax.Precision.HIGHEST


def exact_sum(form, left, right):
    return jnp.einsum(form, left, right, precision=HIGHEST, preferred_element_type=jnp.float32)


def plain_sum(form, left, right):
    return jnp.einsum(form, left, right, preferred_element_type=jnp.float32)


def layer_norm(value, gain, shift):
    center = value - jnp.mean(value, -1, keepdims=True)
    spread = jnp.mean(center * center, -1, keepdims=True)
    return center * lax.rsqrt(spread + EPSILON) * gain + shift


def attn_weights(query_key_value_weight, output_weight):
    return (
        lax.all_gather(query_key_value_weight, "fsdp", axis=0, tiled=True),
        lax.all_gather(output_weight, "fsdp", axis=0, tiled=True),
    )


def mlp_weights(first_feed_weight, second_feed_weight):
    return (
        lax.all_gather(first_feed_weight, "fsdp", axis=0, tiled=True),
        lax.all_gather(second_feed_weight, "fsdp", axis=0, tiled=True),
    )


def to_heads(input_array):
    return input_array.reshape(
        input_array.shape[0], input_array.shape[1], H, input_array.shape[2] // H
    )


def row_block(input_array, block_index, block_rows):
    return lax.dynamic_slice_in_dim(input_array, block_index * block_rows, block_rows, 1)


def block_grads(queries, grad_out, log_total, row_delta, keys_blk, values_blk):
    scores = plain_sum("sqhd,skhd->shqk", queries, keys_blk)
    probs = jnp.exp(scores - log_total[..., None])
    prob_low = probs.astype(jnp.bfloat16)
    grad_probs = plain_sum("sqhd,skhd->shqk", grad_out, values_blk)
    grad_scores = (probs * (grad_probs - row_delta[..., None])).astype(jnp.bfloat16)
    return (prob_low, grad_scores)


def attention_forward(queries_heads, keys_heads, values_heads):
    seq_count, row_count, head_count, head_size = queries_heads.shape
    length = keys_heads.shape[1]
    block_rows = min(512, length)
    block_count = length // block_rows

    def max_step(running, block_index):
        running_max, running_total = running
        scores = plain_sum(
            "sqhd,skhd->shqk", queries_heads, row_block(keys_heads, block_index, block_rows)
        )
        new_max = jnp.maximum(running_max, jnp.max(scores, -1))
        running_total = running_total * jnp.exp(running_max - new_max) + jnp.sum(
            jnp.exp(scores - new_max[..., None]), -1
        )
        return ((new_max, running_total), None)

    start_max = jnp.full((seq_count, head_count, row_count), -1e30, jnp.float32)
    start_total = jnp.zeros((seq_count, head_count, row_count), jnp.float32)
    (final_max, final_total), unused = lax.scan(
        max_step, (start_max, start_total), jnp.arange(block_count)
    )
    log_total = final_max + jnp.log(final_total)

    def value_step(running, block_index):
        scores = plain_sum(
            "sqhd,skhd->shqk", queries_heads, row_block(keys_heads, block_index, block_rows)
        )
        prob_low = jnp.exp(scores - log_total[..., None]).astype(jnp.bfloat16)
        return (
            running
            + plain_sum(
                "shqk,skhd->sqhd", prob_low, row_block(values_heads, block_index, block_rows)
            ),
            None,
        )

    context, unused = lax.scan(
        value_step, jnp.zeros(queries_heads.shape, jnp.float32), jnp.arange(block_count)
    )
    return (context, log_total)


def gather_body(
    tokens,
    cotangent,
    sequence_adapter_index,
    query_key_value_weight,
    output_weight,
    first_feed_weight,
    second_feed_weight,
    biases,
    value_bias_vector,
    first_feed_bias,
    norm_gain_pair,
    adapter_down_factors,
    output_down_factor,
    adapter_up_factors,
    hidden_up_factor,
    hidden_down_factor,
):
    seq_count, row_count, model_width = tokens.shape
    adapter_number = adapter_down_factors.shape[0]
    picker = (
        sequence_adapter_index[:, None] == jnp.arange(adapter_number, dtype=jnp.int32)[None, :]
    ).astype(jnp.float32)

    def select_adapter(table):
        return jnp.einsum("sa,a...->s...", picker, table.astype(jnp.float32), precision=HIGHEST)

    def to_adapters(per_seq):
        return jnp.einsum("sa,s...->a...", picker, per_seq, precision=HIGHEST)

    selected_down = select_adapter(adapter_down_factors)
    selected_output = select_adapter(output_down_factor)
    selected_up = select_adapter(adapter_up_factors)
    hup_sel = select_adapter(hidden_up_factor)
    hdown_sel = select_adapter(hidden_down_factor)
    down_low = selected_down.astype(jnp.bfloat16)
    out_low = selected_output.astype(jnp.bfloat16)
    hdown_low = hdown_sel.astype(jnp.bfloat16)
    wqkv_full, wout_full = attn_weights(query_key_value_weight, output_weight)
    projected = plain_sum("std,de->ste", tokens, wqkv_full)
    down_att = plain_sum("std,sjrd->sjtr", tokens, down_low[:, :3])
    lifted = exact_sum("sjtr,sjrd->sjtd", down_att, selected_up[:, :3])
    queries = ((projected[..., :model_width] + biases[0] + lifted[:, 0]) * 0.125).astype(
        jnp.bfloat16
    )
    keys_own = (projected[..., model_width : 2 * model_width] + lifted[:, 1]).astype(jnp.bfloat16)
    values_own = (projected[..., 2 * model_width :] + value_bias_vector + lifted[:, 2]).astype(
        jnp.bfloat16
    )
    keys_all, values_all = (
        lax.all_gather(keys_own, "ctx", axis=1, tiled=True),
        lax.all_gather(values_own, "ctx", axis=1, tiled=True),
    )
    queries_heads = to_heads(queries)
    keys_heads = to_heads(keys_all)
    values_heads = to_heads(values_all)
    context, log_total = attention_forward(queries_heads, keys_heads, values_heads)
    context = context.reshape(seq_count, row_count, model_width)
    context_low = context.astype(jnp.bfloat16)
    down_out = plain_sum("std,srd->str", context_low, out_low)
    branch = (
        plain_sum("std,de->ste", context_low, wout_full)
        + biases[1]
        + exact_sum("str,srd->std", down_out, selected_up[:, 3])
    )

    def first_norm(value):
        return layer_norm(value, norm_gain_pair[0], biases[3])

    def second_norm(value):
        return layer_norm(value, norm_gain_pair[1], biases[4])

    def gelu_exact(value):
        return jax.nn.gelu(value, approximate=False)

    normed, norm_back = jax.vjp(first_norm, tokens.astype(jnp.float32) + branch)
    normed_low = normed.astype(jnp.bfloat16)
    wfc1_full, wfc2_full = mlp_weights(first_feed_weight, second_feed_weight)
    down_fc1 = plain_sum("std,srd->str", normed_low, down_low[:, 3])
    hidden_pre = (
        plain_sum("std,df->stf", normed_low, wfc1_full)
        + first_feed_bias
        + exact_sum("str,srf->stf", down_fc1, hup_sel)
    )
    activated, gelu_back = jax.vjp(gelu_exact, hidden_pre)
    act_low = activated.astype(jnp.bfloat16)
    down_fc2 = plain_sum("stf,srf->str", act_low, hdown_low)
    mixed_out = (
        plain_sum("stf,fd->std", act_low, wfc2_full)
        + biases[2]
        + exact_sum("str,srd->std", down_fc2, selected_up[:, 4])
    )
    outcome, out_back = jax.vjp(second_norm, normed + mixed_out)
    (grad_sum2,) = out_back(cotangent.astype(jnp.float32))
    grad_mixed = grad_sum2.astype(jnp.bfloat16)
    grad_up_fc2 = exact_sum("str,std->srd", down_fc2, grad_mixed)
    grad_rank_fc2 = exact_sum("std,srd->str", grad_mixed, selected_up[:, 4]).astype(jnp.bfloat16)
    grad_hdown = plain_sum("str,stf->srf", grad_rank_fc2, act_low)
    wfc1_full, wfc2_full = mlp_weights(first_feed_weight, second_feed_weight)
    grad_act = (
        plain_sum("std,fd->stf", grad_mixed, wfc2_full)
        + plain_sum("str,srf->stf", grad_rank_fc2, hdown_low)
    ).astype(jnp.bfloat16)
    (grad_hidden,) = gelu_back(grad_act.astype(jnp.float32))
    grad_hidden = grad_hidden.astype(jnp.bfloat16)
    grad_hup = exact_sum("str,stf->srf", down_fc1, grad_hidden)
    grad_rank_fc1 = exact_sum("stf,srf->str", grad_hidden, hup_sel).astype(jnp.bfloat16)
    grad_down_fc1 = plain_sum("str,std->srd", grad_rank_fc1, normed_low)
    grad_normed_low = (
        plain_sum("stf,df->std", grad_hidden, wfc1_full)
        + plain_sum("str,srd->std", grad_rank_fc1, down_low[:, 3])
    ).astype(jnp.bfloat16)
    (grad_resid,) = norm_back(grad_sum2 + grad_normed_low.astype(jnp.float32))
    mlp_hup = to_adapters(grad_hup)
    mlp_hdown = to_adapters(grad_hdown)
    mlp_fc1 = to_adapters(grad_down_fc1)
    mlp_fc2 = to_adapters(grad_up_fc2)
    mlp_hup, mlp_hdown, mlp_fc1, mlp_fc2 = lax.psum(
        (mlp_hup, mlp_hdown, mlp_fc1, mlp_fc2), ("ctx", "fsdp")
    )
    grad_branch = grad_resid.astype(jnp.bfloat16)
    grad_up_out = exact_sum("str,std->srd", down_out, grad_branch)
    grad_rank_out = exact_sum("std,srd->str", grad_branch, selected_up[:, 3]).astype(jnp.bfloat16)
    grad_out_down = plain_sum("str,std->srd", grad_rank_out, context_low)
    wqkv_full, wout_full = attn_weights(query_key_value_weight, output_weight)
    grad_context = (
        plain_sum("std,ed->ste", grad_branch, wout_full)
        + plain_sum("str,srd->std", grad_rank_out, out_low)
    ).astype(jnp.bfloat16)
    row_delta = jnp.sum(to_heads(grad_context.astype(jnp.float32) * context), -1)
    delta_heads = jnp.swapaxes(row_delta, 1, 2)
    grad_heads = to_heads(grad_context)
    length = keys_all.shape[1]
    block_rows = min(512, length)
    block_count = length // block_rows

    def key_step(block_index, running):
        grad_query, grad_key, grad_value = running
        keys_blk = row_block(keys_heads, block_index, block_rows)
        values_blk = row_block(values_heads, block_index, block_rows)
        prob_low, grad_scores = block_grads(
            queries_heads, grad_heads, log_total, delta_heads, keys_blk, values_blk
        )
        grad_query = grad_query + plain_sum("shqk,skhd->sqhd", grad_scores, keys_blk)
        grad_key = lax.dynamic_update_slice_in_dim(
            grad_key,
            plain_sum("shqk,sqhd->skhd", grad_scores, queries_heads),
            block_index * block_rows,
            1,
        )
        grad_value = lax.dynamic_update_slice_in_dim(
            grad_value,
            plain_sum("shqk,sqhd->skhd", prob_low, grad_heads),
            block_index * block_rows,
            1,
        )
        return (grad_query, grad_key, grad_value)

    start_query = jnp.zeros(queries_heads.shape, jnp.float32)
    start_keys = jnp.zeros(keys_heads.shape, jnp.float32)
    grad_query, grad_key_all, grad_value_all = lax.fori_loop(
        0, block_count, key_step, (start_query, start_keys, start_keys)
    )
    grad_keys, grad_values = (
        lax.psum_scatter(
            grad_key_all.reshape(seq_count, length, model_width).astype(jnp.bfloat16),
            "ctx",
            scatter_dimension=1,
            tiled=True,
        ).astype(jnp.float32),
        lax.psum_scatter(
            grad_value_all.reshape(seq_count, length, model_width).astype(jnp.bfloat16),
            "ctx",
            scatter_dimension=1,
            tiled=True,
        ).astype(jnp.float32),
    )
    grad_qlin = grad_query.reshape(seq_count, row_count, model_width).astype(jnp.bfloat16) * 0.125
    grad_key_low = grad_keys.astype(jnp.bfloat16)
    grad_value_low = grad_values.astype(jnp.bfloat16)
    stacked = jnp.stack([grad_qlin, grad_key_low, grad_value_low], 1)
    grad_up_att = exact_sum("sjtr,sjtd->sjrd", down_att, stacked)
    grad_rank_att = exact_sum("sjtd,sjrd->sjtr", stacked, selected_up[:, :3]).astype(jnp.bfloat16)
    grad_down_att = plain_sum("sjtr,std->sjrd", grad_rank_att, tokens)
    joined = jnp.concatenate([grad_qlin, grad_key_low, grad_value_low], -1)
    grad_tokens = (
        grad_resid
        + plain_sum("ste,de->std", joined, wqkv_full)
        + plain_sum("sjtr,sjrd->std", grad_rank_att, down_low[:, :3])
    )
    attn_down = to_adapters(grad_down_att)
    attn_out = to_adapters(grad_out_down)
    attn_up = to_adapters(jnp.concatenate([grad_up_att, grad_up_out[:, None]], 1))
    attn_down, attn_out, attn_up = lax.psum((attn_down, attn_out, attn_up), ("ctx", "fsdp"))
    total_down = jnp.concatenate([attn_down, mlp_fc1[:, None]], 1)
    total_up = jnp.concatenate([attn_up, mlp_fc2[:, None]], 1)
    return (
        outcome.astype(jnp.bfloat16),
        grad_tokens,
        total_down,
        attn_out,
        total_up,
        mlp_hup,
        mlp_hdown,
    )


BF16 = jnp.bfloat16
F32 = jnp.float32
LOG2E = 1.4426950408889634
VMEM_LIMIT = 56 * 2**20


def dot32(left, right):
    return jnp.dot(left, right, preferred_element_type=F32)


def split_three(value):
    high = value.astype(BF16)
    rest = value - high.astype(F32)
    middle = rest.astype(BF16)
    return high, middle, (rest - middle.astype(F32)).astype(BF16)


def flip(value):
    return value.astype(F32).T.astype(BF16)


def forward_kernel(block_q, block_k, qkv_ref, send_ref, context_ref, lse_ref, qta, kk, vta, scores):
    peers, _, rows = qkv_ref.shape
    length = peers * rows

    def prepare(j, _):
        cols = pl.ds(pl.multiple_of(j * rows, rows), rows)
        query = qkv_ref[j, 0:64, :].astype(F32) * LOG2E
        high = query.astype(BF16)
        qta[0:64, cols] = high
        qta[64:128, cols] = (query - high.astype(F32)).astype(BF16)
        key = qkv_ref[j, 64:128, :]
        kk[cols, :] = flip(jnp.concatenate([key, key], 0))
        vta[0:64, cols] = qkv_ref[j, 128:192, :]
        vta[64:80, cols] = (lax.broadcasted_iota(jnp.int32, (16, rows), 0) == 0).astype(F32).astype(BF16)
        return 0

    lax.fori_loop(0, peers, prepare, 0)
    steps = length // block_k

    def query_step(i, _):
        cols = pl.ds(pl.multiple_of(i * block_q, block_q), block_q)
        query = qta[:, cols]
        scores[0] = dot32(kk[pl.ds(0, block_k), :], query)

        def half(j, now, carry):
            running, total = carry
            later = jnp.minimum(j + 1, steps - 1)
            here = pl.ds(pl.multiple_of(j * block_k, block_k), block_k)
            there = pl.ds(pl.multiple_of(later * block_k, block_k), block_k)
            scores[1 - now] = dot32(kk[there, :], query)
            block = scores[now]
            new = jnp.maximum(running, jnp.max(block, 0, keepdims=True))
            weights = jnp.exp2(block - new).astype(BF16)
            return new, total * jnp.exp2(running - new) + dot32(vta[:, here], weights)

        def pair(j, carry):
            return half(2 * j + 1, 1, half(2 * j, 0, carry))

        start = (jnp.full((1, block_q), -jnp.inf, F32), jnp.zeros((80, block_q), F32))
        top, total = lax.fori_loop(0, steps // 2, pair, start)
        weight_sum = total[64:65]
        context = total[0:64] / weight_sum
        context_ref[:, cols] = context
        lse_ref[:, cols] = top + jnp.log2(weight_sum)
        low = context.astype(BF16)
        for part in range(block_q // rows):
            send_ref[i * (block_q // rows) + part] = low[:, part * rows : (part + 1) * rows]
        return 0

    lax.fori_loop(0, length // block_q, query_step, 0)


def attend_forward(qkv):
    peers, _, rows = qkv.shape
    length = peers * rows
    block_q, block_k = 1024, 512
    return pl.pallas_call(
        functools.partial(forward_kernel, block_q, block_k),
        out_shape=[
            jax.ShapeDtypeStruct((peers, 64, rows), BF16),
            jax.ShapeDtypeStruct((64, length), F32),
            jax.ShapeDtypeStruct((1, length), F32),
        ],
        in_specs=[pl.BlockSpec(memory_space=pltpu.VMEM)],
        out_specs=[pl.BlockSpec(memory_space=pltpu.VMEM)] * 3,
        scratch_shapes=[
            pltpu.VMEM((128, length), BF16),
            pltpu.VMEM((length, 128), BF16),
            pltpu.VMEM((80, length), BF16),
            pltpu.VMEM((2, block_k, block_q), F32),
        ],
        compiler_params=pltpu.CompilerParams(vmem_limit_bytes=VMEM_LIMIT),
        name="attend_forward",
    )(qkv)


def backward_kernel(
    block_q, block_k, qkv_ref, grad_ref, context_ref, lse_ref, dq_ref, dkv_ref, qta, gta, kk, vv, kt, both, dqt
):
    peers, _, rows = qkv_ref.shape
    length = peers * rows
    row_at = lax.broadcasted_iota(jnp.int32, (16, rows), 0)
    lane_at = lax.broadcasted_iota(jnp.int32, (rows, 16), 1)

    def tail(value):
        high, middle, low = (part.astype(F32) for part in split_three(value))
        return jnp.where(row_at == 0, high, jnp.where(row_at == 1, middle, jnp.where(row_at == 2, low, 0.0))).astype(BF16)

    minus = jnp.where(lane_at < 3, -1.0, 0.0).astype(BF16)
    zeros = jnp.zeros((48, rows), BF16)

    def prepare(j, _):
        cols = pl.ds(pl.multiple_of(j * rows, rows), rows)
        raw = qkv_ref[j, 0:64, :]
        query = raw.astype(F32) * LOG2E
        high = query.astype(BF16)
        qta[0:64, cols] = high
        qta[64:128, cols] = (query - high.astype(F32)).astype(BF16)
        qta[128:144, cols] = tail(lse_ref[:, cols])
        key = qkv_ref[j, 64:128, :]
        kt[:, cols] = key
        kk[cols, 0:128] = flip(jnp.concatenate([key, key], 0))
        kk[cols, 128:144] = minus
        grad = grad_ref[j]
        delta = jnp.sum(grad.astype(F32) * context_ref[:, cols], 0, keepdims=True)
        gta[0:64, cols] = grad
        gta[64:80, cols] = tail(delta)
        gta[80:128, cols] = zeros
        head = (lax.broadcasted_iota(jnp.int32, (64, rows), 0) < 3).astype(F32) * -1.0
        vv[cols, :] = flip(jnp.concatenate([qkv_ref[j, 128:192, :], head.astype(BF16)], 0))
        both[cols, :] = flip(jnp.concatenate([raw, grad], 0))
        return 0

    lax.fori_loop(0, peers, prepare, 0)
    dqt[...] = jnp.zeros_like(dqt)
    first = lax.broadcasted_iota(jnp.int32, (block_k, 128), 1) < 64

    def key_step(i, _):
        here = pl.ds(pl.multiple_of(i * block_k, block_k), block_k)

        def query_step(j, carry):
            dk, dv = carry
            cols = pl.ds(pl.multiple_of(j * block_q, block_q), block_q)
            probs = jnp.exp2(dot32(kk[here, :], qta[:, cols]))
            slope = dot32(vv[here, :], gta[:, cols])
            low = (probs * slope).astype(BF16)
            dv = dv + dot32(probs.astype(BF16), both[cols, :])
            dk = dk + dot32(low, both[cols, :])
            dqt[:, cols] += dot32(kt[:, here], low)
            return dk, dv

        start = jnp.zeros((block_k, 128), F32)
        dk, dv = lax.fori_loop(0, length // block_q, query_step, (start, start))
        dkv = jnp.where(first, dk, dv).astype(BF16)
        for part in range(block_k // rows):
            dkv_ref[i * (block_k // rows) + part] = dkv[part * rows : (part + 1) * rows]
        return 0

    lax.fori_loop(0, length // block_k, key_step, 0)

    def finish(j, _):
        cols = pl.ds(pl.multiple_of(j * rows, rows), rows)
        dq_ref[j] = dqt[:, cols].astype(BF16)
        return 0

    lax.fori_loop(0, peers, finish, 0)


def attend_backward(qkv, grad, context, lse):
    peers, _, rows = qkv.shape
    length = peers * rows
    block_q, block_k = 1024, 512
    return pl.pallas_call(
        functools.partial(backward_kernel, block_q, block_k),
        out_shape=[
            jax.ShapeDtypeStruct((peers, 64, rows), BF16),
            jax.ShapeDtypeStruct((peers, rows, 128), BF16),
        ],
        in_specs=[pl.BlockSpec(memory_space=pltpu.VMEM)] * 4,
        out_specs=[pl.BlockSpec(memory_space=pltpu.VMEM)] * 2,
        scratch_shapes=[
            pltpu.VMEM((144, length), BF16),
            pltpu.VMEM((128, length), BF16),
            pltpu.VMEM((length, 144), BF16),
            pltpu.VMEM((length, 128), BF16),
            pltpu.VMEM((64, length), BF16),
            pltpu.VMEM((length, 128), BF16),
            pltpu.VMEM((64, length), F32),
        ],
        compiler_params=pltpu.CompilerParams(vmem_limit_bytes=VMEM_LIMIT),
        name="attend_backward",
    )(qkv, grad, context, lse)


def to_owner(blocks):
    return lax.all_to_all(blocks, "ctx", 0, 0, tiled=True)


def heads_body(
    tokens,
    cotangent,
    sequence_adapter_index,
    query_key_value_weight,
    output_weight,
    first_feed_weight,
    second_feed_weight,
    biases,
    value_bias_vector,
    first_feed_bias,
    norm_gain_pair,
    adapter_down_factors,
    output_down_factor,
    adapter_up_factors,
    hidden_up_factor,
    hidden_down_factor,
):
    _, rows, width = tokens.shape
    adapter_number = adapter_down_factors.shape[0]
    tokens = tokens[0]
    cotangent = cotangent[0]

    def pick(table):
        return lax.dynamic_index_in_dim(table, sequence_adapter_index[0], 0, keepdims=False)

    down, out_down, up, hidden_up, hidden_down = (
        pick(table)
        for table in (
            adapter_down_factors,
            output_down_factor,
            adapter_up_factors,
            hidden_up_factor,
            hidden_down_factor,
        )
    )

    def gather(weight):
        return lax.all_gather(weight, "fsdp", axis=0, tiled=True)

    wqkv = gather(query_key_value_weight)
    wout = gather(output_weight)
    wfc1 = gather(first_feed_weight)
    wfc2 = gather(second_feed_weight)

    def low_sum(form, left, right):
        return plain_sum(form, left.astype(BF16), right.astype(BF16))

    projected = plain_sum("td,de->te", tokens, wqkv)
    rank_att = plain_sum("td,jrd->jtr", tokens, down[:3])
    lifted = low_sum("jtr,jrd->jtd", rank_att, up[:3])
    queries = ((projected[:, :width] + biases[0] + lifted[0]) * 0.125).astype(BF16)
    keys = (projected[:, width : 2 * width] + lifted[1]).astype(BF16)
    values = (projected[:, 2 * width :] + value_bias_vector + lifted[2]).astype(BF16)
    size = width // H
    packed = (
        jnp.stack([queries, keys, values], 0)
        .reshape(3, rows, H, size)
        .transpose(2, 0, 3, 1)
        .reshape(H, 3 * size, rows)
    )
    qkv = to_owner(packed)
    context_blocks, context_head, lse = attend_forward(qkv)
    context_low = to_owner(context_blocks).reshape(width, rows).T
    rank_out = plain_sum("td,rd->tr", context_low, out_down)
    branch = plain_sum("td,de->te", context_low, wout) + biases[1] + low_sum("tr,rd->td", rank_out, up[3])

    def first_norm(value):
        return layer_norm(value, norm_gain_pair[0], biases[3])

    def second_norm(value):
        return layer_norm(value, norm_gain_pair[1], biases[4])

    def gelu_exact(value):
        return jax.nn.gelu(value, approximate=False)

    normed, norm_back = jax.vjp(first_norm, tokens.astype(F32) + branch)
    normed_low = normed.astype(BF16)
    rank_fc1 = plain_sum("td,rd->tr", normed_low, down[3])
    hidden_pre = (
        plain_sum("td,df->tf", normed_low, wfc1) + first_feed_bias + low_sum("tr,rf->tf", rank_fc1, hidden_up)
    )
    activated, gelu_back = jax.vjp(gelu_exact, hidden_pre)
    act_low = activated.astype(BF16)
    rank_fc2 = plain_sum("tf,rf->tr", act_low, hidden_down)
    mixed_out = plain_sum("tf,fd->td", act_low, wfc2) + biases[2] + low_sum("tr,rd->td", rank_fc2, up[4])
    outcome, out_back = jax.vjp(second_norm, normed + mixed_out)
    (grad_sum2,) = out_back(cotangent.astype(F32))
    grad_mixed = grad_sum2.astype(BF16)
    term_u2 = low_sum("tr,td->rd", rank_fc2, grad_mixed)
    grad_rank_fc2 = plain_sum("td,rd->tr", grad_mixed, up[4]).astype(BF16)
    term_hd = plain_sum("tr,tf->rf", grad_rank_fc2, act_low)
    grad_act = (
        plain_sum("td,fd->tf", grad_mixed, wfc2) + plain_sum("tr,rf->tf", grad_rank_fc2, hidden_down)
    ).astype(BF16)
    (grad_hidden,) = gelu_back(grad_act.astype(F32))
    grad_hidden = grad_hidden.astype(BF16)
    term_uh = low_sum("tr,tf->rf", rank_fc1, grad_hidden)
    grad_rank_fc1 = plain_sum("tf,rf->tr", grad_hidden, hidden_up).astype(BF16)
    term_d1 = plain_sum("tr,td->rd", grad_rank_fc1, normed_low)
    grad_normed_low = (
        plain_sum("tf,df->td", grad_hidden, wfc1) + plain_sum("tr,rd->td", grad_rank_fc1, down[3])
    ).astype(BF16)
    (grad_resid,) = norm_back(grad_sum2 + grad_normed_low.astype(F32))
    grad_branch = grad_resid.astype(BF16)
    term_uo = low_sum("tr,td->rd", rank_out, grad_branch)
    grad_rank_out = plain_sum("td,rd->tr", grad_branch, up[3]).astype(BF16)
    term_do = plain_sum("tr,td->rd", grad_rank_out, context_low)
    grad_context = (
        plain_sum("td,ed->te", grad_branch, wout) + plain_sum("tr,rd->td", grad_rank_out, out_down)
    ).astype(BF16)
    grad_blocks = to_owner(grad_context.reshape(rows, H, size).transpose(1, 2, 0))
    dq_blocks, dkv_blocks = attend_backward(qkv, grad_blocks, context_head, lse)
    grad_qlin = to_owner(dq_blocks).reshape(width, rows).T * jnp.asarray(0.125, BF16)
    dkv = to_owner(dkv_blocks).reshape(H, rows, 2, size).transpose(2, 1, 0, 3).reshape(2, rows, width)
    joined = jnp.concatenate([grad_qlin, dkv[0], dkv[1]], -1)
    stacked = joined.reshape(rows, 3, width).swapaxes(0, 1)
    term_up = low_sum("jtr,jtd->jrd", rank_att, stacked)
    grad_rank_att = plain_sum("jtd,jrd->jtr", stacked, up[:3]).astype(BF16)
    term_down = plain_sum("jtr,td->jrd", grad_rank_att, tokens)
    grad_tokens = (
        grad_resid
        + plain_sum("te,de->td", joined, wqkv)
        + plain_sum("jtr,jrd->td", grad_rank_att, down[:3])
    )
    mine = (
        jnp.concatenate([term_down, term_d1[None]], 0),
        term_do,
        jnp.concatenate([term_up, term_uo[None], term_u2[None]], 0),
        term_uh,
        term_hd,
    )
    summed = lax.psum(mine, "ctx")
    index_all = lax.all_gather(sequence_adapter_index, "fsdp", axis=0, tiled=True)
    picker = index_all[:, None] == jnp.arange(adapter_number, dtype=jnp.int32)[None, :]

    def to_table(total):
        every = lax.all_gather(total, "fsdp", axis=0)
        table = 0.0
        for seq in range(every.shape[0]):
            mask = picker[seq].reshape((adapter_number,) + (1,) * total.ndim)
            table = table + jnp.where(mask, every[seq][None], 0.0)
        return table

    tables = [to_table(total) for total in summed]
    return (outcome.astype(BF16)[None], grad_tokens[None], *tables)


def solution(mesh):
    one_head_each = mesh.shape["ctx"] == H
    return jax.shard_map(
        heads_body if one_head_each else gather_body,
        mesh=mesh,
        in_specs=(
            P("fsdp", "ctx", None),
            P("fsdp", "ctx", None),
            P("fsdp"),
            P("fsdp", None),
            P("fsdp", None),
            P("fsdp", None),
            P("fsdp", None),
            P(),
            P(),
            P(),
            P(),
            P(),
            P(),
            P(),
            P(),
            P(),
        ),
        out_specs=(P("fsdp", "ctx", None), P("fsdp", "ctx", None), P(), P(), P(), P(), P()),
        check_vma=False,
    )
```

```python
import functools

import jax
import jax.numpy as jnp
from jax import lax
from jax.experimental import pallas as pl
from jax.experimental.pallas import tpu as pltpu
from jax.sharding import PartitionSpec as P

H = 16


EPSILON = 1e-05
HIGHEST = lax.Precision.HIGHEST


def exact_sum(form, left, right):
    return jnp.einsum(form, left, right, precision=HIGHEST, preferred_element_type=jnp.float32)


def plain_sum(form, left, right):
    return jnp.einsum(form, left, right, preferred_element_type=jnp.float32)


def layer_norm(value, gain, shift):
    center = value - jnp.mean(value, -1, keepdims=True)
    spread = jnp.mean(center * center, -1, keepdims=True)
    return center * lax.rsqrt(spread + EPSILON) * gain + shift


def attn_weights(query_key_value_weight, output_weight):
    return (
        lax.all_gather(query_key_value_weight, "fsdp", axis=0, tiled=True),
        lax.all_gather(output_weight, "fsdp", axis=0, tiled=True),
    )


def mlp_weights(first_feed_weight, second_feed_weight):
    return (
        lax.all_gather(first_feed_weight, "fsdp", axis=0, tiled=True),
        lax.all_gather(second_feed_weight, "fsdp", axis=0, tiled=True),
    )


def to_heads(input_array):
    return input_array.reshape(
        input_array.shape[0], input_array.shape[1], H, input_array.shape[2] // H
    )


def row_block(input_array, block_index, block_rows):
    return lax.dynamic_slice_in_dim(input_array, block_index * block_rows, block_rows, 1)


def block_grads(queries, grad_out, log_total, row_delta, keys_blk, values_blk):
    scores = plain_sum("sqhd,skhd->shqk", queries, keys_blk)
    probs = jnp.exp(scores - log_total[..., None])
    prob_low = probs.astype(jnp.bfloat16)
    grad_probs = plain_sum("sqhd,skhd->shqk", grad_out, values_blk)
    grad_scores = (probs * (grad_probs - row_delta[..., None])).astype(jnp.bfloat16)
    return (prob_low, grad_scores)


def attention_forward(queries_heads, keys_heads, values_heads):
    seq_count, row_count, head_count, head_size = queries_heads.shape
    length = keys_heads.shape[1]
    block_rows = min(512, length)
    block_count = length // block_rows

    def max_step(running, block_index):
        running_max, running_total = running
        scores = plain_sum(
            "sqhd,skhd->shqk", queries_heads, row_block(keys_heads, block_index, block_rows)
        )
        new_max = jnp.maximum(running_max, jnp.max(scores, -1))
        running_total = running_total * jnp.exp(running_max - new_max) + jnp.sum(
            jnp.exp(scores - new_max[..., None]), -1
        )
        return ((new_max, running_total), None)

    start_max = jnp.full((seq_count, head_count, row_count), -1e30, jnp.float32)
    start_total = jnp.zeros((seq_count, head_count, row_count), jnp.float32)
    (final_max, final_total), unused = lax.scan(
        max_step, (start_max, start_total), jnp.arange(block_count)
    )
    log_total = final_max + jnp.log(final_total)

    def value_step(running, block_index):
        scores = plain_sum(
            "sqhd,skhd->shqk", queries_heads, row_block(keys_heads, block_index, block_rows)
        )
        prob_low = jnp.exp(scores - log_total[..., None]).astype(jnp.bfloat16)
        return (
            running
            + plain_sum(
                "shqk,skhd->sqhd", prob_low, row_block(values_heads, block_index, block_rows)
            ),
            None,
        )

    context, unused = lax.scan(
        value_step, jnp.zeros(queries_heads.shape, jnp.float32), jnp.arange(block_count)
    )
    return (context, log_total)


def gather_body(
    tokens,
    cotangent,
    sequence_adapter_index,
    query_key_value_weight,
    output_weight,
    first_feed_weight,
    second_feed_weight,
    biases,
    value_bias_vector,
    first_feed_bias,
    norm_gain_pair,
    adapter_down_factors,
    output_down_factor,
    adapter_up_factors,
    hidden_up_factor,
    hidden_down_factor,
):
    seq_count, row_count, model_width = tokens.shape
    adapter_number = adapter_down_factors.shape[0]
    picker = (
        sequence_adapter_index[:, None] == jnp.arange(adapter_number, dtype=jnp.int32)[None, :]
    ).astype(jnp.float32)

    def select_adapter(table):
        return jnp.einsum("sa,a...->s...", picker, table.astype(jnp.float32), precision=HIGHEST)

    def to_adapters(per_seq):
        return jnp.einsum("sa,s...->a...", picker, per_seq, precision=HIGHEST)

    selected_down = select_adapter(adapter_down_factors)
    selected_output = select_adapter(output_down_factor)
    selected_up = select_adapter(adapter_up_factors)
    hup_sel = select_adapter(hidden_up_factor)
    hdown_sel = select_adapter(hidden_down_factor)
    down_low = selected_down.astype(jnp.bfloat16)
    out_low = selected_output.astype(jnp.bfloat16)
    hdown_low = hdown_sel.astype(jnp.bfloat16)
    wqkv_full, wout_full = attn_weights(query_key_value_weight, output_weight)
    projected = plain_sum("std,de->ste", tokens, wqkv_full)
    down_att = plain_sum("std,sjrd->sjtr", tokens, down_low[:, :3])
    lifted = exact_sum("sjtr,sjrd->sjtd", down_att, selected_up[:, :3])
    queries = ((projected[..., :model_width] + biases[0] + lifted[:, 0]) * 0.125).astype(
        jnp.bfloat16
    )
    keys_own = (projected[..., model_width : 2 * model_width] + lifted[:, 1]).astype(jnp.bfloat16)
    values_own = (projected[..., 2 * model_width :] + value_bias_vector + lifted[:, 2]).astype(
        jnp.bfloat16
    )
    keys_all, values_all = (
        lax.all_gather(keys_own, "ctx", axis=1, tiled=True),
        lax.all_gather(values_own, "ctx", axis=1, tiled=True),
    )
    queries_heads = to_heads(queries)
    keys_heads = to_heads(keys_all)
    values_heads = to_heads(values_all)
    context, log_total = attention_forward(queries_heads, keys_heads, values_heads)
    context = context.reshape(seq_count, row_count, model_width)
    context_low = context.astype(jnp.bfloat16)
    down_out = plain_sum("std,srd->str", context_low, out_low)
    branch = (
        plain_sum("std,de->ste", context_low, wout_full)
        + biases[1]
        + exact_sum("str,srd->std", down_out, selected_up[:, 3])
    )

    def first_norm(value):
        return layer_norm(value, norm_gain_pair[0], biases[3])

    def second_norm(value):
        return layer_norm(value, norm_gain_pair[1], biases[4])

    def gelu_exact(value):
        return jax.nn.gelu(value, approximate=False)

    normed, norm_back = jax.vjp(first_norm, tokens.astype(jnp.float32) + branch)
    normed_low = normed.astype(jnp.bfloat16)
    wfc1_full, wfc2_full = mlp_weights(first_feed_weight, second_feed_weight)
    down_fc1 = plain_sum("std,srd->str", normed_low, down_low[:, 3])
    hidden_pre = (
        plain_sum("std,df->stf", normed_low, wfc1_full)
        + first_feed_bias
        + exact_sum("str,srf->stf", down_fc1, hup_sel)
    )
    activated, gelu_back = jax.vjp(gelu_exact, hidden_pre)
    act_low = activated.astype(jnp.bfloat16)
    down_fc2 = plain_sum("stf,srf->str", act_low, hdown_low)
    mixed_out = (
        plain_sum("stf,fd->std", act_low, wfc2_full)
        + biases[2]
        + exact_sum("str,srd->std", down_fc2, selected_up[:, 4])
    )
    outcome, out_back = jax.vjp(second_norm, normed + mixed_out)
    (grad_sum2,) = out_back(cotangent.astype(jnp.float32))
    grad_mixed = grad_sum2.astype(jnp.bfloat16)
    grad_up_fc2 = exact_sum("str,std->srd", down_fc2, grad_mixed)
    grad_rank_fc2 = exact_sum("std,srd->str", grad_mixed, selected_up[:, 4]).astype(jnp.bfloat16)
    grad_hdown = plain_sum("str,stf->srf", grad_rank_fc2, act_low)
    wfc1_full, wfc2_full = mlp_weights(first_feed_weight, second_feed_weight)
    grad_act = (
        plain_sum("std,fd->stf", grad_mixed, wfc2_full)
        + plain_sum("str,srf->stf", grad_rank_fc2, hdown_low)
    ).astype(jnp.bfloat16)
    (grad_hidden,) = gelu_back(grad_act.astype(jnp.float32))
    grad_hidden = grad_hidden.astype(jnp.bfloat16)
    grad_hup = exact_sum("str,stf->srf", down_fc1, grad_hidden)
    grad_rank_fc1 = exact_sum("stf,srf->str", grad_hidden, hup_sel).astype(jnp.bfloat16)
    grad_down_fc1 = plain_sum("str,std->srd", grad_rank_fc1, normed_low)
    grad_normed_low = (
        plain_sum("stf,df->std", grad_hidden, wfc1_full)
        + plain_sum("str,srd->std", grad_rank_fc1, down_low[:, 3])
    ).astype(jnp.bfloat16)
    (grad_resid,) = norm_back(grad_sum2 + grad_normed_low.astype(jnp.float32))
    mlp_hup = to_adapters(grad_hup)
    mlp_hdown = to_adapters(grad_hdown)
    mlp_fc1 = to_adapters(grad_down_fc1)
    mlp_fc2 = to_adapters(grad_up_fc2)
    mlp_hup, mlp_hdown, mlp_fc1, mlp_fc2 = lax.psum(
        (mlp_hup, mlp_hdown, mlp_fc1, mlp_fc2), ("ctx", "fsdp")
    )
    grad_branch = grad_resid.astype(jnp.bfloat16)
    grad_up_out = exact_sum("str,std->srd", down_out, grad_branch)
    grad_rank_out = exact_sum("std,srd->str", grad_branch, selected_up[:, 3]).astype(jnp.bfloat16)
    grad_out_down = plain_sum("str,std->srd", grad_rank_out, context_low)
    wqkv_full, wout_full = attn_weights(query_key_value_weight, output_weight)
    grad_context = (
        plain_sum("std,ed->ste", grad_branch, wout_full)
        + plain_sum("str,srd->std", grad_rank_out, out_low)
    ).astype(jnp.bfloat16)
    row_delta = jnp.sum(to_heads(grad_context.astype(jnp.float32) * context), -1)
    delta_heads = jnp.swapaxes(row_delta, 1, 2)
    grad_heads = to_heads(grad_context)
    length = keys_all.shape[1]
    block_rows = min(512, length)
    block_count = length // block_rows

    def key_step(block_index, running):
        grad_query, grad_key, grad_value = running
        keys_blk = row_block(keys_heads, block_index, block_rows)
        values_blk = row_block(values_heads, block_index, block_rows)
        prob_low, grad_scores = block_grads(
            queries_heads, grad_heads, log_total, delta_heads, keys_blk, values_blk
        )
        grad_query = grad_query + plain_sum("shqk,skhd->sqhd", grad_scores, keys_blk)
        grad_key = lax.dynamic_update_slice_in_dim(
            grad_key,
            plain_sum("shqk,sqhd->skhd", grad_scores, queries_heads),
            block_index * block_rows,
            1,
        )
        grad_value = lax.dynamic_update_slice_in_dim(
            grad_value,
            plain_sum("shqk,sqhd->skhd", prob_low, grad_heads),
            block_index * block_rows,
            1,
        )
        return (grad_query, grad_key, grad_value)

    start_query = jnp.zeros(queries_heads.shape, jnp.float32)
    start_keys = jnp.zeros(keys_heads.shape, jnp.float32)
    grad_query, grad_key_all, grad_value_all = lax.fori_loop(
        0, block_count, key_step, (start_query, start_keys, start_keys)
    )
    grad_keys, grad_values = (
        lax.psum_scatter(
            grad_key_all.reshape(seq_count, length, model_width).astype(jnp.bfloat16),
            "ctx",
            scatter_dimension=1,
            tiled=True,
        ).astype(jnp.float32),
        lax.psum_scatter(
            grad_value_all.reshape(seq_count, length, model_width).astype(jnp.bfloat16),
            "ctx",
            scatter_dimension=1,
            tiled=True,
        ).astype(jnp.float32),
    )
    grad_qlin = grad_query.reshape(seq_count, row_count, model_width).astype(jnp.bfloat16) * 0.125
    grad_key_low = grad_keys.astype(jnp.bfloat16)
    grad_value_low = grad_values.astype(jnp.bfloat16)
    stacked = jnp.stack([grad_qlin, grad_key_low, grad_value_low], 1)
    grad_up_att = exact_sum("sjtr,sjtd->sjrd", down_att, stacked)
    grad_rank_att = exact_sum("sjtd,sjrd->sjtr", stacked, selected_up[:, :3]).astype(jnp.bfloat16)
    grad_down_att = plain_sum("sjtr,std->sjrd", grad_rank_att, tokens)
    joined = jnp.concatenate([grad_qlin, grad_key_low, grad_value_low], -1)
    grad_tokens = (
        grad_resid
        + plain_sum("ste,de->std", joined, wqkv_full)
        + plain_sum("sjtr,sjrd->std", grad_rank_att, down_low[:, :3])
    )
    attn_down = to_adapters(grad_down_att)
    attn_out = to_adapters(grad_out_down)
    attn_up = to_adapters(jnp.concatenate([grad_up_att, grad_up_out[:, None]], 1))
    attn_down, attn_out, attn_up = lax.psum((attn_down, attn_out, attn_up), ("ctx", "fsdp"))
    total_down = jnp.concatenate([attn_down, mlp_fc1[:, None]], 1)
    total_up = jnp.concatenate([attn_up, mlp_fc2[:, None]], 1)
    return (
        outcome.astype(jnp.bfloat16),
        grad_tokens,
        total_down,
        attn_out,
        total_up,
        mlp_hup,
        mlp_hdown,
    )


BF16 = jnp.bfloat16
F32 = jnp.float32
LOG2E = 1.4426950408889634
VMEM_LIMIT = 56 * 2**20
MESH = pl.DeviceIdType.MESH


def dot32(left, right):
    return jnp.dot(left, right, preferred_element_type=F32)


def split_three(value):
    high = value.astype(BF16)
    rest = value - high.astype(F32)
    middle = rest.astype(BF16)
    return high, middle, (rest - middle.astype(F32)).astype(BF16)


def flip(value):
    return value.astype(F32).T.astype(BF16)


def forward_kernel(block_q, block_k, qkv_ref, send_ref, context_ref, lse_ref, qta, kk, vta, scores):
    peers, _, rows = qkv_ref.shape
    length = peers * rows

    def prepare(j, _):
        cols = pl.ds(pl.multiple_of(j * rows, rows), rows)
        query = qkv_ref[j, 0:64, :].astype(F32) * LOG2E
        high = query.astype(BF16)
        qta[0:64, cols] = high
        qta[64:128, cols] = (query - high.astype(F32)).astype(BF16)
        key = qkv_ref[j, 64:128, :]
        kk[cols, :] = flip(jnp.concatenate([key, key], 0))
        vta[0:64, cols] = qkv_ref[j, 128:192, :]
        vta[64:80, cols] = (lax.broadcasted_iota(jnp.int32, (16, rows), 0) == 0).astype(F32).astype(BF16)
        return 0

    lax.fori_loop(0, peers, prepare, 0)
    steps = length // block_k

    def query_step(i, _):
        cols = pl.ds(pl.multiple_of(i * block_q, block_q), block_q)
        query = qta[:, cols]
        scores[0] = dot32(kk[pl.ds(0, block_k), :], query)

        def half(j, now, carry):
            running, total = carry
            later = jnp.minimum(j + 1, steps - 1)
            here = pl.ds(pl.multiple_of(j * block_k, block_k), block_k)
            there = pl.ds(pl.multiple_of(later * block_k, block_k), block_k)
            scores[1 - now] = dot32(kk[there, :], query)
            block = scores[now]
            new = jnp.maximum(running, jnp.max(block, 0, keepdims=True))
            weights = jnp.exp2(block - new).astype(BF16)
            return new, total * jnp.exp2(running - new) + dot32(vta[:, here], weights)

        def pair(j, carry):
            return half(2 * j + 1, 1, half(2 * j, 0, carry))

        start = (jnp.full((1, block_q), -jnp.inf, F32), jnp.zeros((80, block_q), F32))
        top, total = lax.fori_loop(0, steps // 2, pair, start)
        weight_sum = total[64:65]
        context = total[0:64] / weight_sum
        context_ref[:, cols] = context
        lse_ref[:, cols] = top + jnp.log2(weight_sum)
        low = context.astype(BF16)
        for part in range(block_q // rows):
            send_ref[i * (block_q // rows) + part] = low[:, part * rows : (part + 1) * rows]
        return 0

    lax.fori_loop(0, length // block_q, query_step, 0)


def attend_forward(qkv):
    peers, _, rows = qkv.shape
    length = peers * rows
    block_q, block_k = 1024, 512
    return pl.pallas_call(
        functools.partial(forward_kernel, block_q, block_k),
        out_shape=[
            jax.ShapeDtypeStruct((peers, 64, rows), BF16),
            jax.ShapeDtypeStruct((64, length), F32),
            jax.ShapeDtypeStruct((1, length), F32),
        ],
        in_specs=[pl.BlockSpec(memory_space=pltpu.VMEM)],
        out_specs=[pl.BlockSpec(memory_space=pltpu.VMEM)] * 3,
        scratch_shapes=[
            pltpu.VMEM((128, length), BF16),
            pltpu.VMEM((length, 128), BF16),
            pltpu.VMEM((80, length), BF16),
            pltpu.VMEM((2, block_k, block_q), F32),
        ],
        compiler_params=pltpu.CompilerParams(vmem_limit_bytes=VMEM_LIMIT),
        name="attend_forward",
    )(qkv)


def backward_kernel(
    block_q, block_k, qkv_ref, grad_ref, context_ref, lse_ref, dq_ref, dkv_ref, qta, gta, kk, vv, kt, both, dqt
):
    peers, _, rows = qkv_ref.shape
    length = peers * rows
    row_at = lax.broadcasted_iota(jnp.int32, (16, rows), 0)
    lane_at = lax.broadcasted_iota(jnp.int32, (rows, 16), 1)

    def tail(value):
        high, middle, low = (part.astype(F32) for part in split_three(value))
        return jnp.where(row_at == 0, high, jnp.where(row_at == 1, middle, jnp.where(row_at == 2, low, 0.0))).astype(BF16)

    minus = jnp.where(lane_at < 3, -1.0, 0.0).astype(BF16)
    zeros = jnp.zeros((48, rows), BF16)

    def prepare(j, _):
        cols = pl.ds(pl.multiple_of(j * rows, rows), rows)
        raw = qkv_ref[j, 0:64, :]
        query = raw.astype(F32) * LOG2E
        high = query.astype(BF16)
        qta[0:64, cols] = high
        qta[64:128, cols] = (query - high.astype(F32)).astype(BF16)
        qta[128:144, cols] = tail(lse_ref[:, cols])
        key = qkv_ref[j, 64:128, :]
        kt[:, cols] = key
        kk[cols, 0:128] = flip(jnp.concatenate([key, key], 0))
        kk[cols, 128:144] = minus
        grad = grad_ref[j]
        delta = jnp.sum(grad.astype(F32) * context_ref[:, cols], 0, keepdims=True)
        gta[0:64, cols] = grad
        gta[64:80, cols] = tail(delta)
        gta[80:128, cols] = zeros
        head = (lax.broadcasted_iota(jnp.int32, (64, rows), 0) < 3).astype(F32) * -1.0
        vv[cols, :] = flip(jnp.concatenate([qkv_ref[j, 128:192, :], head.astype(BF16)], 0))
        both[cols, :] = flip(jnp.concatenate([raw, grad], 0))
        return 0

    lax.fori_loop(0, peers, prepare, 0)
    dqt[...] = jnp.zeros_like(dqt)
    first = lax.broadcasted_iota(jnp.int32, (block_k, 128), 1) < 64

    def key_step(i, _):
        here = pl.ds(pl.multiple_of(i * block_k, block_k), block_k)

        def query_step(j, carry):
            dk, dv = carry
            cols = pl.ds(pl.multiple_of(j * block_q, block_q), block_q)
            probs = jnp.exp2(dot32(kk[here, :], qta[:, cols]))
            slope = dot32(vv[here, :], gta[:, cols])
            low = (probs * slope).astype(BF16)
            dv = dv + dot32(probs.astype(BF16), both[cols, :])
            dk = dk + dot32(low, both[cols, :])
            dqt[:, cols] += dot32(kt[:, here], low)
            return dk, dv

        start = jnp.zeros((block_k, 128), F32)
        dk, dv = lax.fori_loop(0, length // block_q, query_step, (start, start))
        dkv = jnp.where(first, dk, dv).astype(BF16)
        for part in range(block_k // rows):
            dkv_ref[i * (block_k // rows) + part] = dkv[part * rows : (part + 1) * rows]
        return 0

    lax.fori_loop(0, length // block_k, key_step, 0)

    def finish(j, _):
        cols = pl.ds(pl.multiple_of(j * rows, rows), rows)
        dq_ref[j] = dqt[:, cols].astype(BF16)
        return 0

    lax.fori_loop(0, peers, finish, 0)


def attend_backward(qkv, grad, context, lse):
    peers, _, rows = qkv.shape
    length = peers * rows
    block_q, block_k = 1024, 512
    return pl.pallas_call(
        functools.partial(backward_kernel, block_q, block_k),
        out_shape=[
            jax.ShapeDtypeStruct((peers, 64, rows), BF16),
            jax.ShapeDtypeStruct((peers, rows, 128), BF16),
        ],
        in_specs=[pl.BlockSpec(memory_space=pltpu.VMEM)] * 4,
        out_specs=[pl.BlockSpec(memory_space=pltpu.VMEM)] * 2,
        scratch_shapes=[
            pltpu.VMEM((144, length), BF16),
            pltpu.VMEM((128, length), BF16),
            pltpu.VMEM((length, 144), BF16),
            pltpu.VMEM((length, 128), BF16),
            pltpu.VMEM((64, length), BF16),
            pltpu.VMEM((length, 128), BF16),
            pltpu.VMEM((64, length), F32),
        ],
        compiler_params=pltpu.CompilerParams(vmem_limit_bytes=VMEM_LIMIT),
        name="attend_backward",
    )(qkv, grad, context, lse)


def reduce_kernel(mine_ref, out_ref, parts, send_one, recv_one, send_two, recv_two, send_last, recv_last):
    peers = mine_ref.shape[0]
    me = lax.axis_index("ctx")
    core = lax.axis_index("fsdp")
    barrier = pltpu.get_barrier_semaphore()
    for step in range(1, peers):
        pl.semaphore_signal(barrier, inc=1, device_id=(me ^ step, core), device_id_type=MESH)
    pl.semaphore_signal(barrier, inc=1, device_id=(me, 1 - core), device_id_type=MESH)
    pl.semaphore_wait(barrier, peers)
    scatter = [
        pltpu.make_async_remote_copy(
            src_ref=mine_ref.at[me ^ step],
            dst_ref=parts.at[step],
            send_sem=send_one.at[step],
            recv_sem=recv_one.at[step],
            device_id=(me ^ step, core),
            device_id_type=MESH,
        )
        for step in range(1, peers)
    ]
    for copy in scatter:
        copy.start()
    total = mine_ref[me].astype(F32)
    for step in range(1, peers):
        scatter[step - 1].wait_recv()
        total = total + parts[step].astype(F32)
    out_ref[core, me] = total.astype(BF16)
    gather = [
        pltpu.make_async_remote_copy(
            src_ref=out_ref.at[core, me],
            dst_ref=out_ref.at[core, me],
            send_sem=send_two.at[step],
            recv_sem=recv_two.at[step],
            device_id=(me ^ step, core),
            device_id_type=MESH,
        )
        for step in range(1, peers)
    ]
    for copy in gather:
        copy.start()
    for copy in gather:
        copy.wait_recv()
    last = pltpu.make_async_remote_copy(
        src_ref=out_ref.at[core],
        dst_ref=out_ref.at[core],
        send_sem=send_last,
        recv_sem=recv_last,
        device_id=(me, 1 - core),
        device_id_type=MESH,
    )
    last.start()
    for copy in scatter + gather:
        copy.wait_send()
    last.wait()


def reduce_terms(mine, collective_id):
    peers, rows, lanes = mine.shape
    return pl.pallas_call(
        reduce_kernel,
        out_shape=jax.ShapeDtypeStruct((2, peers, rows, lanes), BF16),
        in_specs=[pl.BlockSpec(memory_space=pltpu.VMEM)],
        out_specs=pl.BlockSpec(memory_space=pltpu.VMEM),
        scratch_shapes=[pltpu.VMEM((peers, rows, lanes), BF16)]
        + [pltpu.SemaphoreType.DMA((peers,))] * 4
        + [pltpu.SemaphoreType.DMA] * 2,
        compiler_params=pltpu.CompilerParams(
            collective_id=collective_id, has_side_effects=True, vmem_limit_bytes=VMEM_LIMIT
        ),
        name="reduce_terms",
    )(mine)


def to_owner(blocks):
    return lax.all_to_all(blocks, "ctx", 0, 0, tiled=True)


def heads_body(
    tokens,
    cotangent,
    sequence_adapter_index,
    query_key_value_weight,
    output_weight,
    first_feed_weight,
    second_feed_weight,
    biases,
    value_bias_vector,
    first_feed_bias,
    norm_gain_pair,
    adapter_down_factors,
    output_down_factor,
    adapter_up_factors,
    hidden_up_factor,
    hidden_down_factor,
):
    _, rows, width = tokens.shape
    adapter_number = adapter_down_factors.shape[0]
    tokens = tokens[0]
    cotangent = cotangent[0]

    def pick(table):
        return lax.dynamic_index_in_dim(table, sequence_adapter_index[0], 0, keepdims=False)

    down, out_down, up, hidden_up, hidden_down = (
        pick(table)
        for table in (
            adapter_down_factors,
            output_down_factor,
            adapter_up_factors,
            hidden_up_factor,
            hidden_down_factor,
        )
    )

    def gather(weight):
        return lax.all_gather(weight, "fsdp", axis=0, tiled=True)

    wqkv = gather(query_key_value_weight)
    wout = gather(output_weight)
    wfc1 = gather(first_feed_weight)
    wfc2 = gather(second_feed_weight)

    def low_sum(form, left, right):
        return plain_sum(form, left.astype(BF16), right.astype(BF16))

    projected = plain_sum("td,de->te", tokens, wqkv)
    rank_att = plain_sum("td,jrd->jtr", tokens, down[:3])
    lifted = low_sum("jtr,jrd->jtd", rank_att, up[:3])
    queries = ((projected[:, :width] + biases[0] + lifted[0]) * 0.125).astype(BF16)
    keys = (projected[:, width : 2 * width] + lifted[1]).astype(BF16)
    values = (projected[:, 2 * width :] + value_bias_vector + lifted[2]).astype(BF16)
    size = width // H
    packed = (
        jnp.stack([queries, keys, values], 0)
        .reshape(3, rows, H, size)
        .transpose(2, 0, 3, 1)
        .reshape(H, 3 * size, rows)
    )
    qkv = to_owner(packed)
    context_blocks, context_head, lse = attend_forward(qkv)
    context_low = to_owner(context_blocks).reshape(width, rows).T
    rank_out = plain_sum("td,rd->tr", context_low, out_down)
    branch = plain_sum("td,de->te", context_low, wout) + biases[1] + low_sum("tr,rd->td", rank_out, up[3])

    def first_norm(value):
        return layer_norm(value, norm_gain_pair[0], biases[3])

    def second_norm(value):
        return layer_norm(value, norm_gain_pair[1], biases[4])

    def gelu_exact(value):
        return jax.nn.gelu(value, approximate=False)

    normed, norm_back = jax.vjp(first_norm, tokens.astype(F32) + branch)
    normed_low = normed.astype(BF16)
    rank_fc1 = plain_sum("td,rd->tr", normed_low, down[3])
    hidden_pre = (
        plain_sum("td,df->tf", normed_low, wfc1) + first_feed_bias + low_sum("tr,rf->tf", rank_fc1, hidden_up)
    )
    activated, gelu_back = jax.vjp(gelu_exact, hidden_pre)
    act_low = activated.astype(BF16)
    rank_fc2 = plain_sum("tf,rf->tr", act_low, hidden_down)
    mixed_out = plain_sum("tf,fd->td", act_low, wfc2) + biases[2] + low_sum("tr,rd->td", rank_fc2, up[4])
    outcome, out_back = jax.vjp(second_norm, normed + mixed_out)
    (grad_sum2,) = out_back(cotangent.astype(F32))
    grad_mixed = grad_sum2.astype(BF16)
    term_u2 = low_sum("tr,td->rd", rank_fc2, grad_mixed)
    grad_rank_fc2 = plain_sum("td,rd->tr", grad_mixed, up[4]).astype(BF16)
    term_hd = plain_sum("tr,tf->rf", grad_rank_fc2, act_low)
    grad_act = (
        plain_sum("td,fd->tf", grad_mixed, wfc2) + plain_sum("tr,rf->tf", grad_rank_fc2, hidden_down)
    ).astype(BF16)
    (grad_hidden,) = gelu_back(grad_act.astype(F32))
    grad_hidden = grad_hidden.astype(BF16)
    term_uh = low_sum("tr,tf->rf", rank_fc1, grad_hidden)
    grad_rank_fc1 = plain_sum("tf,rf->tr", grad_hidden, hidden_up).astype(BF16)
    term_d1 = plain_sum("tr,td->rd", grad_rank_fc1, normed_low)
    grad_normed_low = (
        plain_sum("tf,df->td", grad_hidden, wfc1) + plain_sum("tr,rd->td", grad_rank_fc1, down[3])
    ).astype(BF16)
    (grad_resid,) = norm_back(grad_sum2 + grad_normed_low.astype(F32))
    grad_branch = grad_resid.astype(BF16)
    term_uo = low_sum("tr,td->rd", rank_out, grad_branch)
    grad_rank_out = plain_sum("td,rd->tr", grad_branch, up[3]).astype(BF16)
    term_do = plain_sum("tr,td->rd", grad_rank_out, context_low)
    grad_context = (
        plain_sum("td,ed->te", grad_branch, wout) + plain_sum("tr,rd->td", grad_rank_out, out_down)
    ).astype(BF16)
    grad_blocks = to_owner(grad_context.reshape(rows, H, size).transpose(1, 2, 0))
    dq_blocks, dkv_blocks = attend_backward(qkv, grad_blocks, context_head, lse)
    grad_qlin = to_owner(dq_blocks).reshape(width, rows).T * jnp.asarray(0.125, BF16)
    dkv = to_owner(dkv_blocks).reshape(H, rows, 2, size).transpose(2, 1, 0, 3).reshape(2, rows, width)
    joined = jnp.concatenate([grad_qlin, dkv[0], dkv[1]], -1)
    stacked = joined.reshape(rows, 3, width).swapaxes(0, 1)
    term_up = low_sum("jtr,jtd->jrd", rank_att, stacked)
    grad_rank_att = plain_sum("jtd,jrd->jtr", stacked, up[:3]).astype(BF16)
    term_down = plain_sum("jtr,td->jrd", grad_rank_att, tokens)
    grad_tokens = (
        grad_resid
        + plain_sum("te,de->td", joined, wqkv)
        + plain_sum("jtr,jrd->td", grad_rank_att, down[:3])
    )
    mine = (
        jnp.concatenate([term_down, term_d1[None]], 0),
        term_do,
        jnp.concatenate([term_up, term_uo[None], term_u2[None]], 0),
        term_uh,
        term_hd,
    )
    flat = jnp.concatenate([term.reshape(-1, 128) for term in mine], 0)
    summed = reduce_terms(flat.astype(BF16).reshape(H, -1, 128), 0).reshape(2, -1, 128)
    index_all = lax.all_gather(sequence_adapter_index, "fsdp", axis=0, tiled=True)
    picker = index_all[:, None] == jnp.arange(adapter_number, dtype=jnp.int32)[None, :]
    tables = []
    at = 0
    for term in mine:
        count = term.size // 128
        every = summed[:, at : at + count].reshape((2,) + term.shape).astype(F32)
        at += count
        table = 0.0
        for seq in range(2):
            mask = picker[seq].reshape((adapter_number,) + (1,) * term.ndim)
            table = table + jnp.where(mask, every[seq][None], 0.0)
        tables.append(table)
    return (outcome.astype(BF16)[None], grad_tokens[None], *tables)


def solution(mesh):
    one_head_each = mesh.shape["ctx"] == H and mesh.shape["fsdp"] == 2
    return jax.shard_map(
        heads_body if one_head_each else gather_body,
        mesh=mesh,
        in_specs=(
            P("fsdp", "ctx", None),
            P("fsdp", "ctx", None),
            P("fsdp"),
            P("fsdp", None),
            P("fsdp", None),
            P("fsdp", None),
            P("fsdp", None),
            P(),
            P(),
            P(),
            P(),
            P(),
            P(),
            P(),
            P(),
            P(),
        ),
        out_specs=(P("fsdp", "ctx", None), P("fsdp", "ctx", None), P(), P(), P(), P(), P()),
        check_vma=False,
    )
```

```python
import functools

import jax
import jax.numpy as jnp
from jax import lax
from jax.experimental import pallas as pl
from jax.experimental.pallas import tpu as pltpu
from jax.sharding import PartitionSpec as P

H = 16


EPSILON = 1e-05
HIGHEST = lax.Precision.HIGHEST


def exact_sum(form, left, right):
    return jnp.einsum(form, left, right, precision=HIGHEST, preferred_element_type=jnp.float32)


def plain_sum(form, left, right):
    return jnp.einsum(form, left, right, preferred_element_type=jnp.float32)


def layer_norm(value, gain, shift):
    center = value - jnp.mean(value, -1, keepdims=True)
    spread = jnp.mean(center * center, -1, keepdims=True)
    return center * lax.rsqrt(spread + EPSILON) * gain + shift


def attn_weights(query_key_value_weight, output_weight):
    return (
        lax.all_gather(query_key_value_weight, "fsdp", axis=0, tiled=True),
        lax.all_gather(output_weight, "fsdp", axis=0, tiled=True),
    )


def mlp_weights(first_feed_weight, second_feed_weight):
    return (
        lax.all_gather(first_feed_weight, "fsdp", axis=0, tiled=True),
        lax.all_gather(second_feed_weight, "fsdp", axis=0, tiled=True),
    )


def to_heads(input_array):
    return input_array.reshape(
        input_array.shape[0], input_array.shape[1], H, input_array.shape[2] // H
    )


def row_block(input_array, block_index, block_rows):
    return lax.dynamic_slice_in_dim(input_array, block_index * block_rows, block_rows, 1)


def block_grads(queries, grad_out, log_total, row_delta, keys_blk, values_blk):
    scores = plain_sum("sqhd,skhd->shqk", queries, keys_blk)
    probs = jnp.exp(scores - log_total[..., None])
    prob_low = probs.astype(jnp.bfloat16)
    grad_probs = plain_sum("sqhd,skhd->shqk", grad_out, values_blk)
    grad_scores = (probs * (grad_probs - row_delta[..., None])).astype(jnp.bfloat16)
    return (prob_low, grad_scores)


def attention_forward(queries_heads, keys_heads, values_heads):
    seq_count, row_count, head_count, head_size = queries_heads.shape
    length = keys_heads.shape[1]
    block_rows = min(512, length)
    block_count = length // block_rows

    def max_step(running, block_index):
        running_max, running_total = running
        scores = plain_sum(
            "sqhd,skhd->shqk", queries_heads, row_block(keys_heads, block_index, block_rows)
        )
        new_max = jnp.maximum(running_max, jnp.max(scores, -1))
        running_total = running_total * jnp.exp(running_max - new_max) + jnp.sum(
            jnp.exp(scores - new_max[..., None]), -1
        )
        return ((new_max, running_total), None)

    start_max = jnp.full((seq_count, head_count, row_count), -1e30, jnp.float32)
    start_total = jnp.zeros((seq_count, head_count, row_count), jnp.float32)
    (final_max, final_total), unused = lax.scan(
        max_step, (start_max, start_total), jnp.arange(block_count)
    )
    log_total = final_max + jnp.log(final_total)

    def value_step(running, block_index):
        scores = plain_sum(
            "sqhd,skhd->shqk", queries_heads, row_block(keys_heads, block_index, block_rows)
        )
        prob_low = jnp.exp(scores - log_total[..., None]).astype(jnp.bfloat16)
        return (
            running
            + plain_sum(
                "shqk,skhd->sqhd", prob_low, row_block(values_heads, block_index, block_rows)
            ),
            None,
        )

    context, unused = lax.scan(
        value_step, jnp.zeros(queries_heads.shape, jnp.float32), jnp.arange(block_count)
    )
    return (context, log_total)


def gather_body(
    tokens,
    cotangent,
    sequence_adapter_index,
    query_key_value_weight,
    output_weight,
    first_feed_weight,
    second_feed_weight,
    biases,
    value_bias_vector,
    first_feed_bias,
    norm_gain_pair,
    adapter_down_factors,
    output_down_factor,
    adapter_up_factors,
    hidden_up_factor,
    hidden_down_factor,
):
    seq_count, row_count, model_width = tokens.shape
    adapter_number = adapter_down_factors.shape[0]
    picker = (
        sequence_adapter_index[:, None] == jnp.arange(adapter_number, dtype=jnp.int32)[None, :]
    ).astype(jnp.float32)

    def select_adapter(table):
        return jnp.einsum("sa,a...->s...", picker, table.astype(jnp.float32), precision=HIGHEST)

    def to_adapters(per_seq):
        return jnp.einsum("sa,s...->a...", picker, per_seq, precision=HIGHEST)

    selected_down = select_adapter(adapter_down_factors)
    selected_output = select_adapter(output_down_factor)
    selected_up = select_adapter(adapter_up_factors)
    hup_sel = select_adapter(hidden_up_factor)
    hdown_sel = select_adapter(hidden_down_factor)
    down_low = selected_down.astype(jnp.bfloat16)
    out_low = selected_output.astype(jnp.bfloat16)
    hdown_low = hdown_sel.astype(jnp.bfloat16)
    wqkv_full, wout_full = attn_weights(query_key_value_weight, output_weight)
    projected = plain_sum("std,de->ste", tokens, wqkv_full)
    down_att = plain_sum("std,sjrd->sjtr", tokens, down_low[:, :3])
    lifted = exact_sum("sjtr,sjrd->sjtd", down_att, selected_up[:, :3])
    queries = ((projected[..., :model_width] + biases[0] + lifted[:, 0]) * 0.125).astype(
        jnp.bfloat16
    )
    keys_own = (projected[..., model_width : 2 * model_width] + lifted[:, 1]).astype(jnp.bfloat16)
    values_own = (projected[..., 2 * model_width :] + value_bias_vector + lifted[:, 2]).astype(
        jnp.bfloat16
    )
    keys_all, values_all = (
        lax.all_gather(keys_own, "ctx", axis=1, tiled=True),
        lax.all_gather(values_own, "ctx", axis=1, tiled=True),
    )
    queries_heads = to_heads(queries)
    keys_heads = to_heads(keys_all)
    values_heads = to_heads(values_all)
    context, log_total = attention_forward(queries_heads, keys_heads, values_heads)
    context = context.reshape(seq_count, row_count, model_width)
    context_low = context.astype(jnp.bfloat16)
    down_out = plain_sum("std,srd->str", context_low, out_low)
    branch = (
        plain_sum("std,de->ste", context_low, wout_full)
        + biases[1]
        + exact_sum("str,srd->std", down_out, selected_up[:, 3])
    )

    def first_norm(value):
        return layer_norm(value, norm_gain_pair[0], biases[3])

    def second_norm(value):
        return layer_norm(value, norm_gain_pair[1], biases[4])

    def gelu_exact(value):
        return jax.nn.gelu(value, approximate=False)

    normed, norm_back = jax.vjp(first_norm, tokens.astype(jnp.float32) + branch)
    normed_low = normed.astype(jnp.bfloat16)
    wfc1_full, wfc2_full = mlp_weights(first_feed_weight, second_feed_weight)
    down_fc1 = plain_sum("std,srd->str", normed_low, down_low[:, 3])
    hidden_pre = (
        plain_sum("std,df->stf", normed_low, wfc1_full)
        + first_feed_bias
        + exact_sum("str,srf->stf", down_fc1, hup_sel)
    )
    activated, gelu_back = jax.vjp(gelu_exact, hidden_pre)
    act_low = activated.astype(jnp.bfloat16)
    down_fc2 = plain_sum("stf,srf->str", act_low, hdown_low)
    mixed_out = (
        plain_sum("stf,fd->std", act_low, wfc2_full)
        + biases[2]
        + exact_sum("str,srd->std", down_fc2, selected_up[:, 4])
    )
    outcome, out_back = jax.vjp(second_norm, normed + mixed_out)
    (grad_sum2,) = out_back(cotangent.astype(jnp.float32))
    grad_mixed = grad_sum2.astype(jnp.bfloat16)
    grad_up_fc2 = exact_sum("str,std->srd", down_fc2, grad_mixed)
    grad_rank_fc2 = exact_sum("std,srd->str", grad_mixed, selected_up[:, 4]).astype(jnp.bfloat16)
    grad_hdown = plain_sum("str,stf->srf", grad_rank_fc2, act_low)
    wfc1_full, wfc2_full = mlp_weights(first_feed_weight, second_feed_weight)
    grad_act = (
        plain_sum("std,fd->stf", grad_mixed, wfc2_full)
        + plain_sum("str,srf->stf", grad_rank_fc2, hdown_low)
    ).astype(jnp.bfloat16)
    (grad_hidden,) = gelu_back(grad_act.astype(jnp.float32))
    grad_hidden = grad_hidden.astype(jnp.bfloat16)
    grad_hup = exact_sum("str,stf->srf", down_fc1, grad_hidden)
    grad_rank_fc1 = exact_sum("stf,srf->str", grad_hidden, hup_sel).astype(jnp.bfloat16)
    grad_down_fc1 = plain_sum("str,std->srd", grad_rank_fc1, normed_low)
    grad_normed_low = (
        plain_sum("stf,df->std", grad_hidden, wfc1_full)
        + plain_sum("str,srd->std", grad_rank_fc1, down_low[:, 3])
    ).astype(jnp.bfloat16)
    (grad_resid,) = norm_back(grad_sum2 + grad_normed_low.astype(jnp.float32))
    mlp_hup = to_adapters(grad_hup)
    mlp_hdown = to_adapters(grad_hdown)
    mlp_fc1 = to_adapters(grad_down_fc1)
    mlp_fc2 = to_adapters(grad_up_fc2)
    mlp_hup, mlp_hdown, mlp_fc1, mlp_fc2 = lax.psum(
        (mlp_hup, mlp_hdown, mlp_fc1, mlp_fc2), ("ctx", "fsdp")
    )
    grad_branch = grad_resid.astype(jnp.bfloat16)
    grad_up_out = exact_sum("str,std->srd", down_out, grad_branch)
    grad_rank_out = exact_sum("std,srd->str", grad_branch, selected_up[:, 3]).astype(jnp.bfloat16)
    grad_out_down = plain_sum("str,std->srd", grad_rank_out, context_low)
    wqkv_full, wout_full = attn_weights(query_key_value_weight, output_weight)
    grad_context = (
        plain_sum("std,ed->ste", grad_branch, wout_full)
        + plain_sum("str,srd->std", grad_rank_out, out_low)
    ).astype(jnp.bfloat16)
    row_delta = jnp.sum(to_heads(grad_context.astype(jnp.float32) * context), -1)
    delta_heads = jnp.swapaxes(row_delta, 1, 2)
    grad_heads = to_heads(grad_context)
    length = keys_all.shape[1]
    block_rows = min(512, length)
    block_count = length // block_rows

    def key_step(block_index, running):
        grad_query, grad_key, grad_value = running
        keys_blk = row_block(keys_heads, block_index, block_rows)
        values_blk = row_block(values_heads, block_index, block_rows)
        prob_low, grad_scores = block_grads(
            queries_heads, grad_heads, log_total, delta_heads, keys_blk, values_blk
        )
        grad_query = grad_query + plain_sum("shqk,skhd->sqhd", grad_scores, keys_blk)
        grad_key = lax.dynamic_update_slice_in_dim(
            grad_key,
            plain_sum("shqk,sqhd->skhd", grad_scores, queries_heads),
            block_index * block_rows,
            1,
        )
        grad_value = lax.dynamic_update_slice_in_dim(
            grad_value,
            plain_sum("shqk,sqhd->skhd", prob_low, grad_heads),
            block_index * block_rows,
            1,
        )
        return (grad_query, grad_key, grad_value)

    start_query = jnp.zeros(queries_heads.shape, jnp.float32)
    start_keys = jnp.zeros(keys_heads.shape, jnp.float32)
    grad_query, grad_key_all, grad_value_all = lax.fori_loop(
        0, block_count, key_step, (start_query, start_keys, start_keys)
    )
    grad_keys, grad_values = (
        lax.psum_scatter(
            grad_key_all.reshape(seq_count, length, model_width).astype(jnp.bfloat16),
            "ctx",
            scatter_dimension=1,
            tiled=True,
        ).astype(jnp.float32),
        lax.psum_scatter(
            grad_value_all.reshape(seq_count, length, model_width).astype(jnp.bfloat16),
            "ctx",
            scatter_dimension=1,
            tiled=True,
        ).astype(jnp.float32),
    )
    grad_qlin = grad_query.reshape(seq_count, row_count, model_width).astype(jnp.bfloat16) * 0.125
    grad_key_low = grad_keys.astype(jnp.bfloat16)
    grad_value_low = grad_values.astype(jnp.bfloat16)
    stacked = jnp.stack([grad_qlin, grad_key_low, grad_value_low], 1)
    grad_up_att = exact_sum("sjtr,sjtd->sjrd", down_att, stacked)
    grad_rank_att = exact_sum("sjtd,sjrd->sjtr", stacked, selected_up[:, :3]).astype(jnp.bfloat16)
    grad_down_att = plain_sum("sjtr,std->sjrd", grad_rank_att, tokens)
    joined = jnp.concatenate([grad_qlin, grad_key_low, grad_value_low], -1)
    grad_tokens = (
        grad_resid
        + plain_sum("ste,de->std", joined, wqkv_full)
        + plain_sum("sjtr,sjrd->std", grad_rank_att, down_low[:, :3])
    )
    attn_down = to_adapters(grad_down_att)
    attn_out = to_adapters(grad_out_down)
    attn_up = to_adapters(jnp.concatenate([grad_up_att, grad_up_out[:, None]], 1))
    attn_down, attn_out, attn_up = lax.psum((attn_down, attn_out, attn_up), ("ctx", "fsdp"))
    total_down = jnp.concatenate([attn_down, mlp_fc1[:, None]], 1)
    total_up = jnp.concatenate([attn_up, mlp_fc2[:, None]], 1)
    return (
        outcome.astype(jnp.bfloat16),
        grad_tokens,
        total_down,
        attn_out,
        total_up,
        mlp_hup,
        mlp_hdown,
    )


BF16 = jnp.bfloat16
F32 = jnp.float32
LOG2E = 1.4426950408889634
VMEM_LIMIT = 60 * 2**20
MESH = pl.DeviceIdType.MESH


def dot32(left, right):
    return jnp.dot(left, right, preferred_element_type=F32)


def dot_nt(left, right):
    return lax.dot_general(left, right, (((1,), (1,)), ((), ())), preferred_element_type=F32)


def dot_tn(left, right):
    return lax.dot_general(left, right, (((0,), (0,)), ((), ())), preferred_element_type=F32)


def split_three(value):
    high = value.astype(BF16)
    rest = value - high.astype(F32)
    middle = rest.astype(BF16)
    return high, middle, (rest - middle.astype(F32)).astype(BF16)


def flip(value):
    return value.astype(F32).T.astype(BF16)


def remote(src, dst, send_sem, recv_sem, ctx, core):
    return pltpu.make_async_remote_copy(
        src_ref=src,
        dst_ref=dst,
        send_sem=send_sem,
        recv_sem=recv_sem,
        device_id=(ctx, core),
        device_id_type=MESH,
    )


def greet(me, core, peers):
    barrier = pltpu.get_barrier_semaphore()
    for step in range(1, peers):
        pl.semaphore_signal(barrier, inc=1, device_id=(me ^ step, core), device_id_type=MESH)
    pl.semaphore_signal(barrier, inc=1, device_id=(me, 1 - core), device_id_type=MESH)
    pl.semaphore_wait(barrier, peers)


def forward_kernel(
    block_q,
    block_k,
    x_ref,
    wqkv_ref,
    wout_ref,
    wfc1_ref,
    wfc2_ref,
    down_ref,
    up_ref,
    biases_ref,
    value_bias_ref,
    qkv_ref,
    arrived_ref,
    context_ref,
    lse_ref,
    rank_ref,
    wqkv_far,
    wout_far,
    wfc1_far,
    wfc2_far,
    weight,
    y,
    outgoing,
    leaving,
    qta,
    kk,
    vta,
    scores,
    weight_sem,
    far_sem,
    near_sem,
    kv_sem,
    q_sem,
    back_sem,
):
    peers, _, rows = qkv_ref.shape
    length = peers * rows
    width = x_ref.shape[1]
    depth = width // 2
    me = lax.axis_index("ctx")
    core = lax.axis_index("fsdp")
    other = 1 - core
    load = pltpu.make_async_copy(wqkv_ref, weight.at[core], weight_sem.at[0])
    load.start()
    greet(me, core, peers)
    fetch = remote(wqkv_ref, weight.at[core], weight_sem.at[1], weight_sem.at[2], me, other)
    fetch.start()

    halves = ((wout_ref, wout_far), (wfc1_ref, wfc1_far), (wfc2_ref, wfc2_far))
    far = [
        remote(half, there, far_sem.at[0, i], far_sem.at[1, i], me, other)
        for i, (half, there) in enumerate(halves)
    ]

    rank_low = dot_nt(x_ref[...], down_ref[0:48]).astype(BF16)
    rank_ref[...] = rank_low
    x_own = x_ref[:, pl.ds(pl.multiple_of(core * depth, depth), depth)]
    x_other = x_ref[:, pl.ds(pl.multiple_of(other * depth, depth), depth)]
    load.wait()
    for part in (1, 2, 0):
        cols = slice(part * width, (part + 1) * width)
        y[:, cols] = dot32(x_own, weight[core, :, cols]) + dot32(rank_low[:, part * 16 : part * 16 + 16], up_ref[part * 16 : part * 16 + 16])
    fetch.wait_recv()

    def project(part):
        cols = slice(part * width, (part + 1) * width)
        value = y[:, cols] + dot32(x_other, weight[other, :, cols])
        if part == 0:
            value = (value + biases_ref[0:1, :]) * 0.125
        if part == 2:
            value = value + value_bias_ref[...]
        for two in range(peers // 2):
            turned = value[:, two * 128 : two * 128 + 128].T.astype(BF16)
            outgoing[2 * two, part * 64 : part * 64 + 64] = turned[0:64]
            outgoing[2 * two + 1, part * 64 : part * 64 + 64] = turned[64:128]

    def kv_copy(step):
        return remote(
            outgoing.at[me ^ step, 64:192], qkv_ref.at[step, 64:192], kv_sem.at[0, step], kv_sem.at[1, step], me ^ step, core
        )

    def q_copy(step):
        return remote(
            outgoing.at[me ^ step, 0:64], qkv_ref.at[step, 0:64], q_sem.at[0, step], q_sem.at[1, step], me ^ step, core
        )

    def back_copy(step):
        return remote(
            leaving.at[step], arrived_ref.at[me], back_sem.at[0, step], back_sem.at[1, step], me ^ step, core
        )

    project(1)
    project(2)
    for step in range(1, peers):
        kv_copy(step).start()
    project(0)
    for step in range(1, peers):
        q_copy(step).start()
    for copy in far:
        copy.start()
    save = pltpu.make_async_copy(weight.at[other], wqkv_far, near_sem)
    save.start()
    qkv_ref[0] = outgoing[me]

    ones = (lax.broadcasted_iota(jnp.int32, (16, rows), 0) == 0).astype(F32).astype(BF16)

    def take_key(step, _):
        cols = pl.ds(pl.multiple_of(step * rows, rows), rows)

        @pl.when(step > 0)
        def _():
            kv_copy(step).wait_recv()

        key = qkv_ref[step, 64:128, :]
        kk[cols, :] = flip(jnp.concatenate([key, key], 0))
        vta[0:64, cols] = qkv_ref[step, 128:192, :]
        vta[64:80, cols] = ones
        return 0

    lax.fori_loop(0, peers, take_key, 0)
    steps = length // block_k
    group = block_q // rows

    def query_step(i, _):
        def take_query(part, _):
            step = i * group + part
            here = pl.ds(pl.multiple_of(part * rows, rows), rows)

            @pl.when(step > 0)
            def _():
                q_copy(step).wait_recv()

            query = qkv_ref[step, 0:64, :].astype(F32) * LOG2E
            high = query.astype(BF16)
            qta[0:64, here] = high
            qta[64:128, here] = (query - high.astype(F32)).astype(BF16)
            return 0

        lax.fori_loop(0, group, take_query, 0)
        cols = pl.ds(pl.multiple_of(i * block_q, block_q), block_q)
        scores[0] = dot32(kk[pl.ds(0, block_k), :], qta[...])

        def half(j, now, carry):
            running, total = carry
            later = jnp.minimum(j + 1, steps - 1)
            here = pl.ds(pl.multiple_of(j * block_k, block_k), block_k)
            there = pl.ds(pl.multiple_of(later * block_k, block_k), block_k)
            scores[1 - now] = dot32(kk[there, :], qta[...])
            block = scores[now]
            new = jnp.maximum(running, jnp.max(block, 0, keepdims=True))
            weights = jnp.exp2(block - new).astype(BF16)
            return new, total * jnp.exp2(running - new) + dot32(vta[:, here], weights)

        def pair(j, carry):
            return half(2 * j + 1, 1, half(2 * j, 0, carry))

        start = (jnp.full((1, block_q), -jnp.inf, F32), jnp.zeros((80, block_q), F32))
        top, total = lax.fori_loop(0, steps // 2, pair, start)
        weight_sum = total[64:65]
        context = total[0:64] / weight_sum
        context_ref[:, cols] = context
        lse_ref[:, cols] = top + jnp.log2(weight_sum)
        low = context.astype(BF16)
        for part in range(group):
            step = i * group + part
            leaving[step] = low[:, part * rows : (part + 1) * rows]

            @pl.when(step > 0)
            def _():
                back_copy(step).start()

        return 0

    lax.fori_loop(0, length // block_q, query_step, 0)
    arrived_ref[me] = leaving[0]
    for step in range(1, peers):
        back_copy(step).wait_recv()
    for step in range(1, peers):
        kv_copy(step).wait_send()
        q_copy(step).wait_send()
        back_copy(step).wait_send()
    fetch.wait_send()
    for copy in far:
        copy.wait()
    save.wait()


def attend_forward(x, wqkv, wout, wfc1, wfc2, down, up, biases, value_bias):
    rows, width = x.shape
    peers = H
    length = peers * rows
    block_q, block_k = 1024, 512
    vmem = pl.BlockSpec(memory_space=pltpu.VMEM)
    hbm = pl.BlockSpec(memory_space=pl.ANY)

    return pl.pallas_call(
        functools.partial(forward_kernel, block_q, block_k),
        out_shape=[
            jax.ShapeDtypeStruct((peers, 192, rows), BF16),
            jax.ShapeDtypeStruct((peers, 64, rows), BF16),
            jax.ShapeDtypeStruct((64, length), F32),
            jax.ShapeDtypeStruct((1, length), F32),
            jax.ShapeDtypeStruct((rows, 48), BF16),
            *(jax.ShapeDtypeStruct(half.shape, BF16) for half in (wqkv, wout, wfc1, wfc2)),
        ],
        in_specs=[vmem] + [hbm] * 4 + [vmem] * 4,
        out_specs=[vmem] * 5 + [hbm] * 4,
        scratch_shapes=[
            pltpu.VMEM((2,) + wqkv.shape, BF16),
            pltpu.VMEM((rows, 3 * width), F32),
            pltpu.VMEM((peers, 192, rows), BF16),
            pltpu.VMEM((peers, 64, rows), BF16),
            pltpu.VMEM((128, block_q), BF16),
            pltpu.VMEM((length, 128), BF16),
            pltpu.VMEM((80, length), BF16),
            pltpu.VMEM((2, block_k, block_q), F32),
            pltpu.SemaphoreType.DMA((3,)),
            pltpu.SemaphoreType.DMA((2, 3)),
            pltpu.SemaphoreType.DMA,
            pltpu.SemaphoreType.DMA((2, peers)),
            pltpu.SemaphoreType.DMA((2, peers)),
            pltpu.SemaphoreType.DMA((2, peers)),
        ],
        compiler_params=pltpu.CompilerParams(
            collective_id=1, has_side_effects=True, vmem_limit_bytes=VMEM_LIMIT
        ),
        name="attend_forward",
    )(x, wqkv, wout, wfc1, wfc2, down, up, biases, value_bias)


def sum_copies(mine, parts, total, sems, me, core):
    peers = mine.shape[0]
    scatter = [
        remote(mine.at[me ^ step], parts.at[step], sems.at[0, step], sems.at[1, step], me ^ step, core)
        for step in range(1, peers)
    ]
    gather = [
        remote(total.at[core, me], total.at[core, me], sems.at[2, step], sems.at[3, step], me ^ step, core)
        for step in range(1, peers)
    ]
    last = remote(total.at[core], total.at[core], sems.at[0, 0], sems.at[1, 0], me, 1 - core)
    return scatter, gather, last


def sum_parts(scatter, mine, parts, total, me, core):
    value = mine[me].astype(F32)
    for step, copy in enumerate(scatter, 1):
        copy.wait_recv()
        value = value + parts[step].astype(F32)
    total[core, me] = value.astype(BF16)


def put_term(mine, base, term):
    units = mine.shape[2] // 128
    for unit in range(term.shape[1] // 128):
        at = base // 128 + unit
        lanes = slice(at % units * 128, at % units * 128 + 128)
        mine[at // units, :, lanes] = term[:, unit * 128 : unit * 128 + 128].astype(BF16)


def backward_kernel(
    block_q,
    block_k,
    x_ref,
    cotangent_ref,
    qkv_ref,
    arrived_ref,
    context_ref,
    lse_ref,
    rank_ref,
    wqkv_ref,
    wqkv_far,
    wout_ref,
    wout_far,
    wfc1_ref,
    wfc1_far,
    wfc2_ref,
    wfc2_far,
    down_ref,
    out_down_ref,
    up_ref,
    hidden_up_ref,
    hidden_down_ref,
    biases_ref,
    hidden_bias_ref,
    gains_ref,
    outcome_ref,
    grad_ref,
    mlp_ref,
    att_ref,
    wout,
    wfc1,
    wfc2,
    slope,
    act,
    grad_resid,
    mlp_mine,
    mlp_parts,
    att_mine,
    att_parts,
    outgoing,
    incoming,
    qta,
    gta,
    kk,
    vv,
    kt,
    both,
    dqt,
    dq_out,
    dq_in,
    dkv_out,
    dkv_in,
    joined,
    load_sem,
    grad_sem,
    dq_sem,
    dkv_sem,
    mlp_sem,
    att_sem,
):
    peers, _, rows = qkv_ref.shape
    length = peers * rows
    width = x_ref.shape[1]
    hidden = hidden_bias_ref.shape[1]
    me = lax.axis_index("ctx")
    core = lax.axis_index("fsdp")
    wqkv = wfc1.at[:, 0 : 3 * width]

    loads = []
    for i, (half, far, full) in enumerate(
        (
            (wout_ref, wout_far, wout),
            (wfc1_ref, wfc1_far, wfc1),
            (wfc2_ref, wfc2_far, wfc2),
            (wqkv_ref, wqkv_far, wqkv),
        )
    ):
        count = half.shape[0]
        for j, (source, owner) in enumerate(((half, core), (far, 1 - core))):
            place = full.at[pl.ds(pl.multiple_of(owner * count, count), count), :]
            loads.append(pltpu.make_async_copy(source, place, load_sem.at[i, j]))
    for copy in loads[:6]:
        copy.start()
    greet(me, core, peers)

    def mean(value):
        return jnp.mean(value, -1, keepdims=True)

    def norm_backward(grad, hat, scale):
        return scale * (grad - mean(grad) - hat * mean(grad * hat))

    def up(j):
        return up_ref[16 * j : 16 * j + 16]

    def down(j):
        return down_ref[16 * j : 16 * j + 16]

    context_low = flip(arrived_ref[...].reshape(width, rows))
    rank_out = dot_nt(context_low, out_down_ref[...]).astype(BF16)
    loads[0].wait()
    loads[1].wait()
    resid = x_ref[...].astype(F32) + dot32(context_low, wout[...]) + biases_ref[1:2] + dot32(rank_out, up(3))
    center = resid - mean(resid)
    scale_one = lax.rsqrt(mean(center * center) + EPSILON)
    hat_one = center * scale_one
    normed = hat_one * gains_ref[0:1] + biases_ref[3:4]
    normed_low = normed.astype(BF16)
    rank_one = dot_nt(normed_low, down(3)).astype(BF16)
    loads[2].wait()
    loads[3].wait()
    loads[4].wait()
    loads[5].wait()
    piece = 1024
    rank_two = jnp.zeros((rows, 16), F32)
    mixed = normed + biases_ref[2:3]
    for part in range(hidden // piece):
        cols = slice(part * piece, (part + 1) * piece)
        pre = (
            dot32(normed_low, wfc1[:, cols])
            + hidden_bias_ref[:, cols]
            + dot32(rank_one, hidden_up_ref[:, cols])
        )
        share = 0.5 + 0.5 * lax.erf(pre * 0.7071067811865476)
        slope[:, cols] = share + pre * (0.3989422804014327 * jnp.exp(-0.5 * pre * pre))
        active = (pre * share).astype(BF16)
        act[:, cols] = active
        rank_two = rank_two + dot_nt(active, hidden_down_ref[:, cols])
        mixed = mixed + dot32(active, wfc2[cols, :])
    rank_two = rank_two.astype(BF16)
    mixed = mixed + dot32(rank_two, up(4))
    center = mixed - mean(mixed)
    scale_two = lax.rsqrt(mean(center * center) + EPSILON)
    hat_two = center * scale_two
    outcome_ref[...] = (hat_two * gains_ref[1:2] + biases_ref[4:5]).astype(BF16)
    grad_sum = norm_backward(cotangent_ref[...].astype(F32) * gains_ref[1:2], hat_two, scale_two)
    grad_mixed = grad_sum.astype(BF16)
    put_term(mlp_mine, 2 * hidden, dot_tn(rank_two, grad_mixed))
    grad_rank = dot_nt(grad_mixed, up(4)).astype(BF16)
    put_term(mlp_mine, 0, dot_tn(grad_rank, act[...]))
    grad_one = jnp.zeros((rows, 16), F32)
    grad_normed = jnp.zeros((rows, width), F32)
    for part in range(hidden // piece):
        cols = slice(part * piece, (part + 1) * piece)
        grad_act = dot_nt(grad_mixed, wfc2[cols, :]) + dot32(grad_rank, hidden_down_ref[:, cols])
        grad_hidden = (grad_act.astype(BF16).astype(F32) * slope[:, cols]).astype(BF16)
        put_term(mlp_mine, hidden + part * piece, dot_tn(rank_one, grad_hidden))
        grad_one = grad_one + dot_nt(grad_hidden, hidden_up_ref[:, cols])
        grad_normed = grad_normed + dot_nt(grad_hidden, wfc1[:, cols])
    grad_one = grad_one.astype(BF16)
    put_term(mlp_mine, 2 * hidden + width, dot_tn(grad_one, normed_low))
    grad_normed = (grad_normed + dot32(grad_one, down(3))).astype(BF16).astype(F32)
    resid_grad = norm_backward((grad_sum + grad_normed) * gains_ref[0:1], hat_one, scale_one)
    grad_resid[...] = resid_grad
    grad_branch = resid_grad.astype(BF16)
    put_term(mlp_mine, 2 * hidden + 2 * width, dot_tn(rank_out, grad_branch))
    grad_rank = dot_nt(grad_branch, up(3)).astype(BF16)
    put_term(mlp_mine, 2 * hidden + 3 * width, dot_tn(grad_rank, context_low))
    turned = dot_nt(wout[...], grad_branch) + lax.dot_general(
        out_down_ref[...], grad_rank, (((0,), (1,)), ((), ())), preferred_element_type=F32
    )
    outgoing[...] = turned.astype(BF16).reshape(peers, 64, rows)

    loads[6].start()
    loads[7].start()

    def grad_copy(step):
        return remote(
            outgoing.at[me ^ step], incoming.at[step], grad_sem.at[0, step], grad_sem.at[1, step], me ^ step, core
        )

    for step in range(1, peers):
        grad_copy(step).start()
    mlp_scatter, mlp_gather, mlp_last = sum_copies(mlp_mine, mlp_parts, mlp_ref, mlp_sem, me, core)
    for copy in mlp_scatter:
        copy.start()
    incoming[0] = outgoing[me]

    row_at = lax.broadcasted_iota(jnp.int32, (16, rows), 0)
    minus = jnp.where(lax.broadcasted_iota(jnp.int32, (rows, 16), 1) < 3, -1.0, 0.0).astype(BF16)
    minus_rows = jnp.where(lax.broadcasted_iota(jnp.int32, (64, rows), 0) < 3, -1.0, 0.0).astype(BF16)

    def tail(value):
        high, middle, low = (part.astype(F32) for part in split_three(value))
        return jnp.where(row_at == 0, high, jnp.where(row_at == 1, middle, jnp.where(row_at == 2, low, 0.0))).astype(
            BF16
        )

    def prepare(step, _):
        cols = pl.ds(pl.multiple_of(step * rows, rows), rows)
        query = qkv_ref[step, 0:64, :].astype(F32) * LOG2E
        high = query.astype(BF16)
        qta[0:64, cols] = high
        qta[64:128, cols] = (query - high.astype(F32)).astype(BF16)
        qta[128:144, cols] = tail(lse_ref[:, cols])
        key = qkv_ref[step, 64:128, :]
        kt[:, cols] = key
        kk[cols, 0:128] = flip(jnp.concatenate([key, key], 0))
        kk[cols, 128:144] = minus
        vv[cols, :] = flip(jnp.concatenate([qkv_ref[step, 128:192, :], minus_rows], 0))
        gta[80:128, cols] = jnp.zeros((48, rows), BF16)
        return 0

    lax.fori_loop(0, peers, prepare, 0)

    def take_grad(step, _):
        cols = pl.ds(pl.multiple_of(step * rows, rows), rows)

        @pl.when(step > 0)
        def _():
            grad_copy(step).wait_recv()

        grad = incoming[step]
        gta[0:64, cols] = grad
        gta[64:80, cols] = tail(jnp.sum(grad.astype(F32) * context_ref[:, cols], 0, keepdims=True))
        both[cols, :] = flip(jnp.concatenate([qkv_ref[step, 0:64, :], grad], 0))
        return 0

    lax.fori_loop(0, peers, take_grad, 0)
    dqt[...] = jnp.zeros_like(dqt)
    first = lax.broadcasted_iota(jnp.int32, (block_k, 128), 1) < 64
    key_steps = length // block_k
    query_group = block_q // rows
    key_group = block_k // rows

    def dq_copy(step):
        return remote(dq_out.at[step], dq_in.at[me], dq_sem.at[0, step], dq_sem.at[1, step], me ^ step, core)

    def dkv_copy(step):
        return remote(dkv_out.at[step], dkv_in.at[me], dkv_sem.at[0, step], dkv_sem.at[1, step], me ^ step, core)

    def key_step(i, last):
        here = pl.ds(pl.multiple_of(i * block_k, block_k), block_k)

        def query_step(j, carry):
            dk, dv = carry
            cols = pl.ds(pl.multiple_of(j * block_q, block_q), block_q)
            probs = jnp.exp2(dot32(kk[here, :], qta[:, cols]))
            change = dot32(vv[here, :], gta[:, cols])
            low = (probs * change).astype(BF16)
            dv = dv + dot32(probs.astype(BF16), both[cols, :])
            dk = dk + dot32(low, both[cols, :])
            dq = dqt[:, cols] + dot32(kt[:, here], low)
            if not last:
                dqt[:, cols] = dq
            else:
                done = dq.astype(BF16)
                for part in range(query_group):
                    step = j * query_group + part
                    dq_out[step] = done[:, part * rows : (part + 1) * rows]

                    @pl.when(step > 0)
                    def _():
                        dq_copy(step).start()

            return dk, dv

        start = jnp.zeros((block_k, 128), F32)
        dk, dv = lax.fori_loop(0, length // block_q, query_step, (start, start))
        dkv = jnp.where(first, dk, dv).astype(BF16)
        for part in range(key_group):
            step = i * key_group + part
            dkv_out[step] = dkv[part * rows : (part + 1) * rows]

            @pl.when(step > 0)
            def _():
                dkv_copy(step).start()

    def key_steps_of(low, high):
        def one(i, _):
            key_step(i, False)
            return 0

        lax.fori_loop(low, high, one, 0)

    third = (key_steps - 1) // 3
    key_steps_of(0, third)
    sum_parts(mlp_scatter, mlp_mine, mlp_parts, mlp_ref, me, core)
    for copy in mlp_gather:
        copy.start()
    key_steps_of(third, 2 * third)
    for copy in mlp_gather:
        copy.wait_recv()
    mlp_last.start()
    key_steps_of(2 * third, key_steps - 1)
    key_step(key_steps - 1, True)

    dq_in[me] = dq_out[0]
    dkv_in[me] = dkv_out[0]
    for step in range(1, peers):
        dq_copy(step).wait_recv()
        dkv_copy(step).wait_recv()
    joined[:, 0:width] = (dq_in[...].reshape(width, rows).astype(F32).T * 0.125).astype(BF16)
    left = lax.broadcasted_iota(jnp.int32, (rows, 128), 1) < 64
    for two in range(peers // 2):
        even = dkv_in[2 * two].astype(F32)
        odd = dkv_in[2 * two + 1].astype(F32)
        cols = slice(width + two * 128, width + two * 128 + 128)
        joined[:, cols] = jnp.where(left, even, pltpu.roll(odd, 64, 1)).astype(BF16)
        cols = slice(2 * width + two * 128, 2 * width + two * 128 + 128)
        joined[:, cols] = jnp.where(left, pltpu.roll(even, 64, 1), odd).astype(BF16)
    ranks = []
    for part in range(3):
        grad = joined[:, part * width : (part + 1) * width]
        rank = dot_nt(grad, up(part)).astype(BF16)
        ranks.append(rank)
        put_term(att_mine, part * width, dot_tn(rank_ref[:, part * 16 : part * 16 + 16], grad))
        put_term(att_mine, (3 + part) * width, dot_tn(rank, x_ref[...]))
    att_scatter, att_gather, att_last = sum_copies(att_mine, att_parts, att_ref, att_sem, me, core)
    for copy in att_scatter:
        copy.start()
    loads[6].wait()
    loads[7].wait()
    total = grad_resid[...] + dot_nt(joined[...], wqkv[...])
    for part in range(3):
        total = total + dot32(ranks[part], down(part))
    grad_ref[...] = total
    sum_parts(att_scatter, att_mine, att_parts, att_ref, me, core)
    for copy in att_gather:
        copy.start()
    for copy in att_gather:
        copy.wait_recv()
    att_last.start()
    for step in range(1, peers):
        grad_copy(step).wait_send()
        dq_copy(step).wait_send()
        dkv_copy(step).wait_send()
    for copy in mlp_scatter + mlp_gather + att_scatter + att_gather:
        copy.wait_send()
    mlp_last.wait()
    att_last.wait()


def run_backward(
    x,
    cotangent,
    saved,
    weights,
    down,
    out_down,
    up,
    hidden_up,
    hidden_down,
    biases,
    hidden_bias,
    gains,
):
    rows, width = x.shape
    peers = H
    length = peers * rows
    hidden = hidden_bias.shape[1]
    block_q, block_k = 1024, 512
    vmem = pl.BlockSpec(memory_space=pltpu.VMEM)
    hbm = pl.BlockSpec(memory_space=pl.ANY)
    mlp_part = (2 * hidden + 4 * width) // peers
    att_part = 6 * width // peers
    return pl.pallas_call(
        functools.partial(backward_kernel, block_q, block_k),
        out_shape=[
            jax.ShapeDtypeStruct((rows, width), BF16),
            jax.ShapeDtypeStruct((rows, width), F32),
            jax.ShapeDtypeStruct((2, peers, 16, mlp_part), BF16),
            jax.ShapeDtypeStruct((2, peers, 16, att_part), BF16),
        ],
        in_specs=[vmem] * 7 + [hbm] * 8 + [vmem] * 8,
        out_specs=[vmem] * 4,
        scratch_shapes=[
            pltpu.VMEM((width, width), BF16),
            pltpu.VMEM((width, hidden), BF16),
            pltpu.VMEM((hidden, width), BF16),
            pltpu.VMEM((rows, hidden), F32),
            pltpu.VMEM((rows, hidden), BF16),
            pltpu.VMEM((rows, width), F32),
            pltpu.VMEM((peers, 16, mlp_part), BF16),
            pltpu.VMEM((peers, 16, mlp_part), BF16),
            pltpu.VMEM((peers, 16, att_part), BF16),
            pltpu.VMEM((peers, 16, att_part), BF16),
            pltpu.VMEM((peers, 64, rows), BF16),
            pltpu.VMEM((peers, 64, rows), BF16),
            pltpu.VMEM((144, length), BF16),
            pltpu.VMEM((128, length), BF16),
            pltpu.VMEM((length, 144), BF16),
            pltpu.VMEM((length, 128), BF16),
            pltpu.VMEM((64, length), BF16),
            pltpu.VMEM((length, 128), BF16),
            pltpu.VMEM((64, length), F32),
            pltpu.VMEM((peers, 64, rows), BF16),
            pltpu.VMEM((peers, 64, rows), BF16),
            pltpu.VMEM((peers, rows, 128), BF16),
            pltpu.VMEM((peers, rows, 128), BF16),
            pltpu.VMEM((rows, 3 * width), BF16),
            pltpu.SemaphoreType.DMA((4, 2)),
            pltpu.SemaphoreType.DMA((2, peers)),
            pltpu.SemaphoreType.DMA((2, peers)),
            pltpu.SemaphoreType.DMA((2, peers)),
            pltpu.SemaphoreType.DMA((4, peers)),
            pltpu.SemaphoreType.DMA((4, peers)),
        ],
        compiler_params=pltpu.CompilerParams(
            collective_id=2, has_side_effects=True, vmem_limit_bytes=VMEM_LIMIT
        ),
        name="run_backward",
    )(x, cotangent, *saved, *weights, down, out_down, up, hidden_up, hidden_down, biases, hidden_bias, gains)


def heads_body(
    tokens,
    cotangent,
    sequence_adapter_index,
    query_key_value_weight,
    output_weight,
    first_feed_weight,
    second_feed_weight,
    biases,
    value_bias_vector,
    first_feed_bias,
    norm_gain_pair,
    adapter_down_factors,
    output_down_factor,
    adapter_up_factors,
    hidden_up_factor,
    hidden_down_factor,
):
    _, rows, width = tokens.shape
    adapter_number = adapter_down_factors.shape[0]
    tokens = tokens[0]
    cotangent = cotangent[0]

    def pick(table):
        return lax.dynamic_index_in_dim(table, sequence_adapter_index[0], 0, keepdims=False)

    down, out_down, up, hidden_up, hidden_down = (
        pick(table)
        for table in (
            adapter_down_factors,
            output_down_factor,
            adapter_up_factors,
            hidden_up_factor,
            hidden_down_factor,
        )
    )

    down = down.reshape(-1, width)
    up = up.reshape(-1, width)
    *saved, wqkv_far, wout_far, wfc1_far, wfc2_far = attend_forward(
        tokens,
        query_key_value_weight,
        output_weight,
        first_feed_weight,
        second_feed_weight,
        down,
        up,
        biases,
        value_bias_vector[None],
    )
    weights = (
        query_key_value_weight,
        wqkv_far,
        output_weight,
        wout_far,
        first_feed_weight,
        wfc1_far,
        second_feed_weight,
        wfc2_far,
    )
    outcome, grad_tokens, mlp_terms, att_terms = run_backward(
        tokens,
        cotangent,
        saved,
        weights,
        down,
        out_down,
        up,
        hidden_up,
        hidden_down,
        biases,
        first_feed_bias[None],
        norm_gain_pair,
    )

    def side_by_side(terms):
        return terms.astype(F32).transpose(0, 2, 1, 3).reshape(2, 16, -1)

    mlp_terms = side_by_side(mlp_terms)
    att_terms = side_by_side(att_terms)
    hidden = first_feed_bias.shape[0]
    term_hd = mlp_terms[:, :, :hidden]
    term_uh = mlp_terms[:, :, hidden : 2 * hidden]
    term_u2, term_d1, term_uo, term_do = (
        mlp_terms[:, :, 2 * hidden + i * width : 2 * hidden + (i + 1) * width] for i in range(4)
    )
    term_at = [att_terms[:, :, i * width : (i + 1) * width] for i in range(6)]
    totals = (
        jnp.stack([*term_at[3:], term_d1], 1),
        term_do,
        jnp.stack([*term_at[:3], term_uo, term_u2], 1),
        term_uh,
        term_hd,
    )
    index_all = lax.all_gather(sequence_adapter_index, "fsdp", axis=0, tiled=True)
    picker = index_all[:, None] == jnp.arange(adapter_number, dtype=jnp.int32)[None, :]
    tables = []
    for every in totals:
        table = 0.0
        for seq in range(2):
            mask = picker[seq].reshape((adapter_number,) + (1,) * (every.ndim - 1))
            table = table + jnp.where(mask, every[seq][None], 0.0)
        tables.append(table)
    return (outcome[None], grad_tokens[None], *tables)


def solution(mesh):
    one_head_each = mesh.shape["ctx"] == H and mesh.shape["fsdp"] == 2
    return jax.shard_map(
        heads_body if one_head_each else gather_body,
        mesh=mesh,
        in_specs=(
            P("fsdp", "ctx", None),
            P("fsdp", "ctx", None),
            P("fsdp"),
            P("fsdp", None),
            P("fsdp", None),
            P("fsdp", None),
            P("fsdp", None),
            P(),
            P(),
            P(),
            P(),
            P(),
            P(),
            P(),
            P(),
            P(),
        ),
        out_specs=(P("fsdp", "ctx", None), P("fsdp", "ctx", None), P(), P(), P(), P(), P()),
        check_vma=False,
    )
```

```python
import functools

import jax
import jax.numpy as jnp
from jax import lax
from jax.experimental import pallas as pl
from jax.experimental.pallas import tpu as pltpu
from jax.sharding import PartitionSpec as P

H = 16


EPSILON = 1e-05
HIGHEST = lax.Precision.HIGHEST


def exact_sum(form, left, right):
    return jnp.einsum(form, left, right, precision=HIGHEST, preferred_element_type=jnp.float32)


def plain_sum(form, left, right):
    return jnp.einsum(form, left, right, preferred_element_type=jnp.float32)


def layer_norm(value, gain, shift):
    center = value - jnp.mean(value, -1, keepdims=True)
    spread = jnp.mean(center * center, -1, keepdims=True)
    return center * lax.rsqrt(spread + EPSILON) * gain + shift


def attn_weights(query_key_value_weight, output_weight):
    return (
        lax.all_gather(query_key_value_weight, "fsdp", axis=0, tiled=True),
        lax.all_gather(output_weight, "fsdp", axis=0, tiled=True),
    )


def mlp_weights(first_feed_weight, second_feed_weight):
    return (
        lax.all_gather(first_feed_weight, "fsdp", axis=0, tiled=True),
        lax.all_gather(second_feed_weight, "fsdp", axis=0, tiled=True),
    )


def to_heads(input_array):
    return input_array.reshape(
        input_array.shape[0], input_array.shape[1], H, input_array.shape[2] // H
    )


def row_block(input_array, block_index, block_rows):
    return lax.dynamic_slice_in_dim(input_array, block_index * block_rows, block_rows, 1)


def block_grads(queries, grad_out, log_total, row_delta, keys_blk, values_blk):
    scores = plain_sum("sqhd,skhd->shqk", queries, keys_blk)
    probs = jnp.exp(scores - log_total[..., None])
    prob_low = probs.astype(jnp.bfloat16)
    grad_probs = plain_sum("sqhd,skhd->shqk", grad_out, values_blk)
    grad_scores = (probs * (grad_probs - row_delta[..., None])).astype(jnp.bfloat16)
    return (prob_low, grad_scores)


def attention_forward(queries_heads, keys_heads, values_heads):
    seq_count, row_count, head_count, head_size = queries_heads.shape
    length = keys_heads.shape[1]
    block_rows = min(512, length)
    block_count = length // block_rows

    def max_step(running, block_index):
        running_max, running_total = running
        scores = plain_sum(
            "sqhd,skhd->shqk", queries_heads, row_block(keys_heads, block_index, block_rows)
        )
        new_max = jnp.maximum(running_max, jnp.max(scores, -1))
        running_total = running_total * jnp.exp(running_max - new_max) + jnp.sum(
            jnp.exp(scores - new_max[..., None]), -1
        )
        return ((new_max, running_total), None)

    start_max = jnp.full((seq_count, head_count, row_count), -1e30, jnp.float32)
    start_total = jnp.zeros((seq_count, head_count, row_count), jnp.float32)
    (final_max, final_total), unused = lax.scan(
        max_step, (start_max, start_total), jnp.arange(block_count)
    )
    log_total = final_max + jnp.log(final_total)

    def value_step(running, block_index):
        scores = plain_sum(
            "sqhd,skhd->shqk", queries_heads, row_block(keys_heads, block_index, block_rows)
        )
        prob_low = jnp.exp(scores - log_total[..., None]).astype(jnp.bfloat16)
        return (
            running
            + plain_sum(
                "shqk,skhd->sqhd", prob_low, row_block(values_heads, block_index, block_rows)
            ),
            None,
        )

    context, unused = lax.scan(
        value_step, jnp.zeros(queries_heads.shape, jnp.float32), jnp.arange(block_count)
    )
    return (context, log_total)


def gather_body(
    tokens,
    cotangent,
    sequence_adapter_index,
    query_key_value_weight,
    output_weight,
    first_feed_weight,
    second_feed_weight,
    biases,
    value_bias_vector,
    first_feed_bias,
    norm_gain_pair,
    adapter_down_factors,
    output_down_factor,
    adapter_up_factors,
    hidden_up_factor,
    hidden_down_factor,
):
    seq_count, row_count, model_width = tokens.shape
    adapter_number = adapter_down_factors.shape[0]
    picker = (
        sequence_adapter_index[:, None] == jnp.arange(adapter_number, dtype=jnp.int32)[None, :]
    ).astype(jnp.float32)

    def select_adapter(table):
        return jnp.einsum("sa,a...->s...", picker, table.astype(jnp.float32), precision=HIGHEST)

    def to_adapters(per_seq):
        return jnp.einsum("sa,s...->a...", picker, per_seq, precision=HIGHEST)

    selected_down = select_adapter(adapter_down_factors)
    selected_output = select_adapter(output_down_factor)
    selected_up = select_adapter(adapter_up_factors)
    hup_sel = select_adapter(hidden_up_factor)
    hdown_sel = select_adapter(hidden_down_factor)
    down_low = selected_down.astype(jnp.bfloat16)
    out_low = selected_output.astype(jnp.bfloat16)
    hdown_low = hdown_sel.astype(jnp.bfloat16)
    wqkv_full, wout_full = attn_weights(query_key_value_weight, output_weight)
    projected = plain_sum("std,de->ste", tokens, wqkv_full)
    down_att = plain_sum("std,sjrd->sjtr", tokens, down_low[:, :3])
    lifted = exact_sum("sjtr,sjrd->sjtd", down_att, selected_up[:, :3])
    queries = ((projected[..., :model_width] + biases[0] + lifted[:, 0]) * 0.125).astype(
        jnp.bfloat16
    )
    keys_own = (projected[..., model_width : 2 * model_width] + lifted[:, 1]).astype(jnp.bfloat16)
    values_own = (projected[..., 2 * model_width :] + value_bias_vector + lifted[:, 2]).astype(
        jnp.bfloat16
    )
    keys_all, values_all = (
        lax.all_gather(keys_own, "ctx", axis=1, tiled=True),
        lax.all_gather(values_own, "ctx", axis=1, tiled=True),
    )
    queries_heads = to_heads(queries)
    keys_heads = to_heads(keys_all)
    values_heads = to_heads(values_all)
    context, log_total = attention_forward(queries_heads, keys_heads, values_heads)
    context = context.reshape(seq_count, row_count, model_width)
    context_low = context.astype(jnp.bfloat16)
    down_out = plain_sum("std,srd->str", context_low, out_low)
    branch = (
        plain_sum("std,de->ste", context_low, wout_full)
        + biases[1]
        + exact_sum("str,srd->std", down_out, selected_up[:, 3])
    )

    def first_norm(value):
        return layer_norm(value, norm_gain_pair[0], biases[3])

    def second_norm(value):
        return layer_norm(value, norm_gain_pair[1], biases[4])

    def gelu_exact(value):
        return jax.nn.gelu(value, approximate=False)

    normed, norm_back = jax.vjp(first_norm, tokens.astype(jnp.float32) + branch)
    normed_low = normed.astype(jnp.bfloat16)
    wfc1_full, wfc2_full = mlp_weights(first_feed_weight, second_feed_weight)
    down_fc1 = plain_sum("std,srd->str", normed_low, down_low[:, 3])
    hidden_pre = (
        plain_sum("std,df->stf", normed_low, wfc1_full)
        + first_feed_bias
        + exact_sum("str,srf->stf", down_fc1, hup_sel)
    )
    activated, gelu_back = jax.vjp(gelu_exact, hidden_pre)
    act_low = activated.astype(jnp.bfloat16)
    down_fc2 = plain_sum("stf,srf->str", act_low, hdown_low)
    mixed_out = (
        plain_sum("stf,fd->std", act_low, wfc2_full)
        + biases[2]
        + exact_sum("str,srd->std", down_fc2, selected_up[:, 4])
    )
    outcome, out_back = jax.vjp(second_norm, normed + mixed_out)
    (grad_sum2,) = out_back(cotangent.astype(jnp.float32))
    grad_mixed = grad_sum2.astype(jnp.bfloat16)
    grad_up_fc2 = exact_sum("str,std->srd", down_fc2, grad_mixed)
    grad_rank_fc2 = exact_sum("std,srd->str", grad_mixed, selected_up[:, 4]).astype(jnp.bfloat16)
    grad_hdown = plain_sum("str,stf->srf", grad_rank_fc2, act_low)
    wfc1_full, wfc2_full = mlp_weights(first_feed_weight, second_feed_weight)
    grad_act = (
        plain_sum("std,fd->stf", grad_mixed, wfc2_full)
        + plain_sum("str,srf->stf", grad_rank_fc2, hdown_low)
    ).astype(jnp.bfloat16)
    (grad_hidden,) = gelu_back(grad_act.astype(jnp.float32))
    grad_hidden = grad_hidden.astype(jnp.bfloat16)
    grad_hup = exact_sum("str,stf->srf", down_fc1, grad_hidden)
    grad_rank_fc1 = exact_sum("stf,srf->str", grad_hidden, hup_sel).astype(jnp.bfloat16)
    grad_down_fc1 = plain_sum("str,std->srd", grad_rank_fc1, normed_low)
    grad_normed_low = (
        plain_sum("stf,df->std", grad_hidden, wfc1_full)
        + plain_sum("str,srd->std", grad_rank_fc1, down_low[:, 3])
    ).astype(jnp.bfloat16)
    (grad_resid,) = norm_back(grad_sum2 + grad_normed_low.astype(jnp.float32))
    mlp_hup = to_adapters(grad_hup)
    mlp_hdown = to_adapters(grad_hdown)
    mlp_fc1 = to_adapters(grad_down_fc1)
    mlp_fc2 = to_adapters(grad_up_fc2)
    mlp_hup, mlp_hdown, mlp_fc1, mlp_fc2 = lax.psum(
        (mlp_hup, mlp_hdown, mlp_fc1, mlp_fc2), ("ctx", "fsdp")
    )
    grad_branch = grad_resid.astype(jnp.bfloat16)
    grad_up_out = exact_sum("str,std->srd", down_out, grad_branch)
    grad_rank_out = exact_sum("std,srd->str", grad_branch, selected_up[:, 3]).astype(jnp.bfloat16)
    grad_out_down = plain_sum("str,std->srd", grad_rank_out, context_low)
    wqkv_full, wout_full = attn_weights(query_key_value_weight, output_weight)
    grad_context = (
        plain_sum("std,ed->ste", grad_branch, wout_full)
        + plain_sum("str,srd->std", grad_rank_out, out_low)
    ).astype(jnp.bfloat16)
    row_delta = jnp.sum(to_heads(grad_context.astype(jnp.float32) * context), -1)
    delta_heads = jnp.swapaxes(row_delta, 1, 2)
    grad_heads = to_heads(grad_context)
    length = keys_all.shape[1]
    block_rows = min(512, length)
    block_count = length // block_rows

    def key_step(block_index, running):
        grad_query, grad_key, grad_value = running
        keys_blk = row_block(keys_heads, block_index, block_rows)
        values_blk = row_block(values_heads, block_index, block_rows)
        prob_low, grad_scores = block_grads(
            queries_heads, grad_heads, log_total, delta_heads, keys_blk, values_blk
        )
        grad_query = grad_query + plain_sum("shqk,skhd->sqhd", grad_scores, keys_blk)
        grad_key = lax.dynamic_update_slice_in_dim(
            grad_key,
            plain_sum("shqk,sqhd->skhd", grad_scores, queries_heads),
            block_index * block_rows,
            1,
        )
        grad_value = lax.dynamic_update_slice_in_dim(
            grad_value,
            plain_sum("shqk,sqhd->skhd", prob_low, grad_heads),
            block_index * block_rows,
            1,
        )
        return (grad_query, grad_key, grad_value)

    start_query = jnp.zeros(queries_heads.shape, jnp.float32)
    start_keys = jnp.zeros(keys_heads.shape, jnp.float32)
    grad_query, grad_key_all, grad_value_all = lax.fori_loop(
        0, block_count, key_step, (start_query, start_keys, start_keys)
    )
    grad_keys, grad_values = (
        lax.psum_scatter(
            grad_key_all.reshape(seq_count, length, model_width).astype(jnp.bfloat16),
            "ctx",
            scatter_dimension=1,
            tiled=True,
        ).astype(jnp.float32),
        lax.psum_scatter(
            grad_value_all.reshape(seq_count, length, model_width).astype(jnp.bfloat16),
            "ctx",
            scatter_dimension=1,
            tiled=True,
        ).astype(jnp.float32),
    )
    grad_qlin = grad_query.reshape(seq_count, row_count, model_width).astype(jnp.bfloat16) * 0.125
    grad_key_low = grad_keys.astype(jnp.bfloat16)
    grad_value_low = grad_values.astype(jnp.bfloat16)
    stacked = jnp.stack([grad_qlin, grad_key_low, grad_value_low], 1)
    grad_up_att = exact_sum("sjtr,sjtd->sjrd", down_att, stacked)
    grad_rank_att = exact_sum("sjtd,sjrd->sjtr", stacked, selected_up[:, :3]).astype(jnp.bfloat16)
    grad_down_att = plain_sum("sjtr,std->sjrd", grad_rank_att, tokens)
    joined = jnp.concatenate([grad_qlin, grad_key_low, grad_value_low], -1)
    grad_tokens = (
        grad_resid
        + plain_sum("ste,de->std", joined, wqkv_full)
        + plain_sum("sjtr,sjrd->std", grad_rank_att, down_low[:, :3])
    )
    attn_down = to_adapters(grad_down_att)
    attn_out = to_adapters(grad_out_down)
    attn_up = to_adapters(jnp.concatenate([grad_up_att, grad_up_out[:, None]], 1))
    attn_down, attn_out, attn_up = lax.psum((attn_down, attn_out, attn_up), ("ctx", "fsdp"))
    total_down = jnp.concatenate([attn_down, mlp_fc1[:, None]], 1)
    total_up = jnp.concatenate([attn_up, mlp_fc2[:, None]], 1)
    return (
        outcome.astype(jnp.bfloat16),
        grad_tokens,
        total_down,
        attn_out,
        total_up,
        mlp_hup,
        mlp_hdown,
    )


BF16 = jnp.bfloat16
F32 = jnp.float32
LOG2E = 1.4426950408889634
VMEM_LIMIT = 60 * 2**20
MESH = pl.DeviceIdType.MESH


def dot32(left, right):
    return jnp.dot(left, right, preferred_element_type=F32)


def dot_nt(left, right):
    return lax.dot_general(left, right, (((1,), (1,)), ((), ())), preferred_element_type=F32)


def dot_tn(left, right):
    return lax.dot_general(left, right, (((0,), (0,)), ((), ())), preferred_element_type=F32)


def split_three(value):
    high = value.astype(BF16)
    rest = value - high.astype(F32)
    middle = rest.astype(BF16)
    return high, middle, (rest - middle.astype(F32)).astype(BF16)


def flip(value):
    return value.astype(F32).T.astype(BF16)


def remote(src, dst, send_sem, recv_sem, device):
    return pltpu.make_async_remote_copy(
        src_ref=src,
        dst_ref=dst,
        send_sem=send_sem,
        recv_sem=recv_sem,
        device_id=device,
        device_id_type=MESH,
    )


class Place:
    def __init__(self):
        self.ctx = lax.axis_index("ctx")
        self.core = lax.axis_index("fsdp")
        self.half = self.ctx // (H // 2)
        self.low = self.ctx % (H // 2)
        self.me = self.low * 2 + self.core
        self.swaps = self.core != self.half
        self.pair = (self.core + self.half) % 2
        self.sibling = (self.ctx, 1 - self.core)
        self.partner = ((self.ctx + H // 2) % H, 1 - self.core)

    def peer(self, step):
        number = self.me ^ step
        return (self.half * (H // 2) + number // 2, number % 2)

    def greet(self):
        barrier = pltpu.get_barrier_semaphore()
        for step in range(1, H):
            pl.semaphore_signal(barrier, inc=1, device_id=self.peer(step), device_id_type=MESH)
        pl.semaphore_signal(barrier, inc=1, device_id=self.partner, device_id_type=MESH)
        pl.semaphore_wait(barrier, H)


def sum_copies(mine, parts, total, sems, place):
    own = total.at[place.low, place.pair, place.half]
    both = total.at[place.low, place.pair]
    scatter = [
        remote(mine.at[place.me ^ step], parts.at[step], sems.at[0, step], sems.at[1, step], place.peer(step))
        for step in range(1, H)
    ]
    cross = remote(own, own, sems.at[0, 0], sems.at[1, 0], place.partner)
    gather = [
        remote(both, both, sems.at[2, step], sems.at[3, step], place.peer(step))
        for step in range(1, H)
    ]
    return scatter, cross, gather


def sum_parts(scatter, mine, parts, total, place):
    value = mine[place.me].astype(F32)
    for step, copy in enumerate(scatter, 1):
        copy.wait_recv()
        value = value + parts[step].astype(F32)
    total[place.low, place.pair, place.half] = value.astype(BF16)


def put_term(mine, base, term):
    units = mine.shape[2] // 128
    for unit in range(term.shape[1] // 128):
        at = base // 128 + unit
        lanes = slice(at % units * 128, at % units * 128 + 128)
        mine[at // units, :, lanes] = term[:, unit * 128 : unit * 128 + 128].astype(BF16)


def layer_kernel(
    block_q,
    block_k,
    index_ref,
    tokens_ref,
    cotangent_ref,
    wqkv_ref,
    wout_ref,
    wfc1_ref,
    wfc2_ref,
    down_table,
    up_table,
    out_down_table,
    hidden_up_table,
    hidden_down_table,
    biases_ref,
    value_bias_ref,
    hidden_bias_ref,
    gains_ref,
    outcome_ref,
    grad_ref,
    index_out,
    hidden_down_out,
    hidden_up_out,
    down_out,
    up_out,
    out_down_out,
    wqkv_far,
    wfc1_far,
    wide,
    wfc2,
    wout,
    big,
    act,
    small,
    small_hidden,
    x,
    cotangent,
    rank_att,
    outgoing,
    qkv,
    leaving,
    arrived,
    incoming,
    context,
    qta,
    gta,
    kk,
    vv,
    kt,
    both,
    dqt,
    dq_in,
    dkv_out,
    dkv_in,
    grad_out,
    grad_in,
    mlp_mine,
    mlp_parts,
    mlp_total,
    att_mine,
    att_parts,
    att_total,
    load_sem,
    core_sem,
    swap_sem,
    kv_sem,
    q_sem,
    back_sem,
    grad_sem,
    dq_sem,
    dkv_sem,
    mlp_sem,
    att_sem,
):
    peers, _, rows = qkv.shape
    length = peers * rows
    width = x.shape[1]
    depth = width // 2
    hidden = hidden_bias_ref.shape[1]
    adapters = hidden_up_table.shape[0] // 16
    place = Place()
    me, core = place.me, place.core
    other = 1 - core
    wqkv = wide.at[:, 0 : 3 * width]
    up_at = down_table.shape[0]
    out_down_at = up_at + up_table.shape[0]

    def half_of(full, owner):
        count = full.shape[0] // 2
        return full.at[pl.ds(pl.multiple_of(owner * count, count), count), :]

    def load(source, target, number):
        return pltpu.make_async_copy(source, target, load_sem.at[number])

    def to_sibling(source, target, number):
        return remote(source, target, core_sem.at[0, number], core_sem.at[1, number], place.sibling)

    load_wqkv = load(wqkv_ref, half_of(wqkv, core), 0)
    load_wout = load(wout_ref, half_of(wout, core), 1)
    load_tables = [
        load(down_table, wfc2.at[0:up_at], 2),
        load(up_table, wfc2.at[up_at:out_down_at], 3),
        load(out_down_table, wfc2.at[out_down_at : out_down_at + out_down_table.shape[0]], 4),
        load(hidden_up_table, act.at[0 : 16 * adapters], 5),
        load(hidden_down_table, act.at[16 * adapters : 32 * adapters], 6),
    ]
    load_x = load(tokens_ref, x, 7)
    load_cotangent = load(cotangent_ref, cotangent, 8)
    load_wfc1 = load(wfc1_ref, half_of(wide, core), 9)
    load_wfc1_far = load(wfc1_far, half_of(wide, other), 10)
    load_wfc2 = load(wfc2_ref, half_of(wfc2, core), 11)
    again_wqkv = load(wqkv_ref, half_of(wqkv, core), 12)
    again_wqkv_far = load(wqkv_far, half_of(wqkv, other), 13)
    give_wqkv = to_sibling(wqkv_ref, half_of(wqkv, core), 0)
    give_wout = to_sibling(wout_ref, half_of(wout, core), 1)
    give_index = to_sibling(index_out.at[core], index_out.at[core], 2)
    count = small.shape[0]
    give_small = [to_sibling(small, wide.at[0:count, 3 * width : 4 * width], 3)] + [
        to_sibling(
            small_hidden.at[:, part * width : (part + 1) * width],
            wide.at[count + 32 * part : count + 32 * part + 32, 3 * width : 4 * width],
            4 + part,
        )
        for part in range(hidden // width)
    ]
    give_wfc2 = to_sibling(wfc2_ref, half_of(wfc2, core), 8)
    give_wfc1 = to_sibling(wfc1_ref, wfc1_far, 9)
    give_wqkv_again = to_sibling(wqkv_ref, wqkv_far, 10)
    swap_x = remote(tokens_ref, x, swap_sem.at[0, 0], swap_sem.at[1, 0], place.partner)
    swap_cotangent = remote(cotangent_ref, cotangent, swap_sem.at[0, 1], swap_sem.at[1, 1], place.partner)

    load_wqkv.start()
    for copy in load_tables:
        copy.start()
    load_wout.start()

    @pl.when(jnp.logical_not(place.swaps))
    def _():
        load_x.start()
        load_cotangent.start()

    adapter = index_ref[0]
    index_out[core] = jnp.full(index_out.shape[1:], adapter, jnp.int32).astype(F32)
    place.greet()

    @pl.when(place.swaps)
    def _():
        swap_x.start()

    give_wqkv.start()
    give_index.start()

    for copy in load_tables:
        copy.wait()

    def select(table, base, group, groups, target, at):
        chosen = jnp.full((16, table.shape[1]), adapter, jnp.int32)
        value = jnp.zeros((16, table.shape[1]), F32)
        for number in range(adapters):
            start = pl.multiple_of(base + 16 * (number * groups + group), 16)
            value = jnp.where(chosen == number, table[pl.ds(start, 16), :].astype(F32), value)
        target[pl.ds(pl.multiple_of(at + 16 * group, 16), 16), :] = value.astype(BF16)

    def select_down(group, _):
        select(wfc2, 0, group, 4, small, 0)
        return 0

    def select_up(group, _):
        select(wfc2, up_at, group, 5, small, 64)
        return 0

    lax.fori_loop(0, 4, select_down, 0)
    lax.fori_loop(0, 5, select_up, 0)
    select(wfc2, out_down_at, 0, 1, small, 144)
    for part in range(2):
        select(act, 16 * adapters * part, 0, 1, small_hidden, 16 * part)
    for copy in give_small:
        copy.start()
    give_wout.start()
    for copy in give_small:
        copy.wait()

    @pl.when(place.swaps)
    def _():
        small[...] = wide[0:count, 3 * width : 4 * width]
        for part in range(hidden // width):
            small_hidden[:, part * width : (part + 1) * width] = wide[
                count + 32 * part : count + 32 * part + 32, 3 * width : 4 * width
            ]

    hidden_up_ref = small_hidden.at[0:16]
    hidden_down_ref = small_hidden.at[16:32]
    out_down_ref = small.at[144:160]

    def down(j):
        return small[16 * j : 16 * j + 16]

    def up(j):
        return small[64 + 16 * j : 80 + 16 * j]

    load_wfc2.start()
    give_wfc2.start()

    @pl.when(place.swaps)
    def _():
        swap_x.wait_recv()

    @pl.when(jnp.logical_not(place.swaps))
    def _():
        load_x.wait()

    rank_att[...] = dot_nt(x[...], small[0:48]).astype(BF16)
    x_own = x[:, pl.ds(pl.multiple_of(core * depth, depth), depth)]
    x_other = x[:, pl.ds(pl.multiple_of(other * depth, depth), depth)]
    load_wqkv.wait()
    for part in (1, 2, 0):
        cols = slice(part * width, (part + 1) * width)
        big[part * rows : (part + 1) * rows] = dot32(x_own, half_of(wqkv, core)[:, cols]) + dot32(
            rank_att[:, part * 16 : part * 16 + 16], up(part)
        )
    give_wqkv.wait_recv()

    def project(part):
        cols = slice(part * width, (part + 1) * width)
        value = big[part * rows : (part + 1) * rows] + dot32(x_other, half_of(wqkv, other)[:, cols])
        if part == 0:
            value = (value + biases_ref[0:1, :]) * 0.125
        if part == 2:
            value = value + value_bias_ref[...]
        for two in range(peers // 2):
            turned = value[:, two * 128 : two * 128 + 128].T.astype(BF16)
            outgoing[2 * two, part * 64 : part * 64 + 64] = turned[0:64]
            outgoing[2 * two + 1, part * 64 : part * 64 + 64] = turned[64:128]

    def kv_copy(step):
        return remote(
            outgoing.at[me ^ step, 64:192], qkv.at[step, 64:192], kv_sem.at[0, step], kv_sem.at[1, step], place.peer(step)
        )

    def q_copy(step):
        return remote(
            outgoing.at[me ^ step, 0:64], qkv.at[step, 0:64], q_sem.at[0, step], q_sem.at[1, step], place.peer(step)
        )

    def back_copy(step):
        return remote(leaving.at[step], arrived.at[me], back_sem.at[0, step], back_sem.at[1, step], place.peer(step))

    project(1)
    project(2)
    for step in range(1, peers):
        kv_copy(step).start()
    project(0)
    for step in range(1, peers):
        q_copy(step).start()
    give_wfc1.start()
    give_wqkv_again.start()
    load_wfc1.start()

    @pl.when(place.swaps)
    def _():
        swap_cotangent.start()

    qkv[0] = outgoing[me]

    row_at = lax.broadcasted_iota(jnp.int32, (16, rows), 0)
    ones = (row_at == 0).astype(F32).astype(BF16)
    minus = jnp.where(lax.broadcasted_iota(jnp.int32, (rows, 16), 1) < 3, -1.0, 0.0).astype(BF16)
    minus_rows = jnp.where(lax.broadcasted_iota(jnp.int32, (64, rows), 0) < 3, -1.0, 0.0).astype(BF16)

    def tail(value):
        at = lax.broadcasted_iota(jnp.int32, (16, value.shape[1]), 0)
        high, middle, low = (part.astype(F32) for part in split_three(value))
        return jnp.where(at == 0, high, jnp.where(at == 1, middle, jnp.where(at == 2, low, 0.0))).astype(BF16)

    def take_key(step, _):
        cols = pl.ds(pl.multiple_of(step * rows, rows), rows)

        @pl.when(step > 0)
        def _():
            kv_copy(step).wait_recv()

        key = qkv[step, 64:128, :]
        value = qkv[step, 128:192, :]
        kt[:, cols] = key
        kk[cols, 0:128] = flip(jnp.concatenate([key, key], 0))
        kk[cols, 128:144] = minus
        vv[cols, :] = flip(jnp.concatenate([value, minus_rows], 0))
        gta[0:64, cols] = value
        gta[64:80, cols] = ones
        gta[80:128, cols] = jnp.zeros((48, rows), BF16)
        return 0

    lax.fori_loop(0, peers, take_key, 0)
    steps = length // block_k
    group = block_q // rows

    def forward_step(i, _):
        def take_query(part, _):
            step = i * group + part
            here = pl.ds(pl.multiple_of(step * rows, rows), rows)

            @pl.when(step > 0)
            def _():
                q_copy(step).wait_recv()

            query = qkv[step, 0:64, :].astype(F32) * LOG2E
            high = query.astype(BF16)
            qta[0:64, here] = high
            qta[64:128, here] = (query - high.astype(F32)).astype(BF16)
            return 0

        lax.fori_loop(0, group, take_query, 0)
        cols = pl.ds(pl.multiple_of(i * block_q, block_q), block_q)
        query = qta.at[0:128, cols]
        block = dot32(kk[0:block_k, 0:128], query[...])
        big[0:block_k] = block

        def half(j, now, carry):
            peak, running, total = carry
            later = jnp.minimum(j + 1, steps - 1)
            here = pl.ds(pl.multiple_of(j * block_k, block_k), block_k)
            there = pl.ds(pl.multiple_of(later * block_k, block_k), block_k)
            ahead = dot32(kk[there, 0:128], query[...])
            big[(1 - now) * block_k : (2 - now) * block_k] = ahead
            new = jnp.maximum(running, peak)
            weights = jnp.exp2(big[now * block_k : (now + 1) * block_k] - new).astype(BF16)
            total = total * jnp.exp2(running - new) + dot32(gta[0:80, here], weights)
            return jnp.max(ahead, 0, keepdims=True), new, total

        def pair(j, carry):
            return half(2 * j + 1, 1, half(2 * j, 0, carry))

        start = (
            jnp.max(block, 0, keepdims=True),
            jnp.full((1, block_q), -jnp.inf, F32),
            jnp.zeros((80, block_q), F32),
        )
        _, top, total = lax.fori_loop(0, steps // 2, pair, start)
        weight_sum = total[64:65]
        result = total[0:64] / weight_sum
        context[:, cols] = result
        qta[128:144, cols] = tail(top + jnp.log2(weight_sum))
        low = result.astype(BF16)
        for part in range(group):
            step = i * group + part
            leaving[step] = low[:, part * rows : (part + 1) * rows]

            @pl.when(step > 0)
            def _():
                back_copy(step).start()

        return 0

    lax.fori_loop(0, 1, forward_step, 0)
    give_wfc1.wait_recv()
    load_wfc1_far.start()
    lax.fori_loop(1, length // block_q, forward_step, 0)
    arrived[me] = leaving[0]

    def mean(value):
        return jnp.mean(value, -1, keepdims=True)

    def norm_backward(grad, hat, scale):
        return scale * (grad - mean(grad) - hat * mean(grad * hat))

    load_wout.wait()
    give_wout.wait_recv()
    for step in range(1, peers):
        back_copy(step).wait_recv()
    context_low = flip(arrived[...].reshape(width, rows))
    rank_out = dot_nt(context_low, out_down_ref[...]).astype(BF16)
    resid = x[...].astype(F32) + dot32(context_low, wout[...]) + biases_ref[1:2] + dot32(rank_out, up(3))
    center = resid - mean(resid)
    scale_one = lax.rsqrt(mean(center * center) + EPSILON)
    hat_one = center * scale_one
    normed = hat_one * gains_ref[0:1] + biases_ref[3:4]
    normed_low = normed.astype(BF16)
    rank_one = dot_nt(normed_low, down(3)).astype(BF16)
    load_wfc1.wait()
    load_wfc1_far.wait()
    load_wfc2.wait()
    give_wfc2.wait_recv()
    piece = 1024
    rank_two = jnp.zeros((rows, 16), F32)
    mixed = normed + biases_ref[2:3]
    for part in range(hidden // piece):
        cols = slice(part * piece, (part + 1) * piece)
        pre = (
            dot32(normed_low, wide[:, cols])
            + hidden_bias_ref[:, cols]
            + dot32(rank_one, hidden_up_ref[:, cols])
        )
        share = 0.5 + 0.5 * lax.erf(pre * 0.7071067811865476)
        big[part * rows : (part + 1) * rows] = share + pre * (0.3989422804014327 * jnp.exp(-0.5 * pre * pre))
        active = (pre * share).astype(BF16)
        act[:, cols] = active
        rank_two = rank_two + dot_nt(active, hidden_down_ref[:, cols])
        mixed = mixed + dot32(active, wfc2[cols, :])
    rank_two = rank_two.astype(BF16)
    mixed = mixed + dot32(rank_two, up(4))
    center = mixed - mean(mixed)
    scale_two = lax.rsqrt(mean(center * center) + EPSILON)
    hat_two = center * scale_two

    @pl.when(place.swaps)
    def _():
        swap_cotangent.wait_recv()

    @pl.when(jnp.logical_not(place.swaps))
    def _():
        load_cotangent.wait()

    grad_sum = norm_backward(cotangent[...].astype(F32) * gains_ref[1:2], hat_two, scale_two)
    outcome = cotangent
    outcome[...] = (hat_two * gains_ref[1:2] + biases_ref[4:5]).astype(BF16)
    home_outcome = remote(outcome, outcome_ref, swap_sem.at[0, 2], swap_sem.at[1, 2], place.partner)

    @pl.when(place.swaps)
    def _():
        home_outcome.start()

    @pl.when(jnp.logical_not(place.swaps))
    def _():
        outcome_ref[...] = outcome[...]

    grad_mixed = grad_sum.astype(BF16)
    put_term(mlp_mine, 2 * hidden, dot_tn(rank_two, grad_mixed))
    grad_rank = dot_nt(grad_mixed, up(4)).astype(BF16)
    put_term(mlp_mine, 0, dot_tn(grad_rank, act[...]))
    grad_one = jnp.zeros((rows, 16), F32)
    grad_normed = jnp.zeros((rows, width), F32)
    for part in range(hidden // piece):
        cols = slice(part * piece, (part + 1) * piece)
        grad_act = dot_nt(grad_mixed, wfc2[cols, :]) + dot32(grad_rank, hidden_down_ref[:, cols])
        grad_hidden = (grad_act.astype(BF16).astype(F32) * big[part * rows : (part + 1) * rows]).astype(BF16)
        put_term(mlp_mine, hidden + part * piece, dot_tn(rank_one, grad_hidden))
        grad_one = grad_one + dot_nt(grad_hidden, hidden_up_ref[:, cols])
        grad_normed = grad_normed + dot_nt(grad_hidden, wide[:, cols])
    grad_one = grad_one.astype(BF16)
    put_term(mlp_mine, 2 * hidden + width, dot_tn(grad_one, normed_low))
    grad_normed = (grad_normed + dot32(grad_one, down(3))).astype(BF16).astype(F32)
    resid_grad = norm_backward((grad_sum + grad_normed) * gains_ref[0:1], hat_one, scale_one)
    grad_resid = big.at[0:rows]
    grad_resid[...] = resid_grad
    grad_branch = resid_grad.astype(BF16)
    put_term(mlp_mine, 2 * hidden + 2 * width, dot_tn(rank_out, grad_branch))
    grad_rank = dot_nt(grad_branch, up(3)).astype(BF16)
    put_term(mlp_mine, 2 * hidden + 3 * width, dot_tn(grad_rank, context_low))
    turned = dot_nt(wout[...], grad_branch) + lax.dot_general(
        out_down_ref[...], grad_rank, (((0,), (1,)), ((), ())), preferred_element_type=F32
    )
    for step in range(1, peers):
        kv_copy(step).wait_send()
        q_copy(step).wait_send()
        back_copy(step).wait_send()
    outgoing[:, 0:64] = turned.astype(BF16).reshape(peers, 64, rows)

    def grad_copy(step):
        return remote(
            outgoing.at[me ^ step, 0:64], incoming.at[step], grad_sem.at[0, step], grad_sem.at[1, step], place.peer(step)
        )

    for step in range(1, peers):
        grad_copy(step).start()
    mlp_scatter, mlp_cross, mlp_gather = sum_copies(mlp_mine, mlp_parts, mlp_total, mlp_sem, place)
    for copy in mlp_scatter:
        copy.start()
    incoming[0] = outgoing[me, 0:64]
    give_wqkv_again.wait_recv()
    again_wqkv.start()
    again_wqkv_far.start()
    dqt[...] = jnp.zeros_like(dqt)

    def take_grad(step, _):
        cols = pl.ds(pl.multiple_of(step * rows, rows), rows)

        @pl.when(step > 0)
        def _():
            grad_copy(step).wait_recv()

        grad = incoming[step]
        gta[0:64, cols] = grad
        gta[64:80, cols] = tail(jnp.sum(grad.astype(F32) * context[:, cols], 0, keepdims=True))
        both[cols, :] = flip(jnp.concatenate([qkv[step, 0:64, :], grad], 0))
        return 0

    lax.fori_loop(0, peers, take_grad, 0)
    first = lax.broadcasted_iota(jnp.int32, (block_k, 128), 1) < 64
    key_group = block_k // rows
    dq_out = leaving

    def dq_copy(step):
        return remote(dq_out.at[step], dq_in.at[me], dq_sem.at[0, step], dq_sem.at[1, step], place.peer(step))

    def dkv_copy(step):
        return remote(dkv_out.at[step], dkv_in.at[me], dkv_sem.at[0, step], dkv_sem.at[1, step], place.peer(step))

    def key_step(i, last):
        here = pl.ds(pl.multiple_of(i * block_k, block_k), block_k)

        def query_step(j, carry):
            dk, dv = carry
            cols = pl.ds(pl.multiple_of(j * block_q, block_q), block_q)
            probs = jnp.exp2(dot32(kk[here, :], qta[:, cols]))
            change = dot32(vv[here, :], gta[:, cols])
            low = (probs * change).astype(BF16)
            dv = dv + dot32(probs.astype(BF16), both[cols, :])
            dk = dk + dot32(low, both[cols, :])
            dq = dqt[:, cols] + dot32(kt[:, here], low)
            if not last:
                dqt[:, cols] = dq
            else:
                done = dq.astype(BF16)
                for part in range(group):
                    step = j * group + part
                    dq_out[step] = done[:, part * rows : (part + 1) * rows]

                    @pl.when(step > 0)
                    def _():
                        dq_copy(step).start()

            return dk, dv

        start = jnp.zeros((block_k, 128), F32)
        dk, dv = lax.fori_loop(0, length // block_q, query_step, (start, start))
        dkv = jnp.where(first, dk, dv).astype(BF16)
        for part in range(key_group):
            step = i * key_group + part
            dkv_out[step] = dkv[part * rows : (part + 1) * rows]

            @pl.when(step > 0)
            def _():
                dkv_copy(step).start()

    def key_steps_of(low, high):
        def one(i, _):
            key_step(i, False)
            return 0

        lax.fori_loop(low, high, one, 0)

    third = (steps - 1) // 3
    key_steps_of(0, third)
    sum_parts(mlp_scatter, mlp_mine, mlp_parts, mlp_total, place)
    mlp_cross.start()
    key_steps_of(third, 2 * third)
    mlp_cross.wait_recv()
    for copy in mlp_gather:
        copy.start()
    key_steps_of(2 * third, steps - 1)
    key_step(steps - 1, True)

    for copy in mlp_gather:
        copy.wait_recv()

    def spread(total, parts):
        units = total.shape[4] // 128
        for half in range(2):
            for unit in range(peers * units):
                peer = unit // units
                lanes = slice(unit % units * 128, unit % units * 128 + 128)
                for target, low, high in parts:
                    if low <= unit * 128 < high:
                        at = unit * 128 - low
                        target(half)[:, at : at + 128] = total[peer // 2, (peer % 2 + half) % 2, half, :, lanes]

    spread(
        mlp_total,
        (
            (lambda half: hidden_down_out.at[half], 0, hidden),
            (lambda half: hidden_up_out.at[half], hidden, 2 * hidden),
            (lambda half: up_out.at[half, 4], 2 * hidden, 2 * hidden + width),
            (lambda half: down_out.at[half, 3], 2 * hidden + width, 2 * hidden + 2 * width),
            (lambda half: up_out.at[half, 3], 2 * hidden + 2 * width, 2 * hidden + 3 * width),
            (lambda half: out_down_out.at[half], 2 * hidden + 3 * width, 2 * hidden + 4 * width),
        ),
    )

    joined = act.at[:, 0 : 3 * width]
    dq_in[me] = dq_out[0]
    dkv_in[me] = dkv_out[0]
    for step in range(1, peers):
        dkv_copy(step).wait_recv()
    left = lax.broadcasted_iota(jnp.int32, (rows, 128), 1) < 64
    for two in range(peers // 2):
        even = dkv_in[2 * two].astype(F32)
        odd = dkv_in[2 * two + 1].astype(F32)
        cols = slice(width + two * 128, width + two * 128 + 128)
        joined[:, cols] = jnp.where(left, even, pltpu.roll(odd, 64, 1)).astype(BF16)
        cols = slice(2 * width + two * 128, 2 * width + two * 128 + 128)
        joined[:, cols] = jnp.where(left, pltpu.roll(even, 64, 1), odd).astype(BF16)
    for step in range(1, peers):
        dq_copy(step).wait_recv()
    joined[:, 0:width] = (dq_in[...].reshape(width, rows).astype(F32).T * 0.125).astype(BF16)
    ranks = []
    for part in range(3):
        grad = joined[:, part * width : (part + 1) * width]
        rank = dot_nt(grad, up(part)).astype(BF16)
        ranks.append(rank)
        put_term(att_mine, part * width, dot_tn(rank_att[:, part * 16 : part * 16 + 16], grad))
        put_term(att_mine, (3 + part) * width, dot_tn(rank, x[...]))
    att_scatter, att_cross, att_gather = sum_copies(att_mine, att_parts, att_total, att_sem, place)
    for copy in att_scatter:
        copy.start()
    again_wqkv.wait()
    again_wqkv_far.wait()
    piece = width // 4
    home = [
        remote(
            grad_out.at[:, part * piece : (part + 1) * piece],
            grad_in.at[:, part * piece : (part + 1) * piece],
            swap_sem.at[0, 3 + part],
            swap_sem.at[1, 3 + part],
            place.partner,
        )
        for part in range(4)
    ]
    for part in range(4):
        cols = slice(part * piece, (part + 1) * piece)
        total = grad_resid[:, cols] + dot_nt(joined[...], wqkv[cols, :])
        for j in range(3):
            total = total + dot32(ranks[j], small[16 * j : 16 * j + 16, cols])
        grad_ref[:, cols] = total
        grad_out[:, cols] = total.astype(BF16)

        @pl.when(place.swaps)
        def _():
            home[part].start()

    sum_parts(att_scatter, att_mine, att_parts, att_total, place)
    att_cross.start()
    att_cross.wait_recv()
    for copy in att_gather:
        copy.start()

    @pl.when(place.swaps)
    def _():
        for part in range(4):
            home[part].wait_recv()
            cols = slice(part * piece, (part + 1) * piece)
            grad_ref[:, cols] = grad_in[:, cols].astype(F32)
        for part in range(4):
            home[part].wait_send()
        home_outcome.wait()
        swap_x.wait_send()
        swap_cotangent.wait_send()

    for copy in att_gather:
        copy.wait_recv()
    spread(
        att_total,
        tuple(
            (functools.partial(lambda part, half: up_out.at[half, part], part), part * width, (part + 1) * width)
            for part in range(3)
        )
        + tuple(
            (functools.partial(lambda part, half: down_out.at[half, part], part), (3 + part) * width, (4 + part) * width)
            for part in range(3)
        ),
    )
    for step in range(1, peers):
        grad_copy(step).wait_send()
        dq_copy(step).wait_send()
        dkv_copy(step).wait_send()
    for copy in mlp_scatter + mlp_gather + att_scatter + att_gather + [mlp_cross, att_cross]:
        copy.wait_send()
    for copy in (give_wqkv, give_wout, give_wfc2, give_wfc1, give_wqkv_again):
        copy.wait_send()
    give_index.wait()


def run_layer(index, tokens, cotangent, weights, tables, biases, value_bias, hidden_bias, gains):
    rows, width = tokens.shape
    peers = H
    length = peers * rows
    hidden = hidden_bias.shape[1]
    block_q, block_k = 1024, 512
    vmem = pl.BlockSpec(memory_space=pltpu.VMEM)
    hbm = pl.BlockSpec(memory_space=pl.ANY)
    mlp_part = (2 * hidden + 4 * width) // peers
    att_part = 6 * width // peers

    def out(shape, dtype=BF16):
        return jax.ShapeDtypeStruct(shape, dtype)

    def total(part):
        return pltpu.VMEM((peers // 2, 2, 2, 16, part), BF16)

    def heads(*shape):
        return pltpu.VMEM((peers,) + shape, BF16)

    def sems(*shape):
        return pltpu.SemaphoreType.DMA(shape)

    return pl.pallas_call(
        functools.partial(layer_kernel, block_q, block_k),
        out_shape=[
            out((rows, width)),
            out((rows, width), F32),
            out((2, 8, 128), F32),
            out((2, 16, hidden)),
            out((2, 16, hidden)),
            out((2, 4, 16, width)),
            out((2, 5, 16, width)),
            out((2, 16, width)),
            out(weights[0].shape),
            out(weights[2].shape),
        ],
        in_specs=[pl.BlockSpec(memory_space=pltpu.SMEM)] + [hbm] * 11 + [vmem] * 4,
        out_specs=[vmem] * 8 + [hbm] * 2,
        scratch_shapes=[
            pltpu.VMEM((width, hidden), BF16),
            pltpu.VMEM((hidden, width), BF16),
            pltpu.VMEM((width, width), BF16),
            pltpu.VMEM((max(4 * rows, 2 * block_k), 1024), F32),
            pltpu.VMEM((rows, hidden), BF16),
            pltpu.VMEM((160, width), BF16),
            pltpu.VMEM((32, hidden), BF16),
            pltpu.VMEM((rows, width), BF16),
            pltpu.VMEM((rows, width), BF16),
            pltpu.VMEM((rows, 48), BF16),
            heads(192, rows),
            heads(192, rows),
            heads(64, rows),
            heads(64, rows),
            heads(64, rows),
            pltpu.VMEM((64, length), F32),
            pltpu.VMEM((144, length), BF16),
            pltpu.VMEM((128, length), BF16),
            pltpu.VMEM((length, 144), BF16),
            pltpu.VMEM((length, 128), BF16),
            pltpu.VMEM((64, length), BF16),
            pltpu.VMEM((length, 128), BF16),
            pltpu.VMEM((64, length), F32),
            heads(64, rows),
            heads(rows, 128),
            heads(rows, 128),
            pltpu.VMEM((rows, width), BF16),
            pltpu.VMEM((rows, width), BF16),
            heads(16, mlp_part),
            heads(16, mlp_part),
            total(mlp_part),
            heads(16, att_part),
            heads(16, att_part),
            total(att_part),
            sems(14),
            sems(2, 11),
            sems(2, 7),
            sems(2, peers),
            sems(2, peers),
            sems(2, peers),
            sems(2, peers),
            sems(2, peers),
            sems(2, peers),
            sems(4, peers),
            sems(4, peers),
        ],
        compiler_params=pltpu.CompilerParams(
            collective_id=0, has_side_effects=True, vmem_limit_bytes=VMEM_LIMIT
        ),
        name="run_layer",
    )(index, tokens, cotangent, *weights, *tables, biases, value_bias, hidden_bias, gains)


def heads_body(
    tokens,
    cotangent,
    sequence_adapter_index,
    query_key_value_weight,
    output_weight,
    first_feed_weight,
    second_feed_weight,
    biases,
    value_bias_vector,
    first_feed_bias,
    norm_gain_pair,
    adapter_down_factors,
    output_down_factor,
    adapter_up_factors,
    hidden_up_factor,
    hidden_down_factor,
):
    width = tokens.shape[2]
    hidden = first_feed_bias.shape[0]
    adapter_number = adapter_down_factors.shape[0]
    outcome, grad_tokens, index_all, term_hd, term_uh, term_down, term_up, term_do, *_ = run_layer(
        sequence_adapter_index,
        tokens[0],
        cotangent[0],
        (query_key_value_weight, output_weight, first_feed_weight, second_feed_weight),
        (
            adapter_down_factors.reshape(-1, width),
            adapter_up_factors.reshape(-1, width),
            output_down_factor.reshape(-1, width),
            hidden_up_factor.reshape(-1, hidden),
            hidden_down_factor.reshape(-1, hidden),
        ),
        biases,
        value_bias_vector[None],
        first_feed_bias[None],
        norm_gain_pair,
    )
    picker = index_all[:, 0, :1] == jnp.arange(adapter_number, dtype=F32)[None, :]
    tables = []
    for every in (term_down, term_do, term_up, term_uh, term_hd):
        table = 0.0
        for seq in range(2):
            mask = picker[seq].reshape((adapter_number,) + (1,) * (every.ndim - 1))
            table = table + jnp.where(mask, every[seq][None].astype(F32), 0.0)
        tables.append(table)
    return (outcome[None], grad_tokens[None], *tables)


def solution(mesh):
    one_head_each = mesh.shape["ctx"] == H and mesh.shape["fsdp"] == 2
    return jax.shard_map(
        heads_body if one_head_each else gather_body,
        mesh=mesh,
        in_specs=(
            P("fsdp", "ctx", None),
            P("fsdp", "ctx", None),
            P("fsdp"),
            P("fsdp", None),
            P("fsdp", None),
            P("fsdp", None),
            P("fsdp", None),
            P(),
            P(),
            P(),
            P(),
            P(),
            P(),
            P(),
            P(),
            P(),
        ),
        out_specs=(P("fsdp", "ctx", None), P("fsdp", "ctx", None), P(), P(), P(), P(), P()),
        check_vma=False,
    )
```

```python
import functools

import jax
import jax.numpy as jnp
from jax import lax
from jax.experimental import pallas as pl
from jax.experimental.pallas import tpu as pltpu
from jax.sharding import PartitionSpec as P

H = 16


EPSILON = 1e-05
HIGHEST = lax.Precision.HIGHEST


def exact_sum(form, left, right):
    return jnp.einsum(form, left, right, precision=HIGHEST, preferred_element_type=jnp.float32)


def plain_sum(form, left, right):
    return jnp.einsum(form, left, right, preferred_element_type=jnp.float32)


def layer_norm(value, gain, shift):
    center = value - jnp.mean(value, -1, keepdims=True)
    spread = jnp.mean(center * center, -1, keepdims=True)
    return center * lax.rsqrt(spread + EPSILON) * gain + shift


def attn_weights(query_key_value_weight, output_weight):
    return (
        lax.all_gather(query_key_value_weight, "fsdp", axis=0, tiled=True),
        lax.all_gather(output_weight, "fsdp", axis=0, tiled=True),
    )


def mlp_weights(first_feed_weight, second_feed_weight):
    return (
        lax.all_gather(first_feed_weight, "fsdp", axis=0, tiled=True),
        lax.all_gather(second_feed_weight, "fsdp", axis=0, tiled=True),
    )


def to_heads(input_array):
    return input_array.reshape(
        input_array.shape[0], input_array.shape[1], H, input_array.shape[2] // H
    )


def row_block(input_array, block_index, block_rows):
    return lax.dynamic_slice_in_dim(input_array, block_index * block_rows, block_rows, 1)


def block_grads(queries, grad_out, log_total, row_delta, keys_blk, values_blk):
    scores = plain_sum("sqhd,skhd->shqk", queries, keys_blk)
    probs = jnp.exp(scores - log_total[..., None])
    prob_low = probs.astype(jnp.bfloat16)
    grad_probs = plain_sum("sqhd,skhd->shqk", grad_out, values_blk)
    grad_scores = (probs * (grad_probs - row_delta[..., None])).astype(jnp.bfloat16)
    return (prob_low, grad_scores)


def attention_forward(queries_heads, keys_heads, values_heads):
    seq_count, row_count, head_count, head_size = queries_heads.shape
    length = keys_heads.shape[1]
    block_rows = min(512, length)
    block_count = length // block_rows

    def max_step(running, block_index):
        running_max, running_total = running
        scores = plain_sum(
            "sqhd,skhd->shqk", queries_heads, row_block(keys_heads, block_index, block_rows)
        )
        new_max = jnp.maximum(running_max, jnp.max(scores, -1))
        running_total = running_total * jnp.exp(running_max - new_max) + jnp.sum(
            jnp.exp(scores - new_max[..., None]), -1
        )
        return ((new_max, running_total), None)

    start_max = jnp.full((seq_count, head_count, row_count), -1e30, jnp.float32)
    start_total = jnp.zeros((seq_count, head_count, row_count), jnp.float32)
    (final_max, final_total), unused = lax.scan(
        max_step, (start_max, start_total), jnp.arange(block_count)
    )
    log_total = final_max + jnp.log(final_total)

    def value_step(running, block_index):
        scores = plain_sum(
            "sqhd,skhd->shqk", queries_heads, row_block(keys_heads, block_index, block_rows)
        )
        prob_low = jnp.exp(scores - log_total[..., None]).astype(jnp.bfloat16)
        return (
            running
            + plain_sum(
                "shqk,skhd->sqhd", prob_low, row_block(values_heads, block_index, block_rows)
            ),
            None,
        )

    context, unused = lax.scan(
        value_step, jnp.zeros(queries_heads.shape, jnp.float32), jnp.arange(block_count)
    )
    return (context, log_total)


def gather_body(
    tokens,
    cotangent,
    sequence_adapter_index,
    query_key_value_weight,
    output_weight,
    first_feed_weight,
    second_feed_weight,
    biases,
    value_bias_vector,
    first_feed_bias,
    norm_gain_pair,
    adapter_down_factors,
    output_down_factor,
    adapter_up_factors,
    hidden_up_factor,
    hidden_down_factor,
):
    seq_count, row_count, model_width = tokens.shape
    adapter_number = adapter_down_factors.shape[0]
    picker = (
        sequence_adapter_index[:, None] == jnp.arange(adapter_number, dtype=jnp.int32)[None, :]
    ).astype(jnp.float32)

    def select_adapter(table):
        return jnp.einsum("sa,a...->s...", picker, table.astype(jnp.float32), precision=HIGHEST)

    def to_adapters(per_seq):
        return jnp.einsum("sa,s...->a...", picker, per_seq, precision=HIGHEST)

    selected_down = select_adapter(adapter_down_factors)
    selected_output = select_adapter(output_down_factor)
    selected_up = select_adapter(adapter_up_factors)
    hup_sel = select_adapter(hidden_up_factor)
    hdown_sel = select_adapter(hidden_down_factor)
    down_low = selected_down.astype(jnp.bfloat16)
    out_low = selected_output.astype(jnp.bfloat16)
    hdown_low = hdown_sel.astype(jnp.bfloat16)
    wqkv_full, wout_full = attn_weights(query_key_value_weight, output_weight)
    projected = plain_sum("std,de->ste", tokens, wqkv_full)
    down_att = plain_sum("std,sjrd->sjtr", tokens, down_low[:, :3])
    lifted = exact_sum("sjtr,sjrd->sjtd", down_att, selected_up[:, :3])
    queries = ((projected[..., :model_width] + biases[0] + lifted[:, 0]) * 0.125).astype(
        jnp.bfloat16
    )
    keys_own = (projected[..., model_width : 2 * model_width] + lifted[:, 1]).astype(jnp.bfloat16)
    values_own = (projected[..., 2 * model_width :] + value_bias_vector + lifted[:, 2]).astype(
        jnp.bfloat16
    )
    keys_all, values_all = (
        lax.all_gather(keys_own, "ctx", axis=1, tiled=True),
        lax.all_gather(values_own, "ctx", axis=1, tiled=True),
    )
    queries_heads = to_heads(queries)
    keys_heads = to_heads(keys_all)
    values_heads = to_heads(values_all)
    context, log_total = attention_forward(queries_heads, keys_heads, values_heads)
    context = context.reshape(seq_count, row_count, model_width)
    context_low = context.astype(jnp.bfloat16)
    down_out = plain_sum("std,srd->str", context_low, out_low)
    branch = (
        plain_sum("std,de->ste", context_low, wout_full)
        + biases[1]
        + exact_sum("str,srd->std", down_out, selected_up[:, 3])
    )

    def first_norm(value):
        return layer_norm(value, norm_gain_pair[0], biases[3])

    def second_norm(value):
        return layer_norm(value, norm_gain_pair[1], biases[4])

    def gelu_exact(value):
        return jax.nn.gelu(value, approximate=False)

    normed, norm_back = jax.vjp(first_norm, tokens.astype(jnp.float32) + branch)
    normed_low = normed.astype(jnp.bfloat16)
    wfc1_full, wfc2_full = mlp_weights(first_feed_weight, second_feed_weight)
    down_fc1 = plain_sum("std,srd->str", normed_low, down_low[:, 3])
    hidden_pre = (
        plain_sum("std,df->stf", normed_low, wfc1_full)
        + first_feed_bias
        + exact_sum("str,srf->stf", down_fc1, hup_sel)
    )
    activated, gelu_back = jax.vjp(gelu_exact, hidden_pre)
    act_low = activated.astype(jnp.bfloat16)
    down_fc2 = plain_sum("stf,srf->str", act_low, hdown_low)
    mixed_out = (
        plain_sum("stf,fd->std", act_low, wfc2_full)
        + biases[2]
        + exact_sum("str,srd->std", down_fc2, selected_up[:, 4])
    )
    outcome, out_back = jax.vjp(second_norm, normed + mixed_out)
    (grad_sum2,) = out_back(cotangent.astype(jnp.float32))
    grad_mixed = grad_sum2.astype(jnp.bfloat16)
    grad_up_fc2 = exact_sum("str,std->srd", down_fc2, grad_mixed)
    grad_rank_fc2 = exact_sum("std,srd->str", grad_mixed, selected_up[:, 4]).astype(jnp.bfloat16)
    grad_hdown = plain_sum("str,stf->srf", grad_rank_fc2, act_low)
    wfc1_full, wfc2_full = mlp_weights(first_feed_weight, second_feed_weight)
    grad_act = (
        plain_sum("std,fd->stf", grad_mixed, wfc2_full)
        + plain_sum("str,srf->stf", grad_rank_fc2, hdown_low)
    ).astype(jnp.bfloat16)
    (grad_hidden,) = gelu_back(grad_act.astype(jnp.float32))
    grad_hidden = grad_hidden.astype(jnp.bfloat16)
    grad_hup = exact_sum("str,stf->srf", down_fc1, grad_hidden)
    grad_rank_fc1 = exact_sum("stf,srf->str", grad_hidden, hup_sel).astype(jnp.bfloat16)
    grad_down_fc1 = plain_sum("str,std->srd", grad_rank_fc1, normed_low)
    grad_normed_low = (
        plain_sum("stf,df->std", grad_hidden, wfc1_full)
        + plain_sum("str,srd->std", grad_rank_fc1, down_low[:, 3])
    ).astype(jnp.bfloat16)
    (grad_resid,) = norm_back(grad_sum2 + grad_normed_low.astype(jnp.float32))
    mlp_hup = to_adapters(grad_hup)
    mlp_hdown = to_adapters(grad_hdown)
    mlp_fc1 = to_adapters(grad_down_fc1)
    mlp_fc2 = to_adapters(grad_up_fc2)
    mlp_hup, mlp_hdown, mlp_fc1, mlp_fc2 = lax.psum(
        (mlp_hup, mlp_hdown, mlp_fc1, mlp_fc2), ("ctx", "fsdp")
    )
    grad_branch = grad_resid.astype(jnp.bfloat16)
    grad_up_out = exact_sum("str,std->srd", down_out, grad_branch)
    grad_rank_out = exact_sum("std,srd->str", grad_branch, selected_up[:, 3]).astype(jnp.bfloat16)
    grad_out_down = plain_sum("str,std->srd", grad_rank_out, context_low)
    wqkv_full, wout_full = attn_weights(query_key_value_weight, output_weight)
    grad_context = (
        plain_sum("std,ed->ste", grad_branch, wout_full)
        + plain_sum("str,srd->std", grad_rank_out, out_low)
    ).astype(jnp.bfloat16)
    row_delta = jnp.sum(to_heads(grad_context.astype(jnp.float32) * context), -1)
    delta_heads = jnp.swapaxes(row_delta, 1, 2)
    grad_heads = to_heads(grad_context)
    length = keys_all.shape[1]
    block_rows = min(512, length)
    block_count = length // block_rows

    def key_step(block_index, running):
        grad_query, grad_key, grad_value = running
        keys_blk = row_block(keys_heads, block_index, block_rows)
        values_blk = row_block(values_heads, block_index, block_rows)
        prob_low, grad_scores = block_grads(
            queries_heads, grad_heads, log_total, delta_heads, keys_blk, values_blk
        )
        grad_query = grad_query + plain_sum("shqk,skhd->sqhd", grad_scores, keys_blk)
        grad_key = lax.dynamic_update_slice_in_dim(
            grad_key,
            plain_sum("shqk,sqhd->skhd", grad_scores, queries_heads),
            block_index * block_rows,
            1,
        )
        grad_value = lax.dynamic_update_slice_in_dim(
            grad_value,
            plain_sum("shqk,sqhd->skhd", prob_low, grad_heads),
            block_index * block_rows,
            1,
        )
        return (grad_query, grad_key, grad_value)

    start_query = jnp.zeros(queries_heads.shape, jnp.float32)
    start_keys = jnp.zeros(keys_heads.shape, jnp.float32)
    grad_query, grad_key_all, grad_value_all = lax.fori_loop(
        0, block_count, key_step, (start_query, start_keys, start_keys)
    )
    grad_keys, grad_values = (
        lax.psum_scatter(
            grad_key_all.reshape(seq_count, length, model_width).astype(jnp.bfloat16),
            "ctx",
            scatter_dimension=1,
            tiled=True,
        ).astype(jnp.float32),
        lax.psum_scatter(
            grad_value_all.reshape(seq_count, length, model_width).astype(jnp.bfloat16),
            "ctx",
            scatter_dimension=1,
            tiled=True,
        ).astype(jnp.float32),
    )
    grad_qlin = grad_query.reshape(seq_count, row_count, model_width).astype(jnp.bfloat16) * 0.125
    grad_key_low = grad_keys.astype(jnp.bfloat16)
    grad_value_low = grad_values.astype(jnp.bfloat16)
    stacked = jnp.stack([grad_qlin, grad_key_low, grad_value_low], 1)
    grad_up_att = exact_sum("sjtr,sjtd->sjrd", down_att, stacked)
    grad_rank_att = exact_sum("sjtd,sjrd->sjtr", stacked, selected_up[:, :3]).astype(jnp.bfloat16)
    grad_down_att = plain_sum("sjtr,std->sjrd", grad_rank_att, tokens)
    joined = jnp.concatenate([grad_qlin, grad_key_low, grad_value_low], -1)
    grad_tokens = (
        grad_resid
        + plain_sum("ste,de->std", joined, wqkv_full)
        + plain_sum("sjtr,sjrd->std", grad_rank_att, down_low[:, :3])
    )
    attn_down = to_adapters(grad_down_att)
    attn_out = to_adapters(grad_out_down)
    attn_up = to_adapters(jnp.concatenate([grad_up_att, grad_up_out[:, None]], 1))
    attn_down, attn_out, attn_up = lax.psum((attn_down, attn_out, attn_up), ("ctx", "fsdp"))
    total_down = jnp.concatenate([attn_down, mlp_fc1[:, None]], 1)
    total_up = jnp.concatenate([attn_up, mlp_fc2[:, None]], 1)
    return (
        outcome.astype(jnp.bfloat16),
        grad_tokens,
        total_down,
        attn_out,
        total_up,
        mlp_hup,
        mlp_hdown,
    )


BF16 = jnp.bfloat16
F32 = jnp.float32
LOG2E = 1.4426950408889634
VMEM_LIMIT = 60 * 2**20
MESH = pl.DeviceIdType.MESH


def dot32(left, right):
    return jnp.dot(left, right, preferred_element_type=F32)


def dot_nt(left, right):
    return lax.dot_general(left, right, (((1,), (1,)), ((), ())), preferred_element_type=F32)


def dot_tn(left, right):
    return lax.dot_general(left, right, (((0,), (0,)), ((), ())), preferred_element_type=F32)


def split_three(value):
    high = value.astype(BF16)
    rest = value - high.astype(F32)
    middle = rest.astype(BF16)
    return high, middle, (rest - middle.astype(F32)).astype(BF16)


def flip(value):
    return value.astype(F32).T.astype(BF16)


def remote(src, dst, send_sem, recv_sem, device):
    return pltpu.make_async_remote_copy(
        src_ref=src,
        dst_ref=dst,
        send_sem=send_sem,
        recv_sem=recv_sem,
        device_id=device,
        device_id_type=MESH,
    )


class Place:
    def __init__(self):
        self.ctx = lax.axis_index("ctx")
        self.core = lax.axis_index("fsdp")
        self.half = self.ctx // (H // 2)
        self.low = self.ctx % (H // 2)
        self.me = self.low * 2 + self.core
        self.swaps = self.core != self.half
        self.pair = (self.core + self.half) % 2
        self.sibling = (self.ctx, 1 - self.core)
        self.partner = ((self.ctx + H // 2) % H, 1 - self.core)

    def peer(self, step):
        number = self.me ^ step
        return (self.half * (H // 2) + number // 2, number % 2)

    def order(self, turn):
        return 2 * (turn % (H // 2)) + (turn // (H // 2) + self.pair) % 2

    def greet(self):
        barrier = pltpu.get_barrier_semaphore()
        for step in range(1, H):
            pl.semaphore_signal(barrier, inc=1, device_id=self.peer(step), device_id_type=MESH)
        pl.semaphore_signal(barrier, inc=1, device_id=self.partner, device_id_type=MESH)
        pl.semaphore_wait(barrier, H)


def sum_copies(mine, parts, total, sems, place):
    own = total.at[place.pair, place.low, place.half]
    other = total.at[place.pair, place.low, 1 - place.half]
    column = total.at[place.pair]
    scatter = [
        remote(mine.at[place.me ^ step], parts.at[step], sems.at[0, step], sems.at[1, step], place.peer(step))
        for step in range(1, H)
    ]
    cross = remote(own, own, sems.at[0, 0], sems.at[1, 0], place.partner)
    first = [
        remote(own, own, sems.at[2, step], sems.at[3, step], place.peer(step))
        for step in range(2, H, 2)
    ]
    second = [
        remote(other, other, sems.at[2, step + 1], sems.at[3, step + 1], place.peer(step))
        for step in range(2, H, 2)
    ]
    last = remote(column, column, sems.at[2, 0], sems.at[3, 0], place.sibling)
    return scatter, cross, first, second, last


def sum_parts(scatter, mine, parts, total, place):
    value = mine[place.me].astype(F32)
    for step, copy in enumerate(scatter, 1):
        copy.wait_recv()
        value = value + parts[step].astype(F32)
    total[place.pair, place.low, place.half] = value.astype(BF16)


def put_term(mine, base, term):
    units = mine.shape[2] // 128
    for unit in range(term.shape[1] // 128):
        at = base // 128 + unit
        lanes = slice(at % units * 128, at % units * 128 + 128)
        mine[at // units, :, lanes] = term[:, unit * 128 : unit * 128 + 128].astype(BF16)


def layer_kernel(
    block_q,
    block_k,
    index_ref,
    tokens_ref,
    cotangent_ref,
    wqkv_ref,
    wout_ref,
    wfc1_ref,
    wfc2_ref,
    down_table,
    up_table,
    out_down_table,
    hidden_up_table,
    hidden_down_table,
    biases_ref,
    value_bias_ref,
    hidden_bias_ref,
    gains_ref,
    outcome_ref,
    grad_ref,
    index_out,
    hidden_down_out,
    hidden_up_out,
    down_out,
    up_out,
    out_down_out,
    wqkv_far,
    wfc1_far,
    wide,
    wfc2,
    wout,
    big,
    act,
    small,
    small_hidden,
    x,
    cotangent,
    rank_att,
    outgoing,
    qkv,
    leaving,
    arrived,
    incoming,
    context,
    state,
    qta,
    gta,
    kk,
    vv,
    kt,
    both,
    dkv_sum,
    dq_in,
    dkv_out,
    dkv_in,
    grad_out,
    grad_in,
    mlp_mine,
    mlp_parts,
    mlp_total,
    att_mine,
    att_parts,
    att_total,
    load_sem,
    core_sem,
    swap_sem,
    kv_sem,
    q_sem,
    back_sem,
    grad_sem,
    dq_sem,
    dkv_sem,
    mlp_sem,
    att_sem,
):
    peers, _, rows = qkv.shape
    length = peers * rows
    width = x.shape[1]
    hidden = hidden_bias_ref.shape[1]
    adapters = hidden_up_table.shape[0] // 16
    place = Place()
    me, core = place.me, place.core
    other = 1 - core
    wqkv = wide.at[:, 0 : 3 * width]
    up_at = down_table.shape[0]
    out_down_at = up_at + up_table.shape[0]

    def half_of(full, owner):
        count = full.shape[0] // 2
        return full.at[pl.ds(pl.multiple_of(owner * count, count), count), :]

    def load(source, target, number):
        return pltpu.make_async_copy(source, target, load_sem.at[number])

    def to_sibling(source, target, number):
        return remote(source, target, core_sem.at[0, number], core_sem.at[1, number], place.sibling)

    load_wqkv = load(wqkv_ref, half_of(wqkv, core), 0)
    load_wout = load(wout_ref, half_of(wout, core), 1)
    load_tables = [
        load(down_table, wfc2.at[0:up_at], 2),
        load(up_table, wfc2.at[up_at:out_down_at], 3),
        load(out_down_table, wfc2.at[out_down_at : out_down_at + out_down_table.shape[0]], 4),
        load(hidden_up_table, act.at[0 : 16 * adapters], 5),
        load(hidden_down_table, act.at[16 * adapters : 32 * adapters], 6),
    ]
    load_x = load(tokens_ref, x, 7)
    load_cotangent = load(cotangent_ref, cotangent, 8)
    load_wfc1 = load(wfc1_ref, half_of(wide, core), 9)
    load_wfc1_far = load(wfc1_far, half_of(wide, other), 10)
    load_wfc2 = load(wfc2_ref, half_of(wfc2, core), 11)
    again_wqkv = load(wqkv_ref, half_of(wqkv, core), 12)
    again_wqkv_far = load(wqkv_far, half_of(wqkv, other), 13)
    give_wqkv = to_sibling(wqkv_ref, half_of(wqkv, core), 0)
    give_wout = to_sibling(wout_ref, half_of(wout, core), 1)
    give_index = to_sibling(index_out.at[core], index_out.at[core], 2)
    count = small.shape[0]
    give_small = [to_sibling(small, wide.at[0:count, 3 * width : 4 * width], 3)] + [
        to_sibling(
            small_hidden.at[:, part * width : (part + 1) * width],
            wide.at[count + 32 * part : count + 32 * part + 32, 3 * width : 4 * width],
            4 + part,
        )
        for part in range(hidden // width)
    ]
    give_wfc2 = to_sibling(wfc2_ref, half_of(wfc2, core), 8)
    give_wfc1 = to_sibling(wfc1_ref, wfc1_far, 9)
    give_wqkv_again = to_sibling(wqkv_ref, wqkv_far, 10)
    half_rows = rows // 2
    swap_x = [
        remote(
            tokens_ref.at[part * half_rows : (part + 1) * half_rows],
            x.at[part * half_rows : (part + 1) * half_rows],
            swap_sem.at[0, 7 + part],
            swap_sem.at[1, 7 + part],
            place.partner,
        )
        for part in range(2)
    ]
    swap_cotangent = remote(cotangent_ref, cotangent, swap_sem.at[0, 1], swap_sem.at[1, 1], place.partner)

    load_wqkv.start()
    for copy in load_tables:
        copy.start()
    load_wout.start()

    @pl.when(jnp.logical_not(place.swaps))
    def _():
        load_x.start()
        load_cotangent.start()

    adapter = index_ref[0]
    index_out[core] = jnp.full(index_out.shape[1:], adapter, jnp.int32).astype(F32)
    place.greet()

    @pl.when(place.swaps)
    def _():
        for copy in swap_x:
            copy.start()

    give_wqkv.start()
    give_index.start()

    for copy in load_tables:
        copy.wait()

    def select(table, base, group, groups, target, at):
        chosen = jnp.full((16, table.shape[1]), adapter, jnp.int32)
        value = jnp.zeros((16, table.shape[1]), F32)
        for number in range(adapters):
            start = pl.multiple_of(base + 16 * (number * groups + group), 16)
            value = jnp.where(chosen == number, table[pl.ds(start, 16), :].astype(F32), value)
        target[pl.ds(pl.multiple_of(at + 16 * group, 16), 16), :] = value.astype(BF16)

    def select_down(group, _):
        select(wfc2, 0, group, 4, small, 0)
        return 0

    def select_up(group, _):
        select(wfc2, up_at, group, 5, small, 64)
        return 0

    lax.fori_loop(0, 4, select_down, 0)
    lax.fori_loop(0, 5, select_up, 0)
    select(wfc2, out_down_at, 0, 1, small, 144)
    for part in range(2):
        select(act, 16 * adapters * part, 0, 1, small_hidden, 16 * part)
    for copy in give_small:
        copy.start()
    give_wout.start()
    for copy in give_small:
        copy.wait()

    @pl.when(place.swaps)
    def _():
        small[...] = wide[0:count, 3 * width : 4 * width]
        for part in range(hidden // width):
            small_hidden[:, part * width : (part + 1) * width] = wide[
                count + 32 * part : count + 32 * part + 32, 3 * width : 4 * width
            ]

    hidden_up_ref = small_hidden.at[0:16]
    hidden_down_ref = small_hidden.at[16:32]
    out_down_ref = small.at[144:160]

    def down(j):
        return small[16 * j : 16 * j + 16]

    def up(j):
        return small[64 + 16 * j : 80 + 16 * j]

    load_wfc2.start()
    give_wfc2.start()

    load_wqkv.wait()
    give_wqkv.wait_recv()

    def project(half, part):
        here = slice(half * half_rows, (half + 1) * half_rows)
        cols = slice(part * width, (part + 1) * width)
        value = dot32(x[here, :], wqkv[:, cols]) + dot32(rank_att[here, part * 16 : part * 16 + 16], up(part))
        if part == 0:
            value = (value + biases_ref[0:1, :]) * 0.125
        if part == 2:
            value = value + value_bias_ref[...]
        for two in range(peers // 2):
            turned = value[:, two * 128 : two * 128 + 128].T.astype(BF16)
            outgoing[2 * two, part * 64 : part * 64 + 64, here] = turned[0:64]
            outgoing[2 * two + 1, part * 64 : part * 64 + 64, here] = turned[64:128]

    def kv_copy(step, half):
        here = slice(half * half_rows, (half + 1) * half_rows)
        return remote(
            outgoing.at[me ^ step, 64:192, here],
            qkv.at[step, 64:192, here],
            kv_sem.at[0, half, step],
            kv_sem.at[1, half, step],
            place.peer(step),
        )

    def q_copy(step):
        return remote(
            outgoing.at[me ^ step, 0:64], qkv.at[step, 0:64], q_sem.at[0, step], q_sem.at[1, step], place.peer(step)
        )

    def back_copy(step):
        return remote(leaving.at[step], arrived.at[me], back_sem.at[0, step], back_sem.at[1, step], place.peer(step))

    steps = length // block_k
    group = block_q // rows
    key_group = block_k // rows
    for half in range(2):
        here = slice(half * half_rows, (half + 1) * half_rows)

        @pl.when(place.swaps)
        def _():
            swap_x[half].wait_recv()

        if half == 0:

            @pl.when(jnp.logical_not(place.swaps))
            def _():
                load_x.wait()

        rank_att[here, :] = dot_nt(x[here, :], small[0:48]).astype(BF16)
        project(half, 1)
        project(half, 2)
        for step in range(1, peers):
            kv_copy(step, half).start()
        project(half, 0)
    for step in range(1, peers):
        q_copy(step).start()
    give_wfc1.start()
    give_wqkv_again.start()
    load_wfc1.start()
    qkv[0] = outgoing[me]

    row_at = lax.broadcasted_iota(jnp.int32, (16, rows), 0)
    ones = (row_at == 0).astype(F32).astype(BF16)
    minus = jnp.where(lax.broadcasted_iota(jnp.int32, (rows, 16), 1) < 3, -1.0, 0.0).astype(BF16)
    minus_rows = jnp.where(lax.broadcasted_iota(jnp.int32, (64, rows), 0) < 3, -1.0, 0.0).astype(BF16)

    def tail(value):
        at = lax.broadcasted_iota(jnp.int32, (16, value.shape[1]), 0)
        high, middle, low = (part.astype(F32) for part in split_three(value))
        return jnp.where(at == 0, high, jnp.where(at == 1, middle, jnp.where(at == 2, low, 0.0))).astype(BF16)

    def take_key(turn):
        cols = pl.ds(pl.multiple_of(turn * rows, rows), rows)
        step = place.order(turn)

        @pl.when(step > 0)
        def _():
            kv_copy(step, 0).wait_recv()
            kv_copy(step, 1).wait_recv()

        key = qkv[step, 64:128, :]
        value = qkv[step, 128:192, :]
        kt[:, cols] = key
        kk[cols, 0:128] = flip(jnp.concatenate([key, key], 0))
        kk[cols, 128:144] = minus
        vv[cols, :] = flip(jnp.concatenate([value, minus_rows], 0))
        gta[0:64, cols] = value
        gta[64:80, cols] = ones
        gta[80:128, cols] = jnp.zeros((48, rows), BF16)

    def take_keys(i):
        def one(part, _):
            take_key(i * key_group + part)
            return 0

        lax.fori_loop(0, key_group, one, 0)

    def forward_part(i, low, high, arriving):
        def take_query(part, _):
            turn = i * group + part
            step = place.order(turn)
            here = pl.ds(pl.multiple_of(turn * rows, rows), rows)

            @pl.when(step > 0)
            def _():
                q_copy(step).wait_recv()

            query = qkv[step, 0:64, :].astype(F32) * LOG2E
            high = query.astype(BF16)
            qta[0:64, here] = high
            qta[64:128, here] = (query - high.astype(F32)).astype(BF16)
            return 0

        if low == 0:
            lax.fori_loop(0, group, take_query, 0)
        cols = pl.ds(pl.multiple_of(i * block_q, block_q), block_q)
        query = qta.at[0:128, cols]
        if arriving:
            take_keys(low)
        block = dot32(kk[low * block_k : (low + 1) * block_k, 0:128], query[...])
        big[0:block_k] = block

        def half(j, now, carry):
            peak, running, total = carry
            later = jnp.minimum(j + 1, high - 1)
            here = pl.ds(pl.multiple_of(j * block_k, block_k), block_k)
            there = pl.ds(pl.multiple_of(later * block_k, block_k), block_k)
            if arriving:

                @pl.when(j + 1 < high)
                def _():
                    take_keys(later)

            ahead = dot32(kk[there, 0:128], query[...])
            big[(1 - now) * block_k : (2 - now) * block_k] = ahead
            new = jnp.maximum(running, peak)
            weights = jnp.exp2(big[now * block_k : (now + 1) * block_k] - new).astype(BF16)
            total = total * jnp.exp2(running - new) + dot32(gta[0:80, here], weights)
            return jnp.max(ahead, 0, keepdims=True), new, total

        def pair(j, carry):
            return half(low + 2 * j + 1, 1, half(low + 2 * j, 0, carry))

        if low == 0:
            running, total = jnp.full((1, block_q), -jnp.inf, F32), jnp.zeros((80, block_q), F32)
        else:
            running = state[1:2, cols]
            total = jnp.concatenate([context[:, cols], state[0:1, cols], jnp.zeros((15, block_q), F32)], 0)
        _, top, total = lax.fori_loop(
            0, (high - low) // 2, pair, (jnp.max(block, 0, keepdims=True), running, total)
        )
        weight_sum = total[64:65]
        if high < steps:
            context[:, cols] = total[0:64]
            state[0:1, cols] = weight_sum
            state[1:2, cols] = top
            return
        result = total[0:64] / weight_sum
        context[:, cols] = result
        qta[128:144, cols] = tail(top + jnp.log2(weight_sum))
        low_result = result.astype(BF16)
        for part in range(group):
            step = place.order(i * group + part)
            leaving[step] = low_result[:, part * rows : (part + 1) * rows]

            @pl.when(step > 0)
            def _():
                back_copy(step).start()

    query_steps = length // block_q
    for i in range(query_steps // 2):
        forward_part(i, 0, steps // 2, i == 0)
    give_wfc1.wait_recv()
    load_wfc1_far.start()
    for i in range(query_steps // 2):
        forward_part(i, steps // 2, steps, i == 0)

    @pl.when(place.swaps)
    def _():
        swap_cotangent.start()

    def forward_whole(i, _):
        forward_part(i, 0, steps, False)
        return 0

    lax.fori_loop(query_steps // 2, query_steps, forward_whole, 0)
    arrived[me] = leaving[0]

    def mean(value):
        return jnp.mean(value, -1, keepdims=True)

    def norm_backward(grad, hat, scale):
        return scale * (grad - mean(grad) - hat * mean(grad * hat))

    load_wout.wait()
    give_wout.wait_recv()
    for step in range(1, peers):
        back_copy(step).wait_recv()
    context_low = flip(arrived[...].reshape(width, rows))
    rank_out = dot_nt(context_low, out_down_ref[...]).astype(BF16)
    resid = x[...].astype(F32) + dot32(context_low, wout[...]) + biases_ref[1:2] + dot32(rank_out, up(3))
    center = resid - mean(resid)
    scale_one = lax.rsqrt(mean(center * center) + EPSILON)
    hat_one = center * scale_one
    normed = hat_one * gains_ref[0:1] + biases_ref[3:4]
    normed_low = normed.astype(BF16)
    rank_one = dot_nt(normed_low, down(3)).astype(BF16)
    load_wfc1.wait()
    load_wfc1_far.wait()
    load_wfc2.wait()
    give_wfc2.wait_recv()
    piece = 1024
    rank_two = jnp.zeros((rows, 16), F32)
    mixed = normed + biases_ref[2:3]
    for part in range(hidden // piece):
        cols = slice(part * piece, (part + 1) * piece)
        pre = (
            dot32(normed_low, wide[:, cols])
            + hidden_bias_ref[:, cols]
            + dot32(rank_one, hidden_up_ref[:, cols])
        )
        share = 0.5 + 0.5 * lax.erf(pre * 0.7071067811865476)
        big[part * rows : (part + 1) * rows] = share + pre * (0.3989422804014327 * jnp.exp(-0.5 * pre * pre))
        active = (pre * share).astype(BF16)
        act[:, cols] = active
        rank_two = rank_two + dot_nt(active, hidden_down_ref[:, cols])
        mixed = mixed + dot32(active, wfc2[cols, :])
    rank_two = rank_two.astype(BF16)
    mixed = mixed + dot32(rank_two, up(4))
    center = mixed - mean(mixed)
    scale_two = lax.rsqrt(mean(center * center) + EPSILON)
    hat_two = center * scale_two

    @pl.when(place.swaps)
    def _():
        swap_cotangent.wait_recv()

    @pl.when(jnp.logical_not(place.swaps))
    def _():
        load_cotangent.wait()

    grad_sum = norm_backward(cotangent[...].astype(F32) * gains_ref[1:2], hat_two, scale_two)
    outcome = cotangent
    outcome[...] = (hat_two * gains_ref[1:2] + biases_ref[4:5]).astype(BF16)
    home_outcome = remote(outcome, outcome_ref, swap_sem.at[0, 2], swap_sem.at[1, 2], place.partner)

    @pl.when(place.swaps)
    def _():
        home_outcome.start()

    @pl.when(jnp.logical_not(place.swaps))
    def _():
        outcome_ref[...] = outcome[...]

    grad_mixed = grad_sum.astype(BF16)
    put_term(mlp_mine, 2 * hidden, dot_tn(rank_two, grad_mixed))
    grad_rank = dot_nt(grad_mixed, up(4)).astype(BF16)
    put_term(mlp_mine, 0, dot_tn(grad_rank, act[...]))
    grad_one = jnp.zeros((rows, 16), F32)
    grad_normed = jnp.zeros((rows, width), F32)
    for part in range(hidden // piece):
        cols = slice(part * piece, (part + 1) * piece)
        grad_act = dot_nt(grad_mixed, wfc2[cols, :]) + dot32(grad_rank, hidden_down_ref[:, cols])
        grad_hidden = (grad_act.astype(BF16).astype(F32) * big[part * rows : (part + 1) * rows]).astype(BF16)
        put_term(mlp_mine, hidden + part * piece, dot_tn(rank_one, grad_hidden))
        grad_one = grad_one + dot_nt(grad_hidden, hidden_up_ref[:, cols])
        grad_normed = grad_normed + dot_nt(grad_hidden, wide[:, cols])
    grad_one = grad_one.astype(BF16)
    put_term(mlp_mine, 2 * hidden + width, dot_tn(grad_one, normed_low))
    grad_normed = (grad_normed + dot32(grad_one, down(3))).astype(BF16).astype(F32)
    resid_grad = norm_backward((grad_sum + grad_normed) * gains_ref[0:1], hat_one, scale_one)
    grad_resid = big.at[0:rows]
    grad_resid[...] = resid_grad
    grad_branch = resid_grad.astype(BF16)
    put_term(mlp_mine, 2 * hidden + 2 * width, dot_tn(rank_out, grad_branch))
    grad_rank = dot_nt(grad_branch, up(3)).astype(BF16)
    put_term(mlp_mine, 2 * hidden + 3 * width, dot_tn(grad_rank, context_low))
    turned = dot_nt(wout[...], grad_branch) + lax.dot_general(
        out_down_ref[...], grad_rank, (((0,), (1,)), ((), ())), preferred_element_type=F32
    )
    for step in range(1, peers):
        kv_copy(step, 0).wait_send()
        kv_copy(step, 1).wait_send()
        q_copy(step).wait_send()
        back_copy(step).wait_send()
    outgoing[:, 0:64] = turned.astype(BF16).reshape(peers, 64, rows)

    def grad_copy(step):
        return remote(
            outgoing.at[me ^ step, 0:64], incoming.at[step], grad_sem.at[0, step], grad_sem.at[1, step], place.peer(step)
        )

    for step in range(1, peers):
        grad_copy(step).start()
    mlp_scatter, mlp_cross, mlp_first, mlp_second, mlp_last = sum_copies(mlp_mine, mlp_parts, mlp_total, mlp_sem, place)
    for copy in mlp_scatter:
        copy.start()
    incoming[0] = outgoing[me, 0:64]
    give_wqkv_again.wait_recv()
    again_wqkv.start()
    again_wqkv_far.start()
    dkv_sum[...] = jnp.zeros_like(dkv_sum)
    first = lax.broadcasted_iota(jnp.int32, (block_k, 128), 1) < 64
    dq_out = leaving

    def dq_copy(step):
        return remote(dq_out.at[step], dq_in.at[me], dq_sem.at[0, step], dq_sem.at[1, step], place.peer(step))

    def dkv_copy(step):
        return remote(dkv_out.at[step], dkv_in.at[me], dkv_sem.at[0, step], dkv_sem.at[1, step], place.peer(step))

    def backward_step(turn, last):
        j = (turn + query_steps // 2) % query_steps

        def take_grad(part, _):
            step = place.order(j * group + part)
            cols = pl.ds(pl.multiple_of((j * group + part) * rows, rows), rows)

            @pl.when(step > 0)
            def _():
                grad_copy(step).wait_recv()

            grad = incoming[step]
            gta[0:64, cols] = grad
            gta[64:80, cols] = tail(jnp.sum(grad.astype(F32) * context[:, cols], 0, keepdims=True))
            both[cols, :] = flip(jnp.concatenate([qkv[step, 0:64, :], grad], 0))
            return 0

        lax.fori_loop(0, group, take_grad, 0)
        cols = pl.ds(pl.multiple_of(j * block_q, block_q), block_q)

        def key_step(key_turn, dq):
            i = (key_turn + steps // 2) % steps
            here = pl.ds(pl.multiple_of(i * block_k, block_k), block_k)
            probs = jnp.exp2(dot32(kk[here, :], qta[:, cols]))
            change = dot32(vv[here, :], gta[:, cols])
            low = (probs * change).astype(BF16)
            dv = dot32(probs.astype(BF16), both[cols, :])
            dk = dot32(low, both[cols, :])
            dkv = dkv_sum[here, :] + jnp.where(first, dk, dv)
            if not last:
                dkv_sum[here, :] = dkv
            else:
                done = dkv.astype(BF16)
                for part in range(key_group):
                    step = place.order(i * key_group + part)
                    dkv_out[step] = done[part * rows : (part + 1) * rows]

                    @pl.when(step > 0)
                    def _():
                        dkv_copy(step).start()

            return dq + dot32(kt[:, here], low)

        dq = lax.fori_loop(0, steps, key_step, jnp.zeros((64, block_q), F32)).astype(BF16)
        for part in range(group):
            step = place.order(j * group + part)
            dq_out[step] = dq[:, part * rows : (part + 1) * rows]

            @pl.when(step > 0)
            def _():
                dq_copy(step).start()

    def backward_steps(low, high):
        def one(j, _):
            backward_step(j, False)
            return 0

        lax.fori_loop(low, high, one, 0)

    backward_steps(0, query_steps // 4)
    sum_parts(mlp_scatter, mlp_mine, mlp_parts, mlp_total, place)
    mlp_cross.start()
    for copy in mlp_first:
        copy.start()
    backward_steps(query_steps // 4, query_steps // 2)
    mlp_cross.wait_recv()
    for copy in mlp_second:
        copy.start()
    backward_steps(query_steps // 2, query_steps - 1)
    for copy in mlp_first + mlp_second:
        copy.wait_recv()
    mlp_last.start()
    backward_step(query_steps - 1, True)

    mlp_last.wait_recv()

    def spread(total, parts):
        units = total.shape[4] // 128
        for half in range(2):
            for unit in range(peers * units):
                peer = unit // units
                lanes = slice(unit % units * 128, unit % units * 128 + 128)
                for target, low, high in parts:
                    if low <= unit * 128 < high:
                        at = unit * 128 - low
                        target(half)[:, at : at + 128] = total[(peer % 2 + half) % 2, peer // 2, half, :, lanes]

    spread(
        mlp_total,
        (
            (lambda half: hidden_down_out.at[half], 0, hidden),
            (lambda half: hidden_up_out.at[half], hidden, 2 * hidden),
            (lambda half: up_out.at[half, 4], 2 * hidden, 2 * hidden + width),
            (lambda half: down_out.at[half, 3], 2 * hidden + width, 2 * hidden + 2 * width),
            (lambda half: up_out.at[half, 3], 2 * hidden + 2 * width, 2 * hidden + 3 * width),
            (lambda half: out_down_out.at[half], 2 * hidden + 3 * width, 2 * hidden + 4 * width),
        ),
    )

    joined = act.at[:, 0 : 3 * width]
    dq_in[me] = dq_out[0]
    dkv_in[me] = dkv_out[0]
    for step in range(1, peers):
        dkv_copy(step).wait_recv()
    left = lax.broadcasted_iota(jnp.int32, (rows, 128), 1) < 64
    for two in range(peers // 2):
        even = dkv_in[2 * two].astype(F32)
        odd = dkv_in[2 * two + 1].astype(F32)
        cols = slice(width + two * 128, width + two * 128 + 128)
        joined[:, cols] = jnp.where(left, even, pltpu.roll(odd, 64, 1)).astype(BF16)
        cols = slice(2 * width + two * 128, 2 * width + two * 128 + 128)
        joined[:, cols] = jnp.where(left, pltpu.roll(even, 64, 1), odd).astype(BF16)
    def ranks_of(part):
        grad = joined[:, part * width : (part + 1) * width]
        rank = dot_nt(grad, up(part)).astype(BF16)
        ranks[part] = rank
        return rank

    def terms_of(part):
        grad = joined[:, part * width : (part + 1) * width]
        put_term(att_mine, part * width, dot_tn(rank_att[:, part * 16 : part * 16 + 16], grad))
        put_term(att_mine, (3 + part) * width, dot_tn(ranks[part], x[...]))

    ranks = {}
    att_scatter, att_cross, att_first, att_second, att_last = sum_copies(att_mine, att_parts, att_total, att_sem, place)
    again_wqkv.wait()
    again_wqkv_far.wait()
    total = dot_nt(joined[:, width:], wqkv[:, width:])
    for part in (1, 2):
        total = total + dot32(ranks_of(part), down(part))
        terms_of(part)
    grad_resid[...] += total
    for step in range(1, peers):
        dq_copy(step).wait_recv()
    joined[:, 0:width] = (dq_in[...].reshape(width, rows).astype(F32).T * 0.125).astype(BF16)
    rank = ranks_of(0)
    piece = width // 4
    home = [
        remote(
            grad_out.at[:, part * piece : (part + 1) * piece],
            grad_in.at[:, part * piece : (part + 1) * piece],
            swap_sem.at[0, 3 + part],
            swap_sem.at[1, 3 + part],
            place.partner,
        )
        for part in range(4)
    ]
    for part in range(4):
        cols = slice(part * piece, (part + 1) * piece)
        total = grad_resid[:, cols] + dot_nt(joined[:, 0:width], wqkv[cols, 0:width]) + dot32(rank, small[0:16, cols])
        grad_ref[:, cols] = total
        grad_out[:, cols] = total.astype(BF16)

        @pl.when(place.swaps)
        def _():
            home[part].start()

        if part == 0:
            terms_of(0)
            for copy in att_scatter:
                copy.start()

    sum_parts(att_scatter, att_mine, att_parts, att_total, place)
    att_cross.start()
    for copy in att_first:
        copy.start()
    att_cross.wait_recv()
    for copy in att_second:
        copy.start()
    for copy in att_first + att_second:
        copy.wait_recv()
    att_last.start()

    @pl.when(place.swaps)
    def _():
        for part in range(4):
            home[part].wait_recv()
            cols = slice(part * piece, (part + 1) * piece)
            grad_ref[:, cols] = grad_in[:, cols].astype(F32)
        for part in range(4):
            home[part].wait_send()
        home_outcome.wait()
        for copy in swap_x:
            copy.wait_send()
        swap_cotangent.wait_send()

    att_last.wait_recv()
    spread(
        att_total,
        tuple(
            (functools.partial(lambda part, half: up_out.at[half, part], part), part * width, (part + 1) * width)
            for part in range(3)
        )
        + tuple(
            (functools.partial(lambda part, half: down_out.at[half, part], part), (3 + part) * width, (4 + part) * width)
            for part in range(3)
        ),
    )
    for step in range(1, peers):
        grad_copy(step).wait_send()
        dq_copy(step).wait_send()
        dkv_copy(step).wait_send()
    for copies in ((mlp_scatter, mlp_first, mlp_second), (att_scatter, att_first, att_second)):
        for copy in copies[0] + copies[1] + copies[2]:
            copy.wait_send()
    for copy in (mlp_cross, mlp_last, att_cross, att_last):
        copy.wait_send()
    for copy in (give_wqkv, give_wout, give_wfc2, give_wfc1, give_wqkv_again):
        copy.wait_send()
    give_index.wait()


def run_layer(index, tokens, cotangent, weights, tables, biases, value_bias, hidden_bias, gains):
    rows, width = tokens.shape
    peers = H
    length = peers * rows
    hidden = hidden_bias.shape[1]
    block_q, block_k = 1024, 512
    vmem = pl.BlockSpec(memory_space=pltpu.VMEM)
    hbm = pl.BlockSpec(memory_space=pl.ANY)
    mlp_part = (2 * hidden + 4 * width) // peers
    att_part = 6 * width // peers

    def out(shape, dtype=BF16):
        return jax.ShapeDtypeStruct(shape, dtype)

    def total(part):
        return pltpu.VMEM((2, peers // 2, 2, 16, part), BF16)

    def heads(*shape):
        return pltpu.VMEM((peers,) + shape, BF16)

    def sems(*shape):
        return pltpu.SemaphoreType.DMA(shape)

    return pl.pallas_call(
        functools.partial(layer_kernel, block_q, block_k),
        out_shape=[
            out((rows, width)),
            out((rows, width), F32),
            out((2, 8, 128), F32),
            out((2, 16, hidden)),
            out((2, 16, hidden)),
            out((2, 4, 16, width)),
            out((2, 5, 16, width)),
            out((2, 16, width)),
            out(weights[0].shape),
            out(weights[2].shape),
        ],
        in_specs=[pl.BlockSpec(memory_space=pltpu.SMEM)] + [hbm] * 11 + [vmem] * 4,
        out_specs=[vmem] * 8 + [hbm] * 2,
        scratch_shapes=[
            pltpu.VMEM((width, hidden), BF16),
            pltpu.VMEM((hidden, width), BF16),
            pltpu.VMEM((width, width), BF16),
            pltpu.VMEM((max(4 * rows, 2 * block_k), 1024), F32),
            pltpu.VMEM((rows, hidden), BF16),
            pltpu.VMEM((160, width), BF16),
            pltpu.VMEM((32, hidden), BF16),
            pltpu.VMEM((rows, width), BF16),
            pltpu.VMEM((rows, width), BF16),
            pltpu.VMEM((rows, 48), BF16),
            heads(192, rows),
            heads(192, rows),
            heads(64, rows),
            heads(64, rows),
            heads(64, rows),
            pltpu.VMEM((64, length), F32),
            pltpu.VMEM((8, length), F32),
            pltpu.VMEM((144, length), BF16),
            pltpu.VMEM((128, length), BF16),
            pltpu.VMEM((length, 144), BF16),
            pltpu.VMEM((length, 128), BF16),
            pltpu.VMEM((64, length), BF16),
            pltpu.VMEM((length, 128), BF16),
            pltpu.VMEM((length, 128), F32),
            heads(64, rows),
            heads(rows, 128),
            heads(rows, 128),
            pltpu.VMEM((rows, width), BF16),
            pltpu.VMEM((rows, width), BF16),
            heads(16, mlp_part),
            heads(16, mlp_part),
            total(mlp_part),
            heads(16, att_part),
            heads(16, att_part),
            total(att_part),
            sems(14),
            sems(2, 11),
            sems(2, 9),
            sems(2, 2, peers),
            sems(2, peers),
            sems(2, peers),
            sems(2, peers),
            sems(2, peers),
            sems(2, peers),
            sems(4, peers),
            sems(4, peers),
        ],
        compiler_params=pltpu.CompilerParams(
            collective_id=0, has_side_effects=True, vmem_limit_bytes=VMEM_LIMIT
        ),
        name="run_layer",
    )(index, tokens, cotangent, *weights, *tables, biases, value_bias, hidden_bias, gains)


def assemble_kernel(
    index_ref, down_in, out_down_in, up_in, hidden_up_in, hidden_down_in, outcome_in, grad_in, outcome_out, grad_out, *tables
):
    number = pl.program_id(0).astype(F32)
    sources = (down_in, out_down_in, up_in, hidden_up_in, hidden_down_in)
    for source, table in zip(sources, tables):
        for i in range(source.shape[1]):
            value = jnp.zeros(source.shape[2:], F32)
            for seq in range(source.shape[0]):
                match = jnp.broadcast_to(index_ref[seq, 0:1, 0:1] == number, value.shape)
                value = value + jnp.where(match, source[seq, i].astype(F32), 0.0)
            table[0, i] = value
    outcome_out[...] = outcome_in[...]
    grad_out[...] = grad_in[...]


def assemble(index_all, terms, outcome, grad_tokens, adapter_number):
    rows, width = outcome.shape
    block = rows // adapter_number
    terms = [term.reshape((2, -1) + term.shape[-2:]) for term in terms]

    def whole(array):
        return pl.BlockSpec(array.shape, lambda i: (0,) * array.ndim)

    def part(shape):
        return pl.BlockSpec(shape, lambda i: (i,) + (0,) * (len(shape) - 1))

    rows_spec = part((block, width))
    tables = [(adapter_number,) + term.shape[1:] for term in terms]
    return pl.pallas_call(
        assemble_kernel,
        grid=(adapter_number,),
        out_shape=[
            jax.ShapeDtypeStruct(outcome.shape, BF16),
            jax.ShapeDtypeStruct(grad_tokens.shape, F32),
            *(jax.ShapeDtypeStruct(shape, F32) for shape in tables),
        ],
        in_specs=[whole(index_all), *(whole(term) for term in terms), rows_spec, rows_spec],
        out_specs=[rows_spec, rows_spec, *(part((1,) + shape[1:]) for shape in tables)],
        compiler_params=pltpu.CompilerParams(vmem_limit_bytes=VMEM_LIMIT),
        name="assemble",
    )(index_all, *terms, outcome, grad_tokens)


def heads_body(
    tokens,
    cotangent,
    sequence_adapter_index,
    query_key_value_weight,
    output_weight,
    first_feed_weight,
    second_feed_weight,
    biases,
    value_bias_vector,
    first_feed_bias,
    norm_gain_pair,
    adapter_down_factors,
    output_down_factor,
    adapter_up_factors,
    hidden_up_factor,
    hidden_down_factor,
):
    width = tokens.shape[2]
    hidden = first_feed_bias.shape[0]
    adapter_number = adapter_down_factors.shape[0]
    outcome, grad_tokens, index_all, term_hd, term_uh, term_down, term_up, term_do, *_ = run_layer(
        sequence_adapter_index,
        tokens[0],
        cotangent[0],
        (query_key_value_weight, output_weight, first_feed_weight, second_feed_weight),
        (
            adapter_down_factors.reshape(-1, width),
            adapter_up_factors.reshape(-1, width),
            output_down_factor.reshape(-1, width),
            hidden_up_factor.reshape(-1, hidden),
            hidden_down_factor.reshape(-1, hidden),
        ),
        biases,
        value_bias_vector[None],
        first_feed_bias[None],
        norm_gain_pair,
    )
    outcome, grad_tokens, total_down, total_out_down, total_up, total_hidden_up, total_hidden_down = assemble(
        index_all, (term_down, term_do, term_up, term_uh, term_hd), outcome, grad_tokens, adapter_number
    )
    return (
        outcome[None],
        grad_tokens[None],
        total_down,
        total_out_down.reshape(output_down_factor.shape),
        total_up,
        total_hidden_up.reshape(hidden_up_factor.shape),
        total_hidden_down.reshape(hidden_down_factor.shape),
    )


def solution(mesh):
    one_head_each = mesh.shape["ctx"] == H and mesh.shape["fsdp"] == 2
    return jax.shard_map(
        heads_body if one_head_each else gather_body,
        mesh=mesh,
        in_specs=(
            P("fsdp", "ctx", None),
            P("fsdp", "ctx", None),
            P("fsdp"),
            P("fsdp", None),
            P("fsdp", None),
            P("fsdp", None),
            P("fsdp", None),
            P(),
            P(),
            P(),
            P(),
            P(),
            P(),
            P(),
            P(),
            P(),
        ),
        out_specs=(P("fsdp", "ctx", None), P("fsdp", "ctx", None), P(), P(), P(), P(), P()),
        check_vma=False,
    )
```

```python
import functools

import jax
import jax.numpy as jnp
from jax import lax
from jax.experimental import pallas as pl
from jax.experimental.pallas import tpu as pltpu
from jax.sharding import PartitionSpec as P

H = 16


EPSILON = 1e-05
HIGHEST = lax.Precision.HIGHEST


def exact_sum(form, left, right):
    return jnp.einsum(form, left, right, precision=HIGHEST, preferred_element_type=jnp.float32)


def plain_sum(form, left, right):
    return jnp.einsum(form, left, right, preferred_element_type=jnp.float32)


def layer_norm(value, gain, shift):
    center = value - jnp.mean(value, -1, keepdims=True)
    spread = jnp.mean(center * center, -1, keepdims=True)
    return center * lax.rsqrt(spread + EPSILON) * gain + shift


def attn_weights(query_key_value_weight, output_weight):
    return (
        lax.all_gather(query_key_value_weight, "fsdp", axis=0, tiled=True),
        lax.all_gather(output_weight, "fsdp", axis=0, tiled=True),
    )


def mlp_weights(first_feed_weight, second_feed_weight):
    return (
        lax.all_gather(first_feed_weight, "fsdp", axis=0, tiled=True),
        lax.all_gather(second_feed_weight, "fsdp", axis=0, tiled=True),
    )


def to_heads(input_array):
    return input_array.reshape(
        input_array.shape[0], input_array.shape[1], H, input_array.shape[2] // H
    )


def row_block(input_array, block_index, block_rows):
    return lax.dynamic_slice_in_dim(input_array, block_index * block_rows, block_rows, 1)


def block_grads(queries, grad_out, log_total, row_delta, keys_blk, values_blk):
    scores = plain_sum("sqhd,skhd->shqk", queries, keys_blk)
    probs = jnp.exp(scores - log_total[..., None])
    prob_low = probs.astype(jnp.bfloat16)
    grad_probs = plain_sum("sqhd,skhd->shqk", grad_out, values_blk)
    grad_scores = (probs * (grad_probs - row_delta[..., None])).astype(jnp.bfloat16)
    return (prob_low, grad_scores)


def attention_forward(queries_heads, keys_heads, values_heads):
    seq_count, row_count, head_count, head_size = queries_heads.shape
    length = keys_heads.shape[1]
    block_rows = min(512, length)
    block_count = length // block_rows

    def max_step(running, block_index):
        running_max, running_total = running
        scores = plain_sum(
            "sqhd,skhd->shqk", queries_heads, row_block(keys_heads, block_index, block_rows)
        )
        new_max = jnp.maximum(running_max, jnp.max(scores, -1))
        running_total = running_total * jnp.exp(running_max - new_max) + jnp.sum(
            jnp.exp(scores - new_max[..., None]), -1
        )
        return ((new_max, running_total), None)

    start_max = jnp.full((seq_count, head_count, row_count), -1e30, jnp.float32)
    start_total = jnp.zeros((seq_count, head_count, row_count), jnp.float32)
    (final_max, final_total), unused = lax.scan(
        max_step, (start_max, start_total), jnp.arange(block_count)
    )
    log_total = final_max + jnp.log(final_total)

    def value_step(running, block_index):
        scores = plain_sum(
            "sqhd,skhd->shqk", queries_heads, row_block(keys_heads, block_index, block_rows)
        )
        prob_low = jnp.exp(scores - log_total[..., None]).astype(jnp.bfloat16)
        return (
            running
            + plain_sum(
                "shqk,skhd->sqhd", prob_low, row_block(values_heads, block_index, block_rows)
            ),
            None,
        )

    context, unused = lax.scan(
        value_step, jnp.zeros(queries_heads.shape, jnp.float32), jnp.arange(block_count)
    )
    return (context, log_total)


def gather_body(
    tokens,
    cotangent,
    sequence_adapter_index,
    query_key_value_weight,
    output_weight,
    first_feed_weight,
    second_feed_weight,
    biases,
    value_bias_vector,
    first_feed_bias,
    norm_gain_pair,
    adapter_down_factors,
    output_down_factor,
    adapter_up_factors,
    hidden_up_factor,
    hidden_down_factor,
):
    seq_count, row_count, model_width = tokens.shape
    adapter_number = adapter_down_factors.shape[0]
    picker = (
        sequence_adapter_index[:, None] == jnp.arange(adapter_number, dtype=jnp.int32)[None, :]
    ).astype(jnp.float32)

    def select_adapter(table):
        return jnp.einsum("sa,a...->s...", picker, table.astype(jnp.float32), precision=HIGHEST)

    def to_adapters(per_seq):
        return jnp.einsum("sa,s...->a...", picker, per_seq, precision=HIGHEST)

    selected_down = select_adapter(adapter_down_factors)
    selected_output = select_adapter(output_down_factor)
    selected_up = select_adapter(adapter_up_factors)
    hup_sel = select_adapter(hidden_up_factor)
    hdown_sel = select_adapter(hidden_down_factor)
    down_low = selected_down.astype(jnp.bfloat16)
    out_low = selected_output.astype(jnp.bfloat16)
    hdown_low = hdown_sel.astype(jnp.bfloat16)
    wqkv_full, wout_full = attn_weights(query_key_value_weight, output_weight)
    projected = plain_sum("std,de->ste", tokens, wqkv_full)
    down_att = plain_sum("std,sjrd->sjtr", tokens, down_low[:, :3])
    lifted = exact_sum("sjtr,sjrd->sjtd", down_att, selected_up[:, :3])
    queries = ((projected[..., :model_width] + biases[0] + lifted[:, 0]) * 0.125).astype(
        jnp.bfloat16
    )
    keys_own = (projected[..., model_width : 2 * model_width] + lifted[:, 1]).astype(jnp.bfloat16)
    values_own = (projected[..., 2 * model_width :] + value_bias_vector + lifted[:, 2]).astype(
        jnp.bfloat16
    )
    keys_all, values_all = (
        lax.all_gather(keys_own, "ctx", axis=1, tiled=True),
        lax.all_gather(values_own, "ctx", axis=1, tiled=True),
    )
    queries_heads = to_heads(queries)
    keys_heads = to_heads(keys_all)
    values_heads = to_heads(values_all)
    context, log_total = attention_forward(queries_heads, keys_heads, values_heads)
    context = context.reshape(seq_count, row_count, model_width)
    context_low = context.astype(jnp.bfloat16)
    down_out = plain_sum("std,srd->str", context_low, out_low)
    branch = (
        plain_sum("std,de->ste", context_low, wout_full)
        + biases[1]
        + exact_sum("str,srd->std", down_out, selected_up[:, 3])
    )

    def first_norm(value):
        return layer_norm(value, norm_gain_pair[0], biases[3])

    def second_norm(value):
        return layer_norm(value, norm_gain_pair[1], biases[4])

    def gelu_exact(value):
        return jax.nn.gelu(value, approximate=False)

    normed, norm_back = jax.vjp(first_norm, tokens.astype(jnp.float32) + branch)
    normed_low = normed.astype(jnp.bfloat16)
    wfc1_full, wfc2_full = mlp_weights(first_feed_weight, second_feed_weight)
    down_fc1 = plain_sum("std,srd->str", normed_low, down_low[:, 3])
    hidden_pre = (
        plain_sum("std,df->stf", normed_low, wfc1_full)
        + first_feed_bias
        + exact_sum("str,srf->stf", down_fc1, hup_sel)
    )
    activated, gelu_back = jax.vjp(gelu_exact, hidden_pre)
    act_low = activated.astype(jnp.bfloat16)
    down_fc2 = plain_sum("stf,srf->str", act_low, hdown_low)
    mixed_out = (
        plain_sum("stf,fd->std", act_low, wfc2_full)
        + biases[2]
        + exact_sum("str,srd->std", down_fc2, selected_up[:, 4])
    )
    outcome, out_back = jax.vjp(second_norm, normed + mixed_out)
    (grad_sum2,) = out_back(cotangent.astype(jnp.float32))
    grad_mixed = grad_sum2.astype(jnp.bfloat16)
    grad_up_fc2 = exact_sum("str,std->srd", down_fc2, grad_mixed)
    grad_rank_fc2 = exact_sum("std,srd->str", grad_mixed, selected_up[:, 4]).astype(jnp.bfloat16)
    grad_hdown = plain_sum("str,stf->srf", grad_rank_fc2, act_low)
    wfc1_full, wfc2_full = mlp_weights(first_feed_weight, second_feed_weight)
    grad_act = (
        plain_sum("std,fd->stf", grad_mixed, wfc2_full)
        + plain_sum("str,srf->stf", grad_rank_fc2, hdown_low)
    ).astype(jnp.bfloat16)
    (grad_hidden,) = gelu_back(grad_act.astype(jnp.float32))
    grad_hidden = grad_hidden.astype(jnp.bfloat16)
    grad_hup = exact_sum("str,stf->srf", down_fc1, grad_hidden)
    grad_rank_fc1 = exact_sum("stf,srf->str", grad_hidden, hup_sel).astype(jnp.bfloat16)
    grad_down_fc1 = plain_sum("str,std->srd", grad_rank_fc1, normed_low)
    grad_normed_low = (
        plain_sum("stf,df->std", grad_hidden, wfc1_full)
        + plain_sum("str,srd->std", grad_rank_fc1, down_low[:, 3])
    ).astype(jnp.bfloat16)
    (grad_resid,) = norm_back(grad_sum2 + grad_normed_low.astype(jnp.float32))
    mlp_hup = to_adapters(grad_hup)
    mlp_hdown = to_adapters(grad_hdown)
    mlp_fc1 = to_adapters(grad_down_fc1)
    mlp_fc2 = to_adapters(grad_up_fc2)
    mlp_hup, mlp_hdown, mlp_fc1, mlp_fc2 = lax.psum(
        (mlp_hup, mlp_hdown, mlp_fc1, mlp_fc2), ("ctx", "fsdp")
    )
    grad_branch = grad_resid.astype(jnp.bfloat16)
    grad_up_out = exact_sum("str,std->srd", down_out, grad_branch)
    grad_rank_out = exact_sum("std,srd->str", grad_branch, selected_up[:, 3]).astype(jnp.bfloat16)
    grad_out_down = plain_sum("str,std->srd", grad_rank_out, context_low)
    wqkv_full, wout_full = attn_weights(query_key_value_weight, output_weight)
    grad_context = (
        plain_sum("std,ed->ste", grad_branch, wout_full)
        + plain_sum("str,srd->std", grad_rank_out, out_low)
    ).astype(jnp.bfloat16)
    row_delta = jnp.sum(to_heads(grad_context.astype(jnp.float32) * context), -1)
    delta_heads = jnp.swapaxes(row_delta, 1, 2)
    grad_heads = to_heads(grad_context)
    length = keys_all.shape[1]
    block_rows = min(512, length)
    block_count = length // block_rows

    def key_step(block_index, running):
        grad_query, grad_key, grad_value = running
        keys_blk = row_block(keys_heads, block_index, block_rows)
        values_blk = row_block(values_heads, block_index, block_rows)
        prob_low, grad_scores = block_grads(
            queries_heads, grad_heads, log_total, delta_heads, keys_blk, values_blk
        )
        grad_query = grad_query + plain_sum("shqk,skhd->sqhd", grad_scores, keys_blk)
        grad_key = lax.dynamic_update_slice_in_dim(
            grad_key,
            plain_sum("shqk,sqhd->skhd", grad_scores, queries_heads),
            block_index * block_rows,
            1,
        )
        grad_value = lax.dynamic_update_slice_in_dim(
            grad_value,
            plain_sum("shqk,sqhd->skhd", prob_low, grad_heads),
            block_index * block_rows,
            1,
        )
        return (grad_query, grad_key, grad_value)

    start_query = jnp.zeros(queries_heads.shape, jnp.float32)
    start_keys = jnp.zeros(keys_heads.shape, jnp.float32)
    grad_query, grad_key_all, grad_value_all = lax.fori_loop(
        0, block_count, key_step, (start_query, start_keys, start_keys)
    )
    grad_keys, grad_values = (
        lax.psum_scatter(
            grad_key_all.reshape(seq_count, length, model_width).astype(jnp.bfloat16),
            "ctx",
            scatter_dimension=1,
            tiled=True,
        ).astype(jnp.float32),
        lax.psum_scatter(
            grad_value_all.reshape(seq_count, length, model_width).astype(jnp.bfloat16),
            "ctx",
            scatter_dimension=1,
            tiled=True,
        ).astype(jnp.float32),
    )
    grad_qlin = grad_query.reshape(seq_count, row_count, model_width).astype(jnp.bfloat16) * 0.125
    grad_key_low = grad_keys.astype(jnp.bfloat16)
    grad_value_low = grad_values.astype(jnp.bfloat16)
    stacked = jnp.stack([grad_qlin, grad_key_low, grad_value_low], 1)
    grad_up_att = exact_sum("sjtr,sjtd->sjrd", down_att, stacked)
    grad_rank_att = exact_sum("sjtd,sjrd->sjtr", stacked, selected_up[:, :3]).astype(jnp.bfloat16)
    grad_down_att = plain_sum("sjtr,std->sjrd", grad_rank_att, tokens)
    joined = jnp.concatenate([grad_qlin, grad_key_low, grad_value_low], -1)
    grad_tokens = (
        grad_resid
        + plain_sum("ste,de->std", joined, wqkv_full)
        + plain_sum("sjtr,sjrd->std", grad_rank_att, down_low[:, :3])
    )
    attn_down = to_adapters(grad_down_att)
    attn_out = to_adapters(grad_out_down)
    attn_up = to_adapters(jnp.concatenate([grad_up_att, grad_up_out[:, None]], 1))
    attn_down, attn_out, attn_up = lax.psum((attn_down, attn_out, attn_up), ("ctx", "fsdp"))
    total_down = jnp.concatenate([attn_down, mlp_fc1[:, None]], 1)
    total_up = jnp.concatenate([attn_up, mlp_fc2[:, None]], 1)
    return (
        outcome.astype(jnp.bfloat16),
        grad_tokens,
        total_down,
        attn_out,
        total_up,
        mlp_hup,
        mlp_hdown,
    )


BF16 = jnp.bfloat16
F32 = jnp.float32
LOG2E = 1.4426950408889634
VMEM_LIMIT = 60 * 2**20
MESH = pl.DeviceIdType.MESH


def dot32(left, right):
    return jnp.dot(left, right, preferred_element_type=F32)


def dot_nt(left, right):
    return lax.dot_general(left, right, (((1,), (1,)), ((), ())), preferred_element_type=F32)


def dot_tn(left, right):
    return lax.dot_general(left, right, (((0,), (0,)), ((), ())), preferred_element_type=F32)


def split_three(value):
    high = value.astype(BF16)
    rest = value - high.astype(F32)
    middle = rest.astype(BF16)
    return high, middle, (rest - middle.astype(F32)).astype(BF16)


def flip(value):
    return value.astype(F32).T.astype(BF16)


def remote(src, dst, send_sem, recv_sem, device):
    return pltpu.make_async_remote_copy(
        src_ref=src,
        dst_ref=dst,
        send_sem=send_sem,
        recv_sem=recv_sem,
        device_id=device,
        device_id_type=MESH,
    )


class Place:
    def __init__(self):
        self.ctx = lax.axis_index("ctx")
        self.core = lax.axis_index("fsdp")
        self.half = self.ctx // (H // 2)
        self.low = self.ctx % (H // 2)
        self.me = self.low * 2 + self.core
        self.swaps = self.core != self.half
        self.pair = (self.core + self.half) % 2
        self.sibling = (self.ctx, 1 - self.core)
        self.partner = ((self.ctx + H // 2) % H, 1 - self.core)

    def peer(self, step):
        number = self.me ^ step
        return (self.half * (H // 2) + number // 2, number % 2)

    def order(self, turn):
        return 2 * (turn % (H // 2)) + (turn // (H // 2) + self.pair) % 2

    def greet(self):
        barrier = pltpu.get_barrier_semaphore()
        for step in range(1, H):
            pl.semaphore_signal(barrier, inc=1, device_id=self.peer(step), device_id_type=MESH)
        pl.semaphore_signal(barrier, inc=1, device_id=self.partner, device_id_type=MESH)
        pl.semaphore_wait(barrier, H)


def sum_copies(mine, parts, total, sems, place):
    own = total.at[place.pair, place.low, place.half]
    other = total.at[place.pair, place.low, 1 - place.half]
    column = total.at[place.pair]
    scatter = [
        remote(mine.at[place.me ^ step], parts.at[step], sems.at[0, step], sems.at[1, step], place.peer(step))
        for step in range(1, H)
    ]
    cross = remote(own, own, sems.at[0, 0], sems.at[1, 0], place.partner)
    first = [
        remote(own, own, sems.at[2, step], sems.at[3, step], place.peer(step))
        for step in range(2, H, 2)
    ]
    second = [
        remote(other, other, sems.at[2, step + 1], sems.at[3, step + 1], place.peer(step))
        for step in range(2, H, 2)
    ]
    last = remote(column, column, sems.at[2, 0], sems.at[3, 0], place.sibling)
    return scatter, cross, first, second, last


def sum_parts(scatter, mine, parts, total, place):
    value = mine[place.me].astype(F32)
    for step, copy in enumerate(scatter, 1):
        copy.wait_recv()
        value = value + parts[step].astype(F32)
    total[place.pair, place.low, place.half] = value.astype(BF16)


def put_term(mine, base, term):
    units = mine.shape[2] // 128
    for unit in range(term.shape[1] // 128):
        at = base // 128 + unit
        lanes = slice(at % units * 128, at % units * 128 + 128)
        mine[at // units, :, lanes] = term[:, unit * 128 : unit * 128 + 128].astype(BF16)


def layer_kernel(
    block_q,
    block_k,
    index_ref,
    tokens_ref,
    cotangent_ref,
    wqkv_ref,
    wout_ref,
    wfc1_ref,
    wfc2_ref,
    down_table,
    up_table,
    out_down_table,
    hidden_up_table,
    hidden_down_table,
    biases_ref,
    value_bias_ref,
    hidden_bias_ref,
    gains_ref,
    outcome_ref,
    grad_ref,
    chosen_out,
    hidden_down_out,
    hidden_up_out,
    down_out,
    up_out,
    out_down_out,
    wqkv_far,
    wfc1_far,
    wide,
    wfc2,
    wout,
    big,
    act,
    small,
    small_hidden,
    x,
    cotangent,
    rank_att,
    outgoing,
    qkv,
    leaving,
    arrived,
    incoming,
    context,
    state,
    qta,
    gta,
    kk,
    vv,
    kt,
    both,
    dkv_sum,
    dq_in,
    dkv_out,
    dkv_in,
    grad_out,
    grad_in,
    mlp_mine,
    mlp_parts,
    mlp_total,
    att_mine,
    att_parts,
    att_total,
    load_sem,
    core_sem,
    swap_sem,
    kv_sem,
    q_sem,
    back_sem,
    grad_sem,
    dq_sem,
    dkv_sem,
    mlp_sem,
    att_sem,
):
    peers, _, rows = qkv.shape
    length = peers * rows
    width = x.shape[1]
    hidden = hidden_bias_ref.shape[1]
    adapters = hidden_up_table.shape[0] // 16
    place = Place()
    me, core = place.me, place.core
    other = 1 - core
    wqkv = wide.at[:, 0 : 3 * width]
    up_at = down_table.shape[0]
    out_down_at = up_at + up_table.shape[0]

    def half_of(full, owner):
        count = full.shape[0] // 2
        return full.at[pl.ds(pl.multiple_of(owner * count, count), count), :]

    def load(source, target, number):
        return pltpu.make_async_copy(source, target, load_sem.at[number])

    def to_sibling(source, target, number):
        return remote(source, target, core_sem.at[0, number], core_sem.at[1, number], place.sibling)

    load_wqkv = load(wqkv_ref, half_of(wqkv, core), 0)
    load_wout = load(wout_ref, half_of(wout, core), 1)
    load_tables = [
        load(down_table, wfc2.at[0:up_at], 2),
        load(up_table, wfc2.at[up_at:out_down_at], 3),
        load(out_down_table, wfc2.at[out_down_at : out_down_at + out_down_table.shape[0]], 4),
        load(hidden_up_table, act.at[0 : 16 * adapters], 5),
        load(hidden_down_table, act.at[16 * adapters : 32 * adapters], 6),
    ]
    load_x = load(tokens_ref, x, 7)
    load_cotangent = load(cotangent_ref, cotangent, 8)
    load_wfc1 = load(wfc1_ref, half_of(wide, core), 9)
    load_wfc1_far = load(wfc1_far, half_of(wide, other), 10)
    load_wfc2 = load(wfc2_ref, half_of(wfc2, core), 11)
    again_wqkv = load(wqkv_ref, half_of(wqkv, core), 12)
    again_wqkv_far = load(wqkv_far, half_of(wqkv, other), 13)
    give_wqkv = to_sibling(wqkv_ref, half_of(wqkv, core), 0)
    give_wout = to_sibling(wout_ref, half_of(wout, core), 1)
    give_chosen = to_sibling(chosen_out.at[core], chosen_out.at[core], 2)
    count = small.shape[0]
    give_small = [to_sibling(small, wide.at[0:count, 3 * width : 4 * width], 3)] + [
        to_sibling(
            small_hidden.at[:, part * width : (part + 1) * width],
            wide.at[count + 32 * part : count + 32 * part + 32, 3 * width : 4 * width],
            4 + part,
        )
        for part in range(hidden // width)
    ]
    give_wfc2 = to_sibling(wfc2_ref, half_of(wfc2, core), 8)
    give_wfc1 = to_sibling(wfc1_ref, wfc1_far, 9)
    give_wqkv_again = to_sibling(wqkv_ref, wqkv_far, 10)
    half_rows = rows // 2
    swap_x = [
        remote(
            tokens_ref.at[part * half_rows : (part + 1) * half_rows],
            x.at[part * half_rows : (part + 1) * half_rows],
            swap_sem.at[0, 7 + part],
            swap_sem.at[1, 7 + part],
            place.partner,
        )
        for part in range(2)
    ]
    swap_cotangent = remote(cotangent_ref, cotangent, swap_sem.at[0, 1], swap_sem.at[1, 1], place.partner)

    load_wqkv.start()
    for copy in load_tables:
        copy.start()
    load_wout.start()

    @pl.when(jnp.logical_not(place.swaps))
    def _():
        load_x.start()
        load_cotangent.start()

    adapter = index_ref[0]
    numbers = lax.broadcasted_iota(jnp.int32, chosen_out.shape[1:], 0)
    chosen_out[core] = (numbers == jnp.full(numbers.shape, adapter, jnp.int32)).astype(F32)
    place.greet()

    @pl.when(place.swaps)
    def _():
        for copy in swap_x:
            copy.start()

    give_wqkv.start()
    give_chosen.start()

    for copy in load_tables:
        copy.wait()

    def select(table, base, group, groups, target, at):
        chosen = jnp.full((16, table.shape[1]), adapter, jnp.int32)
        value = jnp.zeros((16, table.shape[1]), F32)
        for number in range(adapters):
            start = pl.multiple_of(base + 16 * (number * groups + group), 16)
            value = jnp.where(chosen == number, table[pl.ds(start, 16), :].astype(F32), value)
        target[pl.ds(pl.multiple_of(at + 16 * group, 16), 16), :] = value.astype(BF16)

    def select_down(group, _):
        select(wfc2, 0, group, 4, small, 0)
        return 0

    def select_up(group, _):
        select(wfc2, up_at, group, 5, small, 64)
        return 0

    lax.fori_loop(0, 4, select_down, 0)
    lax.fori_loop(0, 5, select_up, 0)
    select(wfc2, out_down_at, 0, 1, small, 144)
    for part in range(2):
        select(act, 16 * adapters * part, 0, 1, small_hidden, 16 * part)
    for copy in give_small:
        copy.start()
    give_wout.start()
    for copy in give_small:
        copy.wait()

    @pl.when(place.swaps)
    def _():
        small[...] = wide[0:count, 3 * width : 4 * width]
        for part in range(hidden // width):
            small_hidden[:, part * width : (part + 1) * width] = wide[
                count + 32 * part : count + 32 * part + 32, 3 * width : 4 * width
            ]

    hidden_up_ref = small_hidden.at[0:16]
    hidden_down_ref = small_hidden.at[16:32]
    out_down_ref = small.at[144:160]

    def down(j):
        return small[16 * j : 16 * j + 16]

    def up(j):
        return small[64 + 16 * j : 80 + 16 * j]

    load_wfc2.start()
    give_wfc2.start()

    load_wqkv.wait()
    give_wqkv.wait_recv()

    def project(half, part):
        here = slice(half * half_rows, (half + 1) * half_rows)
        cols = slice(part * width, (part + 1) * width)
        value = dot32(x[here, :], wqkv[:, cols]) + dot32(rank_att[here, part * 16 : part * 16 + 16], up(part))
        if part == 0:
            value = (value + biases_ref[0:1, :]) * 0.125
        if part == 2:
            value = value + value_bias_ref[...]
        for two in range(peers // 2):
            turned = value[:, two * 128 : two * 128 + 128].T.astype(BF16)
            outgoing[2 * two, part * 64 : part * 64 + 64, here] = turned[0:64]
            outgoing[2 * two + 1, part * 64 : part * 64 + 64, here] = turned[64:128]

    def kv_copy(step, half):
        here = slice(half * half_rows, (half + 1) * half_rows)
        return remote(
            outgoing.at[me ^ step, 64:192, here],
            qkv.at[step, 64:192, here],
            kv_sem.at[0, half, step],
            kv_sem.at[1, half, step],
            place.peer(step),
        )

    def q_copy(step):
        return remote(
            outgoing.at[me ^ step, 0:64], qkv.at[step, 0:64], q_sem.at[0, step], q_sem.at[1, step], place.peer(step)
        )

    def back_copy(step):
        return remote(leaving.at[step], arrived.at[me], back_sem.at[0, step], back_sem.at[1, step], place.peer(step))

    steps = length // block_k
    group = block_q // rows
    key_group = block_k // rows
    for half in range(2):
        here = slice(half * half_rows, (half + 1) * half_rows)

        @pl.when(place.swaps)
        def _():
            swap_x[half].wait_recv()

        if half == 0:

            @pl.when(jnp.logical_not(place.swaps))
            def _():
                load_x.wait()

        rank_att[here, :] = dot_nt(x[here, :], small[0:48]).astype(BF16)
        project(half, 1)
        project(half, 2)
        for step in range(1, peers):
            kv_copy(step, half).start()
        project(half, 0)
    for step in range(1, peers):
        q_copy(step).start()
    give_wfc1.start()
    give_wqkv_again.start()
    load_wfc1.start()
    qkv[0] = outgoing[me]

    row_at = lax.broadcasted_iota(jnp.int32, (16, rows), 0)
    ones = (row_at == 0).astype(F32).astype(BF16)
    minus = jnp.where(lax.broadcasted_iota(jnp.int32, (rows, 16), 1) < 3, -1.0, 0.0).astype(BF16)
    minus_rows = jnp.where(lax.broadcasted_iota(jnp.int32, (64, rows), 0) < 3, -1.0, 0.0).astype(BF16)

    def tail(value):
        at = lax.broadcasted_iota(jnp.int32, (16, value.shape[1]), 0)
        high, middle, low = (part.astype(F32) for part in split_three(value))
        return jnp.where(at == 0, high, jnp.where(at == 1, middle, jnp.where(at == 2, low, 0.0))).astype(BF16)

    def take_key(turn):
        cols = pl.ds(pl.multiple_of(turn * rows, rows), rows)
        step = place.order(turn)

        @pl.when(step > 0)
        def _():
            kv_copy(step, 0).wait_recv()
            kv_copy(step, 1).wait_recv()

        key = qkv[step, 64:128, :]
        value = qkv[step, 128:192, :]
        kt[:, cols] = key
        kk[cols, 0:128] = flip(jnp.concatenate([key, key], 0))
        kk[cols, 128:144] = minus
        vv[cols, :] = flip(jnp.concatenate([value, minus_rows], 0))
        gta[0:64, cols] = value
        gta[64:80, cols] = ones
        gta[80:128, cols] = jnp.zeros((48, rows), BF16)

    def take_keys(i):
        def one(part, _):
            take_key(i * key_group + part)
            return 0

        lax.fori_loop(0, key_group, one, 0)

    def forward_part(i, low, high, arriving):
        def take_query(part, _):
            turn = i * group + part
            step = place.order(turn)
            here = pl.ds(pl.multiple_of(turn * rows, rows), rows)

            @pl.when(step > 0)
            def _():
                q_copy(step).wait_recv()

            query = qkv[step, 0:64, :].astype(F32) * LOG2E
            high = query.astype(BF16)
            qta[0:64, here] = high
            qta[64:128, here] = (query - high.astype(F32)).astype(BF16)
            return 0

        if low == 0:
            lax.fori_loop(0, group, take_query, 0)
        cols = pl.ds(pl.multiple_of(i * block_q, block_q), block_q)
        query = qta.at[0:128, cols]
        if arriving:
            take_keys(low)
        block = dot32(kk[low * block_k : (low + 1) * block_k, 0:128], query[...])
        big[0:block_k] = block

        def half(j, now, carry):
            peak, running, total = carry
            later = jnp.minimum(j + 1, high - 1)
            here = pl.ds(pl.multiple_of(j * block_k, block_k), block_k)
            there = pl.ds(pl.multiple_of(later * block_k, block_k), block_k)
            if arriving:

                @pl.when(j + 1 < high)
                def _():
                    take_keys(later)

            ahead = dot32(kk[there, 0:128], query[...])
            big[(1 - now) * block_k : (2 - now) * block_k] = ahead
            new = jnp.maximum(running, peak)
            weights = jnp.exp2(big[now * block_k : (now + 1) * block_k] - new).astype(BF16)
            total = total * jnp.exp2(running - new) + dot32(gta[0:80, here], weights)
            return jnp.max(ahead, 0, keepdims=True), new, total

        def pair(j, carry):
            return half(low + 2 * j + 1, 1, half(low + 2 * j, 0, carry))

        if low == 0:
            running, total = jnp.full((1, block_q), -jnp.inf, F32), jnp.zeros((80, block_q), F32)
        else:
            running = state[1:2, cols]
            total = jnp.concatenate([context[:, cols], state[0:1, cols], jnp.zeros((15, block_q), F32)], 0)
        _, top, total = lax.fori_loop(
            0, (high - low) // 2, pair, (jnp.max(block, 0, keepdims=True), running, total)
        )
        weight_sum = total[64:65]
        if high < steps:
            context[:, cols] = total[0:64]
            state[0:1, cols] = weight_sum
            state[1:2, cols] = top
            return
        result = total[0:64] / weight_sum
        context[:, cols] = result
        qta[128:144, cols] = tail(top + jnp.log2(weight_sum))
        low_result = result.astype(BF16)
        for part in range(group):
            step = place.order(i * group + part)
            leaving[step] = low_result[:, part * rows : (part + 1) * rows]

            @pl.when(step > 0)
            def _():
                back_copy(step).start()

    query_steps = length // block_q
    for i in range(query_steps // 2):
        forward_part(i, 0, steps // 2, i == 0)
    give_wfc1.wait_recv()
    load_wfc1_far.start()
    for i in range(query_steps // 2):
        forward_part(i, steps // 2, steps, i == 0)

    @pl.when(place.swaps)
    def _():
        swap_cotangent.start()

    def forward_whole(i, _):
        forward_part(i, 0, steps, False)
        return 0

    lax.fori_loop(query_steps // 2, query_steps, forward_whole, 0)
    arrived[me] = leaving[0]

    def mean(value):
        return jnp.mean(value, -1, keepdims=True)

    def norm_backward(grad, hat, scale):
        return scale * (grad - mean(grad) - hat * mean(grad * hat))

    load_wout.wait()
    give_wout.wait_recv()
    for step in range(1, peers):
        back_copy(step).wait_recv()
    context_low = flip(arrived[...].reshape(width, rows))
    rank_out = dot_nt(context_low, out_down_ref[...]).astype(BF16)
    resid = x[...].astype(F32) + dot32(context_low, wout[...]) + biases_ref[1:2] + dot32(rank_out, up(3))
    center = resid - mean(resid)
    scale_one = lax.rsqrt(mean(center * center) + EPSILON)
    hat_one = center * scale_one
    normed = hat_one * gains_ref[0:1] + biases_ref[3:4]
    normed_low = normed.astype(BF16)
    rank_one = dot_nt(normed_low, down(3)).astype(BF16)
    load_wfc1.wait()
    load_wfc1_far.wait()
    load_wfc2.wait()
    give_wfc2.wait_recv()
    piece = 1024
    rank_two = jnp.zeros((rows, 16), F32)
    mixed = normed + biases_ref[2:3]
    for part in range(hidden // piece):
        cols = slice(part * piece, (part + 1) * piece)
        pre = (
            dot32(normed_low, wide[:, cols])
            + hidden_bias_ref[:, cols]
            + dot32(rank_one, hidden_up_ref[:, cols])
        )
        share = 0.5 + 0.5 * lax.erf(pre * 0.7071067811865476)
        big[part * rows : (part + 1) * rows] = share + pre * (0.3989422804014327 * jnp.exp(-0.5 * pre * pre))
        active = (pre * share).astype(BF16)
        act[:, cols] = active
        rank_two = rank_two + dot_nt(active, hidden_down_ref[:, cols])
        mixed = mixed + dot32(active, wfc2[cols, :])
    rank_two = rank_two.astype(BF16)
    mixed = mixed + dot32(rank_two, up(4))
    center = mixed - mean(mixed)
    scale_two = lax.rsqrt(mean(center * center) + EPSILON)
    hat_two = center * scale_two

    @pl.when(place.swaps)
    def _():
        swap_cotangent.wait_recv()

    @pl.when(jnp.logical_not(place.swaps))
    def _():
        load_cotangent.wait()

    grad_sum = norm_backward(cotangent[...].astype(F32) * gains_ref[1:2], hat_two, scale_two)
    outcome = cotangent
    outcome[...] = (hat_two * gains_ref[1:2] + biases_ref[4:5]).astype(BF16)
    home_outcome = remote(outcome, outcome_ref, swap_sem.at[0, 2], swap_sem.at[1, 2], place.partner)

    @pl.when(place.swaps)
    def _():
        home_outcome.start()

    @pl.when(jnp.logical_not(place.swaps))
    def _():
        outcome_ref[...] = outcome[...]

    grad_mixed = grad_sum.astype(BF16)
    put_term(mlp_mine, 2 * hidden, dot_tn(rank_two, grad_mixed))
    grad_rank = dot_nt(grad_mixed, up(4)).astype(BF16)
    put_term(mlp_mine, 0, dot_tn(grad_rank, act[...]))
    grad_one = jnp.zeros((rows, 16), F32)
    grad_normed = jnp.zeros((rows, width), F32)
    for part in range(hidden // piece):
        cols = slice(part * piece, (part + 1) * piece)
        grad_act = dot_nt(grad_mixed, wfc2[cols, :]) + dot32(grad_rank, hidden_down_ref[:, cols])
        grad_hidden = (grad_act.astype(BF16).astype(F32) * big[part * rows : (part + 1) * rows]).astype(BF16)
        put_term(mlp_mine, hidden + part * piece, dot_tn(rank_one, grad_hidden))
        grad_one = grad_one + dot_nt(grad_hidden, hidden_up_ref[:, cols])
        grad_normed = grad_normed + dot_nt(grad_hidden, wide[:, cols])
    grad_one = grad_one.astype(BF16)
    put_term(mlp_mine, 2 * hidden + width, dot_tn(grad_one, normed_low))
    grad_normed = (grad_normed + dot32(grad_one, down(3))).astype(BF16).astype(F32)
    resid_grad = norm_backward((grad_sum + grad_normed) * gains_ref[0:1], hat_one, scale_one)
    grad_resid = big.at[0:rows]
    grad_resid[...] = resid_grad
    grad_branch = resid_grad.astype(BF16)
    put_term(mlp_mine, 2 * hidden + 2 * width, dot_tn(rank_out, grad_branch))
    grad_rank = dot_nt(grad_branch, up(3)).astype(BF16)
    put_term(mlp_mine, 2 * hidden + 3 * width, dot_tn(grad_rank, context_low))
    turned = dot_nt(wout[...], grad_branch) + lax.dot_general(
        out_down_ref[...], grad_rank, (((0,), (1,)), ((), ())), preferred_element_type=F32
    )
    for step in range(1, peers):
        kv_copy(step, 0).wait_send()
        kv_copy(step, 1).wait_send()
        q_copy(step).wait_send()
        back_copy(step).wait_send()
    outgoing[:, 0:64] = turned.astype(BF16).reshape(peers, 64, rows)

    def grad_copy(step):
        return remote(
            outgoing.at[me ^ step, 0:64], incoming.at[step], grad_sem.at[0, step], grad_sem.at[1, step], place.peer(step)
        )

    for step in range(1, peers):
        grad_copy(step).start()
    mlp_scatter, mlp_cross, mlp_first, mlp_second, mlp_last = sum_copies(mlp_mine, mlp_parts, mlp_total, mlp_sem, place)
    incoming[0] = outgoing[me, 0:64]
    give_wqkv_again.wait_recv()
    again_wqkv.start()
    again_wqkv_far.start()
    dkv_sum[...] = jnp.zeros_like(dkv_sum)
    first = lax.broadcasted_iota(jnp.int32, (block_k, 128), 1) < 64
    dq_out = leaving

    def dq_copy(step):
        return remote(dq_out.at[step], dq_in.at[me], dq_sem.at[0, step], dq_sem.at[1, step], place.peer(step))

    def dkv_copy(step):
        return remote(dkv_out.at[step], dkv_in.at[me], dkv_sem.at[0, step], dkv_sem.at[1, step], place.peer(step))

    def backward_step(turn, last):
        j = (turn + query_steps // 2) % query_steps

        def take_grad(part, _):
            step = place.order(j * group + part)
            cols = pl.ds(pl.multiple_of((j * group + part) * rows, rows), rows)

            @pl.when(step > 0)
            def _():
                grad_copy(step).wait_recv()

            grad = incoming[step]
            gta[0:64, cols] = grad
            gta[64:80, cols] = tail(jnp.sum(grad.astype(F32) * context[:, cols], 0, keepdims=True))
            both[cols, :] = flip(jnp.concatenate([qkv[step, 0:64, :], grad], 0))
            return 0

        lax.fori_loop(0, group, take_grad, 0)
        cols = pl.ds(pl.multiple_of(j * block_q, block_q), block_q)

        def key_pair(pair, dq):
            found = []
            for side in range(2):
                i = (2 * pair + side + steps // 2) % steps
                here = pl.ds(pl.multiple_of(i * block_k, block_k), block_k)
                probs = jnp.exp2(dot32(kk[here, :], qta[:, cols]))
                change = dot32(vv[here, :], gta[:, cols])
                found.append((i, here, probs.astype(BF16), (probs * change).astype(BF16)))
            for i, here, probs, low in found:
                dv = dot32(probs, both[cols, :])
                dk = dot32(low, both[cols, :])
                dkv = dkv_sum[here, :] + jnp.where(first, dk, dv)
                if not last:
                    dkv_sum[here, :] = dkv
                else:
                    done = dkv.astype(BF16)
                    for part in range(key_group):
                        step = place.order(i * key_group + part)
                        dkv_out[step] = done[part * rows : (part + 1) * rows]

                        @pl.when(step > 0)
                        def _():
                            dkv_copy(step).start()

                dq = dq + dot32(kt[:, here], low)
            return dq

        dq = lax.fori_loop(0, steps // 2, key_pair, jnp.zeros((64, block_q), F32)).astype(BF16)
        for part in range(group):
            step = place.order(j * group + part)
            dq_out[step] = dq[:, part * rows : (part + 1) * rows]

            @pl.when(step > 0)
            def _():
                dq_copy(step).start()

    def backward_steps(low, high):
        def one(j, _):
            backward_step(j, False)
            return 0

        lax.fori_loop(low, high, one, 0)

    backward_steps(0, query_steps // 4)
    for copy in mlp_scatter:
        copy.start()
    backward_steps(query_steps // 4, query_steps // 2)
    sum_parts(mlp_scatter, mlp_mine, mlp_parts, mlp_total, place)
    mlp_cross.start()
    for copy in mlp_first:
        copy.start()
    backward_steps(query_steps // 2, query_steps - 1)
    mlp_cross.wait_recv()
    for copy in mlp_second:
        copy.start()
    backward_step(query_steps - 1, True)
    for copy in mlp_first + mlp_second:
        copy.wait_recv()
    mlp_last.start()

    def spread(total, parts):
        units = total.shape[4] // 128
        for half in range(2):
            for unit in range(peers * units):
                peer = unit // units
                lanes = slice(unit % units * 128, unit % units * 128 + 128)
                for target, low, high in parts:
                    if low <= unit * 128 < high:
                        at = unit * 128 - low
                        target(half)[:, at : at + 128] = total[(peer % 2 + half) % 2, peer // 2, half, :, lanes]

    joined = act.at[:, 0 : 3 * width]
    dq_in[me] = dq_out[0]
    dkv_in[me] = dkv_out[0]
    for step in range(1, peers):
        dkv_copy(step).wait_recv()
    left = lax.broadcasted_iota(jnp.int32, (rows, 128), 1) < 64
    for two in range(peers // 2):
        even = dkv_in[2 * two].astype(F32)
        odd = dkv_in[2 * two + 1].astype(F32)
        cols = slice(width + two * 128, width + two * 128 + 128)
        joined[:, cols] = jnp.where(left, even, pltpu.roll(odd, 64, 1)).astype(BF16)
        cols = slice(2 * width + two * 128, 2 * width + two * 128 + 128)
        joined[:, cols] = jnp.where(left, pltpu.roll(even, 64, 1), odd).astype(BF16)
    def ranks_of(part):
        grad = joined[:, part * width : (part + 1) * width]
        ranks[part] = dot_nt(grad, up(part)).astype(BF16)

    def terms_of(part):
        grad = joined[:, part * width : (part + 1) * width]
        put_term(att_mine, part * width, dot_tn(rank_att[:, part * 16 : part * 16 + 16], grad))
        put_term(att_mine, (3 + part) * width, dot_tn(ranks[part], x[...]))

    ranks = {}
    att_scatter, att_cross, att_first, att_second, att_last = sum_copies(att_mine, att_parts, att_total, att_sem, place)
    again_wqkv.wait()
    again_wqkv_far.wait()
    for part in (1, 2):
        ranks_of(part)
        terms_of(part)
    for step in range(1, peers):
        dq_copy(step).wait_recv()
    joined[:, 0:width] = (dq_in[...].reshape(width, rows).astype(F32).T * 0.125).astype(BF16)
    ranks_of(0)
    terms_of(0)
    for copy in att_scatter:
        copy.start()
    piece = width // 4
    home = [
        remote(
            grad_out.at[:, part * piece : (part + 1) * piece],
            grad_in.at[:, part * piece : (part + 1) * piece],
            swap_sem.at[0, 3 + part],
            swap_sem.at[1, 3 + part],
            place.partner,
        )
        for part in range(4)
    ]
    mlp_last.wait_recv()
    for part in range(4):
        cols = slice(part * piece, (part + 1) * piece)
        total = grad_resid[:, cols] + dot_nt(joined[...], wqkv[cols, :])
        for j in range(3):
            total = total + dot32(ranks[j], small[16 * j : 16 * j + 16, cols])
        grad_ref[:, cols] = total
        grad_out[:, cols] = total.astype(BF16)

        @pl.when(place.swaps)
        def _():
            home[part].start()

    sum_parts(att_scatter, att_mine, att_parts, att_total, place)
    att_cross.start()
    for copy in att_first:
        copy.start()
    spread(
        mlp_total,
        (
            (lambda half: hidden_down_out.at[half], 0, hidden),
            (lambda half: hidden_up_out.at[half], hidden, 2 * hidden),
            (lambda half: up_out.at[half, 4], 2 * hidden, 2 * hidden + width),
            (lambda half: down_out.at[half, 3], 2 * hidden + width, 2 * hidden + 2 * width),
            (lambda half: up_out.at[half, 3], 2 * hidden + 2 * width, 2 * hidden + 3 * width),
            (lambda half: out_down_out.at[half], 2 * hidden + 3 * width, 2 * hidden + 4 * width),
        ),
    )
    att_cross.wait_recv()
    for copy in att_second:
        copy.start()
    for copy in att_first + att_second:
        copy.wait_recv()
    att_last.start()

    @pl.when(place.swaps)
    def _():
        for part in range(4):
            home[part].wait_recv()
            cols = slice(part * piece, (part + 1) * piece)
            grad_ref[:, cols] = grad_in[:, cols].astype(F32)
        for part in range(4):
            home[part].wait_send()
        home_outcome.wait()
        for copy in swap_x:
            copy.wait_send()
        swap_cotangent.wait_send()

    att_last.wait_recv()
    spread(
        att_total,
        tuple(
            (functools.partial(lambda part, half: up_out.at[half, part], part), part * width, (part + 1) * width)
            for part in range(3)
        )
        + tuple(
            (functools.partial(lambda part, half: down_out.at[half, part], part), (3 + part) * width, (4 + part) * width)
            for part in range(3)
        ),
    )
    for step in range(1, peers):
        grad_copy(step).wait_send()
        dq_copy(step).wait_send()
        dkv_copy(step).wait_send()
    for copies in ((mlp_scatter, mlp_first, mlp_second), (att_scatter, att_first, att_second)):
        for copy in copies[0] + copies[1] + copies[2]:
            copy.wait_send()
    for copy in (mlp_cross, mlp_last, att_cross, att_last):
        copy.wait_send()
    for copy in (give_wqkv, give_wout, give_wfc2, give_wfc1, give_wqkv_again):
        copy.wait_send()
    give_chosen.wait()


def run_layer(index, tokens, cotangent, weights, tables, biases, value_bias, hidden_bias, gains):
    rows, width = tokens.shape
    peers = H
    length = peers * rows
    hidden = hidden_bias.shape[1]
    block_q, block_k = 1024, 512
    vmem = pl.BlockSpec(memory_space=pltpu.VMEM)
    hbm = pl.BlockSpec(memory_space=pl.ANY)
    mlp_part = (2 * hidden + 4 * width) // peers
    att_part = 6 * width // peers

    def out(shape, dtype=BF16):
        return jax.ShapeDtypeStruct(shape, dtype)

    def total(part):
        return pltpu.VMEM((2, peers // 2, 2, 16, part), BF16)

    def heads(*shape):
        return pltpu.VMEM((peers,) + shape, BF16)

    def sems(*shape):
        return pltpu.SemaphoreType.DMA(shape)

    return pl.pallas_call(
        functools.partial(layer_kernel, block_q, block_k),
        out_shape=[
            out((rows, width)),
            out((rows, width), F32),
            out((2, 8, 128), F32),
            out((2, 16, hidden)),
            out((2, 16, hidden)),
            out((2, 4, 16, width)),
            out((2, 5, 16, width)),
            out((2, 16, width)),
            out(weights[0].shape),
            out(weights[2].shape),
        ],
        in_specs=[pl.BlockSpec(memory_space=pltpu.SMEM)] + [hbm] * 11 + [vmem] * 4,
        out_specs=[vmem] * 8 + [hbm] * 2,
        scratch_shapes=[
            pltpu.VMEM((width, hidden), BF16),
            pltpu.VMEM((hidden, width), BF16),
            pltpu.VMEM((width, width), BF16),
            pltpu.VMEM((max(4 * rows, 2 * block_k), 1024), F32),
            pltpu.VMEM((rows, hidden), BF16),
            pltpu.VMEM((160, width), BF16),
            pltpu.VMEM((32, hidden), BF16),
            pltpu.VMEM((rows, width), BF16),
            pltpu.VMEM((rows, width), BF16),
            pltpu.VMEM((rows, 48), BF16),
            heads(192, rows),
            heads(192, rows),
            heads(64, rows),
            heads(64, rows),
            heads(64, rows),
            pltpu.VMEM((64, length), F32),
            pltpu.VMEM((8, length), F32),
            pltpu.VMEM((144, length), BF16),
            pltpu.VMEM((128, length), BF16),
            pltpu.VMEM((length, 144), BF16),
            pltpu.VMEM((length, 128), BF16),
            pltpu.VMEM((64, length), BF16),
            pltpu.VMEM((length, 128), BF16),
            pltpu.VMEM((length, 128), F32),
            heads(64, rows),
            heads(rows, 128),
            heads(rows, 128),
            pltpu.VMEM((rows, width), BF16),
            pltpu.VMEM((rows, width), BF16),
            heads(16, mlp_part),
            heads(16, mlp_part),
            total(mlp_part),
            heads(16, att_part),
            heads(16, att_part),
            total(att_part),
            sems(14),
            sems(2, 11),
            sems(2, 9),
            sems(2, 2, peers),
            sems(2, peers),
            sems(2, peers),
            sems(2, peers),
            sems(2, peers),
            sems(2, peers),
            sems(4, peers),
            sems(4, peers),
        ],
        compiler_params=pltpu.CompilerParams(
            collective_id=0, has_side_effects=True, vmem_limit_bytes=VMEM_LIMIT
        ),
        name="run_layer",
    )(index, tokens, cotangent, *weights, *tables, biases, value_bias, hidden_bias, gains)


def assemble_kernel(
    chosen_ref, down_in, up_in, hidden_up_in, hidden_down_in, out_down_in, outcome_in, grad_in, *results
):
    *tables, out_down, outcome_out, grad_out = results
    number = pl.program_id(0)
    masks = [chosen_ref[seq, pl.ds(number, 1), 0:1] > 0.0 for seq in range(2)]
    for source, table in zip((down_in, up_in, hidden_up_in, hidden_down_in), tables):
        for i in range(source.shape[1]):
            value = jnp.zeros(source.shape[2:], F32)
            for seq, mask in enumerate(masks):
                value = value + jnp.where(mask, source[seq, i].astype(F32), 0.0)
            table[0, i] = value
    for seq, mask in enumerate(masks):
        out_down[seq, 0] = jnp.where(mask, out_down_in[seq].astype(F32), 0.0).astype(BF16)
    outcome_out[...] = outcome_in[...]
    grad_out[...] = grad_in[...]


def assemble(chosen, terms, out_down, outcome, grad_tokens):
    adapters = chosen.shape[1]
    block = outcome.shape[0] // adapters
    terms = [term.reshape((2, -1) + term.shape[-2:]) for term in terms]
    inputs = (chosen, *terms, out_down)

    def whole(array):
        return pl.BlockSpec(array.shape, lambda i: (0,) * array.ndim)

    def part(shape, at=0):
        return pl.BlockSpec(shape, lambda i: (0,) * at + (i,) + (0,) * (len(shape) - 1 - at))

    rows_spec = part((block, outcome.shape[1]))
    tables = [(adapters,) + term.shape[1:] for term in terms]
    each = (2, adapters) + out_down.shape[1:]
    return pl.pallas_call(
        assemble_kernel,
        grid=(adapters,),
        out_shape=[
            *(jax.ShapeDtypeStruct(shape, F32) for shape in tables),
            jax.ShapeDtypeStruct(each, BF16),
            jax.ShapeDtypeStruct(outcome.shape, BF16),
            jax.ShapeDtypeStruct(grad_tokens.shape, F32),
        ],
        in_specs=[*(whole(array) for array in inputs), rows_spec, rows_spec],
        out_specs=[
            *(part((1,) + shape[1:]) for shape in tables),
            part((2, 1) + out_down.shape[1:], 1),
            rows_spec,
            rows_spec,
        ],
        compiler_params=pltpu.CompilerParams(vmem_limit_bytes=VMEM_LIMIT),
        name="assemble",
    )(*inputs, outcome, grad_tokens)


def heads_body(
    tokens,
    cotangent,
    sequence_adapter_index,
    query_key_value_weight,
    output_weight,
    first_feed_weight,
    second_feed_weight,
    biases,
    value_bias_vector,
    first_feed_bias,
    norm_gain_pair,
    adapter_down_factors,
    output_down_factor,
    adapter_up_factors,
    hidden_up_factor,
    hidden_down_factor,
):
    width = tokens.shape[2]
    hidden = first_feed_bias.shape[0]
    outcome, grad_tokens, chosen, term_hd, term_uh, term_down, term_up, term_do, *_ = run_layer(
        sequence_adapter_index,
        tokens[0],
        cotangent[0],
        (query_key_value_weight, output_weight, first_feed_weight, second_feed_weight),
        (
            adapter_down_factors.reshape(-1, width),
            adapter_up_factors.reshape(-1, width),
            output_down_factor.reshape(-1, width),
            hidden_up_factor.reshape(-1, hidden),
            hidden_down_factor.reshape(-1, hidden),
        ),
        biases,
        value_bias_vector[None],
        first_feed_bias[None],
        norm_gain_pair,
    )
    total_down, total_up, total_hidden_up, total_hidden_down, each, outcome, grad_tokens = assemble(
        chosen, (term_down, term_up, term_uh, term_hd), term_do, outcome, grad_tokens
    )
    return (
        outcome[None],
        grad_tokens[None],
        total_down,
        each[0].astype(F32) + each[1].astype(F32),
        total_up,
        total_hidden_up.reshape(hidden_up_factor.shape),
        total_hidden_down.reshape(hidden_down_factor.shape),
    )


def solution(mesh):
    one_head_each = mesh.shape["ctx"] == H and mesh.shape["fsdp"] == 2
    return jax.shard_map(
        heads_body if one_head_each else gather_body,
        mesh=mesh,
        in_specs=(
            P("fsdp", "ctx", None),
            P("fsdp", "ctx", None),
            P("fsdp"),
            P("fsdp", None),
            P("fsdp", None),
            P("fsdp", None),
            P("fsdp", None),
            P(),
            P(),
            P(),
            P(),
            P(),
            P(),
            P(),
            P(),
            P(),
        ),
        out_specs=(P("fsdp", "ctx", None), P("fsdp", "ctx", None), P(), P(), P(), P(), P()),
        check_vma=False,
    )
```

```python
import functools

import jax
import jax.numpy as jnp
from jax import lax
from jax.experimental import pallas as pl
from jax.experimental.pallas import tpu as pltpu
from jax.sharding import PartitionSpec as P

H = 16


EPSILON = 1e-05
HIGHEST = lax.Precision.HIGHEST


def exact_sum(form, left, right):
    return jnp.einsum(form, left, right, precision=HIGHEST, preferred_element_type=jnp.float32)


def plain_sum(form, left, right):
    return jnp.einsum(form, left, right, preferred_element_type=jnp.float32)


def layer_norm(value, gain, shift):
    center = value - jnp.mean(value, -1, keepdims=True)
    spread = jnp.mean(center * center, -1, keepdims=True)
    return center * lax.rsqrt(spread + EPSILON) * gain + shift


def attn_weights(query_key_value_weight, output_weight):
    return (
        lax.all_gather(query_key_value_weight, "fsdp", axis=0, tiled=True),
        lax.all_gather(output_weight, "fsdp", axis=0, tiled=True),
    )


def mlp_weights(first_feed_weight, second_feed_weight):
    return (
        lax.all_gather(first_feed_weight, "fsdp", axis=0, tiled=True),
        lax.all_gather(second_feed_weight, "fsdp", axis=0, tiled=True),
    )


def to_heads(input_array):
    return input_array.reshape(
        input_array.shape[0], input_array.shape[1], H, input_array.shape[2] // H
    )


def row_block(input_array, block_index, block_rows):
    return lax.dynamic_slice_in_dim(input_array, block_index * block_rows, block_rows, 1)


def block_grads(queries, grad_out, log_total, row_delta, keys_blk, values_blk):
    scores = plain_sum("sqhd,skhd->shqk", queries, keys_blk)
    probs = jnp.exp(scores - log_total[..., None])
    prob_low = probs.astype(jnp.bfloat16)
    grad_probs = plain_sum("sqhd,skhd->shqk", grad_out, values_blk)
    grad_scores = (probs * (grad_probs - row_delta[..., None])).astype(jnp.bfloat16)
    return (prob_low, grad_scores)


def attention_forward(queries_heads, keys_heads, values_heads):
    seq_count, row_count, head_count, head_size = queries_heads.shape
    length = keys_heads.shape[1]
    block_rows = min(512, length)
    block_count = length // block_rows

    def max_step(running, block_index):
        running_max, running_total = running
        scores = plain_sum(
            "sqhd,skhd->shqk", queries_heads, row_block(keys_heads, block_index, block_rows)
        )
        new_max = jnp.maximum(running_max, jnp.max(scores, -1))
        running_total = running_total * jnp.exp(running_max - new_max) + jnp.sum(
            jnp.exp(scores - new_max[..., None]), -1
        )
        return ((new_max, running_total), None)

    start_max = jnp.full((seq_count, head_count, row_count), -1e30, jnp.float32)
    start_total = jnp.zeros((seq_count, head_count, row_count), jnp.float32)
    (final_max, final_total), unused = lax.scan(
        max_step, (start_max, start_total), jnp.arange(block_count)
    )
    log_total = final_max + jnp.log(final_total)

    def value_step(running, block_index):
        scores = plain_sum(
            "sqhd,skhd->shqk", queries_heads, row_block(keys_heads, block_index, block_rows)
        )
        prob_low = jnp.exp(scores - log_total[..., None]).astype(jnp.bfloat16)
        return (
            running
            + plain_sum(
                "shqk,skhd->sqhd", prob_low, row_block(values_heads, block_index, block_rows)
            ),
            None,
        )

    context, unused = lax.scan(
        value_step, jnp.zeros(queries_heads.shape, jnp.float32), jnp.arange(block_count)
    )
    return (context, log_total)


def gather_body(
    tokens,
    cotangent,
    sequence_adapter_index,
    query_key_value_weight,
    output_weight,
    first_feed_weight,
    second_feed_weight,
    biases,
    value_bias_vector,
    first_feed_bias,
    norm_gain_pair,
    adapter_down_factors,
    output_down_factor,
    adapter_up_factors,
    hidden_up_factor,
    hidden_down_factor,
):
    seq_count, row_count, model_width = tokens.shape
    adapter_number = adapter_down_factors.shape[0]
    picker = (
        sequence_adapter_index[:, None] == jnp.arange(adapter_number, dtype=jnp.int32)[None, :]
    ).astype(jnp.float32)

    def select_adapter(table):
        return jnp.einsum("sa,a...->s...", picker, table.astype(jnp.float32), precision=HIGHEST)

    def to_adapters(per_seq):
        return jnp.einsum("sa,s...->a...", picker, per_seq, precision=HIGHEST)

    selected_down = select_adapter(adapter_down_factors)
    selected_output = select_adapter(output_down_factor)
    selected_up = select_adapter(adapter_up_factors)
    hup_sel = select_adapter(hidden_up_factor)
    hdown_sel = select_adapter(hidden_down_factor)
    down_low = selected_down.astype(jnp.bfloat16)
    out_low = selected_output.astype(jnp.bfloat16)
    hdown_low = hdown_sel.astype(jnp.bfloat16)
    wqkv_full, wout_full = attn_weights(query_key_value_weight, output_weight)
    projected = plain_sum("std,de->ste", tokens, wqkv_full)
    down_att = plain_sum("std,sjrd->sjtr", tokens, down_low[:, :3])
    lifted = exact_sum("sjtr,sjrd->sjtd", down_att, selected_up[:, :3])
    queries = ((projected[..., :model_width] + biases[0] + lifted[:, 0]) * 0.125).astype(
        jnp.bfloat16
    )
    keys_own = (projected[..., model_width : 2 * model_width] + lifted[:, 1]).astype(jnp.bfloat16)
    values_own = (projected[..., 2 * model_width :] + value_bias_vector + lifted[:, 2]).astype(
        jnp.bfloat16
    )
    keys_all, values_all = (
        lax.all_gather(keys_own, "ctx", axis=1, tiled=True),
        lax.all_gather(values_own, "ctx", axis=1, tiled=True),
    )
    queries_heads = to_heads(queries)
    keys_heads = to_heads(keys_all)
    values_heads = to_heads(values_all)
    context, log_total = attention_forward(queries_heads, keys_heads, values_heads)
    context = context.reshape(seq_count, row_count, model_width)
    context_low = context.astype(jnp.bfloat16)
    down_out = plain_sum("std,srd->str", context_low, out_low)
    branch = (
        plain_sum("std,de->ste", context_low, wout_full)
        + biases[1]
        + exact_sum("str,srd->std", down_out, selected_up[:, 3])
    )

    def first_norm(value):
        return layer_norm(value, norm_gain_pair[0], biases[3])

    def second_norm(value):
        return layer_norm(value, norm_gain_pair[1], biases[4])

    def gelu_exact(value):
        return jax.nn.gelu(value, approximate=False)

    normed, norm_back = jax.vjp(first_norm, tokens.astype(jnp.float32) + branch)
    normed_low = normed.astype(jnp.bfloat16)
    wfc1_full, wfc2_full = mlp_weights(first_feed_weight, second_feed_weight)
    down_fc1 = plain_sum("std,srd->str", normed_low, down_low[:, 3])
    hidden_pre = (
        plain_sum("std,df->stf", normed_low, wfc1_full)
        + first_feed_bias
        + exact_sum("str,srf->stf", down_fc1, hup_sel)
    )
    activated, gelu_back = jax.vjp(gelu_exact, hidden_pre)
    act_low = activated.astype(jnp.bfloat16)
    down_fc2 = plain_sum("stf,srf->str", act_low, hdown_low)
    mixed_out = (
        plain_sum("stf,fd->std", act_low, wfc2_full)
        + biases[2]
        + exact_sum("str,srd->std", down_fc2, selected_up[:, 4])
    )
    outcome, out_back = jax.vjp(second_norm, normed + mixed_out)
    (grad_sum2,) = out_back(cotangent.astype(jnp.float32))
    grad_mixed = grad_sum2.astype(jnp.bfloat16)
    grad_up_fc2 = exact_sum("str,std->srd", down_fc2, grad_mixed)
    grad_rank_fc2 = exact_sum("std,srd->str", grad_mixed, selected_up[:, 4]).astype(jnp.bfloat16)
    grad_hdown = plain_sum("str,stf->srf", grad_rank_fc2, act_low)
    wfc1_full, wfc2_full = mlp_weights(first_feed_weight, second_feed_weight)
    grad_act = (
        plain_sum("std,fd->stf", grad_mixed, wfc2_full)
        + plain_sum("str,srf->stf", grad_rank_fc2, hdown_low)
    ).astype(jnp.bfloat16)
    (grad_hidden,) = gelu_back(grad_act.astype(jnp.float32))
    grad_hidden = grad_hidden.astype(jnp.bfloat16)
    grad_hup = exact_sum("str,stf->srf", down_fc1, grad_hidden)
    grad_rank_fc1 = exact_sum("stf,srf->str", grad_hidden, hup_sel).astype(jnp.bfloat16)
    grad_down_fc1 = plain_sum("str,std->srd", grad_rank_fc1, normed_low)
    grad_normed_low = (
        plain_sum("stf,df->std", grad_hidden, wfc1_full)
        + plain_sum("str,srd->std", grad_rank_fc1, down_low[:, 3])
    ).astype(jnp.bfloat16)
    (grad_resid,) = norm_back(grad_sum2 + grad_normed_low.astype(jnp.float32))
    mlp_hup = to_adapters(grad_hup)
    mlp_hdown = to_adapters(grad_hdown)
    mlp_fc1 = to_adapters(grad_down_fc1)
    mlp_fc2 = to_adapters(grad_up_fc2)
    mlp_hup, mlp_hdown, mlp_fc1, mlp_fc2 = lax.psum(
        (mlp_hup, mlp_hdown, mlp_fc1, mlp_fc2), ("ctx", "fsdp")
    )
    grad_branch = grad_resid.astype(jnp.bfloat16)
    grad_up_out = exact_sum("str,std->srd", down_out, grad_branch)
    grad_rank_out = exact_sum("std,srd->str", grad_branch, selected_up[:, 3]).astype(jnp.bfloat16)
    grad_out_down = plain_sum("str,std->srd", grad_rank_out, context_low)
    wqkv_full, wout_full = attn_weights(query_key_value_weight, output_weight)
    grad_context = (
        plain_sum("std,ed->ste", grad_branch, wout_full)
        + plain_sum("str,srd->std", grad_rank_out, out_low)
    ).astype(jnp.bfloat16)
    row_delta = jnp.sum(to_heads(grad_context.astype(jnp.float32) * context), -1)
    delta_heads = jnp.swapaxes(row_delta, 1, 2)
    grad_heads = to_heads(grad_context)
    length = keys_all.shape[1]
    block_rows = min(512, length)
    block_count = length // block_rows

    def key_step(block_index, running):
        grad_query, grad_key, grad_value = running
        keys_blk = row_block(keys_heads, block_index, block_rows)
        values_blk = row_block(values_heads, block_index, block_rows)
        prob_low, grad_scores = block_grads(
            queries_heads, grad_heads, log_total, delta_heads, keys_blk, values_blk
        )
        grad_query = grad_query + plain_sum("shqk,skhd->sqhd", grad_scores, keys_blk)
        grad_key = lax.dynamic_update_slice_in_dim(
            grad_key,
            plain_sum("shqk,sqhd->skhd", grad_scores, queries_heads),
            block_index * block_rows,
            1,
        )
        grad_value = lax.dynamic_update_slice_in_dim(
            grad_value,
            plain_sum("shqk,sqhd->skhd", prob_low, grad_heads),
            block_index * block_rows,
            1,
        )
        return (grad_query, grad_key, grad_value)

    start_query = jnp.zeros(queries_heads.shape, jnp.float32)
    start_keys = jnp.zeros(keys_heads.shape, jnp.float32)
    grad_query, grad_key_all, grad_value_all = lax.fori_loop(
        0, block_count, key_step, (start_query, start_keys, start_keys)
    )
    grad_keys, grad_values = (
        lax.psum_scatter(
            grad_key_all.reshape(seq_count, length, model_width).astype(jnp.bfloat16),
            "ctx",
            scatter_dimension=1,
            tiled=True,
        ).astype(jnp.float32),
        lax.psum_scatter(
            grad_value_all.reshape(seq_count, length, model_width).astype(jnp.bfloat16),
            "ctx",
            scatter_dimension=1,
            tiled=True,
        ).astype(jnp.float32),
    )
    grad_qlin = grad_query.reshape(seq_count, row_count, model_width).astype(jnp.bfloat16) * 0.125
    grad_key_low = grad_keys.astype(jnp.bfloat16)
    grad_value_low = grad_values.astype(jnp.bfloat16)
    stacked = jnp.stack([grad_qlin, grad_key_low, grad_value_low], 1)
    grad_up_att = exact_sum("sjtr,sjtd->sjrd", down_att, stacked)
    grad_rank_att = exact_sum("sjtd,sjrd->sjtr", stacked, selected_up[:, :3]).astype(jnp.bfloat16)
    grad_down_att = plain_sum("sjtr,std->sjrd", grad_rank_att, tokens)
    joined = jnp.concatenate([grad_qlin, grad_key_low, grad_value_low], -1)
    grad_tokens = (
        grad_resid
        + plain_sum("ste,de->std", joined, wqkv_full)
        + plain_sum("sjtr,sjrd->std", grad_rank_att, down_low[:, :3])
    )
    attn_down = to_adapters(grad_down_att)
    attn_out = to_adapters(grad_out_down)
    attn_up = to_adapters(jnp.concatenate([grad_up_att, grad_up_out[:, None]], 1))
    attn_down, attn_out, attn_up = lax.psum((attn_down, attn_out, attn_up), ("ctx", "fsdp"))
    total_down = jnp.concatenate([attn_down, mlp_fc1[:, None]], 1)
    total_up = jnp.concatenate([attn_up, mlp_fc2[:, None]], 1)
    return (
        outcome.astype(jnp.bfloat16),
        grad_tokens,
        total_down,
        attn_out,
        total_up,
        mlp_hup,
        mlp_hdown,
    )


BF16 = jnp.bfloat16
F32 = jnp.float32
LOG2E = 1.4426950408889634
VMEM_LIMIT = 60 * 2**20
MESH = pl.DeviceIdType.MESH


def dot32(left, right):
    return jnp.dot(left, right, preferred_element_type=F32)


def dot_nt(left, right):
    return lax.dot_general(left, right, (((1,), (1,)), ((), ())), preferred_element_type=F32)


def dot_tn(left, right):
    return lax.dot_general(left, right, (((0,), (0,)), ((), ())), preferred_element_type=F32)


def split_three(value):
    high = value.astype(BF16)
    rest = value - high.astype(F32)
    middle = rest.astype(BF16)
    return high, middle, (rest - middle.astype(F32)).astype(BF16)


def flip(value):
    return value.astype(F32).T.astype(BF16)


def remote(src, dst, send_sem, recv_sem, device):
    return pltpu.make_async_remote_copy(
        src_ref=src,
        dst_ref=dst,
        send_sem=send_sem,
        recv_sem=recv_sem,
        device_id=device,
        device_id_type=MESH,
    )


class Place:
    def __init__(self):
        self.ctx = lax.axis_index("ctx")
        self.core = lax.axis_index("fsdp")
        self.half = self.ctx // (H // 2)
        self.low = self.ctx % (H // 2)
        self.me = self.low * 2 + self.core
        self.swaps = self.core != self.half
        self.pair = (self.core + self.half) % 2
        self.sibling = (self.ctx, 1 - self.core)
        self.partner = ((self.ctx + H // 2) % H, 1 - self.core)

    def peer(self, step):
        number = self.me ^ step
        return (self.half * (H // 2) + number // 2, number % 2)

    def order(self, turn):
        return 2 * (turn % (H // 2)) + (turn // (H // 2) + self.pair) % 2

    def greet(self):
        barrier = pltpu.get_barrier_semaphore()
        for step in range(1, H):
            pl.semaphore_signal(barrier, inc=1, device_id=self.peer(step), device_id_type=MESH)
        pl.semaphore_signal(barrier, inc=1, device_id=self.partner, device_id_type=MESH)
        pl.semaphore_wait(barrier, H)


def sum_copies(mine, parts, total, sems, place):
    own = total.at[place.pair, place.low, place.half]
    other = total.at[place.pair, place.low, 1 - place.half]
    column = total.at[place.pair]
    scatter = [
        remote(mine.at[place.me ^ step], parts.at[step], sems.at[0, step], sems.at[1, step], place.peer(step))
        for step in range(1, H)
    ]
    cross = remote(own, own, sems.at[0, 0], sems.at[1, 0], place.partner)
    first = [
        remote(own, own, sems.at[2, step], sems.at[3, step], place.peer(step))
        for step in range(2, H, 2)
    ]
    second = [
        remote(other, other, sems.at[2, step + 1], sems.at[3, step + 1], place.peer(step))
        for step in range(2, H, 2)
    ]
    last = remote(column, column, sems.at[2, 0], sems.at[3, 0], place.sibling)
    return scatter, cross, first, second, last


def sum_parts(scatter, mine, parts, total, place):
    value = mine[place.me].astype(F32)
    for step, copy in enumerate(scatter, 1):
        copy.wait_recv()
        value = value + parts[step].astype(F32)
    total[place.pair, place.low, place.half] = value.astype(BF16)


def put_term(mine, base, term):
    units = mine.shape[2] // 128
    for unit in range(term.shape[1] // 128):
        at = base // 128 + unit
        lanes = slice(at % units * 128, at % units * 128 + 128)
        mine[at // units, :, lanes] = term[:, unit * 128 : unit * 128 + 128].astype(BF16)


def layer_kernel(
    block_q,
    block_k,
    index_ref,
    tokens_ref,
    cotangent_ref,
    wqkv_ref,
    wout_ref,
    wfc1_ref,
    wfc2_ref,
    down_table,
    up_table,
    out_down_table,
    hidden_up_table,
    hidden_down_table,
    biases_ref,
    value_bias_ref,
    hidden_bias_ref,
    gains_ref,
    outcome_ref,
    grad_ref,
    chosen_out,
    hidden_down_out,
    hidden_up_out,
    down_out,
    up_out,
    out_down_out,
    wqkv_far,
    wfc1_far,
    wide,
    wfc2,
    wout,
    big,
    act,
    small,
    small_hidden,
    x,
    cotangent,
    rank_att,
    outgoing,
    qkv,
    leaving,
    arrived,
    incoming,
    context,
    state,
    qta,
    gta,
    kk,
    vv,
    kt,
    both,
    dkv_sum,
    dq_in,
    dkv_out,
    dkv_in,
    grad_out,
    grad_in,
    mlp_mine,
    mlp_parts,
    mlp_total,
    att_mine,
    att_parts,
    att_total,
    load_sem,
    core_sem,
    swap_sem,
    kv_sem,
    q_sem,
    back_sem,
    grad_sem,
    dq_sem,
    dkv_sem,
    mlp_sem,
    att_sem,
):
    peers, _, rows = qkv.shape
    length = peers * rows
    width = x.shape[1]
    hidden = hidden_bias_ref.shape[1]
    adapters = hidden_up_table.shape[0] // 16
    place = Place()
    me, core = place.me, place.core
    other = 1 - core
    wqkv = wide.at[:, 0 : 3 * width]
    up_at = down_table.shape[0]
    out_down_at = up_at + up_table.shape[0]

    def half_of(full, owner):
        count = full.shape[0] // 2
        return full.at[pl.ds(pl.multiple_of(owner * count, count), count), :]

    def load(source, target, number):
        return pltpu.make_async_copy(source, target, load_sem.at[number])

    def to_sibling(source, target, number):
        return remote(source, target, core_sem.at[0, number], core_sem.at[1, number], place.sibling)

    load_wqkv = load(wqkv_ref, half_of(wqkv, core), 0)
    load_wout = load(wout_ref, half_of(wout, core), 1)
    load_tables = [
        load(down_table, wfc2.at[0:up_at], 2),
        load(up_table, wfc2.at[up_at:out_down_at], 3),
        load(out_down_table, wfc2.at[out_down_at : out_down_at + out_down_table.shape[0]], 4),
        load(hidden_up_table, act.at[0 : 16 * adapters], 5),
        load(hidden_down_table, act.at[16 * adapters : 32 * adapters], 6),
    ]
    load_x = load(tokens_ref, x, 7)
    load_cotangent = load(cotangent_ref, cotangent, 8)
    load_wfc1 = load(wfc1_ref, half_of(wide, core), 9)
    load_wfc1_far = load(wfc1_far, half_of(wide, other), 10)
    load_wfc2 = load(wfc2_ref, half_of(wfc2, core), 11)
    again_wqkv = load(wqkv_ref, half_of(wqkv, core), 12)
    again_wqkv_far = load(wqkv_far, half_of(wqkv, other), 13)
    give_wqkv = to_sibling(wqkv_ref, half_of(wqkv, core), 0)
    give_wout = to_sibling(wout_ref, half_of(wout, core), 1)
    give_chosen = to_sibling(chosen_out.at[core], chosen_out.at[core], 2)
    count = small.shape[0]
    give_small = [to_sibling(small, wide.at[0:count, 3 * width : 4 * width], 3)] + [
        to_sibling(
            small_hidden.at[:, part * width : (part + 1) * width],
            wide.at[count + 32 * part : count + 32 * part + 32, 3 * width : 4 * width],
            4 + part,
        )
        for part in range(hidden // width)
    ]
    give_wfc2 = to_sibling(wfc2_ref, half_of(wfc2, core), 8)
    give_wfc1 = to_sibling(wfc1_ref, wfc1_far, 9)
    give_wqkv_again = to_sibling(wqkv_ref, wqkv_far, 10)
    half_rows = rows // 2
    swap_x = [
        remote(
            tokens_ref.at[part * half_rows : (part + 1) * half_rows],
            x.at[part * half_rows : (part + 1) * half_rows],
            swap_sem.at[0, 7 + part],
            swap_sem.at[1, 7 + part],
            place.partner,
        )
        for part in range(2)
    ]
    swap_cotangent = remote(cotangent_ref, cotangent, swap_sem.at[0, 1], swap_sem.at[1, 1], place.partner)

    load_wqkv.start()
    for copy in load_tables:
        copy.start()
    load_wout.start()

    @pl.when(jnp.logical_not(place.swaps))
    def _():
        load_x.start()
        load_cotangent.start()

    adapter = index_ref[0]
    numbers = lax.broadcasted_iota(jnp.int32, chosen_out.shape[1:], 0)
    chosen_out[core] = (numbers == jnp.full(numbers.shape, adapter, jnp.int32)).astype(F32)
    place.greet()

    @pl.when(place.swaps)
    def _():
        for copy in swap_x:
            copy.start()

    give_wqkv.start()
    give_chosen.start()

    for copy in load_tables:
        copy.wait()

    def select(table, base, group, groups, target, at):
        chosen = jnp.full((16, table.shape[1]), adapter, jnp.int32)
        value = jnp.zeros((16, table.shape[1]), F32)
        for number in range(adapters):
            start = pl.multiple_of(base + 16 * (number * groups + group), 16)
            value = jnp.where(chosen == number, table[pl.ds(start, 16), :].astype(F32), value)
        target[pl.ds(pl.multiple_of(at + 16 * group, 16), 16), :] = value.astype(BF16)

    def select_down(group, _):
        select(wfc2, 0, group, 4, small, 0)
        return 0

    def select_up(group, _):
        select(wfc2, up_at, group, 5, small, 64)
        return 0

    lax.fori_loop(0, 4, select_down, 0)
    lax.fori_loop(0, 5, select_up, 0)
    select(wfc2, out_down_at, 0, 1, small, 144)
    for part in range(2):
        select(act, 16 * adapters * part, 0, 1, small_hidden, 16 * part)
    for copy in give_small:
        copy.start()
    give_wout.start()
    for copy in give_small:
        copy.wait()

    @pl.when(place.swaps)
    def _():
        small[...] = wide[0:count, 3 * width : 4 * width]
        for part in range(hidden // width):
            small_hidden[:, part * width : (part + 1) * width] = wide[
                count + 32 * part : count + 32 * part + 32, 3 * width : 4 * width
            ]

    hidden_up_ref = small_hidden.at[0:16]
    hidden_down_ref = small_hidden.at[16:32]
    out_down_ref = small.at[144:160]

    def down(j):
        return small[16 * j : 16 * j + 16]

    def up(j):
        return small[64 + 16 * j : 80 + 16 * j]

    load_wfc2.start()
    give_wfc2.start()

    load_wqkv.wait()
    give_wqkv.wait_recv()

    def project(half, part):
        here = slice(half * half_rows, (half + 1) * half_rows)
        cols = slice(part * width, (part + 1) * width)
        value = dot32(x[here, :], wqkv[:, cols]) + dot32(rank_att[here, part * 16 : part * 16 + 16], up(part))
        if part == 0:
            value = (value + biases_ref[0:1, :]) * 0.125
        if part == 2:
            value = value + value_bias_ref[...]
        for two in range(peers // 2):
            turned = value[:, two * 128 : two * 128 + 128].T.astype(BF16)
            outgoing[2 * two, part * 64 : part * 64 + 64, here] = turned[0:64]
            outgoing[2 * two + 1, part * 64 : part * 64 + 64, here] = turned[64:128]

    def kv_copy(step, half):
        here = slice(half * half_rows, (half + 1) * half_rows)
        return remote(
            outgoing.at[me ^ step, 64:192, here],
            qkv.at[step, 64:192, here],
            kv_sem.at[0, half, step],
            kv_sem.at[1, half, step],
            place.peer(step),
        )

    def q_copy(step):
        return remote(
            outgoing.at[me ^ step, 0:64], qkv.at[step, 0:64], q_sem.at[0, step], q_sem.at[1, step], place.peer(step)
        )

    def back_copy(step):
        return remote(leaving.at[step], arrived.at[me], back_sem.at[0, step], back_sem.at[1, step], place.peer(step))

    steps = length // block_k
    group = block_q // rows
    key_group = block_k // rows
    for half in range(2):
        here = slice(half * half_rows, (half + 1) * half_rows)

        @pl.when(place.swaps)
        def _():
            swap_x[half].wait_recv()

        if half == 0:

            @pl.when(jnp.logical_not(place.swaps))
            def _():
                load_x.wait()

        rank_att[here, :] = dot_nt(x[here, :], small[0:48]).astype(BF16)
        project(half, 1)
        project(half, 2)
        for step in range(1, peers):
            kv_copy(step, half).start()
        project(half, 0)
    for step in range(1, peers):
        q_copy(step).start()
    give_wfc1.start()
    give_wqkv_again.start()
    load_wfc1.start()
    qkv[0] = outgoing[me]

    row_at = lax.broadcasted_iota(jnp.int32, (16, rows), 0)
    ones = (row_at == 0).astype(F32).astype(BF16)
    minus = jnp.where(lax.broadcasted_iota(jnp.int32, (rows, 16), 1) < 3, -1.0, 0.0).astype(BF16)
    minus_rows = jnp.where(lax.broadcasted_iota(jnp.int32, (64, rows), 0) < 3, -1.0, 0.0).astype(BF16)

    def tail(value):
        at = lax.broadcasted_iota(jnp.int32, (16, value.shape[1]), 0)
        high, middle, low = (part.astype(F32) for part in split_three(value))
        return jnp.where(at == 0, high, jnp.where(at == 1, middle, jnp.where(at == 2, low, 0.0))).astype(BF16)

    def take_key(turn):
        cols = pl.ds(pl.multiple_of(turn * rows, rows), rows)
        step = place.order(turn)

        @pl.when(step > 0)
        def _():
            kv_copy(step, 0).wait_recv()
            kv_copy(step, 1).wait_recv()

        key = qkv[step, 64:128, :]
        value = qkv[step, 128:192, :]
        kt[:, cols] = key
        kk[cols, 0:128] = flip(jnp.concatenate([key, key], 0))
        kk[cols, 128:144] = minus
        vv[cols, :] = flip(jnp.concatenate([value, minus_rows], 0))
        gta[0:64, cols] = value
        gta[64:80, cols] = ones
        gta[80:128, cols] = jnp.zeros((48, rows), BF16)

    def take_keys(i):
        def one(part, _):
            take_key(i * key_group + part)
            return 0

        lax.fori_loop(0, key_group, one, 0)

    def forward_part(i, low, high, arriving):
        def take_query(part, _):
            turn = i * group + part
            step = place.order(turn)
            here = pl.ds(pl.multiple_of(turn * rows, rows), rows)

            @pl.when(step > 0)
            def _():
                q_copy(step).wait_recv()

            query = qkv[step, 0:64, :].astype(F32) * LOG2E
            high = query.astype(BF16)
            qta[0:64, here] = high
            qta[64:128, here] = (query - high.astype(F32)).astype(BF16)
            return 0

        if low == 0:
            lax.fori_loop(0, group, take_query, 0)
        cols = pl.ds(pl.multiple_of(i * block_q, block_q), block_q)
        query = qta.at[0:128, cols]
        if arriving:
            take_keys(low)
        block = dot32(kk[low * block_k : (low + 1) * block_k, 0:128], query[...])
        big[0:block_k] = block

        def half(j, now, carry):
            peak, running, total = carry
            later = jnp.minimum(j + 1, high - 1)
            here = pl.ds(pl.multiple_of(j * block_k, block_k), block_k)
            there = pl.ds(pl.multiple_of(later * block_k, block_k), block_k)
            if arriving:

                @pl.when(j + 1 < high)
                def _():
                    take_keys(later)

            ahead = dot32(kk[there, 0:128], query[...])
            big[(1 - now) * block_k : (2 - now) * block_k] = ahead
            new = jnp.maximum(running, peak)
            weights = jnp.exp2(big[now * block_k : (now + 1) * block_k] - new).astype(BF16)
            total = total * jnp.exp2(running - new) + dot32(gta[0:80, here], weights)
            return jnp.max(ahead, 0, keepdims=True), new, total

        def pair(j, carry):
            return half(low + 2 * j + 1, 1, half(low + 2 * j, 0, carry))

        if low == 0:
            running, total = jnp.full((1, block_q), -jnp.inf, F32), jnp.zeros((80, block_q), F32)
        else:
            running = state[1:2, cols]
            total = jnp.concatenate([context[:, cols], state[0:1, cols], jnp.zeros((15, block_q), F32)], 0)
        _, top, total = lax.fori_loop(
            0, (high - low) // 2, pair, (jnp.max(block, 0, keepdims=True), running, total)
        )
        weight_sum = total[64:65]
        if high < steps:
            context[:, cols] = total[0:64]
            state[0:1, cols] = weight_sum
            state[1:2, cols] = top
            return
        result = total[0:64] / weight_sum
        context[:, cols] = result
        qta[128:144, cols] = tail(top + jnp.log2(weight_sum))
        low_result = result.astype(BF16)
        for part in range(group):
            step = place.order(i * group + part)
            leaving[step] = low_result[:, part * rows : (part + 1) * rows]

            @pl.when(step > 0)
            def _():
                back_copy(step).start()

    query_steps = length // block_q
    for i in range(query_steps // 2):
        forward_part(i, 0, steps // 2, i == 0)
    give_wfc1.wait_recv()
    load_wfc1_far.start()
    for i in range(query_steps // 2):
        forward_part(i, steps // 2, steps, i == 0)

    @pl.when(place.swaps)
    def _():
        swap_cotangent.start()

    def forward_whole(i, _):
        forward_part(i, 0, steps, False)
        return 0

    lax.fori_loop(query_steps // 2, query_steps, forward_whole, 0)
    arrived[me] = leaving[0]

    def mean(value):
        return jnp.mean(value, -1, keepdims=True)

    def norm_backward(grad, hat, scale):
        return scale * (grad - mean(grad) - hat * mean(grad * hat))

    load_wout.wait()
    give_wout.wait_recv()
    for step in range(1, peers):
        back_copy(step).wait_recv()
    context_low = flip(arrived[...].reshape(width, rows))
    rank_out = dot_nt(context_low, out_down_ref[...]).astype(BF16)
    resid = x[...].astype(F32) + dot32(context_low, wout[...]) + biases_ref[1:2] + dot32(rank_out, up(3))
    center = resid - mean(resid)
    scale_one = lax.rsqrt(mean(center * center) + EPSILON)
    hat_one = center * scale_one
    normed = hat_one * gains_ref[0:1] + biases_ref[3:4]
    normed_low = normed.astype(BF16)
    rank_one = dot_nt(normed_low, down(3)).astype(BF16)
    load_wfc1.wait()
    load_wfc1_far.wait()
    load_wfc2.wait()
    give_wfc2.wait_recv()
    piece = 1024
    rank_two = jnp.zeros((rows, 16), F32)
    mixed = normed + biases_ref[2:3]
    for part in range(hidden // piece):
        cols = slice(part * piece, (part + 1) * piece)
        pre = (
            dot32(normed_low, wide[:, cols])
            + hidden_bias_ref[:, cols]
            + dot32(rank_one, hidden_up_ref[:, cols])
        )
        share = 0.5 + 0.5 * lax.erf(pre * 0.7071067811865476)
        big[part * rows : (part + 1) * rows] = share + pre * (0.3989422804014327 * jnp.exp(-0.5 * pre * pre))
        active = (pre * share).astype(BF16)
        act[:, cols] = active
        rank_two = rank_two + dot_nt(active, hidden_down_ref[:, cols])
        mixed = mixed + dot32(active, wfc2[cols, :])
    rank_two = rank_two.astype(BF16)
    mixed = mixed + dot32(rank_two, up(4))
    center = mixed - mean(mixed)
    scale_two = lax.rsqrt(mean(center * center) + EPSILON)
    hat_two = center * scale_two

    @pl.when(place.swaps)
    def _():
        swap_cotangent.wait_recv()

    @pl.when(jnp.logical_not(place.swaps))
    def _():
        load_cotangent.wait()

    grad_sum = norm_backward(cotangent[...].astype(F32) * gains_ref[1:2], hat_two, scale_two)
    outcome = cotangent
    outcome[...] = (hat_two * gains_ref[1:2] + biases_ref[4:5]).astype(BF16)
    home_outcome = remote(outcome, outcome_ref, swap_sem.at[0, 2], swap_sem.at[1, 2], place.partner)

    @pl.when(place.swaps)
    def _():
        home_outcome.start()

    @pl.when(jnp.logical_not(place.swaps))
    def _():
        outcome_ref[...] = outcome[...]

    grad_mixed = grad_sum.astype(BF16)
    put_term(mlp_mine, 2 * hidden, dot_tn(rank_two, grad_mixed))
    grad_rank = dot_nt(grad_mixed, up(4)).astype(BF16)
    put_term(mlp_mine, 0, dot_tn(grad_rank, act[...]))
    grad_one = jnp.zeros((rows, 16), F32)
    grad_normed = jnp.zeros((rows, width), F32)
    for part in range(hidden // piece):
        cols = slice(part * piece, (part + 1) * piece)
        grad_act = dot_nt(grad_mixed, wfc2[cols, :]) + dot32(grad_rank, hidden_down_ref[:, cols])
        grad_hidden = (grad_act.astype(BF16).astype(F32) * big[part * rows : (part + 1) * rows]).astype(BF16)
        put_term(mlp_mine, hidden + part * piece, dot_tn(rank_one, grad_hidden))
        grad_one = grad_one + dot_nt(grad_hidden, hidden_up_ref[:, cols])
        grad_normed = grad_normed + dot_nt(grad_hidden, wide[:, cols])
    grad_one = grad_one.astype(BF16)
    put_term(mlp_mine, 2 * hidden + width, dot_tn(grad_one, normed_low))
    grad_normed = (grad_normed + dot32(grad_one, down(3))).astype(BF16).astype(F32)
    resid_grad = norm_backward((grad_sum + grad_normed) * gains_ref[0:1], hat_one, scale_one)
    grad_resid = big.at[0:rows]
    grad_resid[...] = resid_grad
    grad_branch = resid_grad.astype(BF16)
    put_term(mlp_mine, 2 * hidden + 2 * width, dot_tn(rank_out, grad_branch))
    grad_rank = dot_nt(grad_branch, up(3)).astype(BF16)
    put_term(mlp_mine, 2 * hidden + 3 * width, dot_tn(grad_rank, context_low))
    turned = dot_nt(wout[...], grad_branch) + lax.dot_general(
        out_down_ref[...], grad_rank, (((0,), (1,)), ((), ())), preferred_element_type=F32
    )
    for step in range(1, peers):
        kv_copy(step, 0).wait_send()
        kv_copy(step, 1).wait_send()
        q_copy(step).wait_send()
        back_copy(step).wait_send()
    outgoing[:, 0:64] = turned.astype(BF16).reshape(peers, 64, rows)

    def grad_copy(step):
        return remote(
            outgoing.at[me ^ step, 0:64], incoming.at[step], grad_sem.at[0, step], grad_sem.at[1, step], place.peer(step)
        )

    for step in range(1, peers):
        grad_copy(step).start()
    mlp_scatter, mlp_cross, mlp_first, mlp_second, mlp_last = sum_copies(mlp_mine, mlp_parts, mlp_total, mlp_sem, place)
    incoming[0] = outgoing[me, 0:64]
    give_wqkv_again.wait_recv()
    again_wqkv.start()
    again_wqkv_far.start()
    dkv_sum[...] = jnp.zeros_like(dkv_sum)
    first = lax.broadcasted_iota(jnp.int32, (block_k, 128), 1) < 64
    dq_out = leaving

    def dq_copy(step):
        return remote(dq_out.at[step], dq_in.at[me], dq_sem.at[0, step], dq_sem.at[1, step], place.peer(step))

    def dkv_copy(step):
        return remote(dkv_out.at[step], dkv_in.at[me], dkv_sem.at[0, step], dkv_sem.at[1, step], place.peer(step))

    def backward_step(turn, last):
        j = (turn + query_steps // 2) % query_steps

        def take_grad(part, _):
            step = place.order(j * group + part)
            cols = pl.ds(pl.multiple_of((j * group + part) * rows, rows), rows)

            @pl.when(step > 0)
            def _():
                grad_copy(step).wait_recv()

            grad = incoming[step]
            gta[0:64, cols] = grad
            gta[64:80, cols] = tail(jnp.sum(grad.astype(F32) * context[:, cols], 0, keepdims=True))
            both[cols, :] = flip(jnp.concatenate([qkv[step, 0:64, :], grad], 0))
            return 0

        lax.fori_loop(0, group, take_grad, 0)
        cols = pl.ds(pl.multiple_of(j * block_q, block_q), block_q)

        def key_pair(pair, dq):
            found = []
            for side in range(2):
                i = (2 * pair + side + steps // 2) % steps
                here = pl.ds(pl.multiple_of(i * block_k, block_k), block_k)
                probs = jnp.exp2(dot32(kk[here, :], qta[:, cols]))
                change = dot32(vv[here, :], gta[:, cols])
                found.append((i, here, probs.astype(BF16), (probs * change).astype(BF16)))
            for i, here, probs, low in found:
                dv = dot32(probs, both[cols, :])
                dk = dot32(low, both[cols, :])
                dkv = dkv_sum[here, :] + jnp.where(first, dk, dv)
                if not last:
                    dkv_sum[here, :] = dkv
                else:
                    done = dkv.astype(BF16)
                    for part in range(key_group):
                        step = place.order(i * key_group + part)
                        dkv_out[step] = done[part * rows : (part + 1) * rows]

                        @pl.when(step > 0)
                        def _():
                            dkv_copy(step).start()

                dq = dq + dot32(kt[:, here], low)
            return dq

        dq = lax.fori_loop(0, steps // 2, key_pair, jnp.zeros((64, block_q), F32)).astype(BF16)
        for part in range(group):
            step = place.order(j * group + part)
            dq_out[step] = dq[:, part * rows : (part + 1) * rows]

            @pl.when(step > 0)
            def _():
                dq_copy(step).start()

    def backward_steps(low, high):
        def one(j, _):
            backward_step(j, False)
            return 0

        lax.fori_loop(low, high, one, 0)

    backward_steps(0, query_steps // 4)
    for copy in mlp_scatter:
        copy.start()
    backward_steps(query_steps // 4, query_steps // 2)
    sum_parts(mlp_scatter, mlp_mine, mlp_parts, mlp_total, place)
    mlp_cross.start()
    for copy in mlp_first:
        copy.start()
    backward_steps(query_steps // 2, query_steps - 1)
    mlp_cross.wait_recv()
    for copy in mlp_second:
        copy.start()
    backward_step(query_steps - 1, True)
    for copy in mlp_first + mlp_second:
        copy.wait_recv()
    mlp_last.start()

    def spread(total, parts):
        units = total.shape[4] // 128
        for half in range(2):
            for unit in range(peers * units):
                peer = unit // units
                lanes = slice(unit % units * 128, unit % units * 128 + 128)
                for target, low, high in parts:
                    if low <= unit * 128 < high:
                        at = unit * 128 - low
                        target(half)[:, at : at + 128] = total[(peer % 2 + half) % 2, peer // 2, half, :, lanes]

    joined = act.at[:, 0 : 3 * width]
    dq_in[me] = dq_out[0]
    dkv_in[me] = dkv_out[0]
    for step in range(1, peers):
        dkv_copy(step).wait_recv()
    left = lax.broadcasted_iota(jnp.int32, (rows, 128), 1) < 64
    for two in range(peers // 2):
        even = dkv_in[2 * two].astype(F32)
        odd = dkv_in[2 * two + 1].astype(F32)
        cols = slice(width + two * 128, width + two * 128 + 128)
        joined[:, cols] = jnp.where(left, even, pltpu.roll(odd, 64, 1)).astype(BF16)
        cols = slice(2 * width + two * 128, 2 * width + two * 128 + 128)
        joined[:, cols] = jnp.where(left, pltpu.roll(even, 64, 1), odd).astype(BF16)
    def ranks_of(part):
        grad = joined[:, part * width : (part + 1) * width]
        ranks[part] = dot_nt(grad, up(part)).astype(BF16)

    def terms_of(part):
        grad = joined[:, part * width : (part + 1) * width]
        put_term(att_mine, part * width, dot_tn(rank_att[:, part * 16 : part * 16 + 16], grad))
        put_term(att_mine, (3 + part) * width, dot_tn(ranks[part], x[...]))

    ranks = {}
    att_scatter, att_cross, att_first, att_second, att_last = sum_copies(att_mine, att_parts, att_total, att_sem, place)
    again_wqkv.wait()
    again_wqkv_far.wait()
    for part in (1, 2):
        ranks_of(part)
        terms_of(part)
    for step in range(1, peers):
        dq_copy(step).wait_recv()
    joined[:, 0:width] = (dq_in[...].reshape(width, rows).astype(F32).T * 0.125).astype(BF16)
    ranks_of(0)
    terms_of(0)
    for copy in att_scatter:
        copy.start()
    piece = width // 4
    home = [
        remote(
            grad_out.at[:, part * piece : (part + 1) * piece],
            grad_in.at[:, part * piece : (part + 1) * piece],
            swap_sem.at[0, 3 + part],
            swap_sem.at[1, 3 + part],
            place.partner,
        )
        for part in range(4)
    ]
    mlp_last.wait_recv()
    for part in range(4):
        cols = slice(part * piece, (part + 1) * piece)
        total = grad_resid[:, cols] + dot_nt(joined[...], wqkv[cols, :])
        for j in range(3):
            total = total + dot32(ranks[j], small[16 * j : 16 * j + 16, cols])
        grad_ref[:, cols] = total
        grad_out[:, cols] = total.astype(BF16)

        @pl.when(place.swaps)
        def _():
            home[part].start()

    sum_parts(att_scatter, att_mine, att_parts, att_total, place)
    att_cross.start()
    for copy in att_first:
        copy.start()
    spread(
        mlp_total,
        (
            (lambda half: hidden_down_out.at[half], 0, hidden),
            (lambda half: hidden_up_out.at[half], hidden, 2 * hidden),
            (lambda half: up_out.at[half, 4], 2 * hidden, 2 * hidden + width),
            (lambda half: down_out.at[half, 3], 2 * hidden + width, 2 * hidden + 2 * width),
            (lambda half: up_out.at[half, 3], 2 * hidden + 2 * width, 2 * hidden + 3 * width),
            (lambda half: out_down_out.at[half], 2 * hidden + 3 * width, 2 * hidden + 4 * width),
        ),
    )
    att_cross.wait_recv()
    for copy in att_second:
        copy.start()
    for copy in att_first + att_second:
        copy.wait_recv()
    att_last.start()

    @pl.when(place.swaps)
    def _():
        for part in range(4):
            home[part].wait_recv()
            cols = slice(part * piece, (part + 1) * piece)
            grad_ref[:, cols] = grad_in[:, cols].astype(F32)
        for part in range(4):
            home[part].wait_send()
        home_outcome.wait()
        for copy in swap_x:
            copy.wait_send()
        swap_cotangent.wait_send()

    att_last.wait_recv()
    spread(
        att_total,
        tuple(
            (functools.partial(lambda part, half: up_out.at[half, part], part), part * width, (part + 1) * width)
            for part in range(3)
        )
        + tuple(
            (functools.partial(lambda part, half: down_out.at[half, part], part), (3 + part) * width, (4 + part) * width)
            for part in range(3)
        ),
    )
    for step in range(1, peers):
        grad_copy(step).wait_send()
        dq_copy(step).wait_send()
        dkv_copy(step).wait_send()
    for copies in ((mlp_scatter, mlp_first, mlp_second), (att_scatter, att_first, att_second)):
        for copy in copies[0] + copies[1] + copies[2]:
            copy.wait_send()
    for copy in (mlp_cross, mlp_last, att_cross, att_last):
        copy.wait_send()
    for copy in (give_wqkv, give_wout, give_wfc2, give_wfc1, give_wqkv_again):
        copy.wait_send()
    give_chosen.wait()


def run_layer(index, tokens, cotangent, weights, tables, biases, value_bias, hidden_bias, gains):
    rows, width = tokens.shape
    peers = H
    length = peers * rows
    hidden = hidden_bias.shape[1]
    block_q, block_k = 1024, 512
    vmem = pl.BlockSpec(memory_space=pltpu.VMEM)
    hbm = pl.BlockSpec(memory_space=pl.ANY)
    mlp_part = (2 * hidden + 4 * width) // peers
    att_part = 6 * width // peers

    def out(shape, dtype=BF16):
        return jax.ShapeDtypeStruct(shape, dtype)

    def total(part):
        return pltpu.VMEM((2, peers // 2, 2, 16, part), BF16)

    def heads(*shape):
        return pltpu.VMEM((peers,) + shape, BF16)

    def sems(*shape):
        return pltpu.SemaphoreType.DMA(shape)

    return pl.pallas_call(
        functools.partial(layer_kernel, block_q, block_k),
        out_shape=[
            out((rows, width)),
            out((rows, width), F32),
            out((2, 8, 128), F32),
            out((2, 16, hidden)),
            out((2, 16, hidden)),
            out((2, 4, 16, width)),
            out((2, 5, 16, width)),
            out((2, 16, width)),
            out(weights[0].shape),
            out(weights[2].shape),
        ],
        in_specs=[pl.BlockSpec(memory_space=pltpu.SMEM)] + [hbm] * 11 + [vmem] * 4,
        out_specs=[vmem] * 8 + [hbm] * 2,
        scratch_shapes=[
            pltpu.VMEM((width, hidden), BF16),
            pltpu.VMEM((hidden, width), BF16),
            pltpu.VMEM((width, width), BF16),
            pltpu.VMEM((max(4 * rows, 2 * block_k), 1024), F32),
            pltpu.VMEM((rows, hidden), BF16),
            pltpu.VMEM((160, width), BF16),
            pltpu.VMEM((32, hidden), BF16),
            pltpu.VMEM((rows, width), BF16),
            pltpu.VMEM((rows, width), BF16),
            pltpu.VMEM((rows, 48), BF16),
            heads(192, rows),
            heads(192, rows),
            heads(64, rows),
            heads(64, rows),
            heads(64, rows),
            pltpu.VMEM((64, length), F32),
            pltpu.VMEM((8, length), F32),
            pltpu.VMEM((144, length), BF16),
            pltpu.VMEM((128, length), BF16),
            pltpu.VMEM((length, 144), BF16),
            pltpu.VMEM((length, 128), BF16),
            pltpu.VMEM((64, length), BF16),
            pltpu.VMEM((length, 128), BF16),
            pltpu.VMEM((length, 128), F32),
            heads(64, rows),
            heads(rows, 128),
            heads(rows, 128),
            pltpu.VMEM((rows, width), BF16),
            pltpu.VMEM((rows, width), BF16),
            heads(16, mlp_part),
            heads(16, mlp_part),
            total(mlp_part),
            heads(16, att_part),
            heads(16, att_part),
            total(att_part),
            sems(14),
            sems(2, 11),
            sems(2, 9),
            sems(2, 2, peers),
            sems(2, peers),
            sems(2, peers),
            sems(2, peers),
            sems(2, peers),
            sems(2, peers),
            sems(4, peers),
            sems(4, peers),
        ],
        compiler_params=pltpu.CompilerParams(
            collective_id=0, has_side_effects=True, vmem_limit_bytes=VMEM_LIMIT
        ),
        name="run_layer",
    )(index, tokens, cotangent, *weights, *tables, biases, value_bias, hidden_bias, gains)


def heads_body(
    tokens,
    cotangent,
    sequence_adapter_index,
    query_key_value_weight,
    output_weight,
    first_feed_weight,
    second_feed_weight,
    biases,
    value_bias_vector,
    first_feed_bias,
    norm_gain_pair,
    adapter_down_factors,
    output_down_factor,
    adapter_up_factors,
    hidden_up_factor,
    hidden_down_factor,
):
    width = tokens.shape[2]
    hidden = first_feed_bias.shape[0]
    adapter_number = adapter_down_factors.shape[0]
    outcome, grad_tokens, chosen, term_hd, term_uh, term_down, term_up, term_do, *_ = run_layer(
        sequence_adapter_index,
        tokens[0],
        cotangent[0],
        (query_key_value_weight, output_weight, first_feed_weight, second_feed_weight),
        (
            adapter_down_factors.reshape(-1, width),
            adapter_up_factors.reshape(-1, width),
            output_down_factor.reshape(-1, width),
            hidden_up_factor.reshape(-1, hidden),
            hidden_down_factor.reshape(-1, hidden),
        ),
        biases,
        value_bias_vector[None],
        first_feed_bias[None],
        norm_gain_pair,
    )
    tables = []
    for every in (term_down, term_do, term_up, term_uh, term_hd):
        table = 0.0
        for seq in range(2):
            mask = chosen[seq, :, 0].reshape((adapter_number,) + (1,) * (every.ndim - 1)) > 0.0
            table = table + jnp.where(mask, every[seq][None].astype(F32), 0.0)
        tables.append(table)
    return (outcome[None], grad_tokens[None], *tables)


def solution(mesh):
    one_head_each = mesh.shape["ctx"] == H and mesh.shape["fsdp"] == 2
    return jax.shard_map(
        heads_body if one_head_each else gather_body,
        mesh=mesh,
        in_specs=(
            P("fsdp", "ctx", None),
            P("fsdp", "ctx", None),
            P("fsdp"),
            P("fsdp", None),
            P("fsdp", None),
            P("fsdp", None),
            P("fsdp", None),
            P(),
            P(),
            P(),
            P(),
            P(),
            P(),
            P(),
            P(),
            P(),
        ),
        out_specs=(P("fsdp", "ctx", None), P("fsdp", "ctx", None), P(), P(), P(), P(), P()),
        check_vma=False,
    )
```

```python
import functools

import jax
import jax.numpy as jnp
from jax import lax
from jax.experimental import pallas as pl
from jax.experimental.pallas import tpu as pltpu
from jax.sharding import PartitionSpec as P

H = 16


EPSILON = 1e-05
HIGHEST = lax.Precision.HIGHEST


def exact_sum(form, left, right):
    return jnp.einsum(form, left, right, precision=HIGHEST, preferred_element_type=jnp.float32)


def plain_sum(form, left, right):
    return jnp.einsum(form, left, right, preferred_element_type=jnp.float32)


def layer_norm(value, gain, shift):
    center = value - jnp.mean(value, -1, keepdims=True)
    spread = jnp.mean(center * center, -1, keepdims=True)
    return center * lax.rsqrt(spread + EPSILON) * gain + shift


def attn_weights(query_key_value_weight, output_weight):
    return (
        lax.all_gather(query_key_value_weight, "fsdp", axis=0, tiled=True),
        lax.all_gather(output_weight, "fsdp", axis=0, tiled=True),
    )


def mlp_weights(first_feed_weight, second_feed_weight):
    return (
        lax.all_gather(first_feed_weight, "fsdp", axis=0, tiled=True),
        lax.all_gather(second_feed_weight, "fsdp", axis=0, tiled=True),
    )


def to_heads(input_array):
    return input_array.reshape(
        input_array.shape[0], input_array.shape[1], H, input_array.shape[2] // H
    )


def row_block(input_array, block_index, block_rows):
    return lax.dynamic_slice_in_dim(input_array, block_index * block_rows, block_rows, 1)


def block_grads(queries, grad_out, log_total, row_delta, keys_blk, values_blk):
    scores = plain_sum("sqhd,skhd->shqk", queries, keys_blk)
    probs = jnp.exp(scores - log_total[..., None])
    prob_low = probs.astype(jnp.bfloat16)
    grad_probs = plain_sum("sqhd,skhd->shqk", grad_out, values_blk)
    grad_scores = (probs * (grad_probs - row_delta[..., None])).astype(jnp.bfloat16)
    return (prob_low, grad_scores)


def attention_forward(queries_heads, keys_heads, values_heads):
    seq_count, row_count, head_count, head_size = queries_heads.shape
    length = keys_heads.shape[1]
    block_rows = min(512, length)
    block_count = length // block_rows

    def max_step(running, block_index):
        running_max, running_total = running
        scores = plain_sum(
            "sqhd,skhd->shqk", queries_heads, row_block(keys_heads, block_index, block_rows)
        )
        new_max = jnp.maximum(running_max, jnp.max(scores, -1))
        running_total = running_total * jnp.exp(running_max - new_max) + jnp.sum(
            jnp.exp(scores - new_max[..., None]), -1
        )
        return ((new_max, running_total), None)

    start_max = jnp.full((seq_count, head_count, row_count), -1e30, jnp.float32)
    start_total = jnp.zeros((seq_count, head_count, row_count), jnp.float32)
    (final_max, final_total), unused = lax.scan(
        max_step, (start_max, start_total), jnp.arange(block_count)
    )
    log_total = final_max + jnp.log(final_total)

    def value_step(running, block_index):
        scores = plain_sum(
            "sqhd,skhd->shqk", queries_heads, row_block(keys_heads, block_index, block_rows)
        )
        prob_low = jnp.exp(scores - log_total[..., None]).astype(jnp.bfloat16)
        return (
            running
            + plain_sum(
                "shqk,skhd->sqhd", prob_low, row_block(values_heads, block_index, block_rows)
            ),
            None,
        )

    context, unused = lax.scan(
        value_step, jnp.zeros(queries_heads.shape, jnp.float32), jnp.arange(block_count)
    )
    return (context, log_total)


def gather_body(
    tokens,
    cotangent,
    sequence_adapter_index,
    query_key_value_weight,
    output_weight,
    first_feed_weight,
    second_feed_weight,
    biases,
    value_bias_vector,
    first_feed_bias,
    norm_gain_pair,
    adapter_down_factors,
    output_down_factor,
    adapter_up_factors,
    hidden_up_factor,
    hidden_down_factor,
):
    seq_count, row_count, model_width = tokens.shape
    adapter_number = adapter_down_factors.shape[0]
    picker = (
        sequence_adapter_index[:, None] == jnp.arange(adapter_number, dtype=jnp.int32)[None, :]
    ).astype(jnp.float32)

    def select_adapter(table):
        return jnp.einsum("sa,a...->s...", picker, table.astype(jnp.float32), precision=HIGHEST)

    def to_adapters(per_seq):
        return jnp.einsum("sa,s...->a...", picker, per_seq, precision=HIGHEST)

    selected_down = select_adapter(adapter_down_factors)
    selected_output = select_adapter(output_down_factor)
    selected_up = select_adapter(adapter_up_factors)
    hup_sel = select_adapter(hidden_up_factor)
    hdown_sel = select_adapter(hidden_down_factor)
    down_low = selected_down.astype(jnp.bfloat16)
    out_low = selected_output.astype(jnp.bfloat16)
    hdown_low = hdown_sel.astype(jnp.bfloat16)
    wqkv_full, wout_full = attn_weights(query_key_value_weight, output_weight)
    projected = plain_sum("std,de->ste", tokens, wqkv_full)
    down_att = plain_sum("std,sjrd->sjtr", tokens, down_low[:, :3])
    lifted = exact_sum("sjtr,sjrd->sjtd", down_att, selected_up[:, :3])
    queries = ((projected[..., :model_width] + biases[0] + lifted[:, 0]) * 0.125).astype(
        jnp.bfloat16
    )
    keys_own = (projected[..., model_width : 2 * model_width] + lifted[:, 1]).astype(jnp.bfloat16)
    values_own = (projected[..., 2 * model_width :] + value_bias_vector + lifted[:, 2]).astype(
        jnp.bfloat16
    )
    keys_all, values_all = (
        lax.all_gather(keys_own, "ctx", axis=1, tiled=True),
        lax.all_gather(values_own, "ctx", axis=1, tiled=True),
    )
    queries_heads = to_heads(queries)
    keys_heads = to_heads(keys_all)
    values_heads = to_heads(values_all)
    context, log_total = attention_forward(queries_heads, keys_heads, values_heads)
    context = context.reshape(seq_count, row_count, model_width)
    context_low = context.astype(jnp.bfloat16)
    down_out = plain_sum("std,srd->str", context_low, out_low)
    branch = (
        plain_sum("std,de->ste", context_low, wout_full)
        + biases[1]
        + exact_sum("str,srd->std", down_out, selected_up[:, 3])
    )

    def first_norm(value):
        return layer_norm(value, norm_gain_pair[0], biases[3])

    def second_norm(value):
        return layer_norm(value, norm_gain_pair[1], biases[4])

    def gelu_exact(value):
        return jax.nn.gelu(value, approximate=False)

    normed, norm_back = jax.vjp(first_norm, tokens.astype(jnp.float32) + branch)
    normed_low = normed.astype(jnp.bfloat16)
    wfc1_full, wfc2_full = mlp_weights(first_feed_weight, second_feed_weight)
    down_fc1 = plain_sum("std,srd->str", normed_low, down_low[:, 3])
    hidden_pre = (
        plain_sum("std,df->stf", normed_low, wfc1_full)
        + first_feed_bias
        + exact_sum("str,srf->stf", down_fc1, hup_sel)
    )
    activated, gelu_back = jax.vjp(gelu_exact, hidden_pre)
    act_low = activated.astype(jnp.bfloat16)
    down_fc2 = plain_sum("stf,srf->str", act_low, hdown_low)
    mixed_out = (
        plain_sum("stf,fd->std", act_low, wfc2_full)
        + biases[2]
        + exact_sum("str,srd->std", down_fc2, selected_up[:, 4])
    )
    outcome, out_back = jax.vjp(second_norm, normed + mixed_out)
    (grad_sum2,) = out_back(cotangent.astype(jnp.float32))
    grad_mixed = grad_sum2.astype(jnp.bfloat16)
    grad_up_fc2 = exact_sum("str,std->srd", down_fc2, grad_mixed)
    grad_rank_fc2 = exact_sum("std,srd->str", grad_mixed, selected_up[:, 4]).astype(jnp.bfloat16)
    grad_hdown = plain_sum("str,stf->srf", grad_rank_fc2, act_low)
    wfc1_full, wfc2_full = mlp_weights(first_feed_weight, second_feed_weight)
    grad_act = (
        plain_sum("std,fd->stf", grad_mixed, wfc2_full)
        + plain_sum("str,srf->stf", grad_rank_fc2, hdown_low)
    ).astype(jnp.bfloat16)
    (grad_hidden,) = gelu_back(grad_act.astype(jnp.float32))
    grad_hidden = grad_hidden.astype(jnp.bfloat16)
    grad_hup = exact_sum("str,stf->srf", down_fc1, grad_hidden)
    grad_rank_fc1 = exact_sum("stf,srf->str", grad_hidden, hup_sel).astype(jnp.bfloat16)
    grad_down_fc1 = plain_sum("str,std->srd", grad_rank_fc1, normed_low)
    grad_normed_low = (
        plain_sum("stf,df->std", grad_hidden, wfc1_full)
        + plain_sum("str,srd->std", grad_rank_fc1, down_low[:, 3])
    ).astype(jnp.bfloat16)
    (grad_resid,) = norm_back(grad_sum2 + grad_normed_low.astype(jnp.float32))
    mlp_hup = to_adapters(grad_hup)
    mlp_hdown = to_adapters(grad_hdown)
    mlp_fc1 = to_adapters(grad_down_fc1)
    mlp_fc2 = to_adapters(grad_up_fc2)
    mlp_hup, mlp_hdown, mlp_fc1, mlp_fc2 = lax.psum(
        (mlp_hup, mlp_hdown, mlp_fc1, mlp_fc2), ("ctx", "fsdp")
    )
    grad_branch = grad_resid.astype(jnp.bfloat16)
    grad_up_out = exact_sum("str,std->srd", down_out, grad_branch)
    grad_rank_out = exact_sum("std,srd->str", grad_branch, selected_up[:, 3]).astype(jnp.bfloat16)
    grad_out_down = plain_sum("str,std->srd", grad_rank_out, context_low)
    wqkv_full, wout_full = attn_weights(query_key_value_weight, output_weight)
    grad_context = (
        plain_sum("std,ed->ste", grad_branch, wout_full)
        + plain_sum("str,srd->std", grad_rank_out, out_low)
    ).astype(jnp.bfloat16)
    row_delta = jnp.sum(to_heads(grad_context.astype(jnp.float32) * context), -1)
    delta_heads = jnp.swapaxes(row_delta, 1, 2)
    grad_heads = to_heads(grad_context)
    length = keys_all.shape[1]
    block_rows = min(512, length)
    block_count = length // block_rows

    def key_step(block_index, running):
        grad_query, grad_key, grad_value = running
        keys_blk = row_block(keys_heads, block_index, block_rows)
        values_blk = row_block(values_heads, block_index, block_rows)
        prob_low, grad_scores = block_grads(
            queries_heads, grad_heads, log_total, delta_heads, keys_blk, values_blk
        )
        grad_query = grad_query + plain_sum("shqk,skhd->sqhd", grad_scores, keys_blk)
        grad_key = lax.dynamic_update_slice_in_dim(
            grad_key,
            plain_sum("shqk,sqhd->skhd", grad_scores, queries_heads),
            block_index * block_rows,
            1,
        )
        grad_value = lax.dynamic_update_slice_in_dim(
            grad_value,
            plain_sum("shqk,sqhd->skhd", prob_low, grad_heads),
            block_index * block_rows,
            1,
        )
        return (grad_query, grad_key, grad_value)

    start_query = jnp.zeros(queries_heads.shape, jnp.float32)
    start_keys = jnp.zeros(keys_heads.shape, jnp.float32)
    grad_query, grad_key_all, grad_value_all = lax.fori_loop(
        0, block_count, key_step, (start_query, start_keys, start_keys)
    )
    grad_keys, grad_values = (
        lax.psum_scatter(
            grad_key_all.reshape(seq_count, length, model_width).astype(jnp.bfloat16),
            "ctx",
            scatter_dimension=1,
            tiled=True,
        ).astype(jnp.float32),
        lax.psum_scatter(
            grad_value_all.reshape(seq_count, length, model_width).astype(jnp.bfloat16),
            "ctx",
            scatter_dimension=1,
            tiled=True,
        ).astype(jnp.float32),
    )
    grad_qlin = grad_query.reshape(seq_count, row_count, model_width).astype(jnp.bfloat16) * 0.125
    grad_key_low = grad_keys.astype(jnp.bfloat16)
    grad_value_low = grad_values.astype(jnp.bfloat16)
    stacked = jnp.stack([grad_qlin, grad_key_low, grad_value_low], 1)
    grad_up_att = exact_sum("sjtr,sjtd->sjrd", down_att, stacked)
    grad_rank_att = exact_sum("sjtd,sjrd->sjtr", stacked, selected_up[:, :3]).astype(jnp.bfloat16)
    grad_down_att = plain_sum("sjtr,std->sjrd", grad_rank_att, tokens)
    joined = jnp.concatenate([grad_qlin, grad_key_low, grad_value_low], -1)
    grad_tokens = (
        grad_resid
        + plain_sum("ste,de->std", joined, wqkv_full)
        + plain_sum("sjtr,sjrd->std", grad_rank_att, down_low[:, :3])
    )
    attn_down = to_adapters(grad_down_att)
    attn_out = to_adapters(grad_out_down)
    attn_up = to_adapters(jnp.concatenate([grad_up_att, grad_up_out[:, None]], 1))
    attn_down, attn_out, attn_up = lax.psum((attn_down, attn_out, attn_up), ("ctx", "fsdp"))
    total_down = jnp.concatenate([attn_down, mlp_fc1[:, None]], 1)
    total_up = jnp.concatenate([attn_up, mlp_fc2[:, None]], 1)
    return (
        outcome.astype(jnp.bfloat16),
        grad_tokens,
        total_down,
        attn_out,
        total_up,
        mlp_hup,
        mlp_hdown,
    )


BF16 = jnp.bfloat16
F32 = jnp.float32
LOG2E = 1.4426950408889634
VMEM_LIMIT = 60 * 2**20
MESH = pl.DeviceIdType.MESH


def dot32(left, right):
    return jnp.dot(left, right, preferred_element_type=F32)


def dot_nt(left, right):
    return lax.dot_general(left, right, (((1,), (1,)), ((), ())), preferred_element_type=F32)


def dot_tn(left, right):
    return lax.dot_general(left, right, (((0,), (0,)), ((), ())), preferred_element_type=F32)


def split_three(value):
    high = value.astype(BF16)
    rest = value - high.astype(F32)
    middle = rest.astype(BF16)
    return high, middle, (rest - middle.astype(F32)).astype(BF16)


def flip(value):
    return value.astype(F32).T.astype(BF16)


def remote(src, dst, send_sem, recv_sem, device):
    return pltpu.make_async_remote_copy(
        src_ref=src,
        dst_ref=dst,
        send_sem=send_sem,
        recv_sem=recv_sem,
        device_id=device,
        device_id_type=MESH,
    )


class Place:
    def __init__(self):
        self.ctx = lax.axis_index("ctx")
        self.core = lax.axis_index("fsdp")
        self.half = self.ctx // (H // 2)
        self.low = self.ctx % (H // 2)
        self.me = self.low * 2 + self.core
        self.swaps = self.core != self.half
        self.pair = (self.core + self.half) % 2
        self.sibling = (self.ctx, 1 - self.core)
        self.partner = ((self.ctx + H // 2) % H, 1 - self.core)

    def peer(self, step):
        number = self.me ^ step
        return (self.half * (H // 2) + number // 2, number % 2)

    def order(self, turn):
        return 2 * (turn % (H // 2)) + (turn // (H // 2) + self.pair) % 2

    def greet(self):
        barrier = pltpu.get_barrier_semaphore()
        for step in range(1, H):
            pl.semaphore_signal(barrier, inc=1, device_id=self.peer(step), device_id_type=MESH)
        pl.semaphore_signal(barrier, inc=1, device_id=self.partner, device_id_type=MESH)
        pl.semaphore_wait(barrier, H)


def sum_copies(mine, parts, total, sems, place):
    own = total.at[place.pair, place.low, place.half]
    other = total.at[place.pair, place.low, 1 - place.half]
    column = total.at[place.pair]
    scatter = [
        remote(mine.at[place.me ^ step], parts.at[step], sems.at[0, step], sems.at[1, step], place.peer(step))
        for step in range(1, H)
    ]
    cross = remote(own, own, sems.at[0, 0], sems.at[1, 0], place.partner)
    first = [
        remote(own, own, sems.at[2, step], sems.at[3, step], place.peer(step))
        for step in range(2, H, 2)
    ]
    second = [
        remote(other, other, sems.at[2, step + 1], sems.at[3, step + 1], place.peer(step))
        for step in range(2, H, 2)
    ]
    last = remote(column, column, sems.at[2, 0], sems.at[3, 0], place.sibling)
    return scatter, cross, first, second, last


def sum_parts(scatter, mine, parts, total, place):
    value = mine[place.me].astype(F32)
    for step, copy in enumerate(scatter, 1):
        copy.wait_recv()
        value = value + parts[step].astype(F32)
    total[place.pair, place.low, place.half] = value.astype(BF16)


def put_term(mine, base, term):
    units = mine.shape[2] // 128
    for unit in range(term.shape[1] // 128):
        at = base // 128 + unit
        lanes = slice(at % units * 128, at % units * 128 + 128)
        mine[at // units, :, lanes] = term[:, unit * 128 : unit * 128 + 128].astype(BF16)


def layer_kernel(
    block_q,
    block_k,
    index_ref,
    tokens_ref,
    cotangent_ref,
    wqkv_ref,
    wout_ref,
    wfc1_ref,
    wfc2_ref,
    down_table,
    up_table,
    out_down_table,
    hidden_up_table,
    hidden_down_table,
    biases_ref,
    value_bias_ref,
    hidden_bias_ref,
    gains_ref,
    outcome_ref,
    grad_ref,
    chosen_out,
    hidden_down_out,
    hidden_up_out,
    down_out,
    up_out,
    out_down_out,
    wqkv_far,
    wfc1_far,
    wide,
    wfc2,
    wout,
    big,
    act,
    small,
    small_hidden,
    x,
    cotangent,
    rank_att,
    outgoing,
    qkv,
    leaving,
    arrived,
    incoming,
    context,
    state,
    qta,
    gta,
    kk,
    vv,
    kt,
    both,
    dkv_sum,
    dq_in,
    dkv_out,
    dkv_in,
    grad_out,
    grad_in,
    mlp_mine,
    mlp_parts,
    mlp_total,
    att_mine,
    att_parts,
    att_total,
    load_sem,
    core_sem,
    swap_sem,
    kv_sem,
    q_sem,
    back_sem,
    grad_sem,
    dq_sem,
    dkv_sem,
    mlp_sem,
    att_sem,
):
    peers, _, rows = qkv.shape
    length = peers * rows
    width = x.shape[1]
    hidden = hidden_bias_ref.shape[1]
    adapters = hidden_up_table.shape[0] // 16
    place = Place()
    me, core = place.me, place.core
    other = 1 - core
    wqkv = wide.at[:, 0 : 3 * width]
    up_at = down_table.shape[0]
    out_down_at = up_at + up_table.shape[0]

    def half_of(full, owner):
        count = full.shape[0] // 2
        return full.at[pl.ds(pl.multiple_of(owner * count, count), count), :]

    def load(source, target, number):
        return pltpu.make_async_copy(source, target, load_sem.at[number])

    def to_sibling(source, target, number):
        return remote(source, target, core_sem.at[0, number], core_sem.at[1, number], place.sibling)

    load_wqkv = load(wqkv_ref, half_of(wqkv, core), 0)
    load_wout = load(wout_ref, half_of(wout, core), 1)
    load_tables = [
        load(down_table, wfc2.at[0:up_at], 2),
        load(up_table, wfc2.at[up_at:out_down_at], 3),
        load(out_down_table, wfc2.at[out_down_at : out_down_at + out_down_table.shape[0]], 4),
        load(hidden_up_table, act.at[0 : 16 * adapters], 5),
        load(hidden_down_table, act.at[16 * adapters : 32 * adapters], 6),
    ]
    load_x = load(tokens_ref, x, 7)
    load_cotangent = load(cotangent_ref, cotangent, 8)
    load_wfc1 = load(wfc1_ref, half_of(wide, core), 9)
    load_wfc1_far = load(wfc1_far, half_of(wide, other), 10)
    load_wfc2 = load(wfc2_ref, half_of(wfc2, core), 11)
    again_wqkv = load(wqkv_ref, half_of(wqkv, core), 12)
    again_wqkv_far = load(wqkv_far, half_of(wqkv, other), 13)
    give_wqkv = to_sibling(wqkv_ref, half_of(wqkv, core), 0)
    give_wout = to_sibling(wout_ref, half_of(wout, core), 1)
    give_chosen = to_sibling(chosen_out.at[core], chosen_out.at[core], 2)
    count = small.shape[0]
    give_small = [to_sibling(small, wide.at[0:count, 3 * width : 4 * width], 3)] + [
        to_sibling(
            small_hidden.at[:, part * width : (part + 1) * width],
            wide.at[count + 32 * part : count + 32 * part + 32, 3 * width : 4 * width],
            4 + part,
        )
        for part in range(hidden // width)
    ]
    give_wfc2 = to_sibling(wfc2_ref, half_of(wfc2, core), 8)
    give_wfc1 = to_sibling(wfc1_ref, wfc1_far, 9)
    give_wqkv_again = to_sibling(wqkv_ref, wqkv_far, 10)
    half_rows = rows // 2
    swap_x = [
        remote(
            tokens_ref.at[part * half_rows : (part + 1) * half_rows],
            x.at[part * half_rows : (part + 1) * half_rows],
            swap_sem.at[0, 7 + part],
            swap_sem.at[1, 7 + part],
            place.partner,
        )
        for part in range(2)
    ]
    swap_cotangent = remote(cotangent_ref, cotangent, swap_sem.at[0, 1], swap_sem.at[1, 1], place.partner)

    load_wqkv.start()
    for copy in load_tables:
        copy.start()
    load_wout.start()

    @pl.when(jnp.logical_not(place.swaps))
    def _():
        load_x.start()
        load_cotangent.start()

    adapter = index_ref[0]
    numbers = lax.broadcasted_iota(jnp.int32, chosen_out.shape[1:], 0)
    chosen_out[core] = (numbers == jnp.full(numbers.shape, adapter, jnp.int32)).astype(F32)
    place.greet()

    @pl.when(place.swaps)
    def _():
        for copy in swap_x:
            copy.start()

    give_wqkv.start()
    give_chosen.start()

    for copy in load_tables:
        copy.wait()

    def select(table, base, group, groups, target, at):
        chosen = jnp.full((16, table.shape[1]), adapter, jnp.int32)
        value = jnp.zeros((16, table.shape[1]), F32)
        for number in range(adapters):
            start = pl.multiple_of(base + 16 * (number * groups + group), 16)
            value = jnp.where(chosen == number, table[pl.ds(start, 16), :].astype(F32), value)
        target[pl.ds(pl.multiple_of(at + 16 * group, 16), 16), :] = value.astype(BF16)

    def select_down(group, _):
        select(wfc2, 0, group, 4, small, 0)
        return 0

    def select_up(group, _):
        select(wfc2, up_at, group, 5, small, 64)
        return 0

    lax.fori_loop(0, 4, select_down, 0)
    lax.fori_loop(0, 5, select_up, 0)
    select(wfc2, out_down_at, 0, 1, small, 144)
    for part in range(2):
        select(act, 16 * adapters * part, 0, 1, small_hidden, 16 * part)
    for copy in give_small:
        copy.start()
    give_wout.start()
    for copy in give_small:
        copy.wait()

    @pl.when(place.swaps)
    def _():
        small[...] = wide[0:count, 3 * width : 4 * width]
        for part in range(hidden // width):
            small_hidden[:, part * width : (part + 1) * width] = wide[
                count + 32 * part : count + 32 * part + 32, 3 * width : 4 * width
            ]

    hidden_up_ref = small_hidden.at[0:16]
    hidden_down_ref = small_hidden.at[16:32]
    out_down_ref = small.at[144:160]

    def down(j):
        return small[16 * j : 16 * j + 16]

    def up(j):
        return small[64 + 16 * j : 80 + 16 * j]

    load_wfc2.start()
    give_wfc2.start()

    load_wqkv.wait()
    give_wqkv.wait_recv()

    def project(half, part):
        here = slice(half * half_rows, (half + 1) * half_rows)
        cols = slice(part * width, (part + 1) * width)
        value = dot32(x[here, :], wqkv[:, cols]) + dot32(rank_att[here, part * 16 : part * 16 + 16], up(part))
        if part == 0:
            value = (value + biases_ref[0:1, :]) * 0.125
        if part == 2:
            value = value + value_bias_ref[...]
        for two in range(peers // 2):
            turned = value[:, two * 128 : two * 128 + 128].T.astype(BF16)
            outgoing[2 * two, part * 64 : part * 64 + 64, here] = turned[0:64]
            outgoing[2 * two + 1, part * 64 : part * 64 + 64, here] = turned[64:128]

    def kv_copy(step, half):
        here = slice(half * half_rows, (half + 1) * half_rows)
        return remote(
            outgoing.at[me ^ step, 64:192, here],
            qkv.at[step, 64:192, here],
            kv_sem.at[0, half, step],
            kv_sem.at[1, half, step],
            place.peer(step),
        )

    def q_copy(step):
        return remote(
            outgoing.at[me ^ step, 0:64], qkv.at[step, 0:64], q_sem.at[0, step], q_sem.at[1, step], place.peer(step)
        )

    def back_copy(step):
        return remote(leaving.at[step], arrived.at[me], back_sem.at[0, step], back_sem.at[1, step], place.peer(step))

    steps = length // block_k
    group = block_q // rows
    key_group = block_k // rows
    for half in range(2):
        here = slice(half * half_rows, (half + 1) * half_rows)

        @pl.when(place.swaps)
        def _():
            swap_x[half].wait_recv()

        if half == 0:

            @pl.when(jnp.logical_not(place.swaps))
            def _():
                load_x.wait()

        rank_att[here, :] = dot_nt(x[here, :], small[0:48]).astype(BF16)
        project(half, 1)
        project(half, 2)
        for step in range(1, peers):
            kv_copy(step, half).start()
        project(half, 0)
    for step in range(1, peers):
        q_copy(step).start()
    give_wfc1.start()
    give_wqkv_again.start()
    load_wfc1.start()
    qkv[0] = outgoing[me]

    row_at = lax.broadcasted_iota(jnp.int32, (16, rows), 0)
    ones = (row_at == 0).astype(F32).astype(BF16)
    minus = jnp.where(lax.broadcasted_iota(jnp.int32, (rows, 16), 1) < 3, -1.0, 0.0).astype(BF16)
    minus_rows = jnp.where(lax.broadcasted_iota(jnp.int32, (64, rows), 0) < 3, -1.0, 0.0).astype(BF16)

    def tail(value):
        at = lax.broadcasted_iota(jnp.int32, (16, value.shape[1]), 0)
        high, middle, low = (part.astype(F32) for part in split_three(value))
        return jnp.where(at == 0, high, jnp.where(at == 1, middle, jnp.where(at == 2, low, 0.0))).astype(BF16)

    def take_key(turn):
        cols = pl.ds(pl.multiple_of(turn * rows, rows), rows)
        step = place.order(turn)

        @pl.when(step > 0)
        def _():
            kv_copy(step, 0).wait_recv()
            kv_copy(step, 1).wait_recv()

        key = qkv[step, 64:128, :]
        value = qkv[step, 128:192, :]
        kt[:, cols] = key
        kk[cols, 0:128] = flip(jnp.concatenate([key, key], 0))
        kk[cols, 128:144] = minus
        vv[cols, :] = flip(jnp.concatenate([value, minus_rows], 0))
        gta[0:64, cols] = value
        gta[64:80, cols] = ones
        gta[80:128, cols] = jnp.zeros((48, rows), BF16)

    def take_keys(i):
        def one(part, _):
            take_key(i * key_group + part)
            return 0

        lax.fori_loop(0, key_group, one, 0)

    def forward_part(i, low, high, arriving):
        def take_query(part, _):
            turn = i * group + part
            step = place.order(turn)
            here = pl.ds(pl.multiple_of(turn * rows, rows), rows)

            @pl.when(step > 0)
            def _():
                q_copy(step).wait_recv()

            query = qkv[step, 0:64, :].astype(F32) * LOG2E
            high = query.astype(BF16)
            qta[0:64, here] = high
            qta[64:128, here] = (query - high.astype(F32)).astype(BF16)
            return 0

        if low == 0:
            lax.fori_loop(0, group, take_query, 0)
        cols = pl.ds(pl.multiple_of(i * block_q, block_q), block_q)
        query = qta.at[0:128, cols]
        if arriving:

            @pl.when(i == 0)
            def _():
                take_keys(low)

        block = dot32(kk[low * block_k : (low + 1) * block_k, 0:128], query[...])
        big[0:block_k] = block

        def half(j, now, carry):
            peak, running, total = carry
            later = jnp.minimum(j + 1, high - 1)
            here = pl.ds(pl.multiple_of(j * block_k, block_k), block_k)
            there = pl.ds(pl.multiple_of(later * block_k, block_k), block_k)
            if arriving:

                @pl.when(jnp.logical_and(i == 0, j + 1 < high))
                def _():
                    take_keys(later)

            ahead = dot32(kk[there, 0:128], query[...])
            big[(1 - now) * block_k : (2 - now) * block_k] = ahead
            new = jnp.maximum(running, peak)
            weights = jnp.exp2(big[now * block_k : (now + 1) * block_k] - new).astype(BF16)
            total = total * jnp.exp2(running - new) + dot32(gta[0:80, here], weights)
            return jnp.max(ahead, 0, keepdims=True), new, total

        def pair(j, carry):
            return half(low + 2 * j + 1, 1, half(low + 2 * j, 0, carry))

        if low == 0:
            running, total = jnp.full((1, block_q), -jnp.inf, F32), jnp.zeros((80, block_q), F32)
        else:
            running = state[1:2, cols]
            total = jnp.concatenate([context[:, cols], state[0:1, cols], jnp.zeros((15, block_q), F32)], 0)
        _, top, total = lax.fori_loop(
            0, (high - low) // 2, pair, (jnp.max(block, 0, keepdims=True), running, total)
        )
        weight_sum = total[64:65]
        if high < steps:
            context[:, cols] = total[0:64]
            state[0:1, cols] = weight_sum
            state[1:2, cols] = top
            return
        result = total[0:64] / weight_sum
        context[:, cols] = result
        qta[128:144, cols] = tail(top + jnp.log2(weight_sum))
        low_result = result.astype(BF16)
        for part in range(group):
            step = place.order(i * group + part)
            leaving[step] = low_result[:, part * rows : (part + 1) * rows]

            @pl.when(step > 0)
            def _():
                back_copy(step).start()

    query_steps = length // block_q

    def forward_parts(first, last, low, high, arriving):
        def one(i, _):
            forward_part(i, low, high, arriving)
            return 0

        lax.fori_loop(first, last, one, 0)

    forward_parts(0, query_steps // 2, 0, steps // 2, True)
    give_wfc1.wait_recv()
    load_wfc1_far.start()
    forward_parts(0, query_steps // 2, steps // 2, steps, True)

    @pl.when(place.swaps)
    def _():
        swap_cotangent.start()

    forward_parts(query_steps // 2, query_steps, 0, steps, False)
    arrived[me] = leaving[0]

    def mean(value):
        return jnp.mean(value, -1, keepdims=True)

    def norm_backward(grad, hat, scale):
        return scale * (grad - mean(grad) - hat * mean(grad * hat))

    load_wout.wait()
    give_wout.wait_recv()
    for step in range(1, peers):
        back_copy(step).wait_recv()
    context_low = flip(arrived[...].reshape(width, rows))
    rank_out = dot_nt(context_low, out_down_ref[...]).astype(BF16)
    resid = x[...].astype(F32) + dot32(context_low, wout[...]) + biases_ref[1:2] + dot32(rank_out, up(3))
    center = resid - mean(resid)
    scale_one = lax.rsqrt(mean(center * center) + EPSILON)
    hat_one = center * scale_one
    normed = hat_one * gains_ref[0:1] + biases_ref[3:4]
    normed_low = normed.astype(BF16)
    rank_one = dot_nt(normed_low, down(3)).astype(BF16)
    load_wfc1.wait()
    load_wfc1_far.wait()
    load_wfc2.wait()
    give_wfc2.wait_recv()
    piece = 1024
    rank_two = jnp.zeros((rows, 16), F32)
    mixed = normed + biases_ref[2:3]
    for part in range(hidden // piece):
        cols = slice(part * piece, (part + 1) * piece)
        pre = (
            dot32(normed_low, wide[:, cols])
            + hidden_bias_ref[:, cols]
            + dot32(rank_one, hidden_up_ref[:, cols])
        )
        share = 0.5 + 0.5 * lax.erf(pre * 0.7071067811865476)
        big[part * rows : (part + 1) * rows] = share + pre * (0.3989422804014327 * jnp.exp(-0.5 * pre * pre))
        active = (pre * share).astype(BF16)
        act[:, cols] = active
        rank_two = rank_two + dot_nt(active, hidden_down_ref[:, cols])
        mixed = mixed + dot32(active, wfc2[cols, :])
    rank_two = rank_two.astype(BF16)
    mixed = mixed + dot32(rank_two, up(4))
    center = mixed - mean(mixed)
    scale_two = lax.rsqrt(mean(center * center) + EPSILON)
    hat_two = center * scale_two

    @pl.when(place.swaps)
    def _():
        swap_cotangent.wait_recv()

    @pl.when(jnp.logical_not(place.swaps))
    def _():
        load_cotangent.wait()

    grad_sum = norm_backward(cotangent[...].astype(F32) * gains_ref[1:2], hat_two, scale_two)
    outcome = cotangent
    outcome[...] = (hat_two * gains_ref[1:2] + biases_ref[4:5]).astype(BF16)
    home_outcome = remote(outcome, outcome_ref, swap_sem.at[0, 2], swap_sem.at[1, 2], place.partner)

    @pl.when(place.swaps)
    def _():
        home_outcome.start()

    @pl.when(jnp.logical_not(place.swaps))
    def _():
        outcome_ref[...] = outcome[...]

    grad_mixed = grad_sum.astype(BF16)
    put_term(mlp_mine, 2 * hidden, dot_tn(rank_two, grad_mixed))
    grad_rank = dot_nt(grad_mixed, up(4)).astype(BF16)
    put_term(mlp_mine, 0, dot_tn(grad_rank, act[...]))
    grad_one = jnp.zeros((rows, 16), F32)
    grad_normed = jnp.zeros((rows, width), F32)
    for part in range(hidden // piece):
        cols = slice(part * piece, (part + 1) * piece)
        grad_act = dot_nt(grad_mixed, wfc2[cols, :]) + dot32(grad_rank, hidden_down_ref[:, cols])
        grad_hidden = (grad_act.astype(BF16).astype(F32) * big[part * rows : (part + 1) * rows]).astype(BF16)
        put_term(mlp_mine, hidden + part * piece, dot_tn(rank_one, grad_hidden))
        grad_one = grad_one + dot_nt(grad_hidden, hidden_up_ref[:, cols])
        grad_normed = grad_normed + dot_nt(grad_hidden, wide[:, cols])
    grad_one = grad_one.astype(BF16)
    put_term(mlp_mine, 2 * hidden + width, dot_tn(grad_one, normed_low))
    grad_normed = (grad_normed + dot32(grad_one, down(3))).astype(BF16).astype(F32)
    resid_grad = norm_backward((grad_sum + grad_normed) * gains_ref[0:1], hat_one, scale_one)
    grad_resid = big.at[0:rows]
    grad_resid[...] = resid_grad
    grad_branch = resid_grad.astype(BF16)
    put_term(mlp_mine, 2 * hidden + 2 * width, dot_tn(rank_out, grad_branch))
    grad_rank = dot_nt(grad_branch, up(3)).astype(BF16)
    put_term(mlp_mine, 2 * hidden + 3 * width, dot_tn(grad_rank, context_low))
    turned = dot_nt(wout[...], grad_branch) + lax.dot_general(
        out_down_ref[...], grad_rank, (((0,), (1,)), ((), ())), preferred_element_type=F32
    )
    for step in range(1, peers):
        kv_copy(step, 0).wait_send()
        kv_copy(step, 1).wait_send()
        q_copy(step).wait_send()
        back_copy(step).wait_send()
    outgoing[:, 0:64] = turned.astype(BF16).reshape(peers, 64, rows)

    def grad_copy(step):
        return remote(
            outgoing.at[me ^ step, 0:64], incoming.at[step], grad_sem.at[0, step], grad_sem.at[1, step], place.peer(step)
        )

    for step in range(1, peers):
        grad_copy(step).start()
    mlp_scatter, mlp_cross, mlp_first, mlp_second, mlp_last = sum_copies(mlp_mine, mlp_parts, mlp_total, mlp_sem, place)
    incoming[0] = outgoing[me, 0:64]
    give_wqkv_again.wait_recv()
    again_wqkv.start()
    again_wqkv_far.start()
    dkv_sum[...] = jnp.zeros_like(dkv_sum)
    first = lax.broadcasted_iota(jnp.int32, (block_k, 128), 1) < 64
    dq_out = leaving

    def dq_copy(step):
        return remote(dq_out.at[step], dq_in.at[me], dq_sem.at[0, step], dq_sem.at[1, step], place.peer(step))

    def dkv_copy(step):
        return remote(dkv_out.at[step], dkv_in.at[me], dkv_sem.at[0, step], dkv_sem.at[1, step], place.peer(step))

    def backward_step(turn, _):
        last = turn == query_steps - 1
        j = (turn + query_steps // 2) % query_steps

        def take_grad(part, _):
            step = place.order(j * group + part)
            cols = pl.ds(pl.multiple_of((j * group + part) * rows, rows), rows)

            @pl.when(step > 0)
            def _():
                grad_copy(step).wait_recv()

            grad = incoming[step]
            gta[0:64, cols] = grad
            gta[64:80, cols] = tail(jnp.sum(grad.astype(F32) * context[:, cols], 0, keepdims=True))
            both[cols, :] = flip(jnp.concatenate([qkv[step, 0:64, :], grad], 0))
            return 0

        lax.fori_loop(0, group, take_grad, 0)
        cols = pl.ds(pl.multiple_of(j * block_q, block_q), block_q)

        def key_pair(pair, dq):
            found = []
            for side in range(2):
                i = (2 * pair + side + steps // 2) % steps
                here = pl.ds(pl.multiple_of(i * block_k, block_k), block_k)
                probs = jnp.exp2(dot32(kk[here, :], qta[:, cols]))
                change = dot32(vv[here, :], gta[:, cols])
                found.append((i, here, probs.astype(BF16), (probs * change).astype(BF16)))
            for i, here, probs, low in found:
                dv = dot32(probs, both[cols, :])
                dk = dot32(low, both[cols, :])
                dkv_sum[here, :] += jnp.where(first, dk, dv)
                dq = dq + dot32(kt[:, here], low)

            @pl.when(last)
            def _():
                for i, here, _, _ in found:
                    done = dkv_sum[here, :].astype(BF16)
                    for part in range(key_group):
                        step = place.order(i * key_group + part)
                        dkv_out[step] = done[part * rows : (part + 1) * rows]

                        @pl.when(step > 0)
                        def _():
                            dkv_copy(step).start()

            return dq

        dq = lax.fori_loop(0, steps // 2, key_pair, jnp.zeros((64, block_q), F32)).astype(BF16)
        for part in range(group):
            step = place.order(j * group + part)
            dq_out[step] = dq[:, part * rows : (part + 1) * rows]

            @pl.when(step > 0)
            def _():
                dq_copy(step).start()

        @pl.when(turn == query_steps // 4 - 1)
        def _():
            for copy in mlp_scatter:
                copy.start()

        @pl.when(turn == query_steps // 2 - 1)
        def _():
            sum_parts(mlp_scatter, mlp_mine, mlp_parts, mlp_total, place)
            mlp_cross.start()
            for copy in mlp_first:
                copy.start()

        @pl.when(turn == query_steps - 2)
        def _():
            mlp_cross.wait_recv()
            for copy in mlp_second:
                copy.start()

        return 0

    lax.fori_loop(0, query_steps, backward_step, 0)
    for copy in mlp_first + mlp_second:
        copy.wait_recv()
    mlp_last.start()

    def spread(total, parts):
        units = total.shape[4] // 128
        for half in range(2):
            for unit in range(peers * units):
                peer = unit // units
                lanes = slice(unit % units * 128, unit % units * 128 + 128)
                for target, low, high in parts:
                    if low <= unit * 128 < high:
                        at = unit * 128 - low
                        target(half)[:, at : at + 128] = total[(peer % 2 + half) % 2, peer // 2, half, :, lanes]

    joined = act.at[:, 0 : 3 * width]
    dq_in[me] = dq_out[0]
    dkv_in[me] = dkv_out[0]
    for step in range(1, peers):
        dkv_copy(step).wait_recv()
    left = lax.broadcasted_iota(jnp.int32, (rows, 128), 1) < 64
    for two in range(peers // 2):
        even = dkv_in[2 * two].astype(F32)
        odd = dkv_in[2 * two + 1].astype(F32)
        cols = slice(width + two * 128, width + two * 128 + 128)
        joined[:, cols] = jnp.where(left, even, pltpu.roll(odd, 64, 1)).astype(BF16)
        cols = slice(2 * width + two * 128, 2 * width + two * 128 + 128)
        joined[:, cols] = jnp.where(left, pltpu.roll(even, 64, 1), odd).astype(BF16)
    def ranks_of(part):
        grad = joined[:, part * width : (part + 1) * width]
        ranks[part] = dot_nt(grad, up(part)).astype(BF16)

    def terms_of(part):
        grad = joined[:, part * width : (part + 1) * width]
        put_term(att_mine, part * width, dot_tn(rank_att[:, part * 16 : part * 16 + 16], grad))
        put_term(att_mine, (3 + part) * width, dot_tn(ranks[part], x[...]))

    ranks = {}
    att_scatter, att_cross, att_first, att_second, att_last = sum_copies(att_mine, att_parts, att_total, att_sem, place)
    again_wqkv.wait()
    again_wqkv_far.wait()
    for part in (1, 2):
        ranks_of(part)
        terms_of(part)
    for step in range(1, peers):
        dq_copy(step).wait_recv()
    joined[:, 0:width] = (dq_in[...].reshape(width, rows).astype(F32).T * 0.125).astype(BF16)
    ranks_of(0)
    terms_of(0)
    for copy in att_scatter:
        copy.start()
    piece = width // 4
    home = [
        remote(
            grad_out.at[:, part * piece : (part + 1) * piece],
            grad_in.at[:, part * piece : (part + 1) * piece],
            swap_sem.at[0, 3 + part],
            swap_sem.at[1, 3 + part],
            place.partner,
        )
        for part in range(4)
    ]
    mlp_last.wait_recv()
    for part in range(4):
        cols = slice(part * piece, (part + 1) * piece)
        total = grad_resid[:, cols] + dot_nt(joined[...], wqkv[cols, :])
        for j in range(3):
            total = total + dot32(ranks[j], small[16 * j : 16 * j + 16, cols])
        grad_ref[:, cols] = total
        grad_out[:, cols] = total.astype(BF16)

        @pl.when(place.swaps)
        def _():
            home[part].start()

    sum_parts(att_scatter, att_mine, att_parts, att_total, place)
    att_cross.start()
    for copy in att_first:
        copy.start()
    spread(
        mlp_total,
        (
            (lambda half: hidden_down_out.at[half], 0, hidden),
            (lambda half: hidden_up_out.at[half], hidden, 2 * hidden),
            (lambda half: up_out.at[half, 4], 2 * hidden, 2 * hidden + width),
            (lambda half: down_out.at[half, 3], 2 * hidden + width, 2 * hidden + 2 * width),
            (lambda half: up_out.at[half, 3], 2 * hidden + 2 * width, 2 * hidden + 3 * width),
            (lambda half: out_down_out.at[half], 2 * hidden + 3 * width, 2 * hidden + 4 * width),
        ),
    )
    att_cross.wait_recv()
    for copy in att_second:
        copy.start()
    for copy in att_first + att_second:
        copy.wait_recv()
    att_last.start()

    @pl.when(place.swaps)
    def _():
        for part in range(4):
            home[part].wait_recv()
            cols = slice(part * piece, (part + 1) * piece)
            grad_ref[:, cols] = grad_in[:, cols].astype(F32)
        for part in range(4):
            home[part].wait_send()
        home_outcome.wait()
        for copy in swap_x:
            copy.wait_send()
        swap_cotangent.wait_send()

    att_last.wait_recv()
    spread(
        att_total,
        tuple(
            (functools.partial(lambda part, half: up_out.at[half, part], part), part * width, (part + 1) * width)
            for part in range(3)
        )
        + tuple(
            (functools.partial(lambda part, half: down_out.at[half, part], part), (3 + part) * width, (4 + part) * width)
            for part in range(3)
        ),
    )
    for step in range(1, peers):
        grad_copy(step).wait_send()
        dq_copy(step).wait_send()
        dkv_copy(step).wait_send()
    for copies in ((mlp_scatter, mlp_first, mlp_second), (att_scatter, att_first, att_second)):
        for copy in copies[0] + copies[1] + copies[2]:
            copy.wait_send()
    for copy in (mlp_cross, mlp_last, att_cross, att_last):
        copy.wait_send()
    for copy in (give_wqkv, give_wout, give_wfc2, give_wfc1, give_wqkv_again):
        copy.wait_send()
    give_chosen.wait()


def run_layer(index, tokens, cotangent, weights, tables, biases, value_bias, hidden_bias, gains):
    rows, width = tokens.shape
    peers = H
    length = peers * rows
    hidden = hidden_bias.shape[1]
    block_q, block_k = 1024, 512
    vmem = pl.BlockSpec(memory_space=pltpu.VMEM)
    hbm = pl.BlockSpec(memory_space=pl.ANY)
    mlp_part = (2 * hidden + 4 * width) // peers
    att_part = 6 * width // peers

    def out(shape, dtype=BF16):
        return jax.ShapeDtypeStruct(shape, dtype)

    def total(part):
        return pltpu.VMEM((2, peers // 2, 2, 16, part), BF16)

    def heads(*shape):
        return pltpu.VMEM((peers,) + shape, BF16)

    def sems(*shape):
        return pltpu.SemaphoreType.DMA(shape)

    return pl.pallas_call(
        functools.partial(layer_kernel, block_q, block_k),
        out_shape=[
            out((rows, width)),
            out((rows, width), F32),
            out((2, 8, 128), F32),
            out((2, 16, hidden)),
            out((2, 16, hidden)),
            out((2, 4, 16, width)),
            out((2, 5, 16, width)),
            out((2, 16, width)),
            out(weights[0].shape),
            out(weights[2].shape),
        ],
        in_specs=[pl.BlockSpec(memory_space=pltpu.SMEM)] + [hbm] * 11 + [vmem] * 4,
        out_specs=[vmem] * 8 + [hbm] * 2,
        scratch_shapes=[
            pltpu.VMEM((width, hidden), BF16),
            pltpu.VMEM((hidden, width), BF16),
            pltpu.VMEM((width, width), BF16),
            pltpu.VMEM((max(4 * rows, 2 * block_k), 1024), F32),
            pltpu.VMEM((rows, hidden), BF16),
            pltpu.VMEM((160, width), BF16),
            pltpu.VMEM((32, hidden), BF16),
            pltpu.VMEM((rows, width), BF16),
            pltpu.VMEM((rows, width), BF16),
            pltpu.VMEM((rows, 48), BF16),
            heads(192, rows),
            heads(192, rows),
            heads(64, rows),
            heads(64, rows),
            heads(64, rows),
            pltpu.VMEM((64, length), F32),
            pltpu.VMEM((8, length), F32),
            pltpu.VMEM((144, length), BF16),
            pltpu.VMEM((128, length), BF16),
            pltpu.VMEM((length, 144), BF16),
            pltpu.VMEM((length, 128), BF16),
            pltpu.VMEM((64, length), BF16),
            pltpu.VMEM((length, 128), BF16),
            pltpu.VMEM((length, 128), F32),
            heads(64, rows),
            heads(rows, 128),
            heads(rows, 128),
            pltpu.VMEM((rows, width), BF16),
            pltpu.VMEM((rows, width), BF16),
            heads(16, mlp_part),
            heads(16, mlp_part),
            total(mlp_part),
            heads(16, att_part),
            heads(16, att_part),
            total(att_part),
            sems(14),
            sems(2, 11),
            sems(2, 9),
            sems(2, 2, peers),
            sems(2, peers),
            sems(2, peers),
            sems(2, peers),
            sems(2, peers),
            sems(2, peers),
            sems(4, peers),
            sems(4, peers),
        ],
        compiler_params=pltpu.CompilerParams(
            collective_id=0, has_side_effects=True, vmem_limit_bytes=VMEM_LIMIT
        ),
        name="run_layer",
    )(index, tokens, cotangent, *weights, *tables, biases, value_bias, hidden_bias, gains)


def heads_body(
    tokens,
    cotangent,
    sequence_adapter_index,
    query_key_value_weight,
    output_weight,
    first_feed_weight,
    second_feed_weight,
    biases,
    value_bias_vector,
    first_feed_bias,
    norm_gain_pair,
    adapter_down_factors,
    output_down_factor,
    adapter_up_factors,
    hidden_up_factor,
    hidden_down_factor,
):
    width = tokens.shape[2]
    hidden = first_feed_bias.shape[0]
    adapter_number = adapter_down_factors.shape[0]
    outcome, grad_tokens, chosen, term_hd, term_uh, term_down, term_up, term_do, *_ = run_layer(
        sequence_adapter_index,
        tokens[0],
        cotangent[0],
        (query_key_value_weight, output_weight, first_feed_weight, second_feed_weight),
        (
            adapter_down_factors.reshape(-1, width),
            adapter_up_factors.reshape(-1, width),
            output_down_factor.reshape(-1, width),
            hidden_up_factor.reshape(-1, hidden),
            hidden_down_factor.reshape(-1, hidden),
        ),
        biases,
        value_bias_vector[None],
        first_feed_bias[None],
        norm_gain_pair,
    )
    tables = []
    for every in (term_down, term_do, term_up, term_uh, term_hd):
        table = 0.0
        for seq in range(2):
            mask = chosen[seq, :, 0].reshape((adapter_number,) + (1,) * (every.ndim - 1)) > 0.0
            table = table + jnp.where(mask, every[seq][None].astype(F32), 0.0)
        tables.append(table)
    return (outcome[None], grad_tokens[None], *tables)


def solution(mesh):
    one_head_each = mesh.shape["ctx"] == H and mesh.shape["fsdp"] == 2
    return jax.shard_map(
        heads_body if one_head_each else gather_body,
        mesh=mesh,
        in_specs=(
            P("fsdp", "ctx", None),
            P("fsdp", "ctx", None),
            P("fsdp"),
            P("fsdp", None),
            P("fsdp", None),
            P("fsdp", None),
            P("fsdp", None),
            P(),
            P(),
            P(),
            P(),
            P(),
            P(),
            P(),
            P(),
            P(),
        ),
        out_specs=(P("fsdp", "ctx", None), P("fsdp", "ctx", None), P(), P(), P(), P(), P()),
        check_vma=False,
    )
```

```python
import functools

import jax
import jax.numpy as jnp
from jax import lax
from jax.experimental import pallas as pl
from jax.experimental.pallas import tpu as pltpu
from jax.sharding import PartitionSpec as P

H = 16


EPSILON = 1e-05
HIGHEST = lax.Precision.HIGHEST


def exact_sum(form, left, right):
    return jnp.einsum(form, left, right, precision=HIGHEST, preferred_element_type=jnp.float32)


def plain_sum(form, left, right):
    return jnp.einsum(form, left, right, preferred_element_type=jnp.float32)


def layer_norm(value, gain, shift):
    center = value - jnp.mean(value, -1, keepdims=True)
    spread = jnp.mean(center * center, -1, keepdims=True)
    return center * lax.rsqrt(spread + EPSILON) * gain + shift


def attn_weights(query_key_value_weight, output_weight):
    return (
        lax.all_gather(query_key_value_weight, "fsdp", axis=0, tiled=True),
        lax.all_gather(output_weight, "fsdp", axis=0, tiled=True),
    )


def mlp_weights(first_feed_weight, second_feed_weight):
    return (
        lax.all_gather(first_feed_weight, "fsdp", axis=0, tiled=True),
        lax.all_gather(second_feed_weight, "fsdp", axis=0, tiled=True),
    )


def to_heads(input_array):
    return input_array.reshape(
        input_array.shape[0], input_array.shape[1], H, input_array.shape[2] // H
    )


def row_block(input_array, block_index, block_rows):
    return lax.dynamic_slice_in_dim(input_array, block_index * block_rows, block_rows, 1)


def block_grads(queries, grad_out, log_total, row_delta, keys_blk, values_blk):
    scores = plain_sum("sqhd,skhd->shqk", queries, keys_blk)
    probs = jnp.exp(scores - log_total[..., None])
    prob_low = probs.astype(jnp.bfloat16)
    grad_probs = plain_sum("sqhd,skhd->shqk", grad_out, values_blk)
    grad_scores = (probs * (grad_probs - row_delta[..., None])).astype(jnp.bfloat16)
    return (prob_low, grad_scores)


def attention_forward(queries_heads, keys_heads, values_heads):
    seq_count, row_count, head_count, head_size = queries_heads.shape
    length = keys_heads.shape[1]
    block_rows = min(512, length)
    block_count = length // block_rows

    def max_step(running, block_index):
        running_max, running_total = running
        scores = plain_sum(
            "sqhd,skhd->shqk", queries_heads, row_block(keys_heads, block_index, block_rows)
        )
        new_max = jnp.maximum(running_max, jnp.max(scores, -1))
        running_total = running_total * jnp.exp(running_max - new_max) + jnp.sum(
            jnp.exp(scores - new_max[..., None]), -1
        )
        return ((new_max, running_total), None)

    start_max = jnp.full((seq_count, head_count, row_count), -1e30, jnp.float32)
    start_total = jnp.zeros((seq_count, head_count, row_count), jnp.float32)
    (final_max, final_total), unused = lax.scan(
        max_step, (start_max, start_total), jnp.arange(block_count)
    )
    log_total = final_max + jnp.log(final_total)

    def value_step(running, block_index):
        scores = plain_sum(
            "sqhd,skhd->shqk", queries_heads, row_block(keys_heads, block_index, block_rows)
        )
        prob_low = jnp.exp(scores - log_total[..., None]).astype(jnp.bfloat16)
        return (
            running
            + plain_sum(
                "shqk,skhd->sqhd", prob_low, row_block(values_heads, block_index, block_rows)
            ),
            None,
        )

    context, unused = lax.scan(
        value_step, jnp.zeros(queries_heads.shape, jnp.float32), jnp.arange(block_count)
    )
    return (context, log_total)


def gather_body(
    tokens,
    cotangent,
    sequence_adapter_index,
    query_key_value_weight,
    output_weight,
    first_feed_weight,
    second_feed_weight,
    biases,
    value_bias_vector,
    first_feed_bias,
    norm_gain_pair,
    adapter_down_factors,
    output_down_factor,
    adapter_up_factors,
    hidden_up_factor,
    hidden_down_factor,
):
    seq_count, row_count, model_width = tokens.shape
    adapter_number = adapter_down_factors.shape[0]
    picker = (
        sequence_adapter_index[:, None] == jnp.arange(adapter_number, dtype=jnp.int32)[None, :]
    ).astype(jnp.float32)

    def select_adapter(table):
        return jnp.einsum("sa,a...->s...", picker, table.astype(jnp.float32), precision=HIGHEST)

    def to_adapters(per_seq):
        return jnp.einsum("sa,s...->a...", picker, per_seq, precision=HIGHEST)

    selected_down = select_adapter(adapter_down_factors)
    selected_output = select_adapter(output_down_factor)
    selected_up = select_adapter(adapter_up_factors)
    hup_sel = select_adapter(hidden_up_factor)
    hdown_sel = select_adapter(hidden_down_factor)
    down_low = selected_down.astype(jnp.bfloat16)
    out_low = selected_output.astype(jnp.bfloat16)
    hdown_low = hdown_sel.astype(jnp.bfloat16)
    wqkv_full, wout_full = attn_weights(query_key_value_weight, output_weight)
    projected = plain_sum("std,de->ste", tokens, wqkv_full)
    down_att = plain_sum("std,sjrd->sjtr", tokens, down_low[:, :3])
    lifted = exact_sum("sjtr,sjrd->sjtd", down_att, selected_up[:, :3])
    queries = ((projected[..., :model_width] + biases[0] + lifted[:, 0]) * 0.125).astype(
        jnp.bfloat16
    )
    keys_own = (projected[..., model_width : 2 * model_width] + lifted[:, 1]).astype(jnp.bfloat16)
    values_own = (projected[..., 2 * model_width :] + value_bias_vector + lifted[:, 2]).astype(
        jnp.bfloat16
    )
    keys_all, values_all = (
        lax.all_gather(keys_own, "ctx", axis=1, tiled=True),
        lax.all_gather(values_own, "ctx", axis=1, tiled=True),
    )
    queries_heads = to_heads(queries)
    keys_heads = to_heads(keys_all)
    values_heads = to_heads(values_all)
    context, log_total = attention_forward(queries_heads, keys_heads, values_heads)
    context = context.reshape(seq_count, row_count, model_width)
    context_low = context.astype(jnp.bfloat16)
    down_out = plain_sum("std,srd->str", context_low, out_low)
    branch = (
        plain_sum("std,de->ste", context_low, wout_full)
        + biases[1]
        + exact_sum("str,srd->std", down_out, selected_up[:, 3])
    )

    def first_norm(value):
        return layer_norm(value, norm_gain_pair[0], biases[3])

    def second_norm(value):
        return layer_norm(value, norm_gain_pair[1], biases[4])

    def gelu_exact(value):
        return jax.nn.gelu(value, approximate=False)

    normed, norm_back = jax.vjp(first_norm, tokens.astype(jnp.float32) + branch)
    normed_low = normed.astype(jnp.bfloat16)
    wfc1_full, wfc2_full = mlp_weights(first_feed_weight, second_feed_weight)
    down_fc1 = plain_sum("std,srd->str", normed_low, down_low[:, 3])
    hidden_pre = (
        plain_sum("std,df->stf", normed_low, wfc1_full)
        + first_feed_bias
        + exact_sum("str,srf->stf", down_fc1, hup_sel)
    )
    activated, gelu_back = jax.vjp(gelu_exact, hidden_pre)
    act_low = activated.astype(jnp.bfloat16)
    down_fc2 = plain_sum("stf,srf->str", act_low, hdown_low)
    mixed_out = (
        plain_sum("stf,fd->std", act_low, wfc2_full)
        + biases[2]
        + exact_sum("str,srd->std", down_fc2, selected_up[:, 4])
    )
    outcome, out_back = jax.vjp(second_norm, normed + mixed_out)
    (grad_sum2,) = out_back(cotangent.astype(jnp.float32))
    grad_mixed = grad_sum2.astype(jnp.bfloat16)
    grad_up_fc2 = exact_sum("str,std->srd", down_fc2, grad_mixed)
    grad_rank_fc2 = exact_sum("std,srd->str", grad_mixed, selected_up[:, 4]).astype(jnp.bfloat16)
    grad_hdown = plain_sum("str,stf->srf", grad_rank_fc2, act_low)
    wfc1_full, wfc2_full = mlp_weights(first_feed_weight, second_feed_weight)
    grad_act = (
        plain_sum("std,fd->stf", grad_mixed, wfc2_full)
        + plain_sum("str,srf->stf", grad_rank_fc2, hdown_low)
    ).astype(jnp.bfloat16)
    (grad_hidden,) = gelu_back(grad_act.astype(jnp.float32))
    grad_hidden = grad_hidden.astype(jnp.bfloat16)
    grad_hup = exact_sum("str,stf->srf", down_fc1, grad_hidden)
    grad_rank_fc1 = exact_sum("stf,srf->str", grad_hidden, hup_sel).astype(jnp.bfloat16)
    grad_down_fc1 = plain_sum("str,std->srd", grad_rank_fc1, normed_low)
    grad_normed_low = (
        plain_sum("stf,df->std", grad_hidden, wfc1_full)
        + plain_sum("str,srd->std", grad_rank_fc1, down_low[:, 3])
    ).astype(jnp.bfloat16)
    (grad_resid,) = norm_back(grad_sum2 + grad_normed_low.astype(jnp.float32))
    mlp_hup = to_adapters(grad_hup)
    mlp_hdown = to_adapters(grad_hdown)
    mlp_fc1 = to_adapters(grad_down_fc1)
    mlp_fc2 = to_adapters(grad_up_fc2)
    mlp_hup, mlp_hdown, mlp_fc1, mlp_fc2 = lax.psum(
        (mlp_hup, mlp_hdown, mlp_fc1, mlp_fc2), ("ctx", "fsdp")
    )
    grad_branch = grad_resid.astype(jnp.bfloat16)
    grad_up_out = exact_sum("str,std->srd", down_out, grad_branch)
    grad_rank_out = exact_sum("std,srd->str", grad_branch, selected_up[:, 3]).astype(jnp.bfloat16)
    grad_out_down = plain_sum("str,std->srd", grad_rank_out, context_low)
    wqkv_full, wout_full = attn_weights(query_key_value_weight, output_weight)
    grad_context = (
        plain_sum("std,ed->ste", grad_branch, wout_full)
        + plain_sum("str,srd->std", grad_rank_out, out_low)
    ).astype(jnp.bfloat16)
    row_delta = jnp.sum(to_heads(grad_context.astype(jnp.float32) * context), -1)
    delta_heads = jnp.swapaxes(row_delta, 1, 2)
    grad_heads = to_heads(grad_context)
    length = keys_all.shape[1]
    block_rows = min(512, length)
    block_count = length // block_rows

    def key_step(block_index, running):
        grad_query, grad_key, grad_value = running
        keys_blk = row_block(keys_heads, block_index, block_rows)
        values_blk = row_block(values_heads, block_index, block_rows)
        prob_low, grad_scores = block_grads(
            queries_heads, grad_heads, log_total, delta_heads, keys_blk, values_blk
        )
        grad_query = grad_query + plain_sum("shqk,skhd->sqhd", grad_scores, keys_blk)
        grad_key = lax.dynamic_update_slice_in_dim(
            grad_key,
            plain_sum("shqk,sqhd->skhd", grad_scores, queries_heads),
            block_index * block_rows,
            1,
        )
        grad_value = lax.dynamic_update_slice_in_dim(
            grad_value,
            plain_sum("shqk,sqhd->skhd", prob_low, grad_heads),
            block_index * block_rows,
            1,
        )
        return (grad_query, grad_key, grad_value)

    start_query = jnp.zeros(queries_heads.shape, jnp.float32)
    start_keys = jnp.zeros(keys_heads.shape, jnp.float32)
    grad_query, grad_key_all, grad_value_all = lax.fori_loop(
        0, block_count, key_step, (start_query, start_keys, start_keys)
    )
    grad_keys, grad_values = (
        lax.psum_scatter(
            grad_key_all.reshape(seq_count, length, model_width).astype(jnp.bfloat16),
            "ctx",
            scatter_dimension=1,
            tiled=True,
        ).astype(jnp.float32),
        lax.psum_scatter(
            grad_value_all.reshape(seq_count, length, model_width).astype(jnp.bfloat16),
            "ctx",
            scatter_dimension=1,
            tiled=True,
        ).astype(jnp.float32),
    )
    grad_qlin = grad_query.reshape(seq_count, row_count, model_width).astype(jnp.bfloat16) * 0.125
    grad_key_low = grad_keys.astype(jnp.bfloat16)
    grad_value_low = grad_values.astype(jnp.bfloat16)
    stacked = jnp.stack([grad_qlin, grad_key_low, grad_value_low], 1)
    grad_up_att = exact_sum("sjtr,sjtd->sjrd", down_att, stacked)
    grad_rank_att = exact_sum("sjtd,sjrd->sjtr", stacked, selected_up[:, :3]).astype(jnp.bfloat16)
    grad_down_att = plain_sum("sjtr,std->sjrd", grad_rank_att, tokens)
    joined = jnp.concatenate([grad_qlin, grad_key_low, grad_value_low], -1)
    grad_tokens = (
        grad_resid
        + plain_sum("ste,de->std", joined, wqkv_full)
        + plain_sum("sjtr,sjrd->std", grad_rank_att, down_low[:, :3])
    )
    attn_down = to_adapters(grad_down_att)
    attn_out = to_adapters(grad_out_down)
    attn_up = to_adapters(jnp.concatenate([grad_up_att, grad_up_out[:, None]], 1))
    attn_down, attn_out, attn_up = lax.psum((attn_down, attn_out, attn_up), ("ctx", "fsdp"))
    total_down = jnp.concatenate([attn_down, mlp_fc1[:, None]], 1)
    total_up = jnp.concatenate([attn_up, mlp_fc2[:, None]], 1)
    return (
        outcome.astype(jnp.bfloat16),
        grad_tokens,
        total_down,
        attn_out,
        total_up,
        mlp_hup,
        mlp_hdown,
    )


BF16 = jnp.bfloat16
F32 = jnp.float32
LOG2E = 1.4426950408889634
VMEM_LIMIT = 60 * 2**20
MESH = pl.DeviceIdType.MESH


def dot32(left, right):
    return jnp.dot(left, right, preferred_element_type=F32)


def dot_nt(left, right):
    return lax.dot_general(left, right, (((1,), (1,)), ((), ())), preferred_element_type=F32)


def dot_tn(left, right):
    return lax.dot_general(left, right, (((0,), (0,)), ((), ())), preferred_element_type=F32)


def split_three(value):
    high = value.astype(BF16)
    rest = value - high.astype(F32)
    middle = rest.astype(BF16)
    return high, middle, (rest - middle.astype(F32)).astype(BF16)


def flip(value):
    return value.astype(F32).T.astype(BF16)


def remote(src, dst, send_sem, recv_sem, device):
    return pltpu.make_async_remote_copy(
        src_ref=src,
        dst_ref=dst,
        send_sem=send_sem,
        recv_sem=recv_sem,
        device_id=device,
        device_id_type=MESH,
    )


class Place:
    def __init__(self):
        self.ctx = lax.axis_index("ctx")
        self.core = lax.axis_index("fsdp")
        self.half = self.ctx // (H // 2)
        self.low = self.ctx % (H // 2)
        self.me = self.low * 2 + self.core
        self.swaps = self.core != self.half
        self.pair = (self.core + self.half) % 2
        self.sibling = (self.ctx, 1 - self.core)
        self.partner = ((self.ctx + H // 2) % H, 1 - self.core)

    def peer(self, step):
        number = self.me ^ step
        return (self.half * (H // 2) + number // 2, number % 2)

    def order(self, turn):
        return 2 * (turn % (H // 2)) + (turn // (H // 2) + self.pair) % 2

    def greet(self):
        barrier = pltpu.get_barrier_semaphore()
        for step in range(1, H):
            pl.semaphore_signal(barrier, inc=1, device_id=self.peer(step), device_id_type=MESH)
        pl.semaphore_signal(barrier, inc=1, device_id=self.partner, device_id_type=MESH)
        pl.semaphore_wait(barrier, H)


def sum_copies(mine, parts, total, sems, place):
    own = total.at[place.pair, place.low, place.half]
    other = total.at[place.pair, place.low, 1 - place.half]
    column = total.at[place.pair]
    scatter = [
        remote(mine.at[place.me ^ step], parts.at[step], sems.at[0, step], sems.at[1, step], place.peer(step))
        for step in range(1, H)
    ]
    cross = remote(own, own, sems.at[0, 0], sems.at[1, 0], place.partner)
    first = [
        remote(own, own, sems.at[2, step], sems.at[3, step], place.peer(step))
        for step in range(2, H, 2)
    ]
    second = [
        remote(other, other, sems.at[2, step + 1], sems.at[3, step + 1], place.peer(step))
        for step in range(2, H, 2)
    ]
    last = remote(column, column, sems.at[2, 0], sems.at[3, 0], place.sibling)
    return scatter, cross, first, second, last


def sum_parts(scatter, mine, parts, total, place):
    value = mine[place.me].astype(F32)
    for step, copy in enumerate(scatter, 1):
        copy.wait_recv()
        value = value + parts[step].astype(F32)
    total[place.pair, place.low, place.half] = value.astype(BF16)


def put_term(mine, base, term):
    units = mine.shape[2] // 128
    for unit in range(term.shape[1] // 128):
        at = base // 128 + unit
        lanes = slice(at % units * 128, at % units * 128 + 128)
        mine[at // units, :, lanes] = term[:, unit * 128 : unit * 128 + 128].astype(BF16)


def layer_kernel(
    block_q,
    block_k,
    index_ref,
    tokens_ref,
    cotangent_ref,
    wqkv_ref,
    wout_ref,
    wfc1_ref,
    wfc2_ref,
    down_table,
    up_table,
    out_down_table,
    hidden_up_table,
    hidden_down_table,
    biases_ref,
    value_bias_ref,
    hidden_bias_ref,
    gains_ref,
    outcome_ref,
    grad_ref,
    chosen_out,
    hidden_down_out,
    hidden_up_out,
    down_out,
    up_out,
    out_down_out,
    wqkv_far,
    wfc1_far,
    wide,
    wfc2,
    wout,
    big,
    act,
    small,
    small_hidden,
    x,
    cotangent,
    rank_att,
    outgoing,
    qkv,
    leaving,
    arrived,
    incoming,
    context,
    state,
    qta,
    gta,
    kk,
    vv,
    kt,
    both,
    dkv_sum,
    dq_in,
    dkv_out,
    dkv_in,
    grad_out,
    grad_in,
    mlp_mine,
    mlp_parts,
    mlp_total,
    att_mine,
    att_parts,
    att_total,
    load_sem,
    core_sem,
    swap_sem,
    kv_sem,
    q_sem,
    back_sem,
    grad_sem,
    dq_sem,
    dkv_sem,
    mlp_sem,
    att_sem,
):
    peers, _, rows = qkv.shape
    length = peers * rows
    width = x.shape[1]
    hidden = hidden_bias_ref.shape[1]
    adapters = hidden_up_table.shape[0] // 16
    place = Place()
    me, core = place.me, place.core
    other = 1 - core
    wqkv = wide.at[:, 0 : 3 * width]
    up_at = down_table.shape[0]
    out_down_at = up_at + up_table.shape[0]

    def half_of(full, owner):
        count = full.shape[0] // 2
        return full.at[pl.ds(pl.multiple_of(owner * count, count), count), :]

    def load(source, target, number):
        return pltpu.make_async_copy(source, target, load_sem.at[number])

    def to_sibling(source, target, number):
        return remote(source, target, core_sem.at[0, number], core_sem.at[1, number], place.sibling)

    load_wqkv = load(wqkv_ref, half_of(wqkv, core), 0)
    load_wout = load(wout_ref, half_of(wout, core), 1)
    load_tables = [
        load(down_table, wfc2.at[0:up_at], 2),
        load(up_table, wfc2.at[up_at:out_down_at], 3),
        load(out_down_table, wfc2.at[out_down_at : out_down_at + out_down_table.shape[0]], 4),
        load(hidden_up_table, act.at[0 : 16 * adapters], 5),
        load(hidden_down_table, act.at[16 * adapters : 32 * adapters], 6),
    ]
    load_x = load(tokens_ref, x, 7)
    load_cotangent = load(cotangent_ref, cotangent, 8)
    load_wfc1 = load(wfc1_ref, half_of(wide, core), 9)
    load_wfc1_far = load(wfc1_far, half_of(wide, other), 10)
    load_wfc2 = load(wfc2_ref, half_of(wfc2, core), 11)
    again_wqkv = load(wqkv_ref, half_of(wqkv, core), 12)
    again_wqkv_far = load(wqkv_far, half_of(wqkv, other), 13)
    give_wqkv = to_sibling(wqkv_ref, half_of(wqkv, core), 0)
    give_wout = to_sibling(wout_ref, half_of(wout, core), 1)
    give_chosen = to_sibling(chosen_out.at[core], chosen_out.at[core], 2)
    count = small.shape[0]
    give_small = [to_sibling(small, wide.at[0:count, 3 * width : 4 * width], 3)] + [
        to_sibling(
            small_hidden.at[:, part * width : (part + 1) * width],
            wide.at[count + 32 * part : count + 32 * part + 32, 3 * width : 4 * width],
            4 + part,
        )
        for part in range(hidden // width)
    ]
    give_wfc2 = to_sibling(wfc2_ref, half_of(wfc2, core), 8)
    give_wfc1 = to_sibling(wfc1_ref, wfc1_far, 9)
    give_wqkv_again = to_sibling(wqkv_ref, wqkv_far, 10)
    half_rows = rows // 2
    swap_x = [
        remote(
            tokens_ref.at[part * half_rows : (part + 1) * half_rows],
            x.at[part * half_rows : (part + 1) * half_rows],
            swap_sem.at[0, 7 + part],
            swap_sem.at[1, 7 + part],
            place.partner,
        )
        for part in range(2)
    ]
    swap_cotangent = remote(cotangent_ref, cotangent, swap_sem.at[0, 1], swap_sem.at[1, 1], place.partner)

    load_wqkv.start()
    for copy in load_tables:
        copy.start()
    load_wout.start()

    @pl.when(jnp.logical_not(place.swaps))
    def _():
        load_x.start()
        load_cotangent.start()

    adapter = index_ref[0]
    numbers = lax.broadcasted_iota(jnp.int32, chosen_out.shape[1:], 0)
    chosen_out[core] = (numbers == jnp.full(numbers.shape, adapter, jnp.int32)).astype(F32)
    place.greet()

    @pl.when(place.swaps)
    def _():
        for copy in swap_x:
            copy.start()

    give_wqkv.start()
    give_chosen.start()

    for copy in load_tables:
        copy.wait()

    def select(table, base, group, groups, target, at):
        chosen = jnp.full((16, table.shape[1]), adapter, jnp.int32)
        value = jnp.zeros((16, table.shape[1]), F32)
        for number in range(adapters):
            start = pl.multiple_of(base + 16 * (number * groups + group), 16)
            value = jnp.where(chosen == number, table[pl.ds(start, 16), :].astype(F32), value)
        target[pl.ds(pl.multiple_of(at + 16 * group, 16), 16), :] = value.astype(BF16)

    def select_down(group, _):
        select(wfc2, 0, group, 4, small, 0)
        return 0

    def select_up(group, _):
        select(wfc2, up_at, group, 5, small, 64)
        return 0

    lax.fori_loop(0, 4, select_down, 0)
    lax.fori_loop(0, 5, select_up, 0)
    select(wfc2, out_down_at, 0, 1, small, 144)
    for part in range(2):
        select(act, 16 * adapters * part, 0, 1, small_hidden, 16 * part)
    for copy in give_small:
        copy.start()
    give_wout.start()
    for copy in give_small:
        copy.wait()

    @pl.when(place.swaps)
    def _():
        small[...] = wide[0:count, 3 * width : 4 * width]
        for part in range(hidden // width):
            small_hidden[:, part * width : (part + 1) * width] = wide[
                count + 32 * part : count + 32 * part + 32, 3 * width : 4 * width
            ]

    hidden_up_ref = small_hidden.at[0:16]
    hidden_down_ref = small_hidden.at[16:32]
    out_down_ref = small.at[144:160]

    def down(j):
        return small[16 * j : 16 * j + 16]

    def up(j):
        return small[64 + 16 * j : 80 + 16 * j]

    load_wfc2.start()
    give_wfc2.start()

    load_wqkv.wait()
    give_wqkv.wait_recv()

    def project(half, part):
        here = slice(half * half_rows, (half + 1) * half_rows)
        cols = slice(part * width, (part + 1) * width)
        value = dot32(x[here, :], wqkv[:, cols]) + dot32(rank_att[here, part * 16 : part * 16 + 16], up(part))
        if part == 0:
            value = (value + biases_ref[0:1, :]) * 0.125
        if part == 2:
            value = value + value_bias_ref[...]
        for two in range(peers // 2):
            turned = value[:, two * 128 : two * 128 + 128].T.astype(BF16)
            outgoing[2 * two, part * 64 : part * 64 + 64, here] = turned[0:64]
            outgoing[2 * two + 1, part * 64 : part * 64 + 64, here] = turned[64:128]

    def kv_copy(step, half):
        here = slice(half * half_rows, (half + 1) * half_rows)
        return remote(
            outgoing.at[me ^ step, 64:192, here],
            qkv.at[step, 64:192, here],
            kv_sem.at[0, half, step],
            kv_sem.at[1, half, step],
            place.peer(step),
        )

    def q_copy(step):
        return remote(
            outgoing.at[me ^ step, 0:64], qkv.at[step, 0:64], q_sem.at[0, step], q_sem.at[1, step], place.peer(step)
        )

    def back_copy(step):
        return remote(leaving.at[step], arrived.at[me], back_sem.at[0, step], back_sem.at[1, step], place.peer(step))

    steps = length // block_k
    group = block_q // rows
    key_group = block_k // rows
    for half in range(2):
        here = slice(half * half_rows, (half + 1) * half_rows)

        @pl.when(place.swaps)
        def _():
            swap_x[half].wait_recv()

        if half == 0:

            @pl.when(jnp.logical_not(place.swaps))
            def _():
                load_x.wait()

        rank_att[here, :] = dot_nt(x[here, :], small[0:48]).astype(BF16)
        project(half, 1)
        project(half, 2)
        for step in range(1, peers):
            kv_copy(step, half).start()
        project(half, 0)
    for step in range(1, peers):
        q_copy(step).start()
    give_wfc1.start()
    give_wqkv_again.start()
    load_wfc1.start()
    qkv[0] = outgoing[me]

    row_at = lax.broadcasted_iota(jnp.int32, (16, rows), 0)
    ones = (row_at == 0).astype(F32).astype(BF16)
    minus = jnp.where(lax.broadcasted_iota(jnp.int32, (rows, 16), 1) < 3, -1.0, 0.0).astype(BF16)
    minus_rows = jnp.where(lax.broadcasted_iota(jnp.int32, (64, rows), 0) < 3, -1.0, 0.0).astype(BF16)

    def tail(value):
        at = lax.broadcasted_iota(jnp.int32, (16, value.shape[1]), 0)
        high, middle, low = (part.astype(F32) for part in split_three(value))
        return jnp.where(at == 0, high, jnp.where(at == 1, middle, jnp.where(at == 2, low, 0.0))).astype(BF16)

    def take_key(turn):
        cols = pl.ds(pl.multiple_of(turn * rows, rows), rows)
        step = place.order(turn)

        @pl.when(step > 0)
        def _():
            kv_copy(step, 0).wait_recv()
            kv_copy(step, 1).wait_recv()

        key = qkv[step, 64:128, :]
        value = qkv[step, 128:192, :]
        kt[:, cols] = key
        kk[cols, 0:128] = flip(jnp.concatenate([key, key], 0))
        kk[cols, 128:144] = minus
        vv[cols, :] = flip(jnp.concatenate([value, minus_rows], 0))
        gta[0:64, cols] = value
        gta[64:80, cols] = ones
        gta[80:128, cols] = jnp.zeros((48, rows), BF16)

    def take_keys(i):
        def one(part, _):
            take_key(i * key_group + part)
            return 0

        lax.fori_loop(0, key_group, one, 0)

    def forward_part(i, low, high, arriving):
        def take_query(part, _):
            turn = i * group + part
            step = place.order(turn)
            here = pl.ds(pl.multiple_of(turn * rows, rows), rows)

            @pl.when(step > 0)
            def _():
                q_copy(step).wait_recv()

            query = qkv[step, 0:64, :].astype(F32) * LOG2E
            high = query.astype(BF16)
            qta[0:64, here] = high
            qta[64:128, here] = (query - high.astype(F32)).astype(BF16)
            return 0

        if low == 0:
            lax.fori_loop(0, group, take_query, 0)
        cols = pl.ds(pl.multiple_of(i * block_q, block_q), block_q)
        query = qta.at[0:128, cols]
        if arriving:

            @pl.when(i == 0)
            def _():
                take_keys(low)

        block = dot32(kk[low * block_k : (low + 1) * block_k, 0:128], query[...])
        big[0:block_k] = block

        def half(j, now, carry):
            peak, running, total = carry
            later = jnp.minimum(j + 1, high - 1)
            here = pl.ds(pl.multiple_of(j * block_k, block_k), block_k)
            there = pl.ds(pl.multiple_of(later * block_k, block_k), block_k)
            if arriving:

                @pl.when(jnp.logical_and(i == 0, j + 1 < high))
                def _():
                    take_keys(later)

            ahead = dot32(kk[there, 0:128], query[...])
            big[(1 - now) * block_k : (2 - now) * block_k] = ahead
            new = jnp.maximum(running, peak)
            weights = jnp.exp2(big[now * block_k : (now + 1) * block_k] - new).astype(BF16)
            total = total * jnp.exp2(running - new) + dot32(gta[0:80, here], weights)
            return jnp.max(ahead, 0, keepdims=True), new, total

        def pair(j, carry):
            return half(low + 2 * j + 1, 1, half(low + 2 * j, 0, carry))

        if low == 0:
            running, total = jnp.full((1, block_q), -jnp.inf, F32), jnp.zeros((80, block_q), F32)
        else:
            running = state[1:2, cols]
            total = jnp.concatenate([context[:, cols], state[0:1, cols], jnp.zeros((15, block_q), F32)], 0)
        _, top, total = lax.fori_loop(
            0, (high - low) // 2, pair, (jnp.max(block, 0, keepdims=True), running, total)
        )
        weight_sum = total[64:65]
        if high < steps:
            context[:, cols] = total[0:64]
            state[0:1, cols] = weight_sum
            state[1:2, cols] = top
            return
        result = total[0:64] / weight_sum
        context[:, cols] = result
        qta[128:144, cols] = tail(top + jnp.log2(weight_sum))
        low_result = result.astype(BF16)
        for part in range(group):
            step = place.order(i * group + part)
            leaving[step] = low_result[:, part * rows : (part + 1) * rows]

            @pl.when(step > 0)
            def _():
                back_copy(step).start()

    query_steps = length // block_q

    def forward_parts(first, last, low, high, arriving):
        def one(i, _):
            forward_part(i, low, high, arriving)
            return 0

        lax.fori_loop(first, last, one, 0)

    forward_parts(0, query_steps // 2, 0, steps // 2, True)
    give_wfc1.wait_recv()
    load_wfc1_far.start()
    forward_parts(0, query_steps // 2, steps // 2, steps, True)

    @pl.when(place.swaps)
    def _():
        swap_cotangent.start()

    forward_parts(query_steps // 2, query_steps, 0, steps, False)
    arrived[me] = leaving[0]

    def mean(value):
        return jnp.mean(value, -1, keepdims=True)

    def norm_backward(grad, hat, scale):
        return scale * (grad - mean(grad) - hat * mean(grad * hat))

    load_wout.wait()
    give_wout.wait_recv()
    for step in range(1, peers):
        back_copy(step).wait_recv()
    context_low = flip(arrived[...].reshape(width, rows))
    rank_out = dot_nt(context_low, out_down_ref[...]).astype(BF16)
    resid = x[...].astype(F32) + dot32(context_low, wout[...]) + biases_ref[1:2] + dot32(rank_out, up(3))
    center = resid - mean(resid)
    scale_one = lax.rsqrt(mean(center * center) + EPSILON)
    hat_one = center * scale_one
    normed = hat_one * gains_ref[0:1] + biases_ref[3:4]
    normed_low = normed.astype(BF16)
    rank_one = dot_nt(normed_low, down(3)).astype(BF16)
    load_wfc1.wait()
    load_wfc1_far.wait()
    load_wfc2.wait()
    give_wfc2.wait_recv()
    piece = 1024
    rank_two = jnp.zeros((rows, 16), F32)
    mixed = normed + biases_ref[2:3]
    for part in range(hidden // piece):
        cols = slice(part * piece, (part + 1) * piece)
        pre = (
            dot32(normed_low, wide[:, cols])
            + hidden_bias_ref[:, cols]
            + dot32(rank_one, hidden_up_ref[:, cols])
        )
        share = 0.5 + 0.5 * lax.erf(pre * 0.7071067811865476)
        big[part * rows : (part + 1) * rows] = share + pre * (0.3989422804014327 * jnp.exp(-0.5 * pre * pre))
        active = (pre * share).astype(BF16)
        act[:, cols] = active
        rank_two = rank_two + dot_nt(active, hidden_down_ref[:, cols])
        mixed = mixed + dot32(active, wfc2[cols, :])
    rank_two = rank_two.astype(BF16)
    mixed = mixed + dot32(rank_two, up(4))
    center = mixed - mean(mixed)
    scale_two = lax.rsqrt(mean(center * center) + EPSILON)
    hat_two = center * scale_two

    @pl.when(place.swaps)
    def _():
        swap_cotangent.wait_recv()

    @pl.when(jnp.logical_not(place.swaps))
    def _():
        load_cotangent.wait()

    grad_sum = norm_backward(cotangent[...].astype(F32) * gains_ref[1:2], hat_two, scale_two)
    outcome = cotangent
    outcome[...] = (hat_two * gains_ref[1:2] + biases_ref[4:5]).astype(BF16)
    home_outcome = remote(outcome, outcome_ref, swap_sem.at[0, 2], swap_sem.at[1, 2], place.partner)

    @pl.when(place.swaps)
    def _():
        home_outcome.start()

    @pl.when(jnp.logical_not(place.swaps))
    def _():
        outcome_ref[...] = outcome[...]

    grad_mixed = grad_sum.astype(BF16)
    put_term(mlp_mine, 2 * hidden, dot_tn(rank_two, grad_mixed))
    grad_rank = dot_nt(grad_mixed, up(4)).astype(BF16)
    put_term(mlp_mine, 0, dot_tn(grad_rank, act[...]))
    grad_one = jnp.zeros((rows, 16), F32)
    grad_normed = jnp.zeros((rows, width), F32)
    for part in range(hidden // piece):
        cols = slice(part * piece, (part + 1) * piece)
        grad_act = dot_nt(grad_mixed, wfc2[cols, :]) + dot32(grad_rank, hidden_down_ref[:, cols])
        grad_hidden = (grad_act.astype(BF16).astype(F32) * big[part * rows : (part + 1) * rows]).astype(BF16)
        put_term(mlp_mine, hidden + part * piece, dot_tn(rank_one, grad_hidden))
        grad_one = grad_one + dot_nt(grad_hidden, hidden_up_ref[:, cols])
        grad_normed = grad_normed + dot_nt(grad_hidden, wide[:, cols])
    grad_one = grad_one.astype(BF16)
    put_term(mlp_mine, 2 * hidden + width, dot_tn(grad_one, normed_low))
    grad_normed = (grad_normed + dot32(grad_one, down(3))).astype(BF16).astype(F32)
    resid_grad = norm_backward((grad_sum + grad_normed) * gains_ref[0:1], hat_one, scale_one)
    grad_resid = big.at[0:rows]
    grad_resid[...] = resid_grad
    grad_branch = resid_grad.astype(BF16)
    put_term(mlp_mine, 2 * hidden + 2 * width, dot_tn(rank_out, grad_branch))
    grad_rank = dot_nt(grad_branch, up(3)).astype(BF16)
    put_term(mlp_mine, 2 * hidden + 3 * width, dot_tn(grad_rank, context_low))
    turned = dot_nt(wout[...], grad_branch) + lax.dot_general(
        out_down_ref[...], grad_rank, (((0,), (1,)), ((), ())), preferred_element_type=F32
    )
    for step in range(1, peers):
        kv_copy(step, 0).wait_send()
        kv_copy(step, 1).wait_send()
        q_copy(step).wait_send()
        back_copy(step).wait_send()
    outgoing[:, 0:64] = turned.astype(BF16).reshape(peers, 64, rows)

    def grad_copy(step):
        return remote(
            outgoing.at[me ^ step, 0:64], incoming.at[step], grad_sem.at[0, step], grad_sem.at[1, step], place.peer(step)
        )

    for step in range(1, peers):
        grad_copy(step).start()
    mlp_scatter, mlp_cross, mlp_first, mlp_second, mlp_last = sum_copies(mlp_mine, mlp_parts, mlp_total, mlp_sem, place)
    incoming[0] = outgoing[me, 0:64]
    give_wqkv_again.wait_recv()
    again_wqkv.start()
    again_wqkv_far.start()
    dkv_sum[...] = jnp.zeros_like(dkv_sum)
    first = lax.broadcasted_iota(jnp.int32, (block_k, 128), 1) < 64
    dq_out = leaving

    def dq_copy(step):
        return remote(dq_out.at[step], dq_in.at[me], dq_sem.at[0, step], dq_sem.at[1, step], place.peer(step))

    def dkv_copy(step):
        return remote(dkv_out.at[step], dkv_in.at[me], dkv_sem.at[0, step], dkv_sem.at[1, step], place.peer(step))

    def backward_step(turn, _):
        last = turn == query_steps - 1
        j = (turn + query_steps // 2) % query_steps

        def take_grad(part, _):
            step = place.order(j * group + part)
            cols = pl.ds(pl.multiple_of((j * group + part) * rows, rows), rows)

            @pl.when(step > 0)
            def _():
                grad_copy(step).wait_recv()

            grad = incoming[step]
            gta[0:64, cols] = grad
            gta[64:80, cols] = tail(jnp.sum(grad.astype(F32) * context[:, cols], 0, keepdims=True))
            both[cols, :] = flip(jnp.concatenate([qkv[step, 0:64, :], grad], 0))
            return 0

        lax.fori_loop(0, group, take_grad, 0)
        cols = pl.ds(pl.multiple_of(j * block_q, block_q), block_q)

        def key_pair(pair, dq):
            found = []
            for side in range(2):
                i = (2 * pair + side + steps // 2) % steps
                here = pl.ds(pl.multiple_of(i * block_k, block_k), block_k)
                probs = jnp.exp2(dot32(kk[here, :], qta[:, cols]))
                change = dot32(vv[here, :], gta[:, cols])
                found.append((i, here, probs.astype(BF16), (probs * change).astype(BF16)))
            for i, here, probs, low in found:
                dv = dot32(probs, both[cols, :])
                dk = dot32(low, both[cols, :])
                dkv_sum[here, :] += jnp.where(first, dk, dv)
                dq = dq + dot32(kt[:, here], low)

            @pl.when(last)
            def _():
                for i, here, _, _ in found:
                    done = dkv_sum[here, :].astype(BF16)
                    for part in range(key_group):
                        step = place.order(i * key_group + part)
                        dkv_out[step] = done[part * rows : (part + 1) * rows]

                        @pl.when(step > 0)
                        def _():
                            dkv_copy(step).start()

            return dq

        dq = lax.fori_loop(0, steps // 2, key_pair, jnp.zeros((64, block_q), F32)).astype(BF16)
        for part in range(group):
            step = place.order(j * group + part)
            dq_out[step] = dq[:, part * rows : (part + 1) * rows]

            @pl.when(step > 0)
            def _():
                dq_copy(step).start()

        @pl.when(turn == query_steps // 4 - 1)
        def _():
            for copy in mlp_scatter:
                copy.start()

        @pl.when(turn == query_steps // 2 - 1)
        def _():
            sum_parts(mlp_scatter, mlp_mine, mlp_parts, mlp_total, place)
            mlp_cross.start()
            for copy in mlp_first:
                copy.start()

        @pl.when(turn == query_steps - 2)
        def _():
            mlp_cross.wait_recv()
            for copy in mlp_second:
                copy.start()

        return 0

    lax.fori_loop(0, query_steps, backward_step, 0)
    for copy in mlp_first + mlp_second:
        copy.wait_recv()
    mlp_last.start()

    def spread(total, parts):
        units = total.shape[4] // 128
        for half in range(2):
            for unit in range(peers * units):
                peer = unit // units
                lanes = slice(unit % units * 128, unit % units * 128 + 128)
                for target, low, high in parts:
                    if low <= unit * 128 < high:
                        at = unit * 128 - low
                        target(half)[:, at : at + 128] = total[(peer % 2 + half) % 2, peer // 2, half, :, lanes]

    joined = act.at[:, 0 : 3 * width]
    dq_in[me] = dq_out[0]
    dkv_in[me] = dkv_out[0]
    for step in range(1, peers):
        dkv_copy(step).wait_recv()
    left = lax.broadcasted_iota(jnp.int32, (rows, 128), 1) < 64
    for two in range(peers // 2):
        even = dkv_in[2 * two].astype(F32)
        odd = dkv_in[2 * two + 1].astype(F32)
        cols = slice(width + two * 128, width + two * 128 + 128)
        joined[:, cols] = jnp.where(left, even, pltpu.roll(odd, 64, 1)).astype(BF16)
        cols = slice(2 * width + two * 128, 2 * width + two * 128 + 128)
        joined[:, cols] = jnp.where(left, pltpu.roll(even, 64, 1), odd).astype(BF16)
    def ranks_of(part):
        grad = joined[:, part * width : (part + 1) * width]
        ranks[part] = dot_nt(grad, up(part)).astype(BF16)

    def terms_of(part):
        grad = joined[:, part * width : (part + 1) * width]
        put_term(att_mine, part * width, dot_tn(rank_att[:, part * 16 : part * 16 + 16], grad))
        put_term(att_mine, (3 + part) * width, dot_tn(ranks[part], x[...]))

    ranks = {}
    att_scatter, att_cross, att_first, att_second, att_last = sum_copies(att_mine, att_parts, att_total, att_sem, place)
    again_wqkv.wait()
    again_wqkv_far.wait()
    for part in (1, 2):
        ranks_of(part)
        terms_of(part)
    for step in range(1, peers):
        dq_copy(step).wait_recv()
    joined[:, 0:width] = (dq_in[...].reshape(width, rows).astype(F32).T * 0.125).astype(BF16)
    ranks_of(0)
    terms_of(0)
    for copy in att_scatter:
        copy.start()
    piece = width // 4
    home = [
        remote(
            grad_out.at[:, part * piece : (part + 1) * piece],
            grad_in.at[:, part * piece : (part + 1) * piece],
            swap_sem.at[0, 3 + part],
            swap_sem.at[1, 3 + part],
            place.partner,
        )
        for part in range(4)
    ]
    mlp_last.wait_recv()
    for part in range(4):
        cols = slice(part * piece, (part + 1) * piece)
        total = grad_resid[:, cols] + dot_nt(joined[...], wqkv[cols, :])
        for j in range(3):
            total = total + dot32(ranks[j], small[16 * j : 16 * j + 16, cols])
        grad_ref[:, cols] = total
        grad_out[:, cols] = total.astype(BF16)

        @pl.when(place.swaps)
        def _():
            home[part].start()

    sum_parts(att_scatter, att_mine, att_parts, att_total, place)
    att_cross.start()
    for copy in att_first:
        copy.start()
    spread(
        mlp_total,
        (
            (lambda half: hidden_down_out.at[half], 0, hidden),
            (lambda half: hidden_up_out.at[half], hidden, 2 * hidden),
            (lambda half: up_out.at[half, 4], 2 * hidden, 2 * hidden + width),
            (lambda half: down_out.at[half, 3], 2 * hidden + width, 2 * hidden + 2 * width),
            (lambda half: up_out.at[half, 3], 2 * hidden + 2 * width, 2 * hidden + 3 * width),
            (lambda half: out_down_out.at[half], 2 * hidden + 3 * width, 2 * hidden + 4 * width),
        ),
    )
    att_cross.wait_recv()
    for copy in att_second:
        copy.start()
    for copy in att_first + att_second:
        copy.wait_recv()
    att_last.start()

    @pl.when(place.swaps)
    def _():
        for part in range(4):
            home[part].wait_recv()
            cols = slice(part * piece, (part + 1) * piece)
            grad_ref[:, cols] = grad_in[:, cols].astype(F32)
        for part in range(4):
            home[part].wait_send()
        home_outcome.wait()
        for copy in swap_x:
            copy.wait_send()
        swap_cotangent.wait_send()

    att_last.wait_recv()
    spread(
        att_total,
        tuple(
            (functools.partial(lambda part, half: up_out.at[half, part], part), part * width, (part + 1) * width)
            for part in range(3)
        )
        + tuple(
            (functools.partial(lambda part, half: down_out.at[half, part], part), (3 + part) * width, (4 + part) * width)
            for part in range(3)
        ),
    )
    for step in range(1, peers):
        grad_copy(step).wait_send()
        dq_copy(step).wait_send()
        dkv_copy(step).wait_send()
    for copies in ((mlp_scatter, mlp_first, mlp_second), (att_scatter, att_first, att_second)):
        for copy in copies[0] + copies[1] + copies[2]:
            copy.wait_send()
    for copy in (mlp_cross, mlp_last, att_cross, att_last):
        copy.wait_send()
    for copy in (give_wqkv, give_wout, give_wfc2, give_wfc1, give_wqkv_again):
        copy.wait_send()
    give_chosen.wait()


def run_layer(index, tokens, cotangent, weights, tables, biases, value_bias, hidden_bias, gains):
    rows, width = tokens.shape
    peers = H
    length = peers * rows
    hidden = hidden_bias.shape[1]
    block_q, block_k = 1024, 512
    vmem = pl.BlockSpec(memory_space=pltpu.VMEM)
    hbm = pl.BlockSpec(memory_space=pl.ANY)
    mlp_part = (2 * hidden + 4 * width) // peers
    att_part = 6 * width // peers

    def out(shape, dtype=BF16):
        return jax.ShapeDtypeStruct(shape, dtype)

    def total(part):
        return pltpu.VMEM((2, peers // 2, 2, 16, part), BF16)

    def heads(*shape):
        return pltpu.VMEM((peers,) + shape, BF16)

    def sems(*shape):
        return pltpu.SemaphoreType.DMA(shape)

    return pl.pallas_call(
        functools.partial(layer_kernel, block_q, block_k),
        out_shape=[
            out((rows, width)),
            out((rows, width), F32),
            out((2, 8, 128), F32),
            out((2, 16, hidden)),
            out((2, 16, hidden)),
            out((2, 4, 16, width)),
            out((2, 5, 16, width)),
            out((2, 16, width)),
            out(weights[0].shape),
            out(weights[2].shape),
        ],
        in_specs=[pl.BlockSpec(memory_space=pltpu.SMEM)] + [hbm] * 11 + [vmem] * 4,
        out_specs=[vmem] * 8 + [hbm] * 2,
        scratch_shapes=[
            pltpu.VMEM((width, hidden), BF16),
            pltpu.VMEM((hidden, width), BF16),
            pltpu.VMEM((width, width), BF16),
            pltpu.VMEM((max(4 * rows, 2 * block_k), 1024), F32),
            pltpu.VMEM((rows, hidden), BF16),
            pltpu.VMEM((160, width), BF16),
            pltpu.VMEM((32, hidden), BF16),
            pltpu.VMEM((rows, width), BF16),
            pltpu.VMEM((rows, width), BF16),
            pltpu.VMEM((rows, 48), BF16),
            heads(192, rows),
            heads(192, rows),
            heads(64, rows),
            heads(64, rows),
            heads(64, rows),
            pltpu.VMEM((64, length), F32),
            pltpu.VMEM((8, length), F32),
            pltpu.VMEM((144, length), BF16),
            pltpu.VMEM((128, length), BF16),
            pltpu.VMEM((length, 144), BF16),
            pltpu.VMEM((length, 128), BF16),
            pltpu.VMEM((64, length), BF16),
            pltpu.VMEM((length, 128), BF16),
            pltpu.VMEM((length, 128), F32),
            heads(64, rows),
            heads(rows, 128),
            heads(rows, 128),
            pltpu.VMEM((rows, width), BF16),
            pltpu.VMEM((rows, width), BF16),
            heads(16, mlp_part),
            heads(16, mlp_part),
            total(mlp_part),
            heads(16, att_part),
            heads(16, att_part),
            total(att_part),
            sems(14),
            sems(2, 11),
            sems(2, 9),
            sems(2, 2, peers),
            sems(2, peers),
            sems(2, peers),
            sems(2, peers),
            sems(2, peers),
            sems(2, peers),
            sems(4, peers),
            sems(4, peers),
        ],
        compiler_params=pltpu.CompilerParams(
            collective_id=0, has_side_effects=True, vmem_limit_bytes=VMEM_LIMIT
        ),
        name="run_layer",
    )(index, tokens, cotangent, *weights, *tables, biases, value_bias, hidden_bias, gains)


def assemble_kernel(
    chosen_ref, down_in, out_down_in, up_in, hidden_up_in, hidden_down_in, outcome_in, grad_in, outcome_out, grad_out, *tables
):
    sources = (down_in, out_down_in, up_in, hidden_up_in, hidden_down_in)
    group = tables[0].shape[0]
    for part in range(group):
        number = pl.program_id(0) * group + part
        masks = [chosen_ref[seq, pl.ds(number, 1), 0:1] > 0.0 for seq in range(2)]
        for source, table in zip(sources, tables):
            for i in range(source.shape[1]):
                value = jnp.zeros(source.shape[2:], F32)
                for seq, mask in enumerate(masks):
                    value = value + jnp.where(mask, source[seq, i].astype(F32), 0.0)
                table[part, i] = value
    outcome_out[...] = outcome_in[...]
    grad_out[...] = grad_in[...]


def assemble(chosen, terms, outcome, grad_tokens):
    adapters = chosen.shape[1]
    steps = adapters // 2
    block = outcome.shape[0] // steps
    inputs = (chosen, *(term.reshape((2, -1) + term.shape[-2:]) for term in terms))

    def whole(array):
        return pl.BlockSpec(array.shape, lambda i: (0,) * array.ndim)

    def part(shape):
        return pl.BlockSpec(shape, lambda i: (i,) + (0,) * (len(shape) - 1))

    rows_spec = part((block, outcome.shape[1]))
    tables = [term.shape[1:] for term in inputs[1:]]
    return pl.pallas_call(
        assemble_kernel,
        grid=(steps,),
        out_shape=[
            jax.ShapeDtypeStruct(outcome.shape, BF16),
            jax.ShapeDtypeStruct(grad_tokens.shape, F32),
            *(jax.ShapeDtypeStruct((adapters,) + shape, F32) for shape in tables),
        ],
        in_specs=[*(whole(array) for array in inputs), rows_spec, rows_spec],
        out_specs=[rows_spec, rows_spec, *(part((adapters // steps,) + shape) for shape in tables)],
        compiler_params=pltpu.CompilerParams(vmem_limit_bytes=VMEM_LIMIT),
        name="assemble",
    )(*inputs, outcome, grad_tokens)


def heads_body(
    tokens,
    cotangent,
    sequence_adapter_index,
    query_key_value_weight,
    output_weight,
    first_feed_weight,
    second_feed_weight,
    biases,
    value_bias_vector,
    first_feed_bias,
    norm_gain_pair,
    adapter_down_factors,
    output_down_factor,
    adapter_up_factors,
    hidden_up_factor,
    hidden_down_factor,
):
    width = tokens.shape[2]
    hidden = first_feed_bias.shape[0]
    outcome, grad_tokens, chosen, term_hd, term_uh, term_down, term_up, term_do, *_ = run_layer(
        sequence_adapter_index,
        tokens[0],
        cotangent[0],
        (query_key_value_weight, output_weight, first_feed_weight, second_feed_weight),
        (
            adapter_down_factors.reshape(-1, width),
            adapter_up_factors.reshape(-1, width),
            output_down_factor.reshape(-1, width),
            hidden_up_factor.reshape(-1, hidden),
            hidden_down_factor.reshape(-1, hidden),
        ),
        biases,
        value_bias_vector[None],
        first_feed_bias[None],
        norm_gain_pair,
    )
    outcome, grad_tokens, total_down, total_out_down, total_up, total_hidden_up, total_hidden_down = assemble(
        chosen, (term_down, term_do, term_up, term_uh, term_hd), outcome, grad_tokens
    )
    return (
        outcome[None],
        grad_tokens[None],
        total_down,
        total_out_down.reshape(output_down_factor.shape),
        total_up,
        total_hidden_up.reshape(hidden_up_factor.shape),
        total_hidden_down.reshape(hidden_down_factor.shape),
    )


def solution(mesh):
    one_head_each = mesh.shape["ctx"] == H and mesh.shape["fsdp"] == 2
    return jax.shard_map(
        heads_body if one_head_each else gather_body,
        mesh=mesh,
        in_specs=(
            P("fsdp", "ctx", None),
            P("fsdp", "ctx", None),
            P("fsdp"),
            P("fsdp", None),
            P("fsdp", None),
            P("fsdp", None),
            P("fsdp", None),
            P(),
            P(),
            P(),
            P(),
            P(),
            P(),
            P(),
            P(),
            P(),
        ),
        out_specs=(P("fsdp", "ctx", None), P("fsdp", "ctx", None), P(), P(), P(), P(), P()),
        check_vma=False,
    )
```

```python
import functools

import jax
import jax.numpy as jnp
from jax import lax
from jax.experimental import pallas as pl
from jax.experimental.pallas import tpu as pltpu
from jax.sharding import PartitionSpec as P

H = 16


EPSILON = 1e-05
HIGHEST = lax.Precision.HIGHEST


def exact_sum(form, left, right):
    return jnp.einsum(form, left, right, precision=HIGHEST, preferred_element_type=jnp.float32)


def plain_sum(form, left, right):
    return jnp.einsum(form, left, right, preferred_element_type=jnp.float32)


def layer_norm(value, gain, shift):
    center = value - jnp.mean(value, -1, keepdims=True)
    spread = jnp.mean(center * center, -1, keepdims=True)
    return center * lax.rsqrt(spread + EPSILON) * gain + shift


def attn_weights(query_key_value_weight, output_weight):
    return (
        lax.all_gather(query_key_value_weight, "fsdp", axis=0, tiled=True),
        lax.all_gather(output_weight, "fsdp", axis=0, tiled=True),
    )


def mlp_weights(first_feed_weight, second_feed_weight):
    return (
        lax.all_gather(first_feed_weight, "fsdp", axis=0, tiled=True),
        lax.all_gather(second_feed_weight, "fsdp", axis=0, tiled=True),
    )


def to_heads(input_array):
    return input_array.reshape(
        input_array.shape[0], input_array.shape[1], H, input_array.shape[2] // H
    )


def row_block(input_array, block_index, block_rows):
    return lax.dynamic_slice_in_dim(input_array, block_index * block_rows, block_rows, 1)


def block_grads(queries, grad_out, log_total, row_delta, keys_blk, values_blk):
    scores = plain_sum("sqhd,skhd->shqk", queries, keys_blk)
    probs = jnp.exp(scores - log_total[..., None])
    prob_low = probs.astype(jnp.bfloat16)
    grad_probs = plain_sum("sqhd,skhd->shqk", grad_out, values_blk)
    grad_scores = (probs * (grad_probs - row_delta[..., None])).astype(jnp.bfloat16)
    return (prob_low, grad_scores)


def attention_forward(queries_heads, keys_heads, values_heads):
    seq_count, row_count, head_count, head_size = queries_heads.shape
    length = keys_heads.shape[1]
    block_rows = min(512, length)
    block_count = length // block_rows

    def max_step(running, block_index):
        running_max, running_total = running
        scores = plain_sum(
            "sqhd,skhd->shqk", queries_heads, row_block(keys_heads, block_index, block_rows)
        )
        new_max = jnp.maximum(running_max, jnp.max(scores, -1))
        running_total = running_total * jnp.exp(running_max - new_max) + jnp.sum(
            jnp.exp(scores - new_max[..., None]), -1
        )
        return ((new_max, running_total), None)

    start_max = jnp.full((seq_count, head_count, row_count), -1e30, jnp.float32)
    start_total = jnp.zeros((seq_count, head_count, row_count), jnp.float32)
    (final_max, final_total), unused = lax.scan(
        max_step, (start_max, start_total), jnp.arange(block_count)
    )
    log_total = final_max + jnp.log(final_total)

    def value_step(running, block_index):
        scores = plain_sum(
            "sqhd,skhd->shqk", queries_heads, row_block(keys_heads, block_index, block_rows)
        )
        prob_low = jnp.exp(scores - log_total[..., None]).astype(jnp.bfloat16)
        return (
            running
            + plain_sum(
                "shqk,skhd->sqhd", prob_low, row_block(values_heads, block_index, block_rows)
            ),
            None,
        )

    context, unused = lax.scan(
        value_step, jnp.zeros(queries_heads.shape, jnp.float32), jnp.arange(block_count)
    )
    return (context, log_total)


def gather_body(
    tokens,
    cotangent,
    sequence_adapter_index,
    query_key_value_weight,
    output_weight,
    first_feed_weight,
    second_feed_weight,
    biases,
    value_bias_vector,
    first_feed_bias,
    norm_gain_pair,
    adapter_down_factors,
    output_down_factor,
    adapter_up_factors,
    hidden_up_factor,
    hidden_down_factor,
):
    seq_count, row_count, model_width = tokens.shape
    adapter_number = adapter_down_factors.shape[0]
    picker = (
        sequence_adapter_index[:, None] == jnp.arange(adapter_number, dtype=jnp.int32)[None, :]
    ).astype(jnp.float32)

    def select_adapter(table):
        return jnp.einsum("sa,a...->s...", picker, table.astype(jnp.float32), precision=HIGHEST)

    def to_adapters(per_seq):
        return jnp.einsum("sa,s...->a...", picker, per_seq, precision=HIGHEST)

    selected_down = select_adapter(adapter_down_factors)
    selected_output = select_adapter(output_down_factor)
    selected_up = select_adapter(adapter_up_factors)
    hup_sel = select_adapter(hidden_up_factor)
    hdown_sel = select_adapter(hidden_down_factor)
    down_low = selected_down.astype(jnp.bfloat16)
    out_low = selected_output.astype(jnp.bfloat16)
    hdown_low = hdown_sel.astype(jnp.bfloat16)
    wqkv_full, wout_full = attn_weights(query_key_value_weight, output_weight)
    projected = plain_sum("std,de->ste", tokens, wqkv_full)
    down_att = plain_sum("std,sjrd->sjtr", tokens, down_low[:, :3])
    lifted = exact_sum("sjtr,sjrd->sjtd", down_att, selected_up[:, :3])
    queries = ((projected[..., :model_width] + biases[0] + lifted[:, 0]) * 0.125).astype(
        jnp.bfloat16
    )
    keys_own = (projected[..., model_width : 2 * model_width] + lifted[:, 1]).astype(jnp.bfloat16)
    values_own = (projected[..., 2 * model_width :] + value_bias_vector + lifted[:, 2]).astype(
        jnp.bfloat16
    )
    keys_all, values_all = (
        lax.all_gather(keys_own, "ctx", axis=1, tiled=True),
        lax.all_gather(values_own, "ctx", axis=1, tiled=True),
    )
    queries_heads = to_heads(queries)
    keys_heads = to_heads(keys_all)
    values_heads = to_heads(values_all)
    context, log_total = attention_forward(queries_heads, keys_heads, values_heads)
    context = context.reshape(seq_count, row_count, model_width)
    context_low = context.astype(jnp.bfloat16)
    down_out = plain_sum("std,srd->str", context_low, out_low)
    branch = (
        plain_sum("std,de->ste", context_low, wout_full)
        + biases[1]
        + exact_sum("str,srd->std", down_out, selected_up[:, 3])
    )

    def first_norm(value):
        return layer_norm(value, norm_gain_pair[0], biases[3])

    def second_norm(value):
        return layer_norm(value, norm_gain_pair[1], biases[4])

    def gelu_exact(value):
        return jax.nn.gelu(value, approximate=False)

    normed, norm_back = jax.vjp(first_norm, tokens.astype(jnp.float32) + branch)
    normed_low = normed.astype(jnp.bfloat16)
    wfc1_full, wfc2_full = mlp_weights(first_feed_weight, second_feed_weight)
    down_fc1 = plain_sum("std,srd->str", normed_low, down_low[:, 3])
    hidden_pre = (
        plain_sum("std,df->stf", normed_low, wfc1_full)
        + first_feed_bias
        + exact_sum("str,srf->stf", down_fc1, hup_sel)
    )
    activated, gelu_back = jax.vjp(gelu_exact, hidden_pre)
    act_low = activated.astype(jnp.bfloat16)
    down_fc2 = plain_sum("stf,srf->str", act_low, hdown_low)
    mixed_out = (
        plain_sum("stf,fd->std", act_low, wfc2_full)
        + biases[2]
        + exact_sum("str,srd->std", down_fc2, selected_up[:, 4])
    )
    outcome, out_back = jax.vjp(second_norm, normed + mixed_out)
    (grad_sum2,) = out_back(cotangent.astype(jnp.float32))
    grad_mixed = grad_sum2.astype(jnp.bfloat16)
    grad_up_fc2 = exact_sum("str,std->srd", down_fc2, grad_mixed)
    grad_rank_fc2 = exact_sum("std,srd->str", grad_mixed, selected_up[:, 4]).astype(jnp.bfloat16)
    grad_hdown = plain_sum("str,stf->srf", grad_rank_fc2, act_low)
    wfc1_full, wfc2_full = mlp_weights(first_feed_weight, second_feed_weight)
    grad_act = (
        plain_sum("std,fd->stf", grad_mixed, wfc2_full)
        + plain_sum("str,srf->stf", grad_rank_fc2, hdown_low)
    ).astype(jnp.bfloat16)
    (grad_hidden,) = gelu_back(grad_act.astype(jnp.float32))
    grad_hidden = grad_hidden.astype(jnp.bfloat16)
    grad_hup = exact_sum("str,stf->srf", down_fc1, grad_hidden)
    grad_rank_fc1 = exact_sum("stf,srf->str", grad_hidden, hup_sel).astype(jnp.bfloat16)
    grad_down_fc1 = plain_sum("str,std->srd", grad_rank_fc1, normed_low)
    grad_normed_low = (
        plain_sum("stf,df->std", grad_hidden, wfc1_full)
        + plain_sum("str,srd->std", grad_rank_fc1, down_low[:, 3])
    ).astype(jnp.bfloat16)
    (grad_resid,) = norm_back(grad_sum2 + grad_normed_low.astype(jnp.float32))
    mlp_hup = to_adapters(grad_hup)
    mlp_hdown = to_adapters(grad_hdown)
    mlp_fc1 = to_adapters(grad_down_fc1)
    mlp_fc2 = to_adapters(grad_up_fc2)
    mlp_hup, mlp_hdown, mlp_fc1, mlp_fc2 = lax.psum(
        (mlp_hup, mlp_hdown, mlp_fc1, mlp_fc2), ("ctx", "fsdp")
    )
    grad_branch = grad_resid.astype(jnp.bfloat16)
    grad_up_out = exact_sum("str,std->srd", down_out, grad_branch)
    grad_rank_out = exact_sum("std,srd->str", grad_branch, selected_up[:, 3]).astype(jnp.bfloat16)
    grad_out_down = plain_sum("str,std->srd", grad_rank_out, context_low)
    wqkv_full, wout_full = attn_weights(query_key_value_weight, output_weight)
    grad_context = (
        plain_sum("std,ed->ste", grad_branch, wout_full)
        + plain_sum("str,srd->std", grad_rank_out, out_low)
    ).astype(jnp.bfloat16)
    row_delta = jnp.sum(to_heads(grad_context.astype(jnp.float32) * context), -1)
    delta_heads = jnp.swapaxes(row_delta, 1, 2)
    grad_heads = to_heads(grad_context)
    length = keys_all.shape[1]
    block_rows = min(512, length)
    block_count = length // block_rows

    def key_step(block_index, running):
        grad_query, grad_key, grad_value = running
        keys_blk = row_block(keys_heads, block_index, block_rows)
        values_blk = row_block(values_heads, block_index, block_rows)
        prob_low, grad_scores = block_grads(
            queries_heads, grad_heads, log_total, delta_heads, keys_blk, values_blk
        )
        grad_query = grad_query + plain_sum("shqk,skhd->sqhd", grad_scores, keys_blk)
        grad_key = lax.dynamic_update_slice_in_dim(
            grad_key,
            plain_sum("shqk,sqhd->skhd", grad_scores, queries_heads),
            block_index * block_rows,
            1,
        )
        grad_value = lax.dynamic_update_slice_in_dim(
            grad_value,
            plain_sum("shqk,sqhd->skhd", prob_low, grad_heads),
            block_index * block_rows,
            1,
        )
        return (grad_query, grad_key, grad_value)

    start_query = jnp.zeros(queries_heads.shape, jnp.float32)
    start_keys = jnp.zeros(keys_heads.shape, jnp.float32)
    grad_query, grad_key_all, grad_value_all = lax.fori_loop(
        0, block_count, key_step, (start_query, start_keys, start_keys)
    )
    grad_keys, grad_values = (
        lax.psum_scatter(
            grad_key_all.reshape(seq_count, length, model_width).astype(jnp.bfloat16),
            "ctx",
            scatter_dimension=1,
            tiled=True,
        ).astype(jnp.float32),
        lax.psum_scatter(
            grad_value_all.reshape(seq_count, length, model_width).astype(jnp.bfloat16),
            "ctx",
            scatter_dimension=1,
            tiled=True,
        ).astype(jnp.float32),
    )
    grad_qlin = grad_query.reshape(seq_count, row_count, model_width).astype(jnp.bfloat16) * 0.125
    grad_key_low = grad_keys.astype(jnp.bfloat16)
    grad_value_low = grad_values.astype(jnp.bfloat16)
    stacked = jnp.stack([grad_qlin, grad_key_low, grad_value_low], 1)
    grad_up_att = exact_sum("sjtr,sjtd->sjrd", down_att, stacked)
    grad_rank_att = exact_sum("sjtd,sjrd->sjtr", stacked, selected_up[:, :3]).astype(jnp.bfloat16)
    grad_down_att = plain_sum("sjtr,std->sjrd", grad_rank_att, tokens)
    joined = jnp.concatenate([grad_qlin, grad_key_low, grad_value_low], -1)
    grad_tokens = (
        grad_resid
        + plain_sum("ste,de->std", joined, wqkv_full)
        + plain_sum("sjtr,sjrd->std", grad_rank_att, down_low[:, :3])
    )
    attn_down = to_adapters(grad_down_att)
    attn_out = to_adapters(grad_out_down)
    attn_up = to_adapters(jnp.concatenate([grad_up_att, grad_up_out[:, None]], 1))
    attn_down, attn_out, attn_up = lax.psum((attn_down, attn_out, attn_up), ("ctx", "fsdp"))
    total_down = jnp.concatenate([attn_down, mlp_fc1[:, None]], 1)
    total_up = jnp.concatenate([attn_up, mlp_fc2[:, None]], 1)
    return (
        outcome.astype(jnp.bfloat16),
        grad_tokens,
        total_down,
        attn_out,
        total_up,
        mlp_hup,
        mlp_hdown,
    )


BF16 = jnp.bfloat16
F32 = jnp.float32
LOG2E = 1.4426950408889634
VMEM_LIMIT = 60 * 2**20
MESH = pl.DeviceIdType.MESH


def dot32(left, right):
    return jnp.dot(left, right, preferred_element_type=F32)


def dot_nt(left, right):
    return lax.dot_general(left, right, (((1,), (1,)), ((), ())), preferred_element_type=F32)


def dot_tn(left, right):
    return lax.dot_general(left, right, (((0,), (0,)), ((), ())), preferred_element_type=F32)


def split_three(value):
    high = value.astype(BF16)
    rest = value - high.astype(F32)
    middle = rest.astype(BF16)
    return high, middle, (rest - middle.astype(F32)).astype(BF16)


def flip(value):
    return value.astype(F32).T.astype(BF16)


def remote(src, dst, send_sem, recv_sem, device):
    return pltpu.make_async_remote_copy(
        src_ref=src,
        dst_ref=dst,
        send_sem=send_sem,
        recv_sem=recv_sem,
        device_id=device,
        device_id_type=MESH,
    )


class Place:
    def __init__(self):
        self.ctx = lax.axis_index("ctx")
        self.core = lax.axis_index("fsdp")
        self.half = self.ctx // (H // 2)
        self.low = self.ctx % (H // 2)
        self.me = self.low * 2 + self.core
        self.swaps = self.core != self.half
        self.pair = (self.core + self.half) % 2
        self.sibling = (self.ctx, 1 - self.core)
        self.partner = ((self.ctx + H // 2) % H, 1 - self.core)

    def peer(self, step):
        number = self.me ^ step
        return (self.half * (H // 2) + number // 2, number % 2)

    def order(self, turn):
        return 2 * (turn % (H // 2)) + (turn // (H // 2) + self.pair) % 2

    def greet(self):
        barrier = pltpu.get_barrier_semaphore()
        for step in range(1, H):
            pl.semaphore_signal(barrier, inc=1, device_id=self.peer(step), device_id_type=MESH)
        pl.semaphore_signal(barrier, inc=1, device_id=self.partner, device_id_type=MESH)
        pl.semaphore_wait(barrier, H)


def sum_copies(mine, parts, total, sems, place):
    own = total.at[place.pair, place.low, place.half]
    other = total.at[place.pair, place.low, 1 - place.half]
    column = total.at[place.pair]
    scatter = [
        remote(mine.at[place.me ^ step], parts.at[step], sems.at[0, step], sems.at[1, step], place.peer(step))
        for step in range(1, H)
    ]
    cross = remote(own, own, sems.at[0, 0], sems.at[1, 0], place.partner)
    first = [
        remote(own, own, sems.at[2, step], sems.at[3, step], place.peer(step))
        for step in range(2, H, 2)
    ]
    second = [
        remote(other, other, sems.at[2, step + 1], sems.at[3, step + 1], place.peer(step))
        for step in range(2, H, 2)
    ]
    last = remote(column, column, sems.at[2, 0], sems.at[3, 0], place.sibling)
    return scatter, cross, first, second, last


def sum_parts(scatter, mine, parts, total, place):
    value = mine[place.me].astype(F32)
    for step, copy in enumerate(scatter, 1):
        copy.wait_recv()
        value = value + parts[step].astype(F32)
    total[place.pair, place.low, place.half] = value.astype(BF16)


def put_term(mine, base, term):
    units = mine.shape[2] // 128
    for unit in range(term.shape[1] // 128):
        at = base // 128 + unit
        lanes = slice(at % units * 128, at % units * 128 + 128)
        mine[at // units, :, lanes] = term[:, unit * 128 : unit * 128 + 128].astype(BF16)


def layer_kernel(
    block_q,
    block_k,
    index_ref,
    tokens_ref,
    cotangent_ref,
    wqkv_ref,
    wout_ref,
    wfc1_ref,
    wfc2_ref,
    down_table,
    up_table,
    out_down_table,
    hidden_up_table,
    hidden_down_table,
    biases_ref,
    value_bias_ref,
    hidden_bias_ref,
    gains_ref,
    outcome_ref,
    grad_ref,
    chosen_out,
    hidden_down_out,
    hidden_up_out,
    down_out,
    up_out,
    out_down_out,
    wqkv_far,
    wfc1_far,
    wide,
    wfc2,
    wout,
    big,
    act,
    small,
    small_hidden,
    x,
    cotangent,
    rank_att,
    outgoing,
    qkv,
    leaving,
    arrived,
    incoming,
    context,
    state,
    qta,
    gta,
    kk,
    vv,
    kt,
    both,
    dkv_sum,
    dq_in,
    dkv_out,
    dkv_in,
    grad_out,
    grad_in,
    mlp_mine,
    mlp_parts,
    mlp_total,
    att_mine,
    att_parts,
    att_total,
    load_sem,
    core_sem,
    swap_sem,
    kv_sem,
    q_sem,
    back_sem,
    grad_sem,
    dq_sem,
    dkv_sem,
    mlp_sem,
    att_sem,
):
    peers, _, rows = qkv.shape
    length = peers * rows
    width = x.shape[1]
    hidden = hidden_bias_ref.shape[1]
    adapters = hidden_up_table.shape[0] // 16
    place = Place()
    me, core = place.me, place.core
    other = 1 - core
    wqkv = wide.at[:, 0 : 3 * width]
    up_at = down_table.shape[0]
    out_down_at = up_at + up_table.shape[0]

    def half_of(full, owner):
        count = full.shape[0] // 2
        return full.at[pl.ds(pl.multiple_of(owner * count, count), count), :]

    def load(source, target, number):
        return pltpu.make_async_copy(source, target, load_sem.at[number])

    def to_sibling(source, target, number):
        return remote(source, target, core_sem.at[0, number], core_sem.at[1, number], place.sibling)

    load_wqkv = load(wqkv_ref, half_of(wqkv, core), 0)
    load_wout = load(wout_ref, half_of(wout, core), 1)
    load_tables = [
        load(down_table, wfc2.at[0:up_at], 2),
        load(up_table, wfc2.at[up_at:out_down_at], 3),
        load(out_down_table, wfc2.at[out_down_at : out_down_at + out_down_table.shape[0]], 4),
        load(hidden_up_table, act.at[0 : 16 * adapters], 5),
        load(hidden_down_table, act.at[16 * adapters : 32 * adapters], 6),
    ]
    load_x = load(tokens_ref, x, 7)
    load_cotangent = load(cotangent_ref, cotangent, 8)
    load_wfc1 = load(wfc1_ref, half_of(wide, core), 9)
    load_wfc1_far = load(wfc1_far, half_of(wide, other), 10)
    load_wfc2 = load(wfc2_ref, half_of(wfc2, core), 11)
    again_wqkv = load(wqkv_ref, half_of(wqkv, core), 12)
    again_wqkv_far = load(wqkv_far, half_of(wqkv, other), 13)
    give_wqkv = to_sibling(wqkv_ref, half_of(wqkv, core), 0)
    give_wout = to_sibling(wout_ref, half_of(wout, core), 1)
    give_chosen = to_sibling(chosen_out.at[core], chosen_out.at[core], 2)
    count = small.shape[0]
    give_small = [to_sibling(small, wide.at[0:count, 3 * width : 4 * width], 3)] + [
        to_sibling(
            small_hidden.at[:, part * width : (part + 1) * width],
            wide.at[count + 32 * part : count + 32 * part + 32, 3 * width : 4 * width],
            4 + part,
        )
        for part in range(hidden // width)
    ]
    give_wfc2 = to_sibling(wfc2_ref, half_of(wfc2, core), 8)
    give_wfc1 = to_sibling(wfc1_ref, wfc1_far, 9)
    give_wqkv_again = to_sibling(wqkv_ref, wqkv_far, 10)
    half_rows = rows // 2
    swap_x = [
        remote(
            tokens_ref.at[part * half_rows : (part + 1) * half_rows],
            x.at[part * half_rows : (part + 1) * half_rows],
            swap_sem.at[0, 7 + part],
            swap_sem.at[1, 7 + part],
            place.partner,
        )
        for part in range(2)
    ]
    swap_cotangent = remote(cotangent_ref, cotangent, swap_sem.at[0, 1], swap_sem.at[1, 1], place.partner)

    load_wqkv.start()
    for copy in load_tables:
        copy.start()
    load_wout.start()

    @pl.when(jnp.logical_not(place.swaps))
    def _():
        load_x.start()
        load_cotangent.start()

    adapter = index_ref[0]
    numbers = lax.broadcasted_iota(jnp.int32, chosen_out.shape[1:], 0)
    chosen_out[core] = (numbers == jnp.full(numbers.shape, adapter, jnp.int32)).astype(F32)
    place.greet()

    @pl.when(place.swaps)
    def _():
        for copy in swap_x:
            copy.start()

    give_wqkv.start()
    give_chosen.start()

    for copy in load_tables:
        copy.wait()

    def select(table, base, group, groups, target, at):
        chosen = jnp.full((16, table.shape[1]), adapter, jnp.int32)
        value = jnp.zeros((16, table.shape[1]), F32)
        for number in range(adapters):
            start = pl.multiple_of(base + 16 * (number * groups + group), 16)
            value = jnp.where(chosen == number, table[pl.ds(start, 16), :].astype(F32), value)
        target[pl.ds(pl.multiple_of(at + 16 * group, 16), 16), :] = value.astype(BF16)

    def select_down(group, _):
        select(wfc2, 0, group, 4, small, 0)
        return 0

    def select_up(group, _):
        select(wfc2, up_at, group, 5, small, 64)
        return 0

    lax.fori_loop(0, 4, select_down, 0)
    lax.fori_loop(0, 5, select_up, 0)
    select(wfc2, out_down_at, 0, 1, small, 144)
    for part in range(2):
        select(act, 16 * adapters * part, 0, 1, small_hidden, 16 * part)
    for copy in give_small:
        copy.start()
    give_wout.start()
    for copy in give_small:
        copy.wait()

    @pl.when(place.swaps)
    def _():
        small[...] = wide[0:count, 3 * width : 4 * width]
        for part in range(hidden // width):
            small_hidden[:, part * width : (part + 1) * width] = wide[
                count + 32 * part : count + 32 * part + 32, 3 * width : 4 * width
            ]

    hidden_up_ref = small_hidden.at[0:16]
    hidden_down_ref = small_hidden.at[16:32]
    out_down_ref = small.at[144:160]

    def down(j):
        return small[16 * j : 16 * j + 16]

    def up(j):
        return small[64 + 16 * j : 80 + 16 * j]

    load_wfc2.start()
    give_wfc2.start()

    load_wqkv.wait()
    give_wqkv.wait_recv()

    def project(half, part):
        here = slice(half * half_rows, (half + 1) * half_rows)
        cols = slice(part * width, (part + 1) * width)
        value = dot32(x[here, :], wqkv[:, cols]) + dot32(rank_att[here, part * 16 : part * 16 + 16], up(part))
        if part == 0:
            value = (value + biases_ref[0:1, :]) * 0.125
        if part == 2:
            value = value + value_bias_ref[...]
        for two in range(peers // 2):
            turned = value[:, two * 128 : two * 128 + 128].T.astype(BF16)
            outgoing[2 * two, part * 64 : part * 64 + 64, here] = turned[0:64]
            outgoing[2 * two + 1, part * 64 : part * 64 + 64, here] = turned[64:128]

    def kv_copy(step, half):
        here = slice(half * half_rows, (half + 1) * half_rows)
        return remote(
            outgoing.at[me ^ step, 64:192, here],
            qkv.at[step, 64:192, here],
            kv_sem.at[0, half, step],
            kv_sem.at[1, half, step],
            place.peer(step),
        )

    def q_copy(step):
        return remote(
            outgoing.at[me ^ step, 0:64], qkv.at[step, 0:64], q_sem.at[0, step], q_sem.at[1, step], place.peer(step)
        )

    def back_copy(step):
        return remote(leaving.at[step], arrived.at[me], back_sem.at[0, step], back_sem.at[1, step], place.peer(step))

    steps = length // block_k
    group = block_q // rows
    key_group = block_k // rows
    for half in range(2):
        here = slice(half * half_rows, (half + 1) * half_rows)

        @pl.when(place.swaps)
        def _():
            swap_x[half].wait_recv()

        if half == 0:

            @pl.when(jnp.logical_not(place.swaps))
            def _():
                load_x.wait()

        rank_att[here, :] = dot_nt(x[here, :], small[0:48]).astype(BF16)
        project(half, 1)
        project(half, 2)
        for step in range(1, peers):
            kv_copy(step, half).start()
        project(half, 0)
    for step in range(1, peers):
        q_copy(step).start()
    give_wfc1.start()
    give_wqkv_again.start()
    load_wfc1.start()
    qkv[0] = outgoing[me]

    row_at = lax.broadcasted_iota(jnp.int32, (16, rows), 0)
    ones = (row_at == 0).astype(F32).astype(BF16)
    minus = jnp.where(lax.broadcasted_iota(jnp.int32, (rows, 16), 1) < 3, -1.0, 0.0).astype(BF16)
    minus_rows = jnp.where(lax.broadcasted_iota(jnp.int32, (64, rows), 0) < 3, -1.0, 0.0).astype(BF16)

    def tail(value):
        at = lax.broadcasted_iota(jnp.int32, (16, value.shape[1]), 0)
        high, middle, low = (part.astype(F32) for part in split_three(value))
        return jnp.where(at == 0, high, jnp.where(at == 1, middle, jnp.where(at == 2, low, 0.0))).astype(BF16)

    def take_key(turn):
        cols = pl.ds(pl.multiple_of(turn * rows, rows), rows)
        step = place.order(turn)

        @pl.when(step > 0)
        def _():
            kv_copy(step, 0).wait_recv()
            kv_copy(step, 1).wait_recv()

        key = qkv[step, 64:128, :]
        value = qkv[step, 128:192, :]
        kt[:, cols] = key
        kk[cols, 0:128] = flip(jnp.concatenate([key, key], 0))
        kk[cols, 128:144] = minus
        vv[cols, :] = flip(jnp.concatenate([value, minus_rows], 0))
        gta[0:64, cols] = value
        gta[64:80, cols] = ones
        gta[80:128, cols] = jnp.zeros((48, rows), BF16)

    def take_keys(i):
        def one(part, _):
            take_key(i * key_group + part)
            return 0

        lax.fori_loop(0, key_group, one, 0)

    def forward_part(i, low, high, arriving):
        def take_query(part, _):
            turn = i * group + part
            step = place.order(turn)
            here = pl.ds(pl.multiple_of(turn * rows, rows), rows)

            @pl.when(step > 0)
            def _():
                q_copy(step).wait_recv()

            query = qkv[step, 0:64, :].astype(F32) * LOG2E
            high = query.astype(BF16)
            qta[0:64, here] = high
            qta[64:128, here] = (query - high.astype(F32)).astype(BF16)
            return 0

        if low == 0:
            lax.fori_loop(0, group, take_query, 0)
        cols = pl.ds(pl.multiple_of(i * block_q, block_q), block_q)
        query = qta.at[0:128, cols]
        if arriving:

            @pl.when(i == 0)
            def _():
                take_keys(low)

        block = dot32(kk[low * block_k : (low + 1) * block_k, 0:128], query[...])
        big[0:block_k] = block

        def half(j, now, carry):
            peak, running, total = carry
            later = jnp.minimum(j + 1, high - 1)
            here = pl.ds(pl.multiple_of(j * block_k, block_k), block_k)
            there = pl.ds(pl.multiple_of(later * block_k, block_k), block_k)
            if arriving:

                @pl.when(jnp.logical_and(i == 0, j + 1 < high))
                def _():
                    take_keys(later)

            ahead = dot32(kk[there, 0:128], query[...])
            big[(1 - now) * block_k : (2 - now) * block_k] = ahead
            new = jnp.maximum(running, peak)
            weights = jnp.exp2(big[now * block_k : (now + 1) * block_k] - new).astype(BF16)
            total = total * jnp.exp2(running - new) + dot32(gta[0:80, here], weights)
            return jnp.max(ahead, 0, keepdims=True), new, total

        def pair(j, carry):
            return half(low + 2 * j + 1, 1, half(low + 2 * j, 0, carry))

        if low == 0:
            running, total = jnp.full((1, block_q), -jnp.inf, F32), jnp.zeros((80, block_q), F32)
        else:
            running = state[1:2, cols]
            total = jnp.concatenate([context[:, cols], state[0:1, cols], jnp.zeros((15, block_q), F32)], 0)
        _, top, total = lax.fori_loop(
            0, (high - low) // 2, pair, (jnp.max(block, 0, keepdims=True), running, total)
        )
        weight_sum = total[64:65]
        if high < steps:
            context[:, cols] = total[0:64]
            state[0:1, cols] = weight_sum
            state[1:2, cols] = top
            return
        result = total[0:64] / weight_sum
        context[:, cols] = result
        qta[128:144, cols] = tail(top + jnp.log2(weight_sum))
        low_result = result.astype(BF16)
        for part in range(group):
            step = place.order(i * group + part)
            leaving[step] = low_result[:, part * rows : (part + 1) * rows]

            @pl.when(step > 0)
            def _():
                back_copy(step).start()

    query_steps = length // block_q

    def forward_parts(first, last, low, high, arriving):
        def one(i, _):
            forward_part(i, low, high, arriving)
            return 0

        lax.fori_loop(first, last, one, 0)

    forward_parts(0, query_steps // 2, 0, steps // 2, True)
    give_wfc1.wait_recv()
    load_wfc1_far.start()
    forward_parts(0, query_steps // 2, steps // 2, steps, True)

    @pl.when(place.swaps)
    def _():
        swap_cotangent.start()

    forward_parts(query_steps // 2, query_steps, 0, steps, False)
    arrived[me] = leaving[0]

    def mean(value):
        return jnp.mean(value, -1, keepdims=True)

    def norm_backward(grad, hat, scale):
        return scale * (grad - mean(grad) - hat * mean(grad * hat))

    load_wout.wait()
    give_wout.wait_recv()
    for step in range(1, peers):
        back_copy(step).wait_recv()
    context_low = flip(arrived[...].reshape(width, rows))
    rank_out = dot_nt(context_low, out_down_ref[...]).astype(BF16)
    resid = x[...].astype(F32) + dot32(context_low, wout[...]) + biases_ref[1:2] + dot32(rank_out, up(3))
    center = resid - mean(resid)
    scale_one = lax.rsqrt(mean(center * center) + EPSILON)
    hat_one = center * scale_one
    normed = hat_one * gains_ref[0:1] + biases_ref[3:4]
    normed_low = normed.astype(BF16)
    rank_one = dot_nt(normed_low, down(3)).astype(BF16)
    load_wfc1.wait()
    load_wfc1_far.wait()
    load_wfc2.wait()
    give_wfc2.wait_recv()
    piece = 1024
    rank_two = jnp.zeros((rows, 16), F32)
    mixed = normed + biases_ref[2:3]
    for part in range(hidden // piece):
        cols = slice(part * piece, (part + 1) * piece)
        pre = (
            dot32(normed_low, wide[:, cols])
            + hidden_bias_ref[:, cols]
            + dot32(rank_one, hidden_up_ref[:, cols])
        )
        share = 0.5 + 0.5 * lax.erf(pre * 0.7071067811865476)
        big[part * rows : (part + 1) * rows] = share + pre * (0.3989422804014327 * jnp.exp(-0.5 * pre * pre))
        active = (pre * share).astype(BF16)
        act[:, cols] = active
        rank_two = rank_two + dot_nt(active, hidden_down_ref[:, cols])
        mixed = mixed + dot32(active, wfc2[cols, :])
    rank_two = rank_two.astype(BF16)
    mixed = mixed + dot32(rank_two, up(4))
    center = mixed - mean(mixed)
    scale_two = lax.rsqrt(mean(center * center) + EPSILON)
    hat_two = center * scale_two

    @pl.when(place.swaps)
    def _():
        swap_cotangent.wait_recv()

    @pl.when(jnp.logical_not(place.swaps))
    def _():
        load_cotangent.wait()

    grad_sum = norm_backward(cotangent[...].astype(F32) * gains_ref[1:2], hat_two, scale_two)
    outcome = cotangent
    outcome[...] = (hat_two * gains_ref[1:2] + biases_ref[4:5]).astype(BF16)
    home_outcome = remote(outcome, outcome_ref, swap_sem.at[0, 2], swap_sem.at[1, 2], place.partner)

    @pl.when(place.swaps)
    def _():
        home_outcome.start()

    @pl.when(jnp.logical_not(place.swaps))
    def _():
        outcome_ref[...] = outcome[...]

    grad_mixed = grad_sum.astype(BF16)
    put_term(mlp_mine, 2 * hidden, dot_tn(rank_two, grad_mixed))
    grad_rank = dot_nt(grad_mixed, up(4)).astype(BF16)
    put_term(mlp_mine, 0, dot_tn(grad_rank, act[...]))
    grad_one = jnp.zeros((rows, 16), F32)
    grad_normed = jnp.zeros((rows, width), F32)
    for part in range(hidden // piece):
        cols = slice(part * piece, (part + 1) * piece)
        grad_act = dot_nt(grad_mixed, wfc2[cols, :]) + dot32(grad_rank, hidden_down_ref[:, cols])
        grad_hidden = (grad_act.astype(BF16).astype(F32) * big[part * rows : (part + 1) * rows]).astype(BF16)
        put_term(mlp_mine, hidden + part * piece, dot_tn(rank_one, grad_hidden))
        grad_one = grad_one + dot_nt(grad_hidden, hidden_up_ref[:, cols])
        grad_normed = grad_normed + dot_nt(grad_hidden, wide[:, cols])
    grad_one = grad_one.astype(BF16)
    put_term(mlp_mine, 2 * hidden + width, dot_tn(grad_one, normed_low))
    grad_normed = (grad_normed + dot32(grad_one, down(3))).astype(BF16).astype(F32)
    resid_grad = norm_backward((grad_sum + grad_normed) * gains_ref[0:1], hat_one, scale_one)
    grad_resid = big.at[0:rows]
    grad_resid[...] = resid_grad
    grad_branch = resid_grad.astype(BF16)
    put_term(mlp_mine, 2 * hidden + 2 * width, dot_tn(rank_out, grad_branch))
    grad_rank = dot_nt(grad_branch, up(3)).astype(BF16)
    put_term(mlp_mine, 2 * hidden + 3 * width, dot_tn(grad_rank, context_low))
    turned = dot_nt(wout[...], grad_branch) + lax.dot_general(
        out_down_ref[...], grad_rank, (((0,), (1,)), ((), ())), preferred_element_type=F32
    )
    for step in range(1, peers):
        kv_copy(step, 0).wait_send()
        kv_copy(step, 1).wait_send()
        q_copy(step).wait_send()
        back_copy(step).wait_send()
    outgoing[:, 0:64] = turned.astype(BF16).reshape(peers, 64, rows)

    def grad_copy(step):
        return remote(
            outgoing.at[me ^ step, 0:64], incoming.at[step], grad_sem.at[0, step], grad_sem.at[1, step], place.peer(step)
        )

    for step in range(1, peers):
        grad_copy(step).start()
    mlp_scatter, mlp_cross, mlp_first, mlp_second, mlp_last = sum_copies(mlp_mine, mlp_parts, mlp_total, mlp_sem, place)
    incoming[0] = outgoing[me, 0:64]
    give_wqkv_again.wait_recv()
    again_wqkv.start()
    again_wqkv_far.start()
    dkv_sum[...] = jnp.zeros_like(dkv_sum)
    first = lax.broadcasted_iota(jnp.int32, (block_k, 128), 1) < 64
    dq_out = leaving

    def dq_copy(step):
        return remote(dq_out.at[step], dq_in.at[me], dq_sem.at[0, step], dq_sem.at[1, step], place.peer(step))

    def dkv_copy(step):
        return remote(dkv_out.at[step], dkv_in.at[me], dkv_sem.at[0, step], dkv_sem.at[1, step], place.peer(step))

    def backward_step(turn, _):
        last = turn == query_steps - 1
        j = turn

        def take_grad(part, _):
            step = place.order(j * group + part)
            cols = pl.ds(pl.multiple_of((j * group + part) * rows, rows), rows)

            @pl.when(step > 0)
            def _():
                grad_copy(step).wait_recv()

            grad = incoming[step]
            gta[0:64, cols] = grad
            gta[64:80, cols] = tail(jnp.sum(grad.astype(F32) * context[:, cols], 0, keepdims=True))
            both[cols, :] = flip(jnp.concatenate([qkv[step, 0:64, :], grad], 0))
            return 0

        lax.fori_loop(0, group, take_grad, 0)
        cols = pl.ds(pl.multiple_of(j * block_q, block_q), block_q)

        def key_pair(pair, dq):
            found = []
            for side in range(2):
                i = 2 * pair + side
                here = pl.ds(pl.multiple_of(i * block_k, block_k), block_k)
                probs = jnp.exp2(dot32(kk[here, :], qta[:, cols]))
                change = dot32(vv[here, :], gta[:, cols])
                found.append((i, here, probs.astype(BF16), (probs * change).astype(BF16)))
            for i, here, probs, low in found:
                dv = dot32(probs, both[cols, :])
                dk = dot32(low, both[cols, :])
                dkv_sum[here, :] += jnp.where(first, dk, dv)
                dq = dq + dot32(kt[:, here], low)

            @pl.when(last)
            def _():
                for i, here, _, _ in found:
                    done = dkv_sum[here, :].astype(BF16)
                    for part in range(key_group):
                        step = place.order(i * key_group + part)
                        dkv_out[step] = done[part * rows : (part + 1) * rows]

                        @pl.when(step > 0)
                        def _():
                            dkv_copy(step).start()

            return dq

        dq = lax.fori_loop(0, steps // 2, key_pair, jnp.zeros((64, block_q), F32)).astype(BF16)
        for part in range(group):
            step = place.order(j * group + part)
            dq_out[step] = dq[:, part * rows : (part + 1) * rows]

            @pl.when(step > 0)
            def _():
                dq_copy(step).start()

        @pl.when(turn == query_steps // 4 - 1)
        def _():
            for copy in mlp_scatter:
                copy.start()

        @pl.when(turn == query_steps // 2 - 1)
        def _():
            sum_parts(mlp_scatter, mlp_mine, mlp_parts, mlp_total, place)
            mlp_cross.start()
            for copy in mlp_first:
                copy.start()

        @pl.when(turn == query_steps - 2)
        def _():
            mlp_cross.wait_recv()
            for copy in mlp_second:
                copy.start()

        return 0

    lax.fori_loop(0, query_steps, backward_step, 0)
    for copy in mlp_first + mlp_second:
        copy.wait_recv()
    mlp_last.start()

    def spread(total, parts):
        units = total.shape[4] // 128
        for half in range(2):
            for unit in range(peers * units):
                peer = unit // units
                lanes = slice(unit % units * 128, unit % units * 128 + 128)
                for target, low, high in parts:
                    if low <= unit * 128 < high:
                        at = unit * 128 - low
                        target(half)[:, at : at + 128] = total[(peer % 2 + half) % 2, peer // 2, half, :, lanes]

    joined = act.at[:, 0 : 3 * width]
    dq_in[me] = dq_out[0]
    dkv_in[me] = dkv_out[0]
    for step in range(1, peers):
        dkv_copy(step).wait_recv()
    left = lax.broadcasted_iota(jnp.int32, (rows, 128), 1) < 64
    for two in range(peers // 2):
        even = dkv_in[2 * two].astype(F32)
        odd = dkv_in[2 * two + 1].astype(F32)
        cols = slice(width + two * 128, width + two * 128 + 128)
        joined[:, cols] = jnp.where(left, even, pltpu.roll(odd, 64, 1)).astype(BF16)
        cols = slice(2 * width + two * 128, 2 * width + two * 128 + 128)
        joined[:, cols] = jnp.where(left, pltpu.roll(even, 64, 1), odd).astype(BF16)
    def ranks_of(part):
        grad = joined[:, part * width : (part + 1) * width]
        ranks[part] = dot_nt(grad, up(part)).astype(BF16)

    def terms_of(part):
        grad = joined[:, part * width : (part + 1) * width]
        put_term(att_mine, part * width, dot_tn(rank_att[:, part * 16 : part * 16 + 16], grad))
        put_term(att_mine, (3 + part) * width, dot_tn(ranks[part], x[...]))

    ranks = {}
    att_scatter, att_cross, att_first, att_second, att_last = sum_copies(att_mine, att_parts, att_total, att_sem, place)
    again_wqkv.wait()
    again_wqkv_far.wait()
    for part in (1, 2):
        ranks_of(part)
        terms_of(part)
    for step in range(1, peers):
        dq_copy(step).wait_recv()
    joined[:, 0:width] = (dq_in[...].reshape(width, rows).astype(F32).T * 0.125).astype(BF16)
    ranks_of(0)
    terms_of(0)
    for copy in att_scatter:
        copy.start()
    piece = width // 4
    home = [
        remote(
            grad_out.at[:, part * piece : (part + 1) * piece],
            grad_in.at[:, part * piece : (part + 1) * piece],
            swap_sem.at[0, 3 + part],
            swap_sem.at[1, 3 + part],
            place.partner,
        )
        for part in range(4)
    ]
    mlp_last.wait_recv()
    for part in range(4):
        cols = slice(part * piece, (part + 1) * piece)
        total = grad_resid[:, cols] + dot_nt(joined[...], wqkv[cols, :])
        for j in range(3):
            total = total + dot32(ranks[j], small[16 * j : 16 * j + 16, cols])
        grad_ref[:, cols] = total
        grad_out[:, cols] = total.astype(BF16)

        @pl.when(place.swaps)
        def _():
            home[part].start()

    sum_parts(att_scatter, att_mine, att_parts, att_total, place)
    att_cross.start()
    for copy in att_first:
        copy.start()
    spread(
        mlp_total,
        (
            (lambda half: hidden_down_out.at[half], 0, hidden),
            (lambda half: hidden_up_out.at[half], hidden, 2 * hidden),
            (lambda half: up_out.at[half, 4], 2 * hidden, 2 * hidden + width),
            (lambda half: down_out.at[half, 3], 2 * hidden + width, 2 * hidden + 2 * width),
            (lambda half: up_out.at[half, 3], 2 * hidden + 2 * width, 2 * hidden + 3 * width),
            (lambda half: out_down_out.at[half], 2 * hidden + 3 * width, 2 * hidden + 4 * width),
        ),
    )
    att_cross.wait_recv()
    for copy in att_second:
        copy.start()
    for copy in att_first + att_second:
        copy.wait_recv()
    att_last.start()

    @pl.when(place.swaps)
    def _():
        for part in range(4):
            home[part].wait_recv()
            cols = slice(part * piece, (part + 1) * piece)
            grad_ref[:, cols] = grad_in[:, cols].astype(F32)
        for part in range(4):
            home[part].wait_send()
        home_outcome.wait()
        for copy in swap_x:
            copy.wait_send()
        swap_cotangent.wait_send()

    att_last.wait_recv()
    spread(
        att_total,
        tuple(
            (functools.partial(lambda part, half: up_out.at[half, part], part), part * width, (part + 1) * width)
            for part in range(3)
        )
        + tuple(
            (functools.partial(lambda part, half: down_out.at[half, part], part), (3 + part) * width, (4 + part) * width)
            for part in range(3)
        ),
    )
    for step in range(1, peers):
        grad_copy(step).wait_send()
        dq_copy(step).wait_send()
        dkv_copy(step).wait_send()
    for copies in ((mlp_scatter, mlp_first, mlp_second), (att_scatter, att_first, att_second)):
        for copy in copies[0] + copies[1] + copies[2]:
            copy.wait_send()
    for copy in (mlp_cross, mlp_last, att_cross, att_last):
        copy.wait_send()
    for copy in (give_wqkv, give_wout, give_wfc2, give_wfc1, give_wqkv_again):
        copy.wait_send()
    give_chosen.wait()


def run_layer(index, tokens, cotangent, weights, tables, biases, value_bias, hidden_bias, gains):
    rows, width = tokens.shape
    peers = H
    length = peers * rows
    hidden = hidden_bias.shape[1]
    block_q, block_k = 1024, 512
    vmem = pl.BlockSpec(memory_space=pltpu.VMEM)
    hbm = pl.BlockSpec(memory_space=pl.ANY)
    mlp_part = (2 * hidden + 4 * width) // peers
    att_part = 6 * width // peers

    def out(shape, dtype=BF16):
        return jax.ShapeDtypeStruct(shape, dtype)

    def total(part):
        return pltpu.VMEM((2, peers // 2, 2, 16, part), BF16)

    def heads(*shape):
        return pltpu.VMEM((peers,) + shape, BF16)

    def sems(*shape):
        return pltpu.SemaphoreType.DMA(shape)

    return pl.pallas_call(
        functools.partial(layer_kernel, block_q, block_k),
        out_shape=[
            out((rows, width)),
            out((rows, width), F32),
            out((2, 8, 128), F32),
            out((2, 16, hidden)),
            out((2, 16, hidden)),
            out((2, 4, 16, width)),
            out((2, 5, 16, width)),
            out((2, 16, width)),
            out(weights[0].shape),
            out(weights[2].shape),
        ],
        in_specs=[pl.BlockSpec(memory_space=pltpu.SMEM)] + [hbm] * 11 + [vmem] * 4,
        out_specs=[vmem] * 8 + [hbm] * 2,
        scratch_shapes=[
            pltpu.VMEM((width, hidden), BF16),
            pltpu.VMEM((hidden, width), BF16),
            pltpu.VMEM((width, width), BF16),
            pltpu.VMEM((max(4 * rows, 2 * block_k), 1024), F32),
            pltpu.VMEM((rows, hidden), BF16),
            pltpu.VMEM((160, width), BF16),
            pltpu.VMEM((32, hidden), BF16),
            pltpu.VMEM((rows, width), BF16),
            pltpu.VMEM((rows, width), BF16),
            pltpu.VMEM((rows, 48), BF16),
            heads(192, rows),
            heads(192, rows),
            heads(64, rows),
            heads(64, rows),
            heads(64, rows),
            pltpu.VMEM((64, length), F32),
            pltpu.VMEM((8, length), F32),
            pltpu.VMEM((144, length), BF16),
            pltpu.VMEM((128, length), BF16),
            pltpu.VMEM((length, 144), BF16),
            pltpu.VMEM((length, 128), BF16),
            pltpu.VMEM((64, length), BF16),
            pltpu.VMEM((length, 128), BF16),
            pltpu.VMEM((length, 128), F32),
            heads(64, rows),
            heads(rows, 128),
            heads(rows, 128),
            pltpu.VMEM((rows, width), BF16),
            pltpu.VMEM((rows, width), BF16),
            heads(16, mlp_part),
            heads(16, mlp_part),
            total(mlp_part),
            heads(16, att_part),
            heads(16, att_part),
            total(att_part),
            sems(14),
            sems(2, 11),
            sems(2, 9),
            sems(2, 2, peers),
            sems(2, peers),
            sems(2, peers),
            sems(2, peers),
            sems(2, peers),
            sems(2, peers),
            sems(4, peers),
            sems(4, peers),
        ],
        compiler_params=pltpu.CompilerParams(
            collective_id=0, has_side_effects=True, vmem_limit_bytes=VMEM_LIMIT
        ),
        name="run_layer",
    )(index, tokens, cotangent, *weights, *tables, biases, value_bias, hidden_bias, gains)


def assemble_kernel(
    chosen_ref, down_in, out_down_in, up_in, hidden_up_in, hidden_down_in, outcome_in, grad_in, outcome_out, grad_out, *tables
):
    sources = (down_in, out_down_in, up_in, hidden_up_in, hidden_down_in)
    group = tables[0].shape[0]
    for part in range(group):
        number = pl.program_id(0) * group + part
        masks = [chosen_ref[seq, pl.ds(number, 1), 0:1] > 0.0 for seq in range(2)]
        for source, table in zip(sources, tables):
            for i in range(source.shape[1]):
                value = jnp.zeros(source.shape[2:], F32)
                for seq, mask in enumerate(masks):
                    value = value + jnp.where(mask, source[seq, i].astype(F32), 0.0)
                table[part, i] = value
    outcome_out[...] = outcome_in[...]
    grad_out[...] = grad_in[...]


def assemble(chosen, terms, outcome, grad_tokens):
    adapters = chosen.shape[1]
    steps = adapters // 2
    block = outcome.shape[0] // steps
    inputs = (chosen, *(term.reshape((2, -1) + term.shape[-2:]) for term in terms))

    def whole(array):
        return pl.BlockSpec(array.shape, lambda i: (0,) * array.ndim)

    def part(shape):
        return pl.BlockSpec(shape, lambda i: (i,) + (0,) * (len(shape) - 1))

    rows_spec = part((block, outcome.shape[1]))
    tables = [term.shape[1:] for term in inputs[1:]]
    return pl.pallas_call(
        assemble_kernel,
        grid=(steps,),
        out_shape=[
            jax.ShapeDtypeStruct(outcome.shape, BF16),
            jax.ShapeDtypeStruct(grad_tokens.shape, F32),
            *(jax.ShapeDtypeStruct((adapters,) + shape, F32) for shape in tables),
        ],
        in_specs=[*(whole(array) for array in inputs), rows_spec, rows_spec],
        out_specs=[rows_spec, rows_spec, *(part((adapters // steps,) + shape) for shape in tables)],
        compiler_params=pltpu.CompilerParams(vmem_limit_bytes=VMEM_LIMIT),
        name="assemble",
    )(*inputs, outcome, grad_tokens)


def heads_body(
    tokens,
    cotangent,
    sequence_adapter_index,
    query_key_value_weight,
    output_weight,
    first_feed_weight,
    second_feed_weight,
    biases,
    value_bias_vector,
    first_feed_bias,
    norm_gain_pair,
    adapter_down_factors,
    output_down_factor,
    adapter_up_factors,
    hidden_up_factor,
    hidden_down_factor,
):
    width = tokens.shape[2]
    hidden = first_feed_bias.shape[0]
    outcome, grad_tokens, chosen, term_hd, term_uh, term_down, term_up, term_do, *_ = run_layer(
        sequence_adapter_index,
        tokens[0],
        cotangent[0],
        (query_key_value_weight, output_weight, first_feed_weight, second_feed_weight),
        (
            adapter_down_factors.reshape(-1, width),
            adapter_up_factors.reshape(-1, width),
            output_down_factor.reshape(-1, width),
            hidden_up_factor.reshape(-1, hidden),
            hidden_down_factor.reshape(-1, hidden),
        ),
        biases,
        value_bias_vector[None],
        first_feed_bias[None],
        norm_gain_pair,
    )
    outcome, grad_tokens, total_down, total_out_down, total_up, total_hidden_up, total_hidden_down = assemble(
        chosen, (term_down, term_do, term_up, term_uh, term_hd), outcome, grad_tokens
    )
    return (
        outcome[None],
        grad_tokens[None],
        total_down,
        total_out_down.reshape(output_down_factor.shape),
        total_up,
        total_hidden_up.reshape(hidden_up_factor.shape),
        total_hidden_down.reshape(hidden_down_factor.shape),
    )


def solution(mesh):
    one_head_each = mesh.shape["ctx"] == H and mesh.shape["fsdp"] == 2
    return jax.shard_map(
        heads_body if one_head_each else gather_body,
        mesh=mesh,
        in_specs=(
            P("fsdp", "ctx", None),
            P("fsdp", "ctx", None),
            P("fsdp"),
            P("fsdp", None),
            P("fsdp", None),
            P("fsdp", None),
            P("fsdp", None),
            P(),
            P(),
            P(),
            P(),
            P(),
            P(),
            P(),
            P(),
            P(),
        ),
        out_specs=(P("fsdp", "ctx", None), P("fsdp", "ctx", None), P(), P(), P(), P(), P()),
        check_vma=False,
    )
```

```python
import functools

import jax
import jax.numpy as jnp
from jax import lax
from jax.experimental import pallas as pl
from jax.experimental.pallas import tpu as pltpu
from jax.sharding import PartitionSpec as P

H = 16


EPSILON = 1e-05
HIGHEST = lax.Precision.HIGHEST


def exact_sum(form, left, right):
    return jnp.einsum(form, left, right, precision=HIGHEST, preferred_element_type=jnp.float32)


def plain_sum(form, left, right):
    return jnp.einsum(form, left, right, preferred_element_type=jnp.float32)


def layer_norm(value, gain, shift):
    center = value - jnp.mean(value, -1, keepdims=True)
    spread = jnp.mean(center * center, -1, keepdims=True)
    return center * lax.rsqrt(spread + EPSILON) * gain + shift


def attn_weights(query_key_value_weight, output_weight):
    return (
        lax.all_gather(query_key_value_weight, "fsdp", axis=0, tiled=True),
        lax.all_gather(output_weight, "fsdp", axis=0, tiled=True),
    )


def mlp_weights(first_feed_weight, second_feed_weight):
    return (
        lax.all_gather(first_feed_weight, "fsdp", axis=0, tiled=True),
        lax.all_gather(second_feed_weight, "fsdp", axis=0, tiled=True),
    )


def to_heads(input_array):
    return input_array.reshape(
        input_array.shape[0], input_array.shape[1], H, input_array.shape[2] // H
    )


def row_block(input_array, block_index, block_rows):
    return lax.dynamic_slice_in_dim(input_array, block_index * block_rows, block_rows, 1)


def block_grads(queries, grad_out, log_total, row_delta, keys_blk, values_blk):
    scores = plain_sum("sqhd,skhd->shqk", queries, keys_blk)
    probs = jnp.exp(scores - log_total[..., None])
    prob_low = probs.astype(jnp.bfloat16)
    grad_probs = plain_sum("sqhd,skhd->shqk", grad_out, values_blk)
    grad_scores = (probs * (grad_probs - row_delta[..., None])).astype(jnp.bfloat16)
    return (prob_low, grad_scores)


def attention_forward(queries_heads, keys_heads, values_heads):
    seq_count, row_count, head_count, head_size = queries_heads.shape
    length = keys_heads.shape[1]
    block_rows = min(512, length)
    block_count = length // block_rows

    def max_step(running, block_index):
        running_max, running_total = running
        scores = plain_sum(
            "sqhd,skhd->shqk", queries_heads, row_block(keys_heads, block_index, block_rows)
        )
        new_max = jnp.maximum(running_max, jnp.max(scores, -1))
        running_total = running_total * jnp.exp(running_max - new_max) + jnp.sum(
            jnp.exp(scores - new_max[..., None]), -1
        )
        return ((new_max, running_total), None)

    start_max = jnp.full((seq_count, head_count, row_count), -1e30, jnp.float32)
    start_total = jnp.zeros((seq_count, head_count, row_count), jnp.float32)
    (final_max, final_total), unused = lax.scan(
        max_step, (start_max, start_total), jnp.arange(block_count)
    )
    log_total = final_max + jnp.log(final_total)

    def value_step(running, block_index):
        scores = plain_sum(
            "sqhd,skhd->shqk", queries_heads, row_block(keys_heads, block_index, block_rows)
        )
        prob_low = jnp.exp(scores - log_total[..., None]).astype(jnp.bfloat16)
        return (
            running
            + plain_sum(
                "shqk,skhd->sqhd", prob_low, row_block(values_heads, block_index, block_rows)
            ),
            None,
        )

    context, unused = lax.scan(
        value_step, jnp.zeros(queries_heads.shape, jnp.float32), jnp.arange(block_count)
    )
    return (context, log_total)


def gather_body(
    tokens,
    cotangent,
    sequence_adapter_index,
    query_key_value_weight,
    output_weight,
    first_feed_weight,
    second_feed_weight,
    biases,
    value_bias_vector,
    first_feed_bias,
    norm_gain_pair,
    adapter_down_factors,
    output_down_factor,
    adapter_up_factors,
    hidden_up_factor,
    hidden_down_factor,
):
    seq_count, row_count, model_width = tokens.shape
    adapter_number = adapter_down_factors.shape[0]
    picker = (
        sequence_adapter_index[:, None] == jnp.arange(adapter_number, dtype=jnp.int32)[None, :]
    ).astype(jnp.float32)

    def select_adapter(table):
        return jnp.einsum("sa,a...->s...", picker, table.astype(jnp.float32), precision=HIGHEST)

    def to_adapters(per_seq):
        return jnp.einsum("sa,s...->a...", picker, per_seq, precision=HIGHEST)

    selected_down = select_adapter(adapter_down_factors)
    selected_output = select_adapter(output_down_factor)
    selected_up = select_adapter(adapter_up_factors)
    hup_sel = select_adapter(hidden_up_factor)
    hdown_sel = select_adapter(hidden_down_factor)
    down_low = selected_down.astype(jnp.bfloat16)
    out_low = selected_output.astype(jnp.bfloat16)
    hdown_low = hdown_sel.astype(jnp.bfloat16)
    wqkv_full, wout_full = attn_weights(query_key_value_weight, output_weight)
    projected = plain_sum("std,de->ste", tokens, wqkv_full)
    down_att = plain_sum("std,sjrd->sjtr", tokens, down_low[:, :3])
    lifted = exact_sum("sjtr,sjrd->sjtd", down_att, selected_up[:, :3])
    queries = ((projected[..., :model_width] + biases[0] + lifted[:, 0]) * 0.125).astype(
        jnp.bfloat16
    )
    keys_own = (projected[..., model_width : 2 * model_width] + lifted[:, 1]).astype(jnp.bfloat16)
    values_own = (projected[..., 2 * model_width :] + value_bias_vector + lifted[:, 2]).astype(
        jnp.bfloat16
    )
    keys_all, values_all = (
        lax.all_gather(keys_own, "ctx", axis=1, tiled=True),
        lax.all_gather(values_own, "ctx", axis=1, tiled=True),
    )
    queries_heads = to_heads(queries)
    keys_heads = to_heads(keys_all)
    values_heads = to_heads(values_all)
    context, log_total = attention_forward(queries_heads, keys_heads, values_heads)
    context = context.reshape(seq_count, row_count, model_width)
    context_low = context.astype(jnp.bfloat16)
    down_out = plain_sum("std,srd->str", context_low, out_low)
    branch = (
        plain_sum("std,de->ste", context_low, wout_full)
        + biases[1]
        + exact_sum("str,srd->std", down_out, selected_up[:, 3])
    )

    def first_norm(value):
        return layer_norm(value, norm_gain_pair[0], biases[3])

    def second_norm(value):
        return layer_norm(value, norm_gain_pair[1], biases[4])

    def gelu_exact(value):
        return jax.nn.gelu(value, approximate=False)

    normed, norm_back = jax.vjp(first_norm, tokens.astype(jnp.float32) + branch)
    normed_low = normed.astype(jnp.bfloat16)
    wfc1_full, wfc2_full = mlp_weights(first_feed_weight, second_feed_weight)
    down_fc1 = plain_sum("std,srd->str", normed_low, down_low[:, 3])
    hidden_pre = (
        plain_sum("std,df->stf", normed_low, wfc1_full)
        + first_feed_bias
        + exact_sum("str,srf->stf", down_fc1, hup_sel)
    )
    activated, gelu_back = jax.vjp(gelu_exact, hidden_pre)
    act_low = activated.astype(jnp.bfloat16)
    down_fc2 = plain_sum("stf,srf->str", act_low, hdown_low)
    mixed_out = (
        plain_sum("stf,fd->std", act_low, wfc2_full)
        + biases[2]
        + exact_sum("str,srd->std", down_fc2, selected_up[:, 4])
    )
    outcome, out_back = jax.vjp(second_norm, normed + mixed_out)
    (grad_sum2,) = out_back(cotangent.astype(jnp.float32))
    grad_mixed = grad_sum2.astype(jnp.bfloat16)
    grad_up_fc2 = exact_sum("str,std->srd", down_fc2, grad_mixed)
    grad_rank_fc2 = exact_sum("std,srd->str", grad_mixed, selected_up[:, 4]).astype(jnp.bfloat16)
    grad_hdown = plain_sum("str,stf->srf", grad_rank_fc2, act_low)
    wfc1_full, wfc2_full = mlp_weights(first_feed_weight, second_feed_weight)
    grad_act = (
        plain_sum("std,fd->stf", grad_mixed, wfc2_full)
        + plain_sum("str,srf->stf", grad_rank_fc2, hdown_low)
    ).astype(jnp.bfloat16)
    (grad_hidden,) = gelu_back(grad_act.astype(jnp.float32))
    grad_hidden = grad_hidden.astype(jnp.bfloat16)
    grad_hup = exact_sum("str,stf->srf", down_fc1, grad_hidden)
    grad_rank_fc1 = exact_sum("stf,srf->str", grad_hidden, hup_sel).astype(jnp.bfloat16)
    grad_down_fc1 = plain_sum("str,std->srd", grad_rank_fc1, normed_low)
    grad_normed_low = (
        plain_sum("stf,df->std", grad_hidden, wfc1_full)
        + plain_sum("str,srd->std", grad_rank_fc1, down_low[:, 3])
    ).astype(jnp.bfloat16)
    (grad_resid,) = norm_back(grad_sum2 + grad_normed_low.astype(jnp.float32))
    mlp_hup = to_adapters(grad_hup)
    mlp_hdown = to_adapters(grad_hdown)
    mlp_fc1 = to_adapters(grad_down_fc1)
    mlp_fc2 = to_adapters(grad_up_fc2)
    mlp_hup, mlp_hdown, mlp_fc1, mlp_fc2 = lax.psum(
        (mlp_hup, mlp_hdown, mlp_fc1, mlp_fc2), ("ctx", "fsdp")
    )
    grad_branch = grad_resid.astype(jnp.bfloat16)
    grad_up_out = exact_sum("str,std->srd", down_out, grad_branch)
    grad_rank_out = exact_sum("std,srd->str", grad_branch, selected_up[:, 3]).astype(jnp.bfloat16)
    grad_out_down = plain_sum("str,std->srd", grad_rank_out, context_low)
    wqkv_full, wout_full = attn_weights(query_key_value_weight, output_weight)
    grad_context = (
        plain_sum("std,ed->ste", grad_branch, wout_full)
        + plain_sum("str,srd->std", grad_rank_out, out_low)
    ).astype(jnp.bfloat16)
    row_delta = jnp.sum(to_heads(grad_context.astype(jnp.float32) * context), -1)
    delta_heads = jnp.swapaxes(row_delta, 1, 2)
    grad_heads = to_heads(grad_context)
    length = keys_all.shape[1]
    block_rows = min(512, length)
    block_count = length // block_rows

    def key_step(block_index, running):
        grad_query, grad_key, grad_value = running
        keys_blk = row_block(keys_heads, block_index, block_rows)
        values_blk = row_block(values_heads, block_index, block_rows)
        prob_low, grad_scores = block_grads(
            queries_heads, grad_heads, log_total, delta_heads, keys_blk, values_blk
        )
        grad_query = grad_query + plain_sum("shqk,skhd->sqhd", grad_scores, keys_blk)
        grad_key = lax.dynamic_update_slice_in_dim(
            grad_key,
            plain_sum("shqk,sqhd->skhd", grad_scores, queries_heads),
            block_index * block_rows,
            1,
        )
        grad_value = lax.dynamic_update_slice_in_dim(
            grad_value,
            plain_sum("shqk,sqhd->skhd", prob_low, grad_heads),
            block_index * block_rows,
            1,
        )
        return (grad_query, grad_key, grad_value)

    start_query = jnp.zeros(queries_heads.shape, jnp.float32)
    start_keys = jnp.zeros(keys_heads.shape, jnp.float32)
    grad_query, grad_key_all, grad_value_all = lax.fori_loop(
        0, block_count, key_step, (start_query, start_keys, start_keys)
    )
    grad_keys, grad_values = (
        lax.psum_scatter(
            grad_key_all.reshape(seq_count, length, model_width).astype(jnp.bfloat16),
            "ctx",
            scatter_dimension=1,
            tiled=True,
        ).astype(jnp.float32),
        lax.psum_scatter(
            grad_value_all.reshape(seq_count, length, model_width).astype(jnp.bfloat16),
            "ctx",
            scatter_dimension=1,
            tiled=True,
        ).astype(jnp.float32),
    )
    grad_qlin = grad_query.reshape(seq_count, row_count, model_width).astype(jnp.bfloat16) * 0.125
    grad_key_low = grad_keys.astype(jnp.bfloat16)
    grad_value_low = grad_values.astype(jnp.bfloat16)
    stacked = jnp.stack([grad_qlin, grad_key_low, grad_value_low], 1)
    grad_up_att = exact_sum("sjtr,sjtd->sjrd", down_att, stacked)
    grad_rank_att = exact_sum("sjtd,sjrd->sjtr", stacked, selected_up[:, :3]).astype(jnp.bfloat16)
    grad_down_att = plain_sum("sjtr,std->sjrd", grad_rank_att, tokens)
    joined = jnp.concatenate([grad_qlin, grad_key_low, grad_value_low], -1)
    grad_tokens = (
        grad_resid
        + plain_sum("ste,de->std", joined, wqkv_full)
        + plain_sum("sjtr,sjrd->std", grad_rank_att, down_low[:, :3])
    )
    attn_down = to_adapters(grad_down_att)
    attn_out = to_adapters(grad_out_down)
    attn_up = to_adapters(jnp.concatenate([grad_up_att, grad_up_out[:, None]], 1))
    attn_down, attn_out, attn_up = lax.psum((attn_down, attn_out, attn_up), ("ctx", "fsdp"))
    total_down = jnp.concatenate([attn_down, mlp_fc1[:, None]], 1)
    total_up = jnp.concatenate([attn_up, mlp_fc2[:, None]], 1)
    return (
        outcome.astype(jnp.bfloat16),
        grad_tokens,
        total_down,
        attn_out,
        total_up,
        mlp_hup,
        mlp_hdown,
    )


BF16 = jnp.bfloat16
F32 = jnp.float32
LOG2E = 1.4426950408889634
VMEM_LIMIT = 60 * 2**20
MESH = pl.DeviceIdType.MESH


def dot32(left, right):
    return jnp.dot(left, right, preferred_element_type=F32)


def dot_nt(left, right):
    return lax.dot_general(left, right, (((1,), (1,)), ((), ())), preferred_element_type=F32)


def dot_tn(left, right):
    return lax.dot_general(left, right, (((0,), (0,)), ((), ())), preferred_element_type=F32)


def split_three(value):
    high = value.astype(BF16)
    rest = value - high.astype(F32)
    middle = rest.astype(BF16)
    return high, middle, (rest - middle.astype(F32)).astype(BF16)


def flip(value):
    return value.astype(F32).T.astype(BF16)


def remote(src, dst, send_sem, recv_sem, device):
    return pltpu.make_async_remote_copy(
        src_ref=src,
        dst_ref=dst,
        send_sem=send_sem,
        recv_sem=recv_sem,
        device_id=device,
        device_id_type=MESH,
    )


class Place:
    def __init__(self):
        self.ctx = lax.axis_index("ctx")
        self.core = lax.axis_index("fsdp")
        self.half = self.ctx // (H // 2)
        self.low = self.ctx % (H // 2)
        self.me = self.low * 2 + self.core
        self.swaps = self.core != self.half
        self.pair = (self.core + self.half) % 2
        self.sibling = (self.ctx, 1 - self.core)
        self.partner = ((self.ctx + H // 2) % H, 1 - self.core)

    def peer(self, step):
        number = self.me ^ step
        return (self.half * (H // 2) + number // 2, number % 2)

    def order(self, turn):
        return 2 * (turn % (H // 2)) + (turn // (H // 2) + self.pair) % 2

    def greet(self):
        barrier = pltpu.get_barrier_semaphore()
        for step in range(1, H):
            pl.semaphore_signal(barrier, inc=1, device_id=self.peer(step), device_id_type=MESH)
        pl.semaphore_signal(barrier, inc=1, device_id=self.partner, device_id_type=MESH)
        pl.semaphore_wait(barrier, H)


def sum_copies(mine, parts, total, sems, place):
    own = total.at[place.pair, place.low, place.half]
    other = total.at[place.pair, place.low, 1 - place.half]
    column = total.at[place.pair]
    scatter = [
        remote(mine.at[place.me ^ step], parts.at[step], sems.at[0, step], sems.at[1, step], place.peer(step))
        for step in range(1, H)
    ]
    cross = remote(own, own, sems.at[0, 0], sems.at[1, 0], place.partner)
    first = [
        remote(own, own, sems.at[2, step], sems.at[3, step], place.peer(step))
        for step in range(2, H, 2)
    ]
    second = [
        remote(other, other, sems.at[2, step + 1], sems.at[3, step + 1], place.peer(step))
        for step in range(2, H, 2)
    ]
    last = remote(column, column, sems.at[2, 0], sems.at[3, 0], place.sibling)
    return scatter, cross, first, second, last


def sum_parts(scatter, mine, parts, total, place):
    value = mine[place.me].astype(F32)
    for step, copy in enumerate(scatter, 1):
        copy.wait_recv()
        value = value + parts[step].astype(F32)
    total[place.pair, place.low, place.half] = value.astype(BF16)


def put_term(mine, base, term):
    units = mine.shape[2] // 128
    for unit in range(term.shape[1] // 128):
        at = base // 128 + unit
        lanes = slice(at % units * 128, at % units * 128 + 128)
        mine[at // units, :, lanes] = term[:, unit * 128 : unit * 128 + 128].astype(BF16)


def layer_kernel(
    block_q,
    block_k,
    index_ref,
    tokens_ref,
    cotangent_ref,
    wqkv_ref,
    wout_ref,
    wfc1_ref,
    wfc2_ref,
    down_table,
    up_table,
    out_down_table,
    hidden_up_table,
    hidden_down_table,
    biases_ref,
    value_bias_ref,
    hidden_bias_ref,
    gains_ref,
    outcome_ref,
    grad_ref,
    chosen_out,
    hidden_down_out,
    hidden_up_out,
    down_out,
    up_out,
    out_down_out,
    wqkv_far,
    wfc1_far,
    wide,
    wfc2,
    wout,
    big,
    act,
    small,
    small_hidden,
    x,
    cotangent,
    rank_att,
    outgoing,
    qkv,
    leaving,
    arrived,
    incoming,
    context,
    state,
    qta,
    gta,
    kk,
    vv,
    kt,
    both,
    dkv_sum,
    dq_in,
    dkv_out,
    dkv_in,
    grad_out,
    grad_in,
    mlp_mine,
    mlp_parts,
    mlp_total,
    att_mine,
    att_parts,
    att_total,
    load_sem,
    core_sem,
    swap_sem,
    kv_sem,
    q_sem,
    back_sem,
    grad_sem,
    dq_sem,
    dkv_sem,
    mlp_sem,
    att_sem,
):
    peers, _, rows = qkv.shape
    length = peers * rows
    width = x.shape[1]
    hidden = hidden_bias_ref.shape[1]
    adapters = hidden_up_table.shape[0] // 16
    place = Place()
    me, core = place.me, place.core
    other = 1 - core
    wqkv = wide.at[:, 0 : 3 * width]
    up_at = down_table.shape[0]
    out_down_at = up_at + up_table.shape[0]

    def half_of(full, owner):
        count = full.shape[0] // 2
        return full.at[pl.ds(pl.multiple_of(owner * count, count), count), :]

    def load(source, target, number):
        return pltpu.make_async_copy(source, target, load_sem.at[number])

    def to_sibling(source, target, number):
        return remote(source, target, core_sem.at[0, number], core_sem.at[1, number], place.sibling)

    load_wqkv = load(wqkv_ref, half_of(wqkv, core), 0)
    load_wout = load(wout_ref, half_of(wout, core), 1)
    load_tables = [
        load(down_table, wfc2.at[0:up_at], 2),
        load(up_table, wfc2.at[up_at:out_down_at], 3),
        load(out_down_table, wfc2.at[out_down_at : out_down_at + out_down_table.shape[0]], 4),
        load(hidden_up_table, act.at[0 : 16 * adapters], 5),
        load(hidden_down_table, act.at[16 * adapters : 32 * adapters], 6),
    ]
    load_x = load(tokens_ref, x, 7)
    load_cotangent = load(cotangent_ref, cotangent, 8)
    load_wfc1 = load(wfc1_ref, half_of(wide, core), 9)
    load_wfc1_far = load(wfc1_far, half_of(wide, other), 10)
    load_wfc2 = load(wfc2_ref, half_of(wfc2, core), 11)
    again_wqkv = load(wqkv_ref, half_of(wqkv, core), 12)
    again_wqkv_far = load(wqkv_far, half_of(wqkv, other), 13)
    give_wqkv = to_sibling(wqkv_ref, half_of(wqkv, core), 0)
    give_wout = to_sibling(wout_ref, half_of(wout, core), 1)
    give_chosen = to_sibling(chosen_out.at[core], chosen_out.at[core], 2)
    count = small.shape[0]
    give_small = [to_sibling(small, wide.at[0:count, 3 * width : 4 * width], 3)] + [
        to_sibling(
            small_hidden.at[:, part * width : (part + 1) * width],
            wide.at[count + 32 * part : count + 32 * part + 32, 3 * width : 4 * width],
            4 + part,
        )
        for part in range(hidden // width)
    ]
    give_wfc2 = to_sibling(wfc2_ref, half_of(wfc2, core), 8)
    give_wfc1 = to_sibling(wfc1_ref, wfc1_far, 9)
    give_wqkv_again = to_sibling(wqkv_ref, wqkv_far, 10)
    half_rows = rows // 2
    swap_x = [
        remote(
            tokens_ref.at[part * half_rows : (part + 1) * half_rows],
            x.at[part * half_rows : (part + 1) * half_rows],
            swap_sem.at[0, 7 + part],
            swap_sem.at[1, 7 + part],
            place.partner,
        )
        for part in range(2)
    ]
    swap_cotangent = remote(cotangent_ref, cotangent, swap_sem.at[0, 1], swap_sem.at[1, 1], place.partner)

    load_wqkv.start()
    for copy in load_tables:
        copy.start()
    load_wout.start()

    @pl.when(jnp.logical_not(place.swaps))
    def _():
        load_x.start()
        load_cotangent.start()

    adapter = index_ref[0]
    numbers = lax.broadcasted_iota(jnp.int32, chosen_out.shape[1:], 0)
    chosen_out[core] = (numbers == jnp.full(numbers.shape, adapter, jnp.int32)).astype(F32)
    place.greet()

    @pl.when(place.swaps)
    def _():
        for copy in swap_x:
            copy.start()

    give_wqkv.start()
    give_chosen.start()

    for copy in load_tables:
        copy.wait()

    def select(table, base, group, groups, target, at):
        chosen = jnp.full((16, table.shape[1]), adapter, jnp.int32)
        value = jnp.zeros((16, table.shape[1]), F32)
        for number in range(adapters):
            start = pl.multiple_of(base + 16 * (number * groups + group), 16)
            value = jnp.where(chosen == number, table[pl.ds(start, 16), :].astype(F32), value)
        target[pl.ds(pl.multiple_of(at + 16 * group, 16), 16), :] = value.astype(BF16)

    def select_down(group, _):
        select(wfc2, 0, group, 4, small, 0)
        return 0

    def select_up(group, _):
        select(wfc2, up_at, group, 5, small, 64)
        return 0

    lax.fori_loop(0, 4, select_down, 0)
    lax.fori_loop(0, 5, select_up, 0)
    select(wfc2, out_down_at, 0, 1, small, 144)
    for part in range(2):
        select(act, 16 * adapters * part, 0, 1, small_hidden, 16 * part)
    for copy in give_small:
        copy.start()
    give_wout.start()
    for copy in give_small:
        copy.wait()

    @pl.when(place.swaps)
    def _():
        small[...] = wide[0:count, 3 * width : 4 * width]
        for part in range(hidden // width):
            small_hidden[:, part * width : (part + 1) * width] = wide[
                count + 32 * part : count + 32 * part + 32, 3 * width : 4 * width
            ]

    hidden_up_ref = small_hidden.at[0:16]
    hidden_down_ref = small_hidden.at[16:32]
    out_down_ref = small.at[144:160]

    def down(j):
        return small[16 * j : 16 * j + 16]

    def up(j):
        return small[64 + 16 * j : 80 + 16 * j]

    load_wfc2.start()
    give_wfc2.start()

    load_wqkv.wait()
    give_wqkv.wait_recv()

    def project(half, part):
        here = slice(half * half_rows, (half + 1) * half_rows)
        cols = slice(part * width, (part + 1) * width)
        value = dot32(x[here, :], wqkv[:, cols]) + dot32(rank_att[here, part * 16 : part * 16 + 16], up(part))
        if part == 0:
            value = (value + biases_ref[0:1, :]) * 0.125
        if part == 2:
            value = value + value_bias_ref[...]
        for two in range(peers // 2):
            turned = value[:, two * 128 : two * 128 + 128].T.astype(BF16)
            outgoing[2 * two, part * 64 : part * 64 + 64, here] = turned[0:64]
            outgoing[2 * two + 1, part * 64 : part * 64 + 64, here] = turned[64:128]

    def kv_copy(step, half):
        here = slice(half * half_rows, (half + 1) * half_rows)
        return remote(
            outgoing.at[me ^ step, 64:192, here],
            qkv.at[step, 64:192, here],
            kv_sem.at[0, half, step],
            kv_sem.at[1, half, step],
            place.peer(step),
        )

    def q_copy(step):
        return remote(
            outgoing.at[me ^ step, 0:64], qkv.at[step, 0:64], q_sem.at[0, step], q_sem.at[1, step], place.peer(step)
        )

    def back_copy(step):
        return remote(leaving.at[step], arrived.at[me], back_sem.at[0, step], back_sem.at[1, step], place.peer(step))

    steps = length // block_k
    group = block_q // rows
    key_group = block_k // rows
    for half in range(2):
        here = slice(half * half_rows, (half + 1) * half_rows)

        @pl.when(place.swaps)
        def _():
            swap_x[half].wait_recv()

        if half == 0:

            @pl.when(jnp.logical_not(place.swaps))
            def _():
                load_x.wait()

        rank_att[here, :] = dot_nt(x[here, :], small[0:48]).astype(BF16)
        project(half, 1)
        project(half, 2)
        for step in range(1, peers):
            kv_copy(step, half).start()
        project(half, 0)
    for step in range(1, peers):
        q_copy(step).start()
    give_wfc1.start()
    give_wqkv_again.start()
    load_wfc1.start()
    qkv[0] = outgoing[me]

    row_at = lax.broadcasted_iota(jnp.int32, (16, rows), 0)
    ones = (row_at == 0).astype(F32).astype(BF16)
    minus = jnp.where(lax.broadcasted_iota(jnp.int32, (rows, 16), 1) < 3, -1.0, 0.0).astype(BF16)
    minus_rows = jnp.where(lax.broadcasted_iota(jnp.int32, (64, rows), 0) < 3, -1.0, 0.0).astype(BF16)

    def tail(value):
        at = lax.broadcasted_iota(jnp.int32, (16, value.shape[1]), 0)
        high, middle, low = (part.astype(F32) for part in split_three(value))
        return jnp.where(at == 0, high, jnp.where(at == 1, middle, jnp.where(at == 2, low, 0.0))).astype(BF16)

    def take_key(turn):
        cols = pl.ds(pl.multiple_of(turn * rows, rows), rows)
        step = place.order(turn)

        @pl.when(step > 0)
        def _():
            kv_copy(step, 0).wait_recv()
            kv_copy(step, 1).wait_recv()

        key = qkv[step, 64:128, :]
        value = qkv[step, 128:192, :]
        kt[:, cols] = key
        kk[cols, 0:128] = flip(jnp.concatenate([key, key], 0))
        kk[cols, 128:144] = minus
        vv[cols, :] = flip(jnp.concatenate([value, minus_rows], 0))
        gta[0:64, cols] = value
        gta[64:80, cols] = ones
        gta[80:128, cols] = jnp.zeros((48, rows), BF16)

    def take_keys(i):
        def one(part, _):
            take_key(i * key_group + part)
            return 0

        lax.fori_loop(0, key_group, one, 0)

    def forward_part(i, low, high, arriving):
        def take_query(part, _):
            turn = i * group + part
            step = place.order(turn)
            here = pl.ds(pl.multiple_of(turn * rows, rows), rows)

            @pl.when(step > 0)
            def _():
                q_copy(step).wait_recv()

            query = qkv[step, 0:64, :].astype(F32) * LOG2E
            high = query.astype(BF16)
            qta[0:64, here] = high
            qta[64:128, here] = (query - high.astype(F32)).astype(BF16)
            return 0

        if low == 0:
            lax.fori_loop(0, group, take_query, 0)
        cols = pl.ds(pl.multiple_of(i * block_q, block_q), block_q)
        query = qta.at[0:128, cols]
        if arriving:

            @pl.when(i == 0)
            def _():
                take_keys(low)

        block = dot32(kk[low * block_k : (low + 1) * block_k, 0:128], query[...])
        big[0:block_k] = block

        def half(j, now, carry):
            peak, running, total = carry
            later = jnp.minimum(j + 1, high - 1)
            here = pl.ds(pl.multiple_of(j * block_k, block_k), block_k)
            there = pl.ds(pl.multiple_of(later * block_k, block_k), block_k)
            if arriving:

                @pl.when(jnp.logical_and(i == 0, j + 1 < high))
                def _():
                    take_keys(later)

            ahead = dot32(kk[there, 0:128], query[...])
            big[(1 - now) * block_k : (2 - now) * block_k] = ahead
            new = jnp.maximum(running, peak)
            weights = jnp.exp2(big[now * block_k : (now + 1) * block_k] - new).astype(BF16)
            total = total * jnp.exp2(running - new) + dot32(gta[0:80, here], weights)
            return jnp.max(ahead, 0, keepdims=True), new, total

        def pair(j, carry):
            return half(low + 2 * j + 1, 1, half(low + 2 * j, 0, carry))

        if low == 0:
            running, total = jnp.full((1, block_q), -jnp.inf, F32), jnp.zeros((80, block_q), F32)
        else:
            running = state[1:2, cols]
            total = jnp.concatenate([context[:, cols], state[0:1, cols], jnp.zeros((15, block_q), F32)], 0)
        _, top, total = lax.fori_loop(
            0, (high - low) // 2, pair, (jnp.max(block, 0, keepdims=True), running, total)
        )
        weight_sum = total[64:65]
        if high < steps:
            context[:, cols] = total[0:64]
            state[0:1, cols] = weight_sum
            state[1:2, cols] = top
            return
        result = total[0:64] / weight_sum
        context[:, cols] = result
        qta[128:144, cols] = tail(top + jnp.log2(weight_sum))
        low_result = result.astype(BF16)
        for part in range(group):
            step = place.order(i * group + part)
            leaving[step] = low_result[:, part * rows : (part + 1) * rows]

            @pl.when(step > 0)
            def _():
                back_copy(step).start()

    query_steps = length // block_q

    def forward_parts(first, last, low, high, arriving):
        def one(i, _):
            forward_part(i, low, high, arriving)
            return 0

        lax.fori_loop(first, last, one, 0)

    forward_parts(0, query_steps // 2, 0, steps // 2, True)
    give_wfc1.wait_recv()
    load_wfc1_far.start()
    forward_parts(0, query_steps // 2, steps // 2, steps, True)

    @pl.when(place.swaps)
    def _():
        swap_cotangent.start()

    forward_parts(query_steps // 2, query_steps, 0, steps, False)
    arrived[me] = leaving[0]

    def mean(value):
        return jnp.mean(value, -1, keepdims=True)

    def norm_backward(grad, hat, scale):
        return scale * (grad - mean(grad) - hat * mean(grad * hat))

    load_wout.wait()
    give_wout.wait_recv()
    for step in range(1, peers):
        back_copy(step).wait_recv()
    context_low = flip(arrived[...].reshape(width, rows))
    rank_out = dot_nt(context_low, out_down_ref[...]).astype(BF16)
    resid = x[...].astype(F32) + dot32(context_low, wout[...]) + biases_ref[1:2] + dot32(rank_out, up(3))
    center = resid - mean(resid)
    scale_one = lax.rsqrt(mean(center * center) + EPSILON)
    hat_one = center * scale_one
    normed = hat_one * gains_ref[0:1] + biases_ref[3:4]
    normed_low = normed.astype(BF16)
    rank_one = dot_nt(normed_low, down(3)).astype(BF16)
    load_wfc1.wait()
    load_wfc1_far.wait()
    load_wfc2.wait()
    give_wfc2.wait_recv()
    piece = 1024
    rank_two = jnp.zeros((rows, 16), F32)
    mixed = normed + biases_ref[2:3]
    for part in range(hidden // piece):
        cols = slice(part * piece, (part + 1) * piece)
        pre = (
            dot32(normed_low, wide[:, cols])
            + hidden_bias_ref[:, cols]
            + dot32(rank_one, hidden_up_ref[:, cols])
        )
        share = 0.5 + 0.5 * lax.erf(pre * 0.7071067811865476)
        big[part * rows : (part + 1) * rows] = share + pre * (0.3989422804014327 * jnp.exp(-0.5 * pre * pre))
        active = (pre * share).astype(BF16)
        act[:, cols] = active
        rank_two = rank_two + dot_nt(active, hidden_down_ref[:, cols])
        mixed = mixed + dot32(active, wfc2[cols, :])
    rank_two = rank_two.astype(BF16)
    mixed = mixed + dot32(rank_two, up(4))
    center = mixed - mean(mixed)
    scale_two = lax.rsqrt(mean(center * center) + EPSILON)
    hat_two = center * scale_two

    @pl.when(place.swaps)
    def _():
        swap_cotangent.wait_recv()

    @pl.when(jnp.logical_not(place.swaps))
    def _():
        load_cotangent.wait()

    grad_sum = norm_backward(cotangent[...].astype(F32) * gains_ref[1:2], hat_two, scale_two)
    outcome = cotangent
    outcome[...] = (hat_two * gains_ref[1:2] + biases_ref[4:5]).astype(BF16)
    home_outcome = remote(outcome, outcome_ref, swap_sem.at[0, 2], swap_sem.at[1, 2], place.partner)

    @pl.when(place.swaps)
    def _():
        home_outcome.start()

    @pl.when(jnp.logical_not(place.swaps))
    def _():
        outcome_ref[...] = outcome[...]

    grad_mixed = grad_sum.astype(BF16)
    put_term(mlp_mine, 2 * hidden, dot_tn(rank_two, grad_mixed))
    grad_rank = dot_nt(grad_mixed, up(4)).astype(BF16)
    put_term(mlp_mine, 0, dot_tn(grad_rank, act[...]))
    grad_one = jnp.zeros((rows, 16), F32)
    grad_normed = jnp.zeros((rows, width), F32)
    for part in range(hidden // piece):
        cols = slice(part * piece, (part + 1) * piece)
        grad_act = dot_nt(grad_mixed, wfc2[cols, :]) + dot32(grad_rank, hidden_down_ref[:, cols])
        grad_hidden = (grad_act.astype(BF16).astype(F32) * big[part * rows : (part + 1) * rows]).astype(BF16)
        put_term(mlp_mine, hidden + part * piece, dot_tn(rank_one, grad_hidden))
        grad_one = grad_one + dot_nt(grad_hidden, hidden_up_ref[:, cols])
        grad_normed = grad_normed + dot_nt(grad_hidden, wide[:, cols])
    grad_one = grad_one.astype(BF16)
    put_term(mlp_mine, 2 * hidden + width, dot_tn(grad_one, normed_low))
    grad_normed = (grad_normed + dot32(grad_one, down(3))).astype(BF16).astype(F32)
    resid_grad = norm_backward((grad_sum + grad_normed) * gains_ref[0:1], hat_one, scale_one)
    grad_resid = big.at[0:rows]
    grad_resid[...] = resid_grad
    grad_branch = resid_grad.astype(BF16)
    put_term(mlp_mine, 2 * hidden + 2 * width, dot_tn(rank_out, grad_branch))
    grad_rank = dot_nt(grad_branch, up(3)).astype(BF16)
    put_term(mlp_mine, 2 * hidden + 3 * width, dot_tn(grad_rank, context_low))
    turned = dot_nt(wout[...], grad_branch) + lax.dot_general(
        out_down_ref[...], grad_rank, (((0,), (1,)), ((), ())), preferred_element_type=F32
    )
    for step in range(1, peers):
        kv_copy(step, 0).wait_send()
        kv_copy(step, 1).wait_send()
        q_copy(step).wait_send()
        back_copy(step).wait_send()
    outgoing[:, 0:64] = turned.astype(BF16).reshape(peers, 64, rows)

    def grad_copy(step):
        return remote(
            outgoing.at[me ^ step, 0:64], incoming.at[step], grad_sem.at[0, step], grad_sem.at[1, step], place.peer(step)
        )

    for step in range(1, peers):
        grad_copy(step).start()
    mlp_scatter, mlp_cross, mlp_first, mlp_second, mlp_last = sum_copies(mlp_mine, mlp_parts, mlp_total, mlp_sem, place)
    incoming[0] = outgoing[me, 0:64]
    give_wqkv_again.wait_recv()
    again_wqkv.start()
    again_wqkv_far.start()
    dkv_sum[...] = jnp.zeros_like(dkv_sum)
    first = lax.broadcasted_iota(jnp.int32, (block_k, 128), 1) < 64
    dq_out = leaving

    def dq_copy(step):
        return remote(dq_out.at[step], dq_in.at[me], dq_sem.at[0, step], dq_sem.at[1, step], place.peer(step))

    def dkv_copy(step):
        return remote(dkv_out.at[step], dkv_in.at[me], dkv_sem.at[0, step], dkv_sem.at[1, step], place.peer(step))

    def backward_step(turn, _):
        last = turn == query_steps - 1
        j = turn

        def take_grad(part, _):
            step = place.order(j * group + part)
            cols = pl.ds(pl.multiple_of((j * group + part) * rows, rows), rows)

            @pl.when(step > 0)
            def _():
                grad_copy(step).wait_recv()

            grad = incoming[step]
            gta[0:64, cols] = grad
            gta[64:80, cols] = tail(jnp.sum(grad.astype(F32) * context[:, cols], 0, keepdims=True))
            both[cols, :] = flip(jnp.concatenate([qkv[step, 0:64, :], grad], 0))
            return 0

        lax.fori_loop(0, group, take_grad, 0)
        cols = pl.ds(pl.multiple_of(j * block_q, block_q), block_q)

        def key_pair(pair, dq):
            found = []
            for side in range(2):
                i = 2 * pair + side
                here = pl.ds(pl.multiple_of(i * block_k, block_k), block_k)
                probs = jnp.exp2(dot32(kk[here, :], qta[:, cols]))
                change = dot32(vv[here, :], gta[:, cols])
                found.append((i, here, probs.astype(BF16), (probs * change).astype(BF16)))
            for i, here, probs, low in found:
                dv = dot32(probs, both[cols, :])
                dk = dot32(low, both[cols, :])
                dkv_sum[here, :] += jnp.where(first, dk, dv)
                dq = dq + dot32(kt[:, here], low)

            @pl.when(last)
            def _():
                for i, here, _, _ in found:
                    done = dkv_sum[here, :].astype(BF16)
                    for part in range(key_group):
                        step = place.order(i * key_group + part)
                        dkv_out[step] = done[part * rows : (part + 1) * rows]

                        @pl.when(step > 0)
                        def _():
                            dkv_copy(step).start()

            return dq

        dq = lax.fori_loop(0, steps // 2, key_pair, jnp.zeros((64, block_q), F32)).astype(BF16)
        for part in range(group):
            step = place.order(j * group + part)
            dq_out[step] = dq[:, part * rows : (part + 1) * rows]

            @pl.when(step > 0)
            def _():
                dq_copy(step).start()

        @pl.when(turn == query_steps // 4 - 1)
        def _():
            for copy in mlp_scatter:
                copy.start()

        @pl.when(turn == query_steps // 2 - 1)
        def _():
            sum_parts(mlp_scatter, mlp_mine, mlp_parts, mlp_total, place)
            mlp_cross.start()
            for copy in mlp_first:
                copy.start()

        @pl.when(turn == query_steps - 2)
        def _():
            mlp_cross.wait_recv()
            for copy in mlp_second:
                copy.start()

        return 0

    lax.fori_loop(0, query_steps, backward_step, 0)
    for copy in mlp_first + mlp_second:
        copy.wait_recv()
    mlp_last.start()

    def spread(total, parts):
        units = total.shape[4] // 128
        for half in range(2):
            for unit in range(peers * units):
                peer = unit // units
                lanes = slice(unit % units * 128, unit % units * 128 + 128)
                for target, low, high in parts:
                    if low <= unit * 128 < high:
                        at = unit * 128 - low
                        target(half)[:, at : at + 128] = total[(peer % 2 + half) % 2, peer // 2, half, :, lanes]

    joined = act.at[:, 0 : 3 * width]
    dq_in[me] = dq_out[0]
    dkv_in[me] = dkv_out[0]
    for step in range(1, peers):
        dkv_copy(step).wait_recv()
    left = lax.broadcasted_iota(jnp.int32, (rows, 128), 1) < 64
    for two in range(peers // 2):
        even = dkv_in[2 * two].astype(F32)
        odd = dkv_in[2 * two + 1].astype(F32)
        cols = slice(width + two * 128, width + two * 128 + 128)
        joined[:, cols] = jnp.where(left, even, pltpu.roll(odd, 64, 1)).astype(BF16)
        cols = slice(2 * width + two * 128, 2 * width + two * 128 + 128)
        joined[:, cols] = jnp.where(left, pltpu.roll(even, 64, 1), odd).astype(BF16)
    def ranks_of(part):
        grad = joined[:, part * width : (part + 1) * width]
        ranks[part] = dot_nt(grad, up(part)).astype(BF16)

    def terms_of(part):
        grad = joined[:, part * width : (part + 1) * width]
        put_term(att_mine, part * width, dot_tn(rank_att[:, part * 16 : part * 16 + 16], grad))
        put_term(att_mine, (3 + part) * width, dot_tn(ranks[part], x[...]))

    ranks = {}
    att_scatter, att_cross, att_first, att_second, att_last = sum_copies(att_mine, att_parts, att_total, att_sem, place)
    again_wqkv.wait()
    again_wqkv_far.wait()
    for part in (1, 2):
        ranks_of(part)
        terms_of(part)
    for step in range(1, peers):
        dq_copy(step).wait_recv()
    joined[:, 0:width] = (dq_in[...].reshape(width, rows).astype(F32).T * 0.125).astype(BF16)
    ranks_of(0)
    terms_of(0)
    for copy in att_scatter:
        copy.start()
    piece = width // 4
    home = [
        remote(
            grad_out.at[:, part * piece : (part + 1) * piece],
            grad_in.at[:, part * piece : (part + 1) * piece],
            swap_sem.at[0, 3 + part],
            swap_sem.at[1, 3 + part],
            place.partner,
        )
        for part in range(4)
    ]
    mlp_last.wait_recv()
    for part in range(4):
        cols = slice(part * piece, (part + 1) * piece)
        total = grad_resid[:, cols] + dot_nt(joined[...], wqkv[cols, :])
        for j in range(3):
            total = total + dot32(ranks[j], small[16 * j : 16 * j + 16, cols])
        grad_ref[:, cols] = total
        grad_out[:, cols] = total.astype(BF16)

        @pl.when(place.swaps)
        def _():
            home[part].start()

    sum_parts(att_scatter, att_mine, att_parts, att_total, place)
    att_cross.start()
    for copy in att_first:
        copy.start()
    spread(
        mlp_total,
        (
            (lambda half: hidden_down_out.at[half], 0, hidden),
            (lambda half: hidden_up_out.at[half], hidden, 2 * hidden),
            (lambda half: up_out.at[half, 4], 2 * hidden, 2 * hidden + width),
            (lambda half: down_out.at[half, 3], 2 * hidden + width, 2 * hidden + 2 * width),
            (lambda half: up_out.at[half, 3], 2 * hidden + 2 * width, 2 * hidden + 3 * width),
            (lambda half: out_down_out.at[half], 2 * hidden + 3 * width, 2 * hidden + 4 * width),
        ),
    )
    att_cross.wait_recv()
    for copy in att_second:
        copy.start()
    for copy in att_first + att_second:
        copy.wait_recv()
    att_last.start()

    @pl.when(place.swaps)
    def _():
        for part in range(4):
            home[part].wait_recv()
            cols = slice(part * piece, (part + 1) * piece)
            grad_ref[:, cols] = grad_in[:, cols].astype(F32)
        for part in range(4):
            home[part].wait_send()
        home_outcome.wait()
        for copy in swap_x:
            copy.wait_send()
        swap_cotangent.wait_send()

    att_last.wait_recv()
    spread(
        att_total,
        tuple(
            (functools.partial(lambda part, half: up_out.at[half, part], part), part * width, (part + 1) * width)
            for part in range(3)
        )
        + tuple(
            (functools.partial(lambda part, half: down_out.at[half, part], part), (3 + part) * width, (4 + part) * width)
            for part in range(3)
        ),
    )
    for step in range(1, peers):
        grad_copy(step).wait_send()
        dq_copy(step).wait_send()
        dkv_copy(step).wait_send()
    for copies in ((mlp_scatter, mlp_first, mlp_second), (att_scatter, att_first, att_second)):
        for copy in copies[0] + copies[1] + copies[2]:
            copy.wait_send()
    for copy in (mlp_cross, mlp_last, att_cross, att_last):
        copy.wait_send()
    for copy in (give_wqkv, give_wout, give_wfc2, give_wfc1, give_wqkv_again):
        copy.wait_send()
    give_chosen.wait()


def run_layer(index, tokens, cotangent, weights, tables, biases, value_bias, hidden_bias, gains):
    rows, width = tokens.shape
    peers = H
    length = peers * rows
    hidden = hidden_bias.shape[1]
    block_q, block_k = 1024, 512
    vmem = pl.BlockSpec(memory_space=pltpu.VMEM)
    hbm = pl.BlockSpec(memory_space=pl.ANY)
    mlp_part = (2 * hidden + 4 * width) // peers
    att_part = 6 * width // peers

    def out(shape, dtype=BF16):
        return jax.ShapeDtypeStruct(shape, dtype)

    def total(part):
        return pltpu.VMEM((2, peers // 2, 2, 16, part), BF16)

    def heads(*shape):
        return pltpu.VMEM((peers,) + shape, BF16)

    def sems(*shape):
        return pltpu.SemaphoreType.DMA(shape)

    return pl.pallas_call(
        functools.partial(layer_kernel, block_q, block_k),
        out_shape=[
            out((rows, width)),
            out((rows, width), F32),
            out((2, 8, 128), F32),
            out((2, 16, hidden)),
            out((2, 16, hidden)),
            out((2, 4, 16, width)),
            out((2, 5, 16, width)),
            out((2, 16, width)),
            out(weights[0].shape),
            out(weights[2].shape),
        ],
        in_specs=[pl.BlockSpec(memory_space=pltpu.SMEM)] + [hbm] * 11 + [vmem] * 4,
        out_specs=[vmem] * 8 + [hbm] * 2,
        scratch_shapes=[
            pltpu.VMEM((width, hidden), BF16),
            pltpu.VMEM((hidden, width), BF16),
            pltpu.VMEM((width, width), BF16),
            pltpu.VMEM((max(4 * rows, 2 * block_k), 1024), F32),
            pltpu.VMEM((rows, hidden), BF16),
            pltpu.VMEM((160, width), BF16),
            pltpu.VMEM((32, hidden), BF16),
            pltpu.VMEM((rows, width), BF16),
            pltpu.VMEM((rows, width), BF16),
            pltpu.VMEM((rows, 48), BF16),
            heads(192, rows),
            heads(192, rows),
            heads(64, rows),
            heads(64, rows),
            heads(64, rows),
            pltpu.VMEM((64, length), F32),
            pltpu.VMEM((8, length), F32),
            pltpu.VMEM((144, length), BF16),
            pltpu.VMEM((128, length), BF16),
            pltpu.VMEM((length, 144), BF16),
            pltpu.VMEM((length, 128), BF16),
            pltpu.VMEM((64, length), BF16),
            pltpu.VMEM((length, 128), BF16),
            pltpu.VMEM((length, 128), F32),
            heads(64, rows),
            heads(rows, 128),
            heads(rows, 128),
            pltpu.VMEM((rows, width), BF16),
            pltpu.VMEM((rows, width), BF16),
            heads(16, mlp_part),
            heads(16, mlp_part),
            total(mlp_part),
            heads(16, att_part),
            heads(16, att_part),
            total(att_part),
            sems(14),
            sems(2, 11),
            sems(2, 9),
            sems(2, 2, peers),
            sems(2, peers),
            sems(2, peers),
            sems(2, peers),
            sems(2, peers),
            sems(2, peers),
            sems(4, peers),
            sems(4, peers),
        ],
        compiler_params=pltpu.CompilerParams(
            collective_id=0, has_side_effects=True, vmem_limit_bytes=VMEM_LIMIT
        ),
        name="run_layer",
    )(index, tokens, cotangent, *weights, *tables, biases, value_bias, hidden_bias, gains)


def assemble_kernel(
    chosen_ref, down_in, out_down_in, up_in, hidden_up_in, hidden_down_in, outcome_in, grad_in, outcome_out, grad_out, *tables
):
    sources = (down_in, out_down_in, up_in, hidden_up_in, hidden_down_in)
    group = tables[0].shape[0]
    for part in range(group):
        number = pl.program_id(0) * group + part
        masks = [chosen_ref[seq, pl.ds(number, 1), 0:1] > 0.0 for seq in range(2)]
        for source, table in zip(sources, tables):
            for i in range(source.shape[1]):
                value = jnp.zeros(source.shape[2:], F32)
                for seq, mask in enumerate(masks):
                    value = value + jnp.where(mask, source[seq, i].astype(F32), 0.0)
                table[part, i] = value
    outcome_out[...] = outcome_in[...]
    grad_out[...] = grad_in[...]


def assemble(chosen, terms, outcome, grad_tokens):
    adapters = chosen.shape[1]
    steps = adapters // 4
    block = outcome.shape[0] // steps
    inputs = (chosen, *(term.reshape((2, -1) + term.shape[-2:]) for term in terms))

    def whole(array):
        return pl.BlockSpec(array.shape, lambda i: (0,) * array.ndim)

    def part(shape):
        return pl.BlockSpec(shape, lambda i: (i,) + (0,) * (len(shape) - 1))

    rows_spec = part((block, outcome.shape[1]))
    tables = [term.shape[1:] for term in inputs[1:]]
    return pl.pallas_call(
        assemble_kernel,
        grid=(steps,),
        out_shape=[
            jax.ShapeDtypeStruct(outcome.shape, BF16),
            jax.ShapeDtypeStruct(grad_tokens.shape, F32),
            *(jax.ShapeDtypeStruct((adapters,) + shape, F32) for shape in tables),
        ],
        in_specs=[*(whole(array) for array in inputs), rows_spec, rows_spec],
        out_specs=[rows_spec, rows_spec, *(part((adapters // steps,) + shape) for shape in tables)],
        compiler_params=pltpu.CompilerParams(vmem_limit_bytes=VMEM_LIMIT),
        name="assemble",
    )(*inputs, outcome, grad_tokens)


def heads_body(
    tokens,
    cotangent,
    sequence_adapter_index,
    query_key_value_weight,
    output_weight,
    first_feed_weight,
    second_feed_weight,
    biases,
    value_bias_vector,
    first_feed_bias,
    norm_gain_pair,
    adapter_down_factors,
    output_down_factor,
    adapter_up_factors,
    hidden_up_factor,
    hidden_down_factor,
):
    width = tokens.shape[2]
    hidden = first_feed_bias.shape[0]
    outcome, grad_tokens, chosen, term_hd, term_uh, term_down, term_up, term_do, *_ = run_layer(
        sequence_adapter_index,
        tokens[0],
        cotangent[0],
        (query_key_value_weight, output_weight, first_feed_weight, second_feed_weight),
        (
            adapter_down_factors.reshape(-1, width),
            adapter_up_factors.reshape(-1, width),
            output_down_factor.reshape(-1, width),
            hidden_up_factor.reshape(-1, hidden),
            hidden_down_factor.reshape(-1, hidden),
        ),
        biases,
        value_bias_vector[None],
        first_feed_bias[None],
        norm_gain_pair,
    )
    outcome, grad_tokens, total_down, total_out_down, total_up, total_hidden_up, total_hidden_down = assemble(
        chosen, (term_down, term_do, term_up, term_uh, term_hd), outcome, grad_tokens
    )
    return (
        outcome[None],
        grad_tokens[None],
        total_down,
        total_out_down.reshape(output_down_factor.shape),
        total_up,
        total_hidden_up.reshape(hidden_up_factor.shape),
        total_hidden_down.reshape(hidden_down_factor.shape),
    )


def solution(mesh):
    one_head_each = mesh.shape["ctx"] == H and mesh.shape["fsdp"] == 2
    return jax.shard_map(
        heads_body if one_head_each else gather_body,
        mesh=mesh,
        in_specs=(
            P("fsdp", "ctx", None),
            P("fsdp", "ctx", None),
            P("fsdp"),
            P("fsdp", None),
            P("fsdp", None),
            P("fsdp", None),
            P("fsdp", None),
            P(),
            P(),
            P(),
            P(),
            P(),
            P(),
            P(),
            P(),
            P(),
        ),
        out_specs=(P("fsdp", "ctx", None), P("fsdp", "ctx", None), P(), P(), P(), P(), P()),
        check_vma=False,
    )
```
